32 devices in a mesh: section: 2 (over core), ctx: 4 (over y, x), fsdp: 4 (over z).
Axes of the slice: x: 2, y: 2, z: 4, core: 2. Of those that a mesh axis runs over, the one named last changes fastest.
Arguments:
- tokens: bfloat16 [2, 4, 1024, 1536], P(None, 'fsdp', 'ctx'), may hold values from -6 to 6
- block_of: int32 [8], replicated, may hold values from 0 to 7, as said below
- routes: int32 [2, 2, 4, 1024, 4], P('section', None, 'fsdp', 'ctx'), may hold values from 0 to 7, all different within a row; in each aligned block of 256 rows (0 to 255, 256 to 511, ..., all dimensions but the last counted through in order) at most 160 rows name the same one
- combine: float32 [2, 2, 4, 1024, 4], P('section', None, 'fsdp', 'ctx'), may hold values from 0.25 to 0.75
- attn_norm: bfloat16 [2, 1536], P('section', ('ctx', 'fsdp')), may hold values from 0.5 to 1.5
- w_query: bfloat16 [2, 1536, 1536], P('section', ('ctx', 'fsdp')), may hold values from -0.15625 to 0.15625
- w_key: bfloat16 [2, 1536, 256], P('section', ('ctx', 'fsdp')), may hold values from -0.15625 to 0.15625
- w_value: bfloat16 [2, 1536, 256], P('section', ('ctx', 'fsdp')), may hold values from -0.15625 to 0.15625
- w_out: bfloat16 [2, 1536, 1536], P('section', ('ctx', 'fsdp')), may hold values from -0.875 to 0.875
- ffn_norm: bfloat16 [2, 1536], P('section', ('ctx', 'fsdp')), may hold values from 0.5 to 1.5
- w_gate: bfloat16 [2, 8, 1536, 768], P('section', None, ('ctx', 'fsdp')), may hold values from -0.15625 to 0.15625
- w_up: bfloat16 [2, 8, 1536, 768], P('section', None, ('ctx', 'fsdp')), may hold values from -0.15625 to 0.15625
- w_down: bfloat16 [2, 8, 768, 1536], P('section', None, ('ctx', 'fsdp')), may hold values from -0.21875 to 0.21875
- out_grad: bfloat16 [2, 4, 1024, 1536], P(None, 'fsdp', 'ctx'), may hold values from -6 to 6
Outputs:
- layer_out: bfloat16 [2, 2, 4, 1024, 1536], P('section', None, 'fsdp', 'ctx')
- input_grads: float32 [2, 2, 4, 1024, 1536], P('section', None, 'fsdp', 'ctx')
- grad_attn_norm: float32 [2, 1536], P('section', ('ctx', 'fsdp'))
- grad_query: float32 [2, 1536, 1536], P('section', ('ctx', 'fsdp'))
- grad_key: float32 [2, 1536, 256], P('section', ('ctx', 'fsdp'))
- grad_value: float32 [2, 1536, 256], P('section', ('ctx', 'fsdp'))
- grad_out: float32 [2, 1536, 1536], P('section', ('ctx', 'fsdp'))
- grad_ffn_norm: float32 [2, 1536], P('section', ('ctx', 'fsdp'))
- grad_gate: float32 [2, 8, 1536, 768], P('section', None, ('ctx', 'fsdp'))
- grad_up: float32 [2, 8, 1536, 768], P('section', None, ('ctx', 'fsdp'))
- grad_down: float32 [2, 8, 768, 1536], P('section', None, ('ctx', 'fsdp'))
The draws below stay inside these ranges and needn't reach their ends.
Inputs may be any that keep to these rules, and one draw needn't show every extreme that they name: `block_of`: context index c holds slots 2c and 2c + 1 of every sequence; these hold causal blocks k and 7 - k for some k, and every block is held once. `routes`: A token's 4 experts differ. In each aligned block of 256 rows (the rows of one device in one micro-batch, one section) no expert is named by more than 160 rows, and in some blocks one is named by exactly 160.
All inputs are finite; a program needn't handle non-finite values.
Results may differ from the reference program's by a relative error of at most 0.025.
Values may be sent and summed in bfloat16 or wider, within the bound.
No kernel may reach another device: no remote copies, remote signals or barrier semaphores. Data moves between devices by JAX's collectives and lax.ppermute only.
A program may use at most 448 MiB of HBM per device.

```python
import math
from functools import partial
import jax
import jax.numpy as jnp
import numpy as np
from jax import lax

D = 1536
QH = 12
KVH = 2
HD = 128
F = 768
TOP = 4
EXPERTS = 8
MB = 2
ROWS = 256
LEN = 1024
HALF = 128
NBLK = 8
SEQS = 4
QW = 1536
KW = 256
CAP = 160


def draw_block_of(key, part):
    key = jax.random.fold_in(key, 7)
    order_key, flip_key = jax.random.split(key)
    pair_count = NBLK // 2
    order = jax.random.permutation(order_key, pair_count).astype(jnp.int32)
    flips = jax.random.randint(flip_key, (pair_count,), 0, 2).astype(jnp.int32)
    mirror = (NBLK - 1 - order).astype(jnp.int32)
    former = jnp.where(flips == 1, mirror, order)
    latter = jnp.where(flips == 1, order, mirror)
    return jnp.stack([former, latter], axis=1).reshape(NBLK).astype(jnp.int32)


def steps_of(own_key, dims, cuts, least, largest):
    def one(position, blocks):
        steps = jax.random.uniform(jax.random.fold_in(jax.random.fold_in(own_key, 6), position), (blocks,), jnp.float32, least / len(cuts), largest / len(cuts))
        return jnp.repeat(jnp.exp(steps), dims[position] // blocks).reshape((-1,) + (1,) * (len(dims) - position - 1))

    level = one(*cuts[0])
    for cut in cuts[1:]:
        level = level * one(*cut)
    return level


def deal_out(own_key, own, number, rows, count, top, reach, lean):
    order = jax.random.permutation(own_key, count)
    crowded, ordinary = portions_of(count, rows * top, reach, lean, True), portions_of(count, rows * top, reach, lean, False)
    places = jnp.arange(count)

    def named(sizes, offset_by):
        used = int((sizes > 0).sum())
        fixed = max(1, used // 4)
        moved = fixed + (places - fixed + offset_by * (used - fixed)) % max(1, count - fixed)
        return jnp.zeros((count,), jnp.int32).at[order[jnp.where(places < fixed, places, moved)]].set(jnp.asarray(sizes, jnp.int32))

    sizes = jnp.where(number % 4 == 0, named(crowded, number // 4), named(ordinary, number - number // 4 - 1))
    mixed = jax.random.permutation(jax.random.fold_in(own, 3), count)
    source_of, sink = mixed[0:count // 2 * 2:2], mixed[1:count // 2 * 2:2]
    room = jnp.minimum(sizes[source_of] - 1, reach - sizes[sink]) // 2
    room = jnp.where((source_of == order[0]) | (sink == order[0]) | (sizes[sink] == 0), 0, jnp.maximum(room, 0))
    moved = jax.random.randint(jax.random.fold_in(own, 4), (count // 2,), 0, 1 << 20) % (room + 1)
    sizes = sizes.at[source_of].add(-moved).at[sink].add(moved)
    members = jnp.searchsorted(jnp.cumsum(sizes), jnp.arange(rows * top), side="right").astype(jnp.int32)
    table = members.reshape(top, rows).T
    table = table[jax.random.permutation(jax.random.fold_in(own, 1), rows)]
    offset_by = jax.random.randint(jax.random.fold_in(own, 2), (rows, 1), 0, top)
    return jnp.take_along_axis(table, (jnp.arange(top)[None, :] + offset_by) % top, axis=1)


def portions_of(count, total, bound, slope, full):
    portions = [(1 << 20) // math.isqrt(rank ** slope) + 1 for rank in range(1, count + 1)]
    largest = bound if full else min(bound, max(-(-total // count), total * portions[0] // sum(portions)))
    least = 1 if total - largest >= count - 1 else 0
    counts, rest = [largest] + [least] * (count - 1), total - largest - least * (count - 1)
    while rest > 0:
        free = [i for i in range(1, count) if counts[i] < largest] or [i for i in range(1, count) if counts[i] < bound]
        whole, remaining = sum([portions[i] for i in free]), rest
        for i in free:
            more = min(bound - counts[i], max(1, remaining * portions[i] // whole), rest)
            counts[i] = counts[i] + more
            rest = rest - more
    return np.array(counts)


def scatter_about(stream_key, extent, deviation, bound, shards=(), held_as=jnp.bfloat16):
    result = jax.random.normal(stream_key, extent, jnp.float32) * deviation
    if len(shards) > 0:
        result = steps_of(stream_key, extent, shards, -0.22, 0.18) * result
    return jnp.clip(result, min=-bound, max=bound).astype(held_as)


def setup_inputs(seed: int = 0) -> dict:
    arg_keys = jax.random.split(jax.random.key(seed), 15)
    tokens = scatter_about(arg_keys[0], (MB, SEQS, LEN, D), 1.0, 6.0, ((1, 4), (2, 4)))
    block_of = draw_block_of(jax.random.fold_in(arg_keys[14], 71), 0)
    routes_keys = jax.random.split(jax.random.fold_in(arg_keys[2], 1), 2 * MB * SEQS * LEN // ROWS)
    routes_turns = jax.random.permutation(jax.random.fold_in(arg_keys[2], 3), 2 * MB * SEQS * LEN // ROWS)
    routes = jax.vmap(lambda own, number: deal_out(jax.random.fold_in(arg_keys[2], 2), own, number, ROWS, EXPERTS, TOP, CAP, 1))(routes_keys, routes_turns).reshape((2, MB, SEQS, LEN, TOP))
    combine = jnp.clip(0.25 + 0.5 * jax.random.uniform(arg_keys[3], (2, MB, SEQS, LEN, TOP), jnp.float32) ** steps_of(arg_keys[3], (2, MB, SEQS, LEN, TOP), ((0, 2), (2, 4), (3, 4)), -0.2, 0.2), 0.25, 0.75)
    attn_norm = jnp.clip(1.0 + 0.1 * jax.random.normal(arg_keys[4], (2, D), jnp.float32), 0.5, 1.5).astype(jnp.bfloat16)
    w_query = scatter_about(arg_keys[5], (2, D, QW), D ** -0.5, 0.15625, ((0, 2), (1, 16)))
    w_key = scatter_about(arg_keys[6], (2, D, KW), D ** -0.5, 0.15625, ((0, 2), (1, 16)))
    w_value = scatter_about(arg_keys[7], (2, D, KW), D ** -0.5, 0.15625, ((0, 2), (1, 16)))
    w_out = scatter_about(arg_keys[8], (2, QW, D), (QW // 32) ** -0.5, 0.875, ((0, 2), (1, 16)))
    ffn_norm = jnp.clip(1.0 + 0.1 * jax.random.normal(arg_keys[9], (2, D), jnp.float32), 0.5, 1.5).astype(jnp.bfloat16)
    w_gate = scatter_about(arg_keys[10], (2, EXPERTS, D, F), D ** -0.5, 0.15625, ((0, 2), (2, 16)))
    w_up = scatter_about(arg_keys[11], (2, EXPERTS, D, F), D ** -0.5, 0.15625, ((0, 2), (2, 16)))
    w_down = scatter_about(arg_keys[12], (2, EXPERTS, F, D), F ** -0.5, 0.21875, ((0, 2), (2, 16)))
    out_grad = scatter_about(arg_keys[13], (MB, SEQS, LEN, D), 1.0, 6.0, ((1, 4), (2, 4)))
    return {"tokens": tokens, "block_of": block_of, "routes": routes, "combine": combine, "attn_norm": attn_norm, "w_query": w_query, "w_key": w_key, "w_value": w_value, "w_out": w_out, "ffn_norm": ffn_norm, "w_gate": w_gate, "w_up": w_up, "w_down": w_down, "out_grad": out_grad}


epsilon = 1e-06
masked_out = -1e+30
highest = lax.Precision.HIGHEST

@jax.custom_vjp
def low(v):
    return lax.optimization_barrier(v.astype(jnp.bfloat16)).astype(jnp.float32)

@jax.custom_vjp
def low_back(v):
    return v

def low_keep(v):
    return (low(v), None)

def low_pass(kept, grad):
    return (grad,)

def back_keep(v):
    return (v, None)

def back_low(kept, grad):
    return (low(grad),)
low.defvjp(low_keep, low_pass)
low_back.defvjp(back_keep, back_low)

def product(left, right):
    return jnp.dot(left, right, precision=highest, preferred_element_type=jnp.float32)

def rms_norm(rows_in, gain):
    return rows_in * lax.rsqrt(lax.optimization_barrier(jnp.mean(rows_in * rows_in, axis=-1, keepdims=True)) + epsilon) * gain

def dispatch(route_rows, capacity):
    flat_routes = route_rows.reshape(-1).astype(jnp.int32)
    expert_hits = (flat_routes[:, None] == jnp.arange(EXPERTS, dtype=jnp.int32)[None, :]).astype(jnp.int32)
    slot_rank = lax.optimization_barrier(jnp.sum((jnp.cumsum(expert_hits, axis=0) - expert_hits) * expert_hits, axis=1))
    placing = (flat_routes * capacity + slot_rank).astype(jnp.int32)
    owners = jnp.arange(flat_routes.shape[0], dtype=jnp.int32) // TOP
    slot_rows = jnp.zeros((EXPERTS * capacity,), jnp.int32).at[placing].set(owners)
    filled = jnp.zeros((EXPERTS * capacity,), jnp.float32).at[placing].set(1.0)
    return (placing, slot_rows, filled)

def attend(params, positions, sequence_in):
    gain_attn, weight_query, weight_key, weight_value, weight_out = params[:5]
    normed = low(rms_norm(sequence_in, gain_attn))
    queries = low(low_back(product(normed, weight_query))).reshape(LEN, KVH, QH // KVH, HD)
    key_rows = low(low_back(product(normed, weight_key))).reshape(LEN, KVH, HD)
    value_rows = low(low_back(product(normed, weight_value))).reshape(LEN, KVH, HD)
    scores = jnp.einsum('qkgd,skd->kgqs', queries, key_rows, precision=highest) * HD ** (-0.5)
    scores = low_back(scores)
    allowed = positions[:, None] >= positions[None, :]
    scores = jnp.where(allowed[None, None], scores, masked_out)
    row_max = lax.optimization_barrier(jnp.max(scores, axis=-1, keepdims=True))
    shifted = jnp.exp(scores - row_max)
    attention_weights = low(shifted / lax.optimization_barrier(jnp.sum(shifted, axis=-1, keepdims=True)))
    attended = jnp.einsum('kgqs,skd->qkgd', attention_weights, value_rows, precision=highest).reshape(LEN, QW)
    attended = low(low_back(attended))
    return sequence_in + low_back(product(attended, weight_out))

def experts_block(params, packed):
    gain_ffn, weight_gate, weight_up, weight_down = params[5:]
    block_rows, route_rows, share_rows = packed
    placing, slot_rows, filled = dispatch(route_rows, CAP)
    ffn_normed = low(rms_norm(block_rows, gain_ffn))
    picked = (ffn_normed[slot_rows] * filled[:, None]).reshape(EXPERTS, CAP, D)
    gate_pre = low_back(jnp.einsum('ecd,edf->ecf', picked, weight_gate, precision=highest))
    up_pre = low_back(jnp.einsum('ecd,edf->ecf', picked, weight_up, precision=highest))
    active = low(jax.nn.gelu(gate_pre, approximate=True) * up_pre)
    expert_out = low_back(jnp.einsum('ecf,efd->ecd', active, weight_down, precision=highest)).reshape(EXPERTS * CAP, D)
    returned = expert_out[placing].reshape(ROWS, TOP, D)
    return block_rows + lax.optimization_barrier(jnp.sum(returned * share_rows[:, :, None], axis=1))

def whole_layer(layer_in, params, route_all, share_all, positions):
    after_attention = lax.map(jax.checkpoint(partial(attend, params, positions)), layer_in)
    blocks = after_attention.reshape(-1, ROWS, D)
    packed = (blocks, route_all.reshape(-1, ROWS, TOP), share_all.reshape(-1, ROWS, TOP))
    out_blocks = lax.map(jax.checkpoint(partial(experts_block, params)), packed)
    return out_blocks.reshape(layer_in.shape)

def reference(tokens, block_of, routes, combine, attn_norm, w_query, w_key, w_value, w_out, ffn_norm, w_gate, w_up, w_down, out_grad):
    positions = (block_of[:, None] * HALF + jnp.arange(HALF, dtype=jnp.int32)[None, :]).reshape(LEN).astype(jnp.int32)
    weights = (attn_norm, w_query, w_key, w_value, w_out, ffn_norm, w_gate, w_up, w_down)
    first_params = tuple((array[0].astype(jnp.float32) for array in weights))
    second_params = tuple((array[1].astype(jnp.float32) for array in weights))
    shape_flat = (MB * SEQS, LEN, D)
    shares = combine.astype(jnp.float32)

    def first_layer(layer_in, params):
        return whole_layer(layer_in, params, routes[0], shares[0], positions)

    def second_layer(layer_in, params):
        return whole_layer(layer_in, params, routes[1], shares[1], positions)
    first_out, first_back = jax.vjp(first_layer, tokens.astype(jnp.float32).reshape(shape_flat), first_params)
    second_in = lax.optimization_barrier(first_out.astype(jnp.bfloat16)).astype(jnp.float32)
    second_out, second_back = jax.vjp(second_layer, second_in, second_params)
    second_grad, second_terms = second_back(out_grad.astype(jnp.float32).reshape(shape_flat))
    sent_grad = lax.optimization_barrier(second_grad.astype(jnp.bfloat16)).astype(jnp.float32)
    first_grad, first_terms = first_back(sent_grad)
    full = (2, MB, SEQS, LEN, D)
    layer_out = jnp.stack([first_out, second_out]).reshape(full).astype(jnp.bfloat16)
    input_grads = jnp.stack([first_grad, second_grad]).reshape(full).astype(jnp.float32)
    grads = [jnp.stack([former, latter]).astype(jnp.float32) for former, latter in zip(first_terms, second_terms)]
    return (layer_out, input_grads, grads[0], grads[1], grads[2], grads[3], grads[4], grads[5], grads[6], grads[7], grads[8])
```

```python
import jax
import jax.numpy as jnp
from jax import lax
from jax.sharding import PartitionSpec as P

QH = 12
KVH = 2
HD = 128
GROUP = QH // KVH
TOP = 4
EXPERTS = 8
bf16 = jnp.bfloat16
f32 = jnp.float32


epsilon = 1e-06
masked_out = -1e30


def swap(value, axis, bit):
    count = lax.axis_size(axis)
    return lax.ppermute(value, axis, [(source, source ^ bit) for source in range(count)])


def rms_norm(rows_in, gain):
    return rows_in * lax.rsqrt(jnp.mean(rows_in * rows_in, axis=-1, keepdims=True) + epsilon) * gain


def gated_unit(gate_pre, up_pre):
    return jax.nn.gelu(gate_pre, approximate=True) * up_pre


def dot(spec, left, right, kind=f32):
    return jnp.einsum(spec, left, right, preferred_element_type=kind)


def body(
    tokens,
    block_of,
    routes,
    combine,
    attn_norm,
    w_query,
    w_key,
    w_value,
    w_out,
    ffn_norm,
    w_gate,
    w_up,
    w_down,
    out_grad,
):
    layers, micro_count = (2, tokens.shape[0])
    rows = tokens.shape[2]
    width = tokens.shape[3]
    half = rows // 2
    n_ctx = lax.axis_size("ctx")
    n_fsdp = lax.axis_size("fsdp")
    shard_count = n_ctx * n_fsdp
    core = lax.axis_index("section")
    place = lax.axis_index("ctx")
    seq_len = rows * n_ctx
    capacity = rows * TOP * 5 // (4 * EXPERTS)
    score_scale = HD ** (-0.5)
    own_experts = EXPERTS // n_ctx
    hidden = w_gate.shape[3]
    qw = w_query.shape[2]
    kw = w_key.shape[2]
    pieces = max(1, 2 * n_ctx // EXPERTS)

    def to_units(shard):
        count, deep, wide = shard.shape
        if pieces == 1:
            return shard.reshape(2 * n_ctx, count // (2 * n_ctx), deep, wide)
        cut = shard.reshape(count, deep, pieces, wide // pieces).transpose(0, 2, 1, 3)
        return cut.reshape(2 * n_ctx, 1, deep, wide // pieces)

    def join_units(both):
        if pieces == 1:
            return both.reshape((own_experts,) + both.shape[2:])
        return both.transpose(1, 2, 0, 3).reshape(1, both.shape[2], both.shape[3] * pieces)

    def cut_units(whole):
        if pieces == 1:
            return whole.reshape((2, own_experts // 2) + whole.shape[1:])
        deep, wide = whole.shape[1:]
        return whole.reshape(1, deep, pieces, wide // pieces).transpose(2, 0, 1, 3)

    attn_shard = jnp.concatenate([w_query[0], w_key[0], w_value[0], w_out[0]], axis=1)
    attn_own = lax.all_gather(attn_shard, ("ctx", "fsdp"), axis=0, tiled=True)
    attn_both = lax.all_gather(attn_own, "section")
    gain_shard = jnp.stack([attn_norm[0], ffn_norm[0]]).astype(f32)
    gains = lax.all_gather(gain_shard, ("section", "ctx", "fsdp"))
    gains = gains.reshape(layers, shard_count, 2, -1).transpose(0, 2, 1, 3).reshape(layers, 2, width)

    units = [
        lax.all_to_all(to_units(shard[0]), ("ctx", "section"), 0, 0)
        for shard in (w_gate, w_up, w_down)
    ]
    expert_weights = []
    for layer in range(layers):
        gathered = []
        for unit in units:
            mine = unit.reshape((n_ctx, 2) + unit.shape[1:])[:, layer]
            mine = lax.all_gather(mine.transpose(1, 0, 2, 3), "fsdp", axis=2)
            mine = mine.reshape(mine.shape[0], -1, mine.shape[-1])
            gathered.append(join_units(lax.all_gather(mine, "section")))
        expert_weights.append(gathered)

    info = jnp.concatenate([routes.astype(f32), combine], axis=-1)[0, :, 0]
    info = lax.all_gather(info, ("section", "ctx"))
    info = info.reshape((layers, n_ctx) + info.shape[1:])
    info = lax.dynamic_index_in_dim(info, core, 2, keepdims=False)
    order = place ^ jnp.arange(n_ctx, dtype=jnp.int32)
    info = jnp.take(info, order, axis=1)
    named = place * own_experts + jnp.arange(own_experts, dtype=jnp.int32)
    matches = info[:, None, :, :, :TOP] == named.astype(f32)[None, :, None, None, None]
    hits = jnp.any(matches, axis=-1)
    shares = jnp.sum(jnp.where(matches, info[:, None, :, :, TOP:], 0.0), axis=-1)
    earlier = jnp.arange(rows)[:, None] < jnp.arange(rows)[None, :]
    rank = dot("ledr,rq->ledq", hits.astype(bf16), earlier.astype(bf16))
    slots = jnp.arange(capacity, dtype=f32)
    picks = hits[:, :, :, None, :] & (rank[:, :, :, None, :] == slots[:, None])
    slot_shares = jnp.sum(jnp.where(picks, shares[:, :, :, None, :], 0.0), axis=-1)
    picks = picks.astype(bf16)

    slot_ids = block_of.reshape(n_ctx, 2)
    block_ids = jnp.take(slot_ids, order, axis=0)
    positions = (block_ids[:, :, None] * half + jnp.arange(half, dtype=jnp.int32)).reshape(seq_len)
    allowed = positions[:rows, None] >= positions[None, :]

    def spread(value):
        return jnp.stack([value] + [swap(value, "ctx", bit) for bit in range(1, n_ctx)])

    def collect(blocks):
        total = blocks[0].astype(f32)
        for bit in range(1, n_ctx):
            total = total + swap(blocks[bit].astype(bf16), "ctx", bit).astype(f32)
        return total

    def soft_scores(queries, key_all):
        query_heads = queries.reshape(rows, KVH, GROUP, HD)
        key_heads = key_all.reshape(seq_len, KVH, HD)
        scores = dot("qkgd,skd->kgqs", query_heads, key_heads) * score_scale
        return jnp.where(allowed[None, None], scores, masked_out)

    def split_attn(layer):
        whole = attn_both[layer]
        return (
            whole[:, :qw],
            whole[:, qw : qw + kw],
            whole[:, qw + kw : qw + 2 * kw],
            whole[:, qw + 2 * kw :],
        )

    def forward(layer, layer_input):
        weight_query, weight_key, weight_value, weight_out = split_attn(layer)
        normed = rms_norm(layer_input, gains[layer, 0]).astype(bf16)
        queries = dot("qa,ab->qb", normed, weight_query).astype(bf16)
        key_value = jnp.concatenate(
            [
                dot("qa,ab->qb", normed, weight_key).astype(bf16),
                dot("qa,ab->qb", normed, weight_value).astype(bf16),
            ],
            axis=1,
        )
        key_value_all = spread(key_value).reshape(seq_len, 2 * kw)
        key_all, value_all = (key_value_all[:, :kw], key_value_all[:, kw:])
        scores = soft_scores(queries, key_all)
        row_max = jnp.max(scores, axis=-1, keepdims=True)
        shifted = jnp.exp(scores - row_max)
        total = jnp.sum(shifted, axis=-1, keepdims=True)
        attention_weights = (shifted / total).astype(bf16)
        attended = dot("kgqs,skd->qkgd", attention_weights, value_all.reshape(seq_len, KVH, HD))
        attended = attended.reshape(rows, qw).astype(bf16)
        after_attention = layer_input + dot("qa,ab->qb", attended, weight_out)
        ffn_normed = rms_norm(after_attention, gains[layer, 1]).astype(bf16)
        weight_gate, weight_up, weight_down = expert_weights[layer]
        picked = dot("edsr,drw->edsw", picks[layer], spread(ffn_normed), bf16)
        picked = picked.reshape(own_experts, n_ctx * capacity, width)
        gate_pre = dot("emw,ewf->emf", picked, weight_gate)
        up_pre = dot("emw,ewf->emf", picked, weight_up)
        active = gated_unit(gate_pre, up_pre).astype(bf16)
        expert_out = dot("emf,efw->emw", active, weight_down)
        expert_out = expert_out.reshape(own_experts, n_ctx, capacity, width)
        expert_out = (expert_out * slot_shares[layer][..., None]).astype(bf16)
        returned = dot("edsr,edsw->drw", picks[layer], expert_out)
        layer_output = after_attention + collect(returned)
        kept = (
            layer_input,
            normed,
            queries,
            key_all,
            value_all,
            row_max + jnp.log(total),
            attended,
            after_attention,
            picked,
            gate_pre,
            up_pre,
            active,
        )
        return (layer_output, kept)

    def backward(layer, kept, cotangent):
        (
            layer_input,
            normed,
            queries,
            key_all,
            value_all,
            log_totals,
            attended,
            after_attention,
            picked,
            gate_pre,
            up_pre,
            active,
        ) = kept
        weight_query, weight_key, weight_value, weight_out = split_attn(layer)
        weight_gate, weight_up, weight_down = expert_weights[layer]
        cot_slots = dot("edsr,drw->edsw", picks[layer], spread(cotangent))
        cot_slots = (cot_slots * slot_shares[layer][..., None]).astype(bf16)
        cot_slots = cot_slots.reshape(own_experts, n_ctx * capacity, width)
        d_active = dot("emw,efw->emf", cot_slots, weight_down)
        d_gate, d_up = jax.vjp(gated_unit, gate_pre, up_pre)[1](d_active)
        d_gate = d_gate.astype(bf16)
        d_up = d_up.astype(bf16)
        d_picked = dot("emf,ewf->emw", d_gate, weight_gate) + dot("emf,ewf->emw", d_up, weight_up)
        d_picked = d_picked.astype(bf16).reshape(own_experts, n_ctx, capacity, width)
        d_ffn_normed = collect(dot("edsr,edsw->drw", picks[layer], d_picked))
        grad_down = dot("emf,emw->efw", active, cot_slots, bf16)
        grad_gate = dot("emw,emf->ewf", picked, d_gate, bf16)
        grad_up = dot("emw,emf->ewf", picked, d_up, bf16)
        ffn_back = jax.vjp(rms_norm, after_attention, gains[layer, 1])[1]
        d_after, grad_gain_ffn = ffn_back(d_ffn_normed)
        d_after = d_after + cotangent.astype(f32)
        d_branch = d_after.astype(bf16)
        grad_out = dot("qa,qb->ab", attended, d_branch, bf16)
        d_attended = dot("qb,ab->qa", d_branch, weight_out).astype(bf16)
        probs_full = jnp.exp(soft_scores(queries, key_all) - log_totals)
        attention_weights = probs_full.astype(bf16)
        d_heads = d_attended.reshape(rows, KVH, GROUP, HD)
        key_heads = key_all.reshape(seq_len, KVH, HD)
        value_heads = value_all.reshape(seq_len, KVH, HD)
        query_heads = queries.reshape(rows, KVH, GROUP, HD)
        d_value_all = dot("kgqs,qkgd->skd", attention_weights, d_heads)
        d_probs = dot("qkgd,skd->kgqs", d_heads, value_heads)
        inner = jnp.sum(probs_full * d_probs, axis=-1, keepdims=True)
        d_scores = (probs_full * (d_probs - inner)).astype(bf16)
        d_queries = dot("kgqs,skd->qkgd", d_scores, key_heads) * score_scale
        d_queries = d_queries.reshape(rows, qw).astype(bf16)
        d_key_all = dot("kgqs,qkgd->skd", d_scores, query_heads) * score_scale
        d_key_value = jnp.concatenate(
            [d_key_all.reshape(n_ctx, rows, kw), d_value_all.reshape(n_ctx, rows, kw)], axis=2
        )
        d_key_value = collect(d_key_value).astype(bf16)
        d_key, d_value = (d_key_value[:, :kw], d_key_value[:, kw:])
        d_normed = dot("qb,ab->qa", d_queries, weight_query)
        d_normed = d_normed + dot("qb,ab->qa", d_key, weight_key)
        d_normed = d_normed + dot("qb,ab->qa", d_value, weight_value)
        grad_query = dot("qa,qb->ab", normed, d_queries, bf16)
        grad_key = dot("qa,qb->ab", normed, d_key, bf16)
        grad_value = dot("qa,qb->ab", normed, d_value, bf16)
        attn_back = jax.vjp(rms_norm, layer_input, gains[layer, 0])[1]
        d_input, grad_gain_attn = attn_back(d_normed)
        d_entry = d_input + d_after
        attn_grads = jnp.stack(
            [
                jnp.concatenate([grad_query, grad_key], axis=1),
                jnp.concatenate([grad_out, grad_value], axis=1),
            ]
        )
        attn_grads = lax.psum_scatter(attn_grads, "section", scatter_dimension=0)
        attn_grads = lax.psum_scatter(
            attn_grads, ("ctx", "fsdp"), scatter_dimension=0, tiled=True
        )
        expert_grads = []
        for grad in (grad_gate, grad_up, grad_down):
            part = lax.psum_scatter(cut_units(grad), "section", scatter_dimension=0)
            part = part.reshape(part.shape[0], n_ctx, n_fsdp, -1, part.shape[-1])
            part = lax.psum_scatter(part, "fsdp", scatter_dimension=2)
            part = lax.all_to_all(part.transpose(1, 0, 2, 3), "ctx", 0, 0)
            expert_grads.append(part)
        return (d_entry, (grad_gain_attn, grad_gain_ffn), attn_grads, expert_grads)

    def on_core(former, latter):
        return jnp.where(core == 0, former, latter)

    first_in = lax.dynamic_index_in_dim(tokens, core, 0, keepdims=False)[0].astype(f32)
    first_out, first_kept = forward(0, first_in)
    first_sent = first_out.astype(bf16)
    second_out, second_kept = forward(1, first_sent.astype(f32))
    second_sent = second_out.astype(bf16)
    cotangent = lax.dynamic_index_in_dim(out_grad, core, 0, keepdims=False)[0]
    second_entry, second_gains, second_attn, second_experts = backward(1, second_kept, cotangent)
    first_entry, first_gains, first_attn, first_experts = backward(
        0, first_kept, second_entry.astype(bf16)
    )

    def keep_own(first, second):
        mine, other = (on_core(first, second), swap(on_core(second, first), "section", 1))
        return (on_core(mine, other), on_core(other, mine))

    layer_out = jnp.stack(keep_own(first_sent, second_sent))
    input_grads = jnp.stack(keep_own(first_entry, second_entry))
    former, latter = keep_own(first_attn.astype(f32), second_attn.astype(f32))
    grad_query, grad_key = (former[:, :qw], former[:, qw:])
    grad_out, grad_value = (latter[:, :qw], latter[:, qw:])
    grad_experts = []
    for first, second in zip(first_experts, second_experts):
        former, latter = keep_own(first, second)
        if pieces == 1:
            whole = jnp.stack([former, latter], axis=1)
            whole = whole.reshape((EXPERTS,) + whole.shape[3:])
        else:
            whole = jnp.concatenate([former, latter], axis=-1)[:, 0]
        grad_experts.append(whole.astype(f32))
    gain_grads = jnp.stack([jnp.stack(first_gains), jnp.stack(second_gains)])
    gain_grads = gain_grads.reshape(layers, 2, shard_count, -1).transpose(0, 2, 1, 3)
    gain_grads = gain_grads.reshape(layers * shard_count, 2, -1)
    gain_grads = lax.psum_scatter(gain_grads, ("section", "ctx", "fsdp"), scatter_dimension=0)
    return (
        layer_out[None, :, None],
        input_grads[None, :, None],
        gain_grads[0][None],
        grad_query[None],
        grad_key[None],
        grad_value[None],
        grad_out[None],
        gain_grads[1][None],
        grad_experts[0][None],
        grad_experts[1][None],
        grad_experts[2][None],
    )


def solution(mesh):
    rows_placed = P(None, "fsdp", "ctx", None)
    kept_placed = P("section", None, "fsdp", "ctx", None)
    gain_placed = P("section", ("ctx", "fsdp"))
    dense_placed = P("section", ("ctx", "fsdp"), None)
    expert_placed = P("section", None, ("ctx", "fsdp"), None)
    return jax.shard_map(
        body,
        mesh=mesh,
        in_specs=(
            rows_placed,
            P(),
            kept_placed,
            kept_placed,
            gain_placed,
            dense_placed,
            dense_placed,
            dense_placed,
            dense_placed,
            gain_placed,
            expert_placed,
            expert_placed,
            expert_placed,
            rows_placed,
        ),
        out_specs=(
            kept_placed,
            kept_placed,
            gain_placed,
            dense_placed,
            dense_placed,
            dense_placed,
            dense_placed,
            gain_placed,
            expert_placed,
            expert_placed,
            expert_placed,
        ),
        check_vma=False,
    )
```

```python
import jax
import jax.numpy as jnp
from jax import lax
from jax.sharding import PartitionSpec as P

QH = 12
KVH = 2
HD = 128
GROUP = QH // KVH
TOP = 4
EXPERTS = 8
bf16 = jnp.bfloat16
f32 = jnp.float32


epsilon = 1e-06
masked_out = -1e30


def swap(value, axis, bit):
    count = lax.axis_size(axis)
    return lax.ppermute(value, axis, [(source, source ^ bit) for source in range(count)])


def rms_norm(rows_in, gain):
    return rows_in * lax.rsqrt(jnp.mean(rows_in * rows_in, axis=-1, keepdims=True) + epsilon) * gain


def gated_unit(gate_pre, up_pre):
    return jax.nn.gelu(gate_pre, approximate=True) * up_pre


def dot(spec, left, right, kind=f32):
    return jnp.einsum(spec, left, right, preferred_element_type=kind)


def body(
    tokens,
    block_of,
    routes,
    combine,
    attn_norm,
    w_query,
    w_key,
    w_value,
    w_out,
    ffn_norm,
    w_gate,
    w_up,
    w_down,
    out_grad,
):
    layers, micro_count = (2, tokens.shape[0])
    rows = tokens.shape[2]
    width = tokens.shape[3]
    half = rows // 2
    n_ctx = lax.axis_size("ctx")
    n_fsdp = lax.axis_size("fsdp")
    shard_count = n_ctx * n_fsdp
    core = lax.axis_index("section")
    place = lax.axis_index("ctx")
    depth = lax.axis_index("fsdp")
    seq_len = rows * n_ctx
    capacity = rows * TOP * 5 // (4 * EXPERTS)
    score_scale = HD ** (-0.5)
    own_experts = EXPERTS // n_ctx
    hidden = w_gate.shape[3]
    qw = w_query.shape[2]
    kw = w_key.shape[2]
    pieces = max(1, 2 * n_ctx // EXPERTS)
    per_core = max(1, EXPERTS // (2 * n_ctx))
    gap = 128

    def on_core(former, latter):
        return jnp.where(core == 0, former, latter)

    def at(value, index, axis=0):
        return lax.dynamic_index_in_dim(value, index, axis, keepdims=False)

    def put(buffer, value, index, axis=0):
        return lax.dynamic_update_index_in_dim(buffer, value, index, axis)

    def after(value, earlier):
        return lax.optimization_barrier((value, earlier))[0]

    def column(gain):
        return jnp.pad(gain.astype(bf16)[:, None], ((0, 0), (0, gap - 1)))

    def to_units(shard):
        count, deep, wide = shard.shape
        if pieces == 1:
            return shard
        cut = shard.reshape(count, deep, pieces, wide // pieces).transpose(0, 2, 1, 3)
        return cut.reshape(2 * n_ctx, deep, wide // pieces)

    def ring_gather(value, axis):
        ring = list(range(0, n_fsdp, 2)) + list(range(1, n_fsdp, 2))[::-1]
        spot = [ring.index(index) for index in range(n_fsdp)]
        here = jnp.array(spot, jnp.int32)[depth]
        order = jnp.array(ring, jnp.int32)
        steps = [(ring[i], ring[(i + 1) % n_fsdp]) for i in range(n_fsdp)]
        lead, rest = (value.shape[:axis], value.shape[axis:])
        buffer = put(jnp.zeros(lead + (n_fsdp,) + rest, value.dtype), value, depth, axis)
        for step in range(1, n_fsdp):
            value = lax.ppermute(value, "fsdp", steps)
            buffer = put(buffer, value, order[(here - step) % n_fsdp], axis)
        return buffer

    def square(value):
        if n_ctx != 4:
            return [value] + [swap(value, "ctx", bit) for bit in range(1, n_ctx)]
        beside, below = (swap(value, "ctx", 1), swap(value, "ctx", 2))
        cut = value.shape[0] // 2
        far = (swap(below[:cut], "ctx", 1), swap(beside[cut:], "ctx", 2))
        return [value, beside, below, jnp.concatenate(far)]

    info = jnp.concatenate([routes.astype(f32), combine], axis=-1)[0, :, 0].transpose(0, 2, 1)
    info_own, info_other = (at(info, core), swap(at(info, 1 - core), "section", 1))
    info = jnp.stack([on_core(info_own, info_other), on_core(info_other, info_own)])
    info = jnp.stack([info] + [swap(info, "ctx", bit) for bit in range(1, n_ctx)], axis=1)

    own_first = jnp.concatenate([w_query[0], w_key[0], column(attn_norm[0])], axis=1)
    own_last = jnp.concatenate([w_out[0], w_value[0], column(ffn_norm[0])], axis=1)
    lent = swap(on_core(own_last, own_first), "section", 1)
    attn_shards = [on_core(own_first, lent), on_core(lent, own_last)]

    def gather_attn(shard):
        deep = ring_gather(shard, 0)
        blocks = square(deep)
        buffer = jnp.zeros((n_ctx,) + deep.shape, bf16)
        for bit in range(n_ctx):
            buffer = put(buffer, blocks[bit], place ^ bit)
        return buffer.reshape(width, shard.shape[1])

    def pair_attn(mine):
        other = swap(mine, "section", 1)
        first, last = (on_core(mine, other), on_core(other, mine))
        gain_attn, gain_ffn = (first[:, qw + kw].astype(f32), last[:, qw + kw].astype(f32))
        return (
            (first[:, :qw], first[:, qw : qw + kw], last[:, qw : qw + kw], last[:, :qw]),
            (gain_attn, gain_ffn),
        )

    unit_stack = jnp.concatenate(
        [
            jnp.concatenate([to_units(w_gate[0]), to_units(w_up[0])], axis=2),
            to_units(w_down[0]),
        ],
        axis=1,
    )
    unit_stack = unit_stack.reshape((n_ctx, 2, per_core) + unit_stack.shape[1:])
    both_axes = ("section", "ctx")

    def deal_units(layer, stack):
        received = jnp.zeros((n_ctx,) + stack.shape[2:], bf16)
        for bit in range(n_ctx):
            target = at(stack, place ^ bit)
            straight = [(layer * n_ctx + c, layer * n_ctx + (c ^ bit)) for c in range(n_ctx)]
            across = [(layer * n_ctx + c, (1 - layer) * n_ctx + (c ^ bit)) for c in range(n_ctx)]
            same = target[layer]
            if bit > 0:
                same = lax.ppermute(same, both_axes, straight)
            cross = lax.ppermute(target[1 - layer], both_axes, across)
            block = jnp.where(core == layer, same, cross)
            received = put(received, block, place ^ bit)
        return received.transpose(1, 0, 2, 3)

    def pair_units(mine):
        mine = (mine[:, :, :, : width // shard_count], mine[:, :, :, width // shard_count :])
        mine = [part.reshape(part.shape[0], -1, part.shape[-1]) for part in mine]
        other = [swap(part, "section", 1) for part in mine]
        if pieces == 1:
            return [jnp.concatenate([a, b]) for a, b in zip(mine, other)]
        low = [on_core(a, b) for a, b in zip(mine, other)]
        high = [on_core(b, a) for a, b in zip(mine, other)]
        cut = low[0].shape[-1] // 2
        gates = [low[0][..., :cut], high[0][..., :cut], low[0][..., cut:], high[0][..., cut:]]
        return [jnp.concatenate(gates, axis=-1), jnp.concatenate([low[1], high[1]], axis=-1)]

    units_first = deal_units(0, unit_stack)
    attn_first = gather_attn(attn_shards[0])
    gathered_first = ring_gather(units_first, 2)
    units_second = deal_units(1, after(unit_stack, attn_first))
    attn_second = gather_attn(after(attn_shards[1], gathered_first))
    gathered_second = lax.all_gather(after(units_second, attn_second), "fsdp", axis=2)
    attn_pairs = [pair_attn(attn_first), pair_attn(attn_second)]
    expert_weights = [pair_units(gathered_first), pair_units(gathered_second)]
    gains = [pair[1] for pair in attn_pairs]

    units_here = jnp.arange(per_core, dtype=jnp.int32)
    if pieces == 1:
        units_here = jnp.concatenate([core * per_core + units_here, (1 - core) * per_core + units_here])
    named = (place * own_experts + units_here).astype(f32)
    matches = info[:, None, :, :TOP] == named[None, :, None, None, None]
    hits = jnp.any(matches, axis=3)
    shares = jnp.sum(jnp.where(matches, info[:, None, :, TOP:], 0.0), axis=3)
    earlier = jnp.arange(rows)[:, None] < jnp.arange(rows)[None, :]
    rank = dot("ledr,rq->ledq", hits.astype(bf16), earlier.astype(bf16))
    slots = jnp.arange(capacity, dtype=f32)
    picks = hits[:, :, :, None, :] & (rank[:, :, :, None, :] == slots[:, None])
    slot_shares = jnp.sum(jnp.where(picks, shares[:, :, :, None, :], 0.0), axis=-1)
    picks = picks.astype(bf16)
    order = place ^ jnp.arange(n_ctx, dtype=jnp.int32)

    slot_ids = block_of.reshape(n_ctx, 2)
    block_ids = jnp.take(slot_ids, order, axis=0)
    positions = (block_ids[:, :, None] * half + jnp.arange(half, dtype=jnp.int32)).reshape(seq_len)
    allowed = positions[:rows, None] >= positions[None, :]

    def spread(value):
        return jnp.stack(square(value))

    def collect(blocks):
        total = blocks[0].astype(f32)
        for bit in range(1, n_ctx):
            total = total + swap(blocks[bit].astype(bf16), "ctx", bit).astype(f32)
        return total

    def soft_scores(queries, key_all):
        query_heads = queries.reshape(rows, KVH, GROUP, HD)
        key_heads = key_all.reshape(seq_len, KVH, HD)
        scores = dot("qkgd,skd->kgqs", query_heads, key_heads) * score_scale
        return jnp.where(allowed[None, None], scores, masked_out)

    def reduce_attn(first, last):
        mine = on_core(first, last).astype(f32)
        mine = (mine + swap(on_core(last, first), "section", 1).astype(f32)).astype(bf16)
        mine = mine.reshape((n_ctx, n_fsdp, -1) + mine.shape[1:])
        total = at(mine, place).astype(f32)
        for bit in range(1, n_ctx):
            total = total + swap(at(mine, place ^ bit), "ctx", bit).astype(f32)
        mine = total.astype(bf16)
        total = at(mine, depth).astype(f32)
        for bit in range(1, n_fsdp):
            total = total + swap(at(mine, depth ^ bit), "fsdp", bit).astype(f32)
        return total

    def cut_units(whole):
        if pieces == 1:
            return (whole[:per_core], whole[per_core:])
        if whole.shape[1] == width:
            deep, wide = whole.shape[1:]
            whole = whole.reshape(1, deep, 2, pieces, wide // (2 * pieces))
            halves = [whole[:, :, :, half].reshape(1, deep, -1) for half in range(2)]
        else:
            halves = jnp.split(whole, 2, axis=2)
        return (on_core(halves[0], halves[1]), on_core(halves[1], halves[0]))

    def reduce_units(grad):
        own, other = cut_units(grad)
        mine = (own.astype(f32) + swap(other, "section", 1).astype(f32)).astype(bf16)
        mine = mine.reshape(mine.shape[0], n_ctx, n_fsdp, -1, mine.shape[-1])
        mine = lax.psum_scatter(mine, "fsdp", scatter_dimension=2)
        return lax.all_to_all(mine.transpose(1, 0, 2, 3), "ctx", 0, 0)

    def forward(layer, layer_input):
        weight_query, weight_key, weight_value, weight_out = attn_pairs[layer][0]
        normed = rms_norm(layer_input, gains[layer][0]).astype(bf16)
        queries = dot("qa,ab->qb", normed, weight_query).astype(bf16)
        key_value = jnp.concatenate(
            [
                dot("qa,ab->qb", normed, weight_key).astype(bf16),
                dot("qa,ab->qb", normed, weight_value).astype(bf16),
            ],
            axis=1,
        )
        key_value_all = spread(key_value).reshape(seq_len, 2 * kw)
        key_all, value_all = (key_value_all[:, :kw], key_value_all[:, kw:])
        scores = soft_scores(queries, key_all)
        row_max = jnp.max(scores, axis=-1, keepdims=True)
        shifted = jnp.exp(scores - row_max)
        total = jnp.sum(shifted, axis=-1, keepdims=True)
        attention_weights = (shifted / total).astype(bf16)
        attended = dot("kgqs,skd->qkgd", attention_weights, value_all.reshape(seq_len, KVH, HD))
        attended = attended.reshape(rows, qw).astype(bf16)
        after_attention = layer_input + dot("qa,ab->qb", attended, weight_out)
        ffn_normed = rms_norm(after_attention, gains[layer][1]).astype(bf16)
        weight_pair, weight_down = expert_weights[layer]
        picked = dot("edsr,drw->edsw", picks[layer], spread(ffn_normed), bf16)
        picked = picked.reshape(own_experts, n_ctx * capacity, width)
        pair_pre = dot("emw,ewf->emf", picked, weight_pair)
        gate_pre, up_pre = (pair_pre[:, :, :hidden], pair_pre[:, :, hidden:])
        active = gated_unit(gate_pre, up_pre).astype(bf16)
        expert_out = dot("emf,efw->emw", active, weight_down)
        expert_out = expert_out.reshape(own_experts, n_ctx, capacity, width)
        expert_out = (expert_out * slot_shares[layer][..., None]).astype(bf16)
        returned = dot("edsr,edsw->drw", picks[layer], expert_out)
        layer_output = after_attention + collect(returned)
        kept = (
            layer_input,
            normed,
            queries,
            key_all,
            value_all,
            row_max + jnp.log(total),
            attended,
            after_attention,
            picked,
            gate_pre,
            up_pre,
            active,
        )
        return (layer_output, kept)

    def backward(layer, kept, cotangent):
        (
            layer_input,
            normed,
            queries,
            key_all,
            value_all,
            log_totals,
            attended,
            after_attention,
            picked,
            gate_pre,
            up_pre,
            active,
        ) = kept
        weight_query, weight_key, weight_value, weight_out = attn_pairs[layer][0]
        weight_pair, weight_down = expert_weights[layer]
        cot_slots = dot("edsr,drw->edsw", picks[layer], spread(cotangent))
        cot_slots = (cot_slots * slot_shares[layer][..., None]).astype(bf16)
        cot_slots = cot_slots.reshape(own_experts, n_ctx * capacity, width)
        d_active = dot("emw,efw->emf", cot_slots, weight_down)
        d_gate, d_up = jax.vjp(gated_unit, gate_pre, up_pre)[1](d_active)
        d_pair = jnp.concatenate([d_gate, d_up], axis=2).astype(bf16)
        d_picked = dot("emf,ewf->emw", d_pair, weight_pair)
        d_picked = d_picked.astype(bf16).reshape(own_experts, n_ctx, capacity, width)
        d_ffn_normed = collect(dot("edsr,edsw->drw", picks[layer], d_picked))
        grad_down = dot("emf,emw->efw", active, cot_slots, bf16)
        grad_pair = dot("emw,emf->ewf", picked, d_pair, bf16)
        expert_grads = [reduce_units(grad) for grad in (grad_pair, grad_down)]
        ffn_back = jax.vjp(rms_norm, after_attention, gains[layer][1])[1]
        d_after, grad_gain_ffn = ffn_back(d_ffn_normed)
        d_after = d_after + cotangent.astype(f32)
        d_branch = d_after.astype(bf16)
        grad_out = dot("qa,qb->ab", attended, d_branch, bf16)
        d_attended = dot("qb,ab->qa", d_branch, weight_out).astype(bf16)
        probs_full = jnp.exp(soft_scores(queries, key_all) - log_totals)
        attention_weights = probs_full.astype(bf16)
        d_heads = d_attended.reshape(rows, KVH, GROUP, HD)
        key_heads = key_all.reshape(seq_len, KVH, HD)
        value_heads = value_all.reshape(seq_len, KVH, HD)
        query_heads = queries.reshape(rows, KVH, GROUP, HD)
        d_value_all = dot("kgqs,qkgd->skd", attention_weights, d_heads)
        d_probs = dot("qkgd,skd->kgqs", d_heads, value_heads)
        inner = jnp.sum(probs_full * d_probs, axis=-1, keepdims=True)
        d_scores = (probs_full * (d_probs - inner)).astype(bf16)
        d_queries = dot("kgqs,skd->qkgd", d_scores, key_heads) * score_scale
        d_queries = d_queries.reshape(rows, qw).astype(bf16)
        d_key_all = dot("kgqs,qkgd->skd", d_scores, query_heads) * score_scale
        d_key_value = jnp.concatenate(
            [d_key_all.reshape(n_ctx, rows, kw), d_value_all.reshape(n_ctx, rows, kw)], axis=2
        )
        d_key_value = collect(d_key_value).astype(bf16)
        d_key, d_value = (d_key_value[:, :kw], d_key_value[:, kw:])
        d_normed = dot("qb,ab->qa", d_queries, weight_query)
        d_normed = d_normed + dot("qb,ab->qa", d_key, weight_key)
        d_normed = d_normed + dot("qb,ab->qa", d_value, weight_value)
        grad_query = dot("qa,qb->ab", normed, d_queries, bf16)
        grad_key = dot("qa,qb->ab", normed, d_key, bf16)
        grad_value = dot("qa,qb->ab", normed, d_value, bf16)
        attn_back = jax.vjp(rms_norm, layer_input, gains[layer][0])[1]
        d_input, grad_gain_attn = attn_back(d_normed)
        d_entry = d_input + d_after
        attn_grads = reduce_attn(
            jnp.concatenate([grad_query, grad_key, column(grad_gain_attn)], axis=1),
            jnp.concatenate([grad_out, grad_value, column(grad_gain_ffn)], axis=1),
        )
        return (d_entry, attn_grads, expert_grads)

    first_in = lax.dynamic_index_in_dim(tokens, core, 0, keepdims=False)[0].astype(f32)
    first_out, first_kept = forward(0, first_in)
    first_sent = first_out.astype(bf16)
    second_out, second_kept = forward(1, first_sent.astype(f32))
    second_sent = second_out.astype(bf16)
    cotangent = lax.dynamic_index_in_dim(out_grad, core, 0, keepdims=False)[0]
    second_entry, second_attn, second_experts = backward(1, second_kept, cotangent)
    first_entry, first_attn, first_experts = backward(
        0, first_kept, second_entry.astype(bf16)
    )

    def keep_own(first, second):
        mine, other = (on_core(first, second), swap(on_core(second, first), "section", 1))
        return (on_core(mine, other), on_core(other, mine))

    layer_out = jnp.stack(keep_own(first_sent, second_sent))
    input_grads = jnp.stack(keep_own(first_entry, second_entry))
    former, latter = keep_own(first_attn, second_attn)
    grad_query, grad_key, grad_gain_attn = (former[:, :qw], former[:, qw : qw + kw], former[:, qw + kw])
    grad_out, grad_value, grad_gain_ffn = (latter[:, :qw], latter[:, qw : qw + kw], latter[:, qw + kw])
    grad_experts = []
    for first, second in zip(first_experts, second_experts):
        former, latter = keep_own(first, second)
        if pieces == 1:
            whole = jnp.stack([former, latter], axis=1)
            grad_experts.append(whole.reshape((EXPERTS,) + whole.shape[3:]).astype(f32))
        else:
            whole = jnp.stack([former[:, 0], latter[:, 0]], axis=2).astype(f32)
            grad_experts.append(whole)
    grad_pair, grad_down = grad_experts
    if pieces == 1:
        grad_gate, grad_up = (grad_pair[:, :, :hidden], grad_pair[:, :, hidden:])
    else:
        cut = hidden // 2
        grad_gate = grad_pair[..., :cut].reshape(EXPERTS, -1, hidden)
        grad_up = grad_pair[..., cut:].reshape(EXPERTS, -1, hidden)
        grad_down = grad_down.reshape(EXPERTS, -1, width)
    return (
        layer_out[None, :, None],
        input_grads[None, :, None],
        grad_gain_attn[None],
        grad_query[None],
        grad_key[None],
        grad_value[None],
        grad_out[None],
        grad_gain_ffn[None],
        grad_gate[None],
        grad_up[None],
        grad_down[None],
    )


def solution(mesh):
    rows_placed = P(None, "fsdp", "ctx", None)
    kept_placed = P("section", None, "fsdp", "ctx", None)
    gain_placed = P("section", ("ctx", "fsdp"))
    dense_placed = P("section", ("ctx", "fsdp"), None)
    expert_placed = P("section", None, ("ctx", "fsdp"), None)
    return jax.shard_map(
        body,
        mesh=mesh,
        in_specs=(
            rows_placed,
            P(),
            kept_placed,
            kept_placed,
            gain_placed,
            dense_placed,
            dense_placed,
            dense_placed,
            dense_placed,
            gain_placed,
            expert_placed,
            expert_placed,
            expert_placed,
            rows_placed,
        ),
        out_specs=(
            kept_placed,
            kept_placed,
            gain_placed,
            dense_placed,
            dense_placed,
            dense_placed,
            dense_placed,
            gain_placed,
            expert_placed,
            expert_placed,
            expert_placed,
        ),
        check_vma=False,
    )
```

```python
import jax
import jax.numpy as jnp
from jax import lax
from jax.sharding import PartitionSpec as P

QH = 12
KVH = 2
HD = 128
GROUP = QH // KVH
TOP = 4
EXPERTS = 8
bf16 = jnp.bfloat16
f32 = jnp.float32


epsilon = 1e-06
masked_out = -1e30
gap = 256


def swap(value, axis, bit):
    count = lax.axis_size(axis)
    return lax.ppermute(value, axis, [(source, source ^ bit) for source in range(count)])


def after(value, earlier):
    return lax.optimization_barrier((value, earlier))[0]


def at(value, index, axis=0):
    return lax.dynamic_index_in_dim(value, index, axis, keepdims=False)


def rms_norm(rows_in, gain):
    return rows_in * lax.rsqrt(jnp.mean(rows_in * rows_in, axis=-1, keepdims=True) + epsilon) * gain


def gated_unit(gate_pre, up_pre):
    return jax.nn.gelu(gate_pre, approximate=True) * up_pre


def dot(spec, left, right, kind=f32):
    return jnp.einsum(spec, left, right, preferred_element_type=kind)


def body(
    tokens,
    block_of,
    routes,
    combine,
    attn_norm,
    w_query,
    w_key,
    w_value,
    w_out,
    ffn_norm,
    w_gate,
    w_up,
    w_down,
    out_grad,
):
    rows = tokens.shape[2]
    width = tokens.shape[3]
    half = rows // 2
    n_ctx = lax.axis_size("ctx")
    n_fsdp = lax.axis_size("fsdp")
    core = lax.axis_index("section")
    place = lax.axis_index("ctx")
    depth = lax.axis_index("fsdp")
    seq_len = rows * n_ctx
    capacity = rows * TOP * 5 // (4 * EXPERTS)
    score_scale = HD ** (-0.5)
    own_experts = EXPERTS // n_ctx
    hidden = w_gate.shape[3]
    shard_rows = w_query.shape[1]
    down_rows = w_down.shape[2]
    qw = w_query.shape[2]
    kw = w_key.shape[2]
    pieces = max(1, 2 * n_ctx // EXPERTS)
    per_core = max(1, EXPERTS // (2 * n_ctx))

    def on_core(former, latter):
        return jnp.where(core == 0, former, latter)

    def own_other(low, high):
        return (on_core(low, high), on_core(high, low))

    def to_units(shard):
        count, deep, wide = shard.shape
        if pieces == 1:
            return shard
        cut = shard.reshape(count, deep, pieces, wide // pieces).transpose(0, 2, 1, 3)
        return cut.reshape(2 * n_ctx, deep, wide // pieces)

    def spread(value):
        return jnp.stack([value] + [swap(value, "ctx", bit) for bit in range(1, n_ctx)])

    def collect(blocks):
        total = blocks[0].astype(f32)
        for bit in range(1, n_ctx):
            total = total + swap(blocks[bit].astype(bf16), "ctx", bit).astype(f32)
        return total

    info = jnp.concatenate([routes.astype(f32), combine], axis=-1)[0, :, 0].transpose(0, 2, 1)
    info_own, info_other = (at(info, core), swap(at(info, 1 - core), "section", 1))
    info = jnp.stack(own_other(info_own, info_other))
    info = jnp.stack([info] + [swap(info, "ctx", bit) for bit in range(1, n_ctx)], axis=1)

    gain_columns = jnp.stack([attn_norm[0], ffn_norm[0]], axis=1)
    gain_columns = jnp.pad(gain_columns, ((0, 0), (0, gap - 2)))
    enter_shard = jnp.concatenate([w_query[0], w_key[0], w_value[0], gain_columns], axis=1)
    enter_cut = enter_shard.shape[1] // 2
    leave_cut = w_out.shape[2] // 2
    low_shard = jnp.concatenate([enter_shard[:, :enter_cut], w_out[0, :, :leave_cut]], axis=1)
    high_shard = jnp.concatenate([enter_shard[:, enter_cut:], w_out[0, :, leave_cut:]], axis=1)
    lent = swap(on_core(high_shard, low_shard), "section", 1)
    dense_shards = (on_core(low_shard, lent), on_core(lent, high_shard))

    def assemble(blocks, index, height):
        buffer = jnp.zeros((height * len(blocks), blocks[0].shape[1]), blocks[0].dtype)
        for bit, block in enumerate(blocks):
            buffer = lax.dynamic_update_slice(buffer, block, ((index ^ bit) * height, 0))
        return buffer

    def gather_deep(shard):
        blocks = [shard] + [swap(shard, "fsdp", bit) for bit in range(1, n_fsdp)]
        return assemble(blocks, depth, shard_rows)

    def gather_square(deep):
        blocks = [deep] + [swap(deep, "ctx", bit) for bit in range(1, n_ctx)]
        return assemble(blocks, place, shard_rows * n_fsdp)

    unit_stack = jnp.concatenate(
        [
            jnp.concatenate([to_units(w_gate[0]), to_units(w_up[0])], axis=2),
            to_units(w_down[0]),
        ],
        axis=1,
    )
    unit_stack = unit_stack.reshape((n_ctx, 2, per_core) + unit_stack.shape[1:])

    def deal_units(layer, stack):
        received = jnp.zeros((n_ctx,) + stack.shape[2:], bf16)
        for bit in range(n_ctx):
            target = at(stack, place ^ bit)
            straight = [(layer * n_ctx + c, layer * n_ctx + (c ^ bit)) for c in range(n_ctx)]
            across = [(layer * n_ctx + c, (1 - layer) * n_ctx + (c ^ bit)) for c in range(n_ctx)]
            same = target[layer]
            if bit > 0:
                same = lax.ppermute(same, ("section", "ctx"), straight)
            cross = lax.ppermute(target[1 - layer], ("section", "ctx"), across)
            block = jnp.where(core == layer, same, cross)
            received = lax.dynamic_update_index_in_dim(received, block, place ^ bit, 0)
        return (received[:, :, :shard_rows], received[:, :, shard_rows:])

    def gather_units(dealt):
        whole = lax.all_gather(dealt, "fsdp", axis=2)
        return [whole[:, unit].reshape(-1, whole.shape[-1]) for unit in range(per_core)]

    def pair_units(mine):
        other = [swap(part, "section", 1) for part in mine]
        if pieces == 1:
            return list(mine) + other
        low, high = own_other(mine[0], other[0])
        if mine[0].shape[0] == width:
            cut = hidden // 2
            parts = [low[:, :cut], high[:, :cut], low[:, cut:], high[:, cut:]]
            return [jnp.concatenate(parts, axis=1)]
        return [jnp.concatenate([low, high], axis=1)]

    def cut_units(grads):
        if pieces == 1:
            return (grads[:per_core], grads[per_core:])
        whole = grads[0]
        if whole.shape[0] == width:
            parts = whole.reshape(width, 2, 2, -1)
            halves = [parts[:, :, side].reshape(width, -1) for side in range(2)]
        else:
            halves = jnp.split(whole, 2, axis=1)
        own, other = own_other(halves[0], halves[1])
        return ([own], [other])

    def reduce_units(grads):
        own, other = cut_units(grads)
        results = []
        for mine, lended in zip(own, other):
            total = (mine.astype(f32) + swap(lended, "section", 1).astype(f32)).astype(bf16)
            total = total.reshape(n_ctx, n_fsdp, -1, total.shape[-1])
            received = at(total, depth, 1).astype(f32)
            for bit in range(1, n_fsdp):
                received = received + swap(at(total, depth ^ bit, 1), "fsdp", bit).astype(f32)
            results.append(received.astype(bf16))
        return results

    def reduce_dense(own, other):
        mine = (own.astype(f32) + swap(other, "section", 1).astype(f32)).astype(bf16)
        mine = mine.reshape(n_ctx, n_fsdp * shard_rows, -1)
        total = at(mine, place).astype(f32)
        for bit in range(1, n_ctx):
            total = total + swap(at(mine, place ^ bit), "ctx", bit).astype(f32)
        mine = total.astype(bf16).reshape(n_fsdp, shard_rows, -1)
        total = at(mine, depth).astype(f32)
        for bit in range(1, n_fsdp):
            total = total + swap(at(mine, depth ^ bit), "fsdp", bit).astype(f32)
        return total

    if pieces == 1:
        units_here = jnp.arange(per_core, dtype=jnp.int32)
        units_here = jnp.concatenate(
            [core * per_core + units_here, (1 - core) * per_core + units_here]
        )
    else:
        units_here = jnp.zeros((1,), jnp.int32)
    named = (place * own_experts + units_here).astype(f32)
    matches = info[:, None, :, :TOP] == named[None, :, None, None, None]
    hits = jnp.any(matches, axis=3)
    shares = jnp.sum(jnp.where(matches, info[:, None, :, TOP:], 0.0), axis=3)
    earlier = jnp.arange(rows)[:, None] < jnp.arange(rows)[None, :]
    rank = dot("ledr,rq->ledq", hits.astype(bf16), earlier.astype(bf16))
    slots = jnp.arange(capacity, dtype=f32)
    picks = hits[:, :, :, None, :] & (rank[:, :, :, None, :] == slots[:, None])
    slot_shares = jnp.sum(jnp.where(picks, shares[:, :, :, None, :], 0.0), axis=-1)
    picks = picks.astype(bf16)

    order = place ^ jnp.arange(n_ctx, dtype=jnp.int32)
    block_ids = jnp.take(block_of.reshape(n_ctx, 2), order, axis=0)
    positions = (block_ids[:, :, None] * half + jnp.arange(half, dtype=jnp.int32)).reshape(seq_len)
    allowed = positions[:rows, None] >= positions[None, :]

    def soft_scores(queries, key_all):
        query_heads = queries.reshape(rows, KVH, GROUP, HD)
        key_heads = key_all.reshape(seq_len, KVH, HD)
        scores = dot("qkgd,skd->kgqs", query_heads, key_heads) * score_scale
        return jnp.where(allowed[None, None], scores, masked_out)

    def project(value, halves):
        own, other = (dot("qa,ab->qb", value, part) for part in halves)
        return jnp.concatenate(own_other(own, other), axis=1)

    def project_back(value, halves):
        cut = value.shape[1] // 2
        own, other = own_other(value[:, :cut], value[:, cut:])
        total = dot("qb,ab->qa", own, halves[0]) + dot("qb,ab->qa", other, halves[1])
        return (total, own, other)

    def gains_of(halves):
        pair = on_core(halves[1][:, -gap : 2 - gap], halves[0][:, -gap : 2 - gap]).astype(f32)
        return (pair[:, 0], pair[:, 1])

    def enter(layer_input, halves):
        normed = rms_norm(layer_input, gains_of(halves)[0]).astype(bf16)
        entered = project(normed, halves).astype(bf16)
        return (normed, entered[:, :qw], entered[:, qw : qw + 2 * kw])

    def attend(queries, key_value_all):
        scores = soft_scores(queries, key_value_all[:, :kw])
        row_max = jnp.max(scores, axis=-1, keepdims=True)
        shifted = jnp.exp(scores - row_max)
        total = jnp.sum(shifted, axis=-1, keepdims=True)
        attention_weights = (shifted / total).astype(bf16)
        value_heads = key_value_all[:, kw:].reshape(seq_len, KVH, HD)
        attended = dot("kgqs,skd->qkgd", attention_weights, value_heads)
        return (attended.reshape(rows, qw).astype(bf16), row_max + jnp.log(total))

    def experts(layer, blocks, pairs, downs):
        returned = 0.0
        kept = []
        for j in range(own_experts):
            picked = dot("dsr,drw->dsw", picks[layer, j], blocks, bf16).reshape(-1, width)
            pair_pre = dot("mw,wf->mf", picked, pairs[j])
            gate_pre, up_pre = (pair_pre[:, :hidden], pair_pre[:, hidden:])
            active = gated_unit(gate_pre, up_pre).astype(bf16)
            expert_out = dot("mf,fw->mw", active, downs[j]).reshape(n_ctx, capacity, width)
            expert_out = (expert_out * slot_shares[layer, j][..., None]).astype(bf16)
            returned = returned + dot("dsr,dsw->drw", picks[layer, j], expert_out)
            kept.append((picked, gate_pre, up_pre, active))
        return (returned, kept)

    def experts_back(layer, blocks, pairs, downs, kept):
        returned = 0.0
        down_grads, pair_grads = ([], [])
        for j in range(own_experts):
            picked, gate_pre, up_pre, active = kept[j]
            cot_slots = dot("dsr,drw->dsw", picks[layer, j], blocks)
            cot_slots = (cot_slots * slot_shares[layer, j][..., None]).astype(bf16)
            cot_slots = cot_slots.reshape(-1, width)
            d_active = dot("mw,fw->mf", cot_slots, downs[j])
            d_gate, d_up = jax.vjp(gated_unit, gate_pre, up_pre)[1](d_active)
            d_pair = jnp.concatenate([d_gate, d_up], axis=1).astype(bf16)
            d_picked = dot("mf,wf->mw", d_pair, pairs[j]).astype(bf16)
            d_picked = d_picked.reshape(n_ctx, capacity, width)
            returned = returned + dot("dsr,dsw->drw", picks[layer, j], d_picked)
            down_grads.append(dot("mf,mw->fw", active, cot_slots, bf16))
            pair_grads.append(dot("mw,mf->wf", picked, d_pair, bf16))
        return (returned, pair_grads, down_grads)

    def leave_back(cotangent, d_ffn_normed, after_attention, attended, enter_halves, leave_halves):
        ffn_back = jax.vjp(rms_norm, after_attention, gains_of(enter_halves)[1])[1]
        d_after, grad_gain = ffn_back(d_ffn_normed)
        d_after = d_after + cotangent.astype(f32)
        d_attended, own, other = project_back(d_after.astype(bf16), leave_halves)
        grads = [dot("qa,qb->ab", attended, part, bf16) for part in (own, other)]
        return (d_after, grad_gain, d_attended.astype(bf16), grads)

    def attend_back(queries, key_value_all, log_totals, d_attended):
        probs_full = jnp.exp(soft_scores(queries, key_value_all[:, :kw]) - log_totals)
        attention_weights = probs_full.astype(bf16)
        d_heads = d_attended.reshape(rows, KVH, GROUP, HD)
        key_heads = key_value_all[:, :kw].reshape(seq_len, KVH, HD)
        value_heads = key_value_all[:, kw:].reshape(seq_len, KVH, HD)
        query_heads = queries.reshape(rows, KVH, GROUP, HD)
        d_values = dot("kgqs,qkgd->skd", attention_weights, d_heads)
        d_probs = dot("qkgd,skd->kgqs", d_heads, value_heads)
        inner = jnp.sum(probs_full * d_probs, axis=-1, keepdims=True)
        d_scores = (probs_full * (d_probs - inner)).astype(bf16)
        d_queries = dot("kgqs,skd->qkgd", d_scores, key_heads) * score_scale
        d_keys = dot("kgqs,qkgd->skd", d_scores, query_heads) * score_scale
        d_key_value = jnp.concatenate(
            [d_keys.reshape(n_ctx, rows, kw), d_values.reshape(n_ctx, rows, kw)], axis=2
        )
        return (d_queries.reshape(rows, qw).astype(bf16), d_key_value)

    def enter_back(d_queries, d_key_value, d_after, grad_gain_ffn, layer_input, normed, halves):
        blank = jnp.zeros((rows, gap), bf16)
        d_entered = jnp.concatenate([d_queries, d_key_value, blank], axis=1)
        d_normed, own, other = project_back(d_entered, halves)
        attn_back = jax.vjp(rms_norm, layer_input, gains_of(halves)[0])[1]
        d_input, grad_gain = attn_back(d_normed)
        gain_columns = jnp.stack([grad_gain, grad_gain_ffn], axis=1)
        gain_columns = jnp.pad(gain_columns, ((0, 0), (enter_cut - gap, gap - 2)))
        own, other = (dot("qa,qb->ab", normed, part) for part in (own, other))
        own = own + on_core(0.0, gain_columns)
        other = other + on_core(gain_columns, 0.0)
        return (d_input + d_after, [own.astype(bf16), other.astype(bf16)])

    pair_first, down_first = deal_units(0, unit_stack)
    enter_deep = gather_deep(dense_shards[0][:, :enter_cut])
    leave_deep = gather_deep(dense_shards[0][:, enter_cut:])
    pair_first, down_first = after((pair_first, down_first), (enter_deep, leave_deep))
    pair_first, down_first = (gather_units(pair_first), gather_units(down_first))
    enter_own = gather_square(enter_deep)
    enter_first = (enter_own, swap(enter_own, "section", 1))
    leave_own = gather_square(after(leave_deep, enter_own))
    leave_first = (leave_own, swap(leave_own, "section", 1))

    first_in = at(tokens, core)[0].astype(f32)
    first_normed, first_queries, key_value = enter(first_in, enter_first)
    first_kv = spread(key_value).reshape(seq_len, 2 * kw)
    unit_stack, shard_second = after((unit_stack, dense_shards[1]), key_value)
    pair_second, down_second = deal_units(1, unit_stack)
    deep_second = gather_deep(shard_second)
    first_attended, first_logs = attend(first_queries, first_kv)
    first_mid = first_in + project(first_attended, leave_first)
    ffn_normed = rms_norm(first_mid, gains_of(enter_first)[1]).astype(bf16)
    first_pairs, first_downs = (pair_units(pair_first), pair_units(down_first))
    blocks = spread(ffn_normed)
    pair_second, down_second = after((pair_second, down_second), ffn_normed)
    pair_second, down_second = (gather_units(pair_second), gather_units(down_second))
    dense_second = gather_square(after(deep_second, blocks))
    dense_other = swap(dense_second, "section", 1)
    enter_second = (dense_second[:, :enter_cut], dense_other[:, :enter_cut])
    leave_second = (dense_second[:, enter_cut:], dense_other[:, enter_cut:])
    returned, first_kept = experts(0, blocks, first_pairs, first_downs)
    first_out = first_mid + collect(returned)
    first_sent = first_out.astype(bf16)

    second_in = first_sent.astype(f32)
    second_normed, second_queries, key_value = enter(second_in, enter_second)
    second_kv = spread(key_value).reshape(seq_len, 2 * kw)
    second_attended, second_logs = attend(second_queries, second_kv)
    second_mid = second_in + project(second_attended, leave_second)
    ffn_normed = rms_norm(second_mid, gains_of(enter_second)[1]).astype(bf16)
    second_pairs, second_downs = (pair_units(pair_second), pair_units(down_second))
    returned, second_kept = experts(1, spread(ffn_normed), second_pairs, second_downs)
    second_sent = (second_mid + collect(returned)).astype(bf16)

    cotangent = at(out_grad, core)[0]
    returned, pair_grads, down_grads = experts_back(
        1, spread(cotangent), second_pairs, second_downs, second_kept
    )
    second_pair_grads, second_down_grads = (reduce_units(pair_grads), reduce_units(down_grads))
    d_after, grad_gain, d_attended, grads = leave_back(
        cotangent, collect(returned), second_mid, second_attended, enter_second, leave_second
    )
    second_leave_grad = reduce_dense(*grads)
    d_queries, d_key_value = attend_back(second_queries, second_kv, second_logs, d_attended)
    d_key_value = collect(d_key_value).astype(bf16)
    second_entry, grads = enter_back(
        d_queries, d_key_value, d_after, grad_gain, second_in, second_normed, enter_second
    )
    second_enter_grad = reduce_dense(*grads)

    cotangent = second_entry.astype(bf16)
    returned, pair_grads, down_grads = experts_back(
        0, spread(cotangent), first_pairs, first_downs, first_kept
    )
    first_pair_grads, first_down_grads = (reduce_units(pair_grads), reduce_units(down_grads))
    d_after, grad_gain, d_attended, grads = leave_back(
        cotangent, collect(returned), first_mid, first_attended, enter_first, leave_first
    )
    first_leave_grad = reduce_dense(*grads)
    d_attended = after(
        d_attended, (second_pair_grads, second_down_grads, second_leave_grad, second_enter_grad)
    )
    d_queries, d_key_value = attend_back(first_queries, first_kv, first_logs, d_attended)
    d_key_value = collect(d_key_value).astype(bf16)
    first_entry, grads = enter_back(
        d_queries, d_key_value, d_after, grad_gain, first_in, first_normed, enter_first
    )
    first_enter_grad = reduce_dense(*grads)

    def keep_own(first, second):
        other = swap(on_core(second, first), "section", 1)
        return own_other(on_core(first, second), other)

    layer_out = jnp.stack(keep_own(first_sent, second_sent))
    input_grads = jnp.stack(keep_own(first_entry, second_entry))
    enter_grad = jnp.concatenate(keep_own(first_enter_grad, second_enter_grad), axis=1)
    grad_out = jnp.concatenate(keep_own(first_leave_grad, second_leave_grad), axis=1)
    grad_gains = enter_grad[:, qw + 2 * kw :]

    def keep_experts(first, second):
        first, second = (
            lax.all_to_all(jnp.stack(part, axis=1), "ctx", 0, 0) for part in (first, second)
        )
        former, latter = keep_own(first, second)
        if pieces == 1:
            whole = jnp.stack([former, latter], axis=1)
            return whole.reshape((EXPERTS,) + whole.shape[3:]).astype(f32)
        return jnp.stack([former[:, 0], latter[:, 0]], axis=2).astype(f32)

    grad_down = keep_experts(first_down_grads, second_down_grads)
    grad_pair = keep_experts(first_pair_grads, second_pair_grads)
    if pieces == 1:
        grad_gate, grad_up = (grad_pair[:, :, :hidden], grad_pair[:, :, hidden:])
    else:
        cut = hidden // 2
        grad_gate = grad_pair[..., :cut].reshape(EXPERTS, shard_rows, hidden)
        grad_up = grad_pair[..., cut:].reshape(EXPERTS, shard_rows, hidden)
        grad_down = grad_down.reshape(EXPERTS, down_rows, width)
    return (
        layer_out[None, :, None],
        input_grads[None, :, None],
        grad_gains[:, 0][None],
        enter_grad[:, :qw][None],
        enter_grad[:, qw : qw + kw][None],
        enter_grad[:, qw + kw : qw + 2 * kw][None],
        grad_out[None],
        grad_gains[:, 1][None],
        grad_gate[None],
        grad_up[None],
        grad_down[None],
    )


def solution(mesh):
    rows_placed = P(None, "fsdp", "ctx", None)
    kept_placed = P("section", None, "fsdp", "ctx", None)
    gain_placed = P("section", ("ctx", "fsdp"))
    dense_placed = P("section", ("ctx", "fsdp"), None)
    expert_placed = P("section", None, ("ctx", "fsdp"), None)
    dense_all = (dense_placed,) * 4
    expert_all = (expert_placed,) * 3
    layer_placed = (gain_placed,) + dense_all + (gain_placed,) + expert_all
    return jax.shard_map(
        body,
        mesh=mesh,
        in_specs=(rows_placed, P(), kept_placed, kept_placed) + layer_placed + (rows_placed,),
        out_specs=(kept_placed, kept_placed) + layer_placed,
        check_vma=False,
    )
```

```python
import functools

import jax
import jax.numpy as jnp
from jax import lax
from jax.experimental import pallas as pl
from jax.experimental.pallas import tpu as pltpu
from jax.sharding import PartitionSpec as P

QH = 12
KVH = 2
HD = 128
GROUP = QH // KVH
TOP = 4
EXPERTS = 8
bf16 = jnp.bfloat16
f32 = jnp.float32


epsilon = 1e-06
masked_out = -1e30
gap = 256


def swap(value, axis, bit):
    count = lax.axis_size(axis)
    return lax.ppermute(value, axis, [(source, source ^ bit) for source in range(count)])


def after(value, earlier):
    return lax.optimization_barrier((value, earlier))[0]


def at(value, index, axis=0):
    return lax.dynamic_index_in_dim(value, index, axis, keepdims=False)


def rms_norm(rows_in, gain):
    return rows_in * lax.rsqrt(jnp.mean(rows_in * rows_in, axis=-1, keepdims=True) + epsilon) * gain


def dot(spec, left, right, kind=f32):
    return jnp.einsum(spec, left, right, preferred_element_type=kind)


TINY = pl.CostEstimate(flops=1000, bytes_accessed=1000, transcendentals=0)


def kernel_params():
    return pltpu.CompilerParams(vmem_limit_bytes=56 * 1024 * 1024)


def nt(left, right):
    return lax.dot_general(left, right, (((1,), (1,)), ((), ())), preferred_element_type=f32)


def nn(left, right):
    return jnp.dot(left, right, preferred_element_type=f32)


def head_rows(ref):
    return jnp.concatenate([ref[:, i * HD : (i + 1) * HD] for i in range(GROUP)], axis=0)


def softmax_rows(ids_ref, queries, keys, half, own):
    scores = nt(queries, keys) * HD ** (-0.5)
    tall, wide = scores.shape
    row = lax.broadcasted_iota(jnp.int32, (half, 1), 0)
    row = jnp.concatenate([row] * (tall // half), axis=0) + ids_ref[own] * half
    lane = lax.broadcasted_iota(jnp.int32, (1, half), 1)
    column = [lane + ids_ref[block] * half for block in range(wide // half)]
    column = jnp.concatenate(column, axis=1)
    scores = jnp.where(row >= column, scores, masked_out)
    shifted = jnp.exp(scores - jnp.max(scores, axis=1, keepdims=True))
    return shifted / jnp.sum(shifted, axis=1, keepdims=True)


def attend_kernel(ids_ref, query_ref, key_ref, value_ref, out_ref):
    half = query_ref.shape[0]
    probs = softmax_rows(ids_ref, head_rows(query_ref), key_ref[...], half, pl.program_id(1))
    out = nn(probs.astype(bf16), value_ref[...]).astype(bf16)
    for i in range(GROUP):
        out_ref[:, i * HD : (i + 1) * HD] = out[i * half : (i + 1) * half]


def attend_specs(rows, seq_len):
    half = rows // 2
    by_head = pl.BlockSpec((half, GROUP * HD), lambda g, h, ids: (h, g))
    keys = pl.BlockSpec((seq_len, HD), lambda g, h, ids: (0, g))
    values = pl.BlockSpec((seq_len, HD), lambda g, h, ids: (0, KVH + g))
    return by_head, keys, values


def attend_call(ids, queries, key_value):
    rows, seq_len = (queries.shape[0], key_value.shape[0])
    by_head, keys, values = attend_specs(rows, seq_len)
    return pl.pallas_call(
        attend_kernel,
        grid_spec=pltpu.PrefetchScalarGridSpec(
            num_scalar_prefetch=1,
            grid=(KVH, 2),
            in_specs=[by_head, keys, values],
            out_specs=by_head,
        ),
        out_shape=jax.ShapeDtypeStruct(queries.shape, bf16),
        compiler_params=kernel_params(),
        cost_estimate=TINY,
        name="attend",
    )(ids, queries, key_value, key_value)


def attend_back_kernel(ids_ref, query_ref, key_ref, value_ref, cot_ref, dq_ref, dk_ref, dv_ref):
    half = query_ref.shape[0]
    own = pl.program_id(1)
    queries, cot = (head_rows(query_ref), head_rows(cot_ref))
    probs = softmax_rows(ids_ref, queries, key_ref[...], half, own)
    d_probs = nt(cot, value_ref[...])
    inner = jnp.sum(probs * d_probs, axis=1, keepdims=True)
    d_scores = (probs * (d_probs - inner)).astype(bf16)
    d_queries = (nn(d_scores, key_ref[...]) * HD ** (-0.5)).astype(bf16)
    for i in range(GROUP):
        dq_ref[:, i * HD : (i + 1) * HD] = d_queries[i * half : (i + 1) * half]
    d_keys = nn(d_scores.T, queries) * HD ** (-0.5)
    d_values = nn(probs.astype(bf16).T, cot)

    @pl.when(own == 0)
    def _():
        dk_ref[...] = d_keys
        dv_ref[...] = d_values

    @pl.when(own != 0)
    def _():
        dk_ref[...] += d_keys
        dv_ref[...] += d_values


def attend_back_call(ids, queries, key_value, cot):
    rows, seq_len = (queries.shape[0], key_value.shape[0])
    by_head, keys, values = attend_specs(rows, seq_len)
    summed = jax.ShapeDtypeStruct((seq_len, KVH * HD), f32)
    return pl.pallas_call(
        attend_back_kernel,
        grid_spec=pltpu.PrefetchScalarGridSpec(
            num_scalar_prefetch=1,
            grid=(KVH, 2),
            in_specs=[by_head, keys, values, by_head],
            out_specs=[by_head, keys, keys],
        ),
        out_shape=[jax.ShapeDtypeStruct(queries.shape, bf16), summed, summed],
        compiler_params=kernel_params(),
        cost_estimate=TINY,
        name="attend_back",
    )(ids, queries, key_value, key_value, cot)


def gelu_parts(gate):
    root = 0.7978845608028654
    inner = root * (gate + 0.044715 * gate * gate * gate)
    bent = jnp.tanh(inner)
    value = 0.5 * gate * (1.0 + bent)
    slope = root * (1.0 + 3.0 * 0.044715 * gate * gate)
    return value, 0.5 * (1.0 + bent) + 0.5 * gate * (1.0 - bent * bent) * slope


def give_back(pick_ref, total_ref, share_ref, before, out):
    blocks, capacity, _ = pick_ref.shape
    for d in range(blocks):
        part = total_ref[d * capacity : (d + 1) * capacity, :]
        if share_ref is not None:
            part = part * share_ref[d]
        back = nn(pick_ref[d].T, part.astype(bf16))
        if before:
            back = back + before[d][...]
        out[d][...] = back.astype(out[d].dtype)


def expert_kernel(blocks, adds, pick_ref, share_ref, gate_ref, up_ref, down_ref, *refs):
    rows, refs = (refs[:blocks], refs[blocks:])
    before, refs = (refs[: blocks * adds], refs[blocks * adds :])
    out, (picked_ref, gate_pre_ref, up_pre_ref, total_ref) = (refs[:blocks], refs[blocks:])
    step = pl.program_id(0)
    capacity = pick_ref.shape[1]

    @pl.when(step == 0)
    def _():
        for d in range(blocks):
            block = nn(pick_ref[d], rows[d][...]).astype(bf16)
            picked_ref[d * capacity : (d + 1) * capacity, :] = block

    gate_pre = nn(picked_ref[...], gate_ref[...])
    up_pre = nn(picked_ref[...], up_ref[...])
    gate_pre_ref[...] = gate_pre
    up_pre_ref[...] = up_pre
    active = (gelu_parts(gate_pre)[0] * up_pre).astype(bf16)
    part = nn(active, down_ref[...])

    @pl.when(step == 0)
    def _():
        total_ref[...] = part

    @pl.when(step != 0)
    def _():
        total_ref[...] += part

    @pl.when(step == pl.num_programs(0) - 1)
    def _():
        give_back(pick_ref, total_ref, share_ref, before, out)


def whole_spec(shape):
    return pl.BlockSpec(shape, lambda step: (0,) * len(shape))


def expert_call(picks, shares, rows, pair, down, before):
    blocks, capacity, _ = picks.shape
    width, hidden = (rows[0].shape[1], down.shape[0])
    cut = 256
    tall = blocks * capacity
    columns = pl.BlockSpec((tall, cut), lambda step: (0, step))
    row_specs = [whole_spec(block.shape) for block in rows]
    kind = bf16 if before else f32
    result = pl.pallas_call(
        functools.partial(expert_kernel, blocks, 1 if before else 0),
        grid=(hidden // cut,),
        in_specs=[
            whole_spec(picks.shape),
            whole_spec(shares.shape),
            pl.BlockSpec((width, cut), lambda step: (0, step)),
            pl.BlockSpec((width, cut), lambda step: (0, hidden // cut + step)),
            pl.BlockSpec((cut, width), lambda step: (step, 0)),
        ]
        + row_specs * (2 if before else 1),
        out_specs=row_specs + [whole_spec((tall, width)), columns, columns],
        out_shape=[jax.ShapeDtypeStruct(block.shape, kind) for block in rows]
        + [
            jax.ShapeDtypeStruct((tall, width), bf16),
            jax.ShapeDtypeStruct((tall, hidden), f32),
            jax.ShapeDtypeStruct((tall, hidden), f32),
        ],
        scratch_shapes=[pltpu.VMEM((tall, width), f32)],
        compiler_params=kernel_params(),
        cost_estimate=TINY,
        name="expert",
    )(picks, shares, pair, pair, down, *rows, *before)
    return (result[:blocks], result[blocks:])


def expert_back_kernel(
    blocks, adds, pick_ref, share_ref, picked_ref, gate_pre_ref, up_pre_ref,
    gate_ref, up_ref, down_ref, *refs
):
    rows, refs = (refs[:blocks], refs[blocks:])
    before, refs = (refs[: blocks * adds], refs[blocks * adds :])
    out, refs = (refs[:blocks], refs[blocks:])
    pair_ref, down_grad_ref, slots_ref, turned_ref, total_ref = refs
    capacity = pick_ref.shape[1]
    step = pl.program_id(0)

    @pl.when(step == 0)
    def _():
        for d in range(blocks):
            block = nn(pick_ref[d], rows[d][...]) * share_ref[d]
            slots_ref[d * capacity : (d + 1) * capacity, :] = block.astype(bf16)
        turned_ref[...] = picked_ref[...].T

    d_active = nt(slots_ref[...], down_ref[...])
    value, slope = gelu_parts(gate_pre_ref[...])
    up_pre = up_pre_ref[...]
    active = (value * up_pre).astype(bf16)
    d_gate = (d_active * up_pre * slope).astype(bf16)
    d_up = (d_active * value).astype(bf16)
    down_grad_ref[...] = nn(active.T, slots_ref[...]).astype(bf16)
    pair_ref[0] = nn(turned_ref[...], d_gate).astype(bf16)
    pair_ref[1] = nn(turned_ref[...], d_up).astype(bf16)
    part = nt(d_gate, gate_ref[...]) + nt(d_up, up_ref[...])

    @pl.when(step == 0)
    def _():
        total_ref[...] = part

    @pl.when(step != 0)
    def _():
        total_ref[...] += part

    @pl.when(step == pl.num_programs(0) - 1)
    def _():
        give_back(pick_ref, total_ref, None, before, out)


def expert_back_call(picks, shares, rows, kept, pair, down, before):
    blocks, capacity, _ = picks.shape
    width, hidden = (rows[0].shape[1], down.shape[0])
    cut = 256
    tall = blocks * capacity
    columns = pl.BlockSpec((tall, cut), lambda step: (0, step))
    row_specs = [whole_spec(block.shape) for block in rows]
    kind = bf16 if before else f32
    result = pl.pallas_call(
        functools.partial(expert_back_kernel, blocks, 1 if before else 0),
        grid=(hidden // cut,),
        in_specs=[
            whole_spec(picks.shape),
            whole_spec(shares.shape),
            whole_spec((tall, width)),
            columns,
            columns,
            pl.BlockSpec((width, cut), lambda step: (0, step)),
            pl.BlockSpec((width, cut), lambda step: (0, hidden // cut + step)),
            pl.BlockSpec((cut, width), lambda step: (step, 0)),
        ]
        + row_specs * (2 if before else 1),
        out_specs=row_specs
        + [
            pl.BlockSpec((2, width, cut), lambda step: (0, 0, step)),
            pl.BlockSpec((cut, width), lambda step: (step, 0)),
        ],
        out_shape=[jax.ShapeDtypeStruct(block.shape, kind) for block in rows]
        + [
            jax.ShapeDtypeStruct((2, width, hidden), bf16),
            jax.ShapeDtypeStruct((hidden, width), bf16),
        ],
        scratch_shapes=[
            pltpu.VMEM((tall, width), bf16),
            pltpu.VMEM((width, tall), bf16),
            pltpu.VMEM((tall, width), f32),
        ],
        compiler_params=kernel_params(),
        cost_estimate=TINY,
        name="expert_back",
    )(picks, shares, *kept, pair, pair, down, *rows, *before)
    return (result[:blocks], result[blocks], result[blocks + 1])


def place_kernel(count, height, index_ref, *refs):
    blocks, out_ref, sems = (refs[:count], refs[count], refs[count + 1])
    copies = []
    for bit in range(count):
        start = pl.multiple_of((index_ref[0] ^ bit) * height, height)
        target = out_ref.at[pl.ds(start, height)]
        copies.append(pltpu.make_async_copy(blocks[bit], target, sems.at[bit]))
    for copy in copies:
        copy.start()
    for copy in copies:
        copy.wait()


def place_call(blocks, index):
    count = len(blocks)
    height, wide = blocks[0].shape
    anywhere = pl.BlockSpec(memory_space=pl.ANY)
    return pl.pallas_call(
        functools.partial(place_kernel, count, height),
        grid_spec=pltpu.PrefetchScalarGridSpec(
            num_scalar_prefetch=1,
            grid=(1,),
            in_specs=[anywhere] * count,
            out_specs=anywhere,
            scratch_shapes=[pltpu.SemaphoreType.DMA((count,))],
        ),
        out_shape=jax.ShapeDtypeStruct((count * height, wide), blocks[0].dtype),
        cost_estimate=TINY,
        name="place",
    )(index.reshape(1), *blocks)


def deal_kernel(count, layer, deep, index_ref, *refs):
    straight, across = (refs[:count], refs[count : 2 * count])
    top_ref, rest_ref, sems = refs[2 * count :]
    place, keeps = (index_ref[0], index_ref[1] == layer)

    def copies(blocks):
        made = []
        for bit in range(count):
            block, row = (blocks[bit], place ^ bit)
            parts = ((block.at[:, :deep], top_ref), (block.at[:, deep:], rest_ref))
            for part, (source, target) in enumerate(parts):
                made.append(pltpu.make_async_copy(source, target.at[row], sems.at[bit, part]))
        return made

    def run(blocks):
        made = copies(blocks)
        for copy in made:
            copy.start()
        for copy in made:
            copy.wait()

    @pl.when(keeps)
    def _():
        run(straight)

    @pl.when(jnp.logical_not(keeps))
    def _():
        run(across)


def deal_call(straight, across, layer, deep, place, core):
    count = len(straight)
    units, tall, wide = straight[0].shape
    anywhere = pl.BlockSpec(memory_space=pl.ANY)
    return pl.pallas_call(
        functools.partial(deal_kernel, count, layer, deep),
        grid_spec=pltpu.PrefetchScalarGridSpec(
            num_scalar_prefetch=1,
            grid=(1,),
            in_specs=[anywhere] * (2 * count),
            out_specs=[anywhere] * 2,
            scratch_shapes=[pltpu.SemaphoreType.DMA((count, 2))],
        ),
        out_shape=[
            jax.ShapeDtypeStruct((count, units, deep, wide), bf16),
            jax.ShapeDtypeStruct((count, units, tall - deep, wide), bf16),
        ],
        cost_estimate=TINY,
        name="deal",
    )(jnp.stack([place, core]), *straight, *across)


def body(
    tokens,
    block_of,
    routes,
    combine,
    attn_norm,
    w_query,
    w_key,
    w_value,
    w_out,
    ffn_norm,
    w_gate,
    w_up,
    w_down,
    out_grad,
):
    rows = tokens.shape[2]
    width = tokens.shape[3]
    half = rows // 2
    n_ctx = lax.axis_size("ctx")
    n_fsdp = lax.axis_size("fsdp")
    core = lax.axis_index("section")
    place = lax.axis_index("ctx")
    depth = lax.axis_index("fsdp")
    seq_len = rows * n_ctx
    capacity = rows * TOP * 5 // (4 * EXPERTS)
    score_scale = HD ** (-0.5)
    own_experts = EXPERTS // n_ctx
    hidden = w_gate.shape[3]
    shard_rows = w_query.shape[1]
    down_rows = w_down.shape[2]
    qw = w_query.shape[2]
    kw = w_key.shape[2]
    pieces = max(1, 2 * n_ctx // EXPERTS)
    per_core = max(1, EXPERTS // (2 * n_ctx))

    def on_core(former, latter):
        return jnp.where(core == 0, former, latter)

    def own_other(low, high):
        return (on_core(low, high), on_core(high, low))

    def to_units(shard):
        count, deep, wide = shard.shape
        if pieces == 1:
            return shard
        cut = shard.reshape(count, deep, pieces, wide // pieces).transpose(0, 2, 1, 3)
        return cut.reshape(2 * n_ctx, deep, wide // pieces)

    def spread(value):
        return [value] + [swap(value, "ctx", bit) for bit in range(1, n_ctx)]

    def collect(blocks):
        total = blocks[0].astype(f32)
        for bit in range(1, n_ctx):
            total = total + swap(blocks[bit].astype(bf16), "ctx", bit).astype(f32)
        return total

    info = jnp.concatenate([routes.astype(f32), combine], axis=-1)[0, :, 0].transpose(0, 2, 1)
    info_own, info_other = (at(info, core), swap(at(info, 1 - core), "section", 1))
    info = jnp.stack(own_other(info_own, info_other))
    info = jnp.stack([info] + [swap(info, "ctx", bit) for bit in range(1, n_ctx)], axis=1)

    gain_columns = jnp.stack([attn_norm[0], ffn_norm[0]], axis=1)
    gain_columns = jnp.pad(gain_columns, ((0, 0), (0, gap - 2)))
    enter_shard = jnp.concatenate([w_query[0], w_key[0], w_value[0], gain_columns], axis=1)
    enter_cut = enter_shard.shape[1] // 2
    leave_cut = w_out.shape[2] // 2
    low_shard = jnp.concatenate([enter_shard[:, :enter_cut], w_out[0, :, :leave_cut]], axis=1)
    high_shard = jnp.concatenate([enter_shard[:, enter_cut:], w_out[0, :, leave_cut:]], axis=1)
    lent = swap(on_core(high_shard, low_shard), "section", 1)
    dense_shards = (on_core(low_shard, lent), on_core(lent, high_shard))

    def assemble(blocks, index):
        height = blocks[0].shape[0]
        if height % 16 == 0:
            return place_call(blocks, index)
        buffer = jnp.zeros((height * len(blocks), blocks[0].shape[1]), blocks[0].dtype)
        for bit, block in enumerate(blocks):
            buffer = lax.dynamic_update_slice(buffer, block, ((index ^ bit) * height, 0))
        return buffer

    def gather_deep(shard):
        return assemble([shard] + [swap(shard, "fsdp", bit) for bit in range(1, n_fsdp)], depth)

    def gather_square(deep):
        return assemble(spread(deep), place)

    unit_stack = jnp.concatenate(
        [
            jnp.concatenate([to_units(w_gate[0]), to_units(w_up[0])], axis=2),
            to_units(w_down[0]),
        ],
        axis=1,
    )
    unit_stack = unit_stack.reshape((n_ctx, 2, per_core) + unit_stack.shape[1:])

    def deal_units(layer, stack):
        straight, across = ([], [])
        for bit in range(n_ctx):
            target = at(stack, place ^ bit)
            steps = [(layer * n_ctx + c, layer * n_ctx + (c ^ bit)) for c in range(n_ctx)]
            sides = [(layer * n_ctx + c, (1 - layer) * n_ctx + (c ^ bit)) for c in range(n_ctx)]
            same = target[layer]
            if bit > 0:
                same = lax.ppermute(same, ("section", "ctx"), steps)
            straight.append(same)
            across.append(lax.ppermute(target[1 - layer], ("section", "ctx"), sides))
        if shard_rows % 16 == 0 and down_rows % 16 == 0:
            return deal_call(straight, across, layer, shard_rows, place, core)
        received = jnp.zeros((n_ctx,) + stack.shape[2:], bf16)
        for bit in range(n_ctx):
            block = jnp.where(core == layer, straight[bit], across[bit])
            received = lax.dynamic_update_index_in_dim(received, block, place ^ bit, 0)
        return (received[:, :, :shard_rows], received[:, :, shard_rows:])

    def gather_units(dealt):
        whole = lax.all_gather(dealt, "fsdp", axis=2)
        return [whole[:, unit].reshape(-1, whole.shape[-1]) for unit in range(per_core)]

    def pair_units(mine):
        other = [swap(part, "section", 1) for part in mine]
        if pieces == 1:
            return list(mine) + other
        low, high = own_other(mine[0], other[0])
        if mine[0].shape[0] == width:
            cut = hidden // 2
            parts = [low[:, :cut], high[:, :cut], low[:, cut:], high[:, cut:]]
            return [jnp.concatenate(parts, axis=1)]
        return [jnp.concatenate([low, high], axis=1)]

    def cut_units(grads):
        if pieces == 1:
            return (grads[:per_core], grads[per_core:])
        own, other = own_other(*jnp.split(grads[0], 2, axis=-1))
        return ([own], [other])

    def trade_units(grads):
        own, other = cut_units(grads)
        received = [swap(part, "section", 1) for part in other]
        return [(a.astype(f32) + b.astype(f32)).astype(bf16) for a, b in zip(own, received)]

    def reduce_units(totals, deep):
        results = []
        for total in totals:
            total = total.reshape(-1, n_ctx, n_fsdp, deep, total.shape[-1])
            received = at(total, depth, 2).astype(f32)
            for bit in range(1, n_fsdp):
                received = received + swap(at(total, depth ^ bit, 2), "fsdp", bit).astype(f32)
            results.append(received.astype(bf16))
        return results

    def scatter_units(parts):
        return lax.all_to_all(jnp.stack(parts, axis=2), "ctx", 1, 1)

    def trade_dense(own, other):
        return (own.astype(f32) + swap(other, "section", 1).astype(f32)).astype(bf16)

    def reduce_square(mine):
        mine = mine.reshape(n_ctx, n_fsdp * shard_rows, -1)
        total = at(mine, place).astype(f32)
        for bit in range(1, n_ctx):
            total = total + swap(at(mine, place ^ bit), "ctx", bit).astype(f32)
        return total.astype(bf16)

    def reduce_deep(mine):
        mine = mine.reshape(n_fsdp, shard_rows, -1)
        total = at(mine, depth).astype(f32)
        for bit in range(1, n_fsdp):
            total = total + swap(at(mine, depth ^ bit), "fsdp", bit).astype(f32)
        return total

    if pieces == 1:
        units_here = jnp.arange(per_core, dtype=jnp.int32)
        units_here = jnp.concatenate(
            [core * per_core + units_here, (1 - core) * per_core + units_here]
        )
    else:
        units_here = jnp.zeros((1,), jnp.int32)
    named = (place * own_experts + units_here).astype(f32)
    matches = info[:, None, :, :TOP] == named[None, :, None, None, None]
    hits = jnp.any(matches, axis=3)
    shares = jnp.sum(jnp.where(matches, info[:, None, :, TOP:], 0.0), axis=3)
    earlier = jnp.arange(rows)[:, None] < jnp.arange(rows)[None, :]
    rank = dot("ledr,rq->ledq", hits.astype(bf16), earlier.astype(bf16))
    slots = jnp.arange(capacity, dtype=f32)
    picks = hits[:, :, :, None, :] & (rank[:, :, :, None, :] == slots[:, None])
    slot_shares = jnp.sum(jnp.where(picks, shares[:, :, :, None, :], 0.0), axis=-1, keepdims=True)
    picks = picks.astype(bf16)

    order = place ^ jnp.arange(n_ctx, dtype=jnp.int32)
    block_ids = jnp.take(block_of.reshape(n_ctx, 2), order, axis=0)
    block_ids = block_ids.reshape(-1)

    def project(value, halves):
        own, other = (dot("qa,ab->qb", value, part) for part in halves)
        return jnp.concatenate(own_other(own, other), axis=1)

    def project_back(value, halves):
        cut = value.shape[1] // 2
        own, other = own_other(value[:, :cut], value[:, cut:])
        total = dot("qb,ab->qa", own, halves[0]) + dot("qb,ab->qa", other, halves[1])
        return (total, own, other)

    def gains_of(halves):
        pair = on_core(halves[1][:, -gap : 2 - gap], halves[0][:, -gap : 2 - gap]).astype(f32)
        return (pair[:, 0], pair[:, 1])

    def enter(layer_input, halves):
        normed = rms_norm(layer_input, gains_of(halves)[0]).astype(bf16)
        entered = project(normed, halves).astype(bf16)
        return (normed, entered[:, :qw], entered[:, qw : qw + 2 * kw])

    def experts(layer, blocks, pairs, downs):
        returned, kept = ([], [])
        for j in range(own_experts):
            returned, saved = expert_call(
                picks[layer, j], slot_shares[layer, j], blocks, pairs[j], downs[j], returned
            )
            kept.append(saved)
        return (returned, kept)

    def experts_back(layer, blocks, pairs, downs, kept):
        returned, pair_grads, down_grads = ([], [], [])
        for j in range(own_experts):
            returned, pair_grad, down_grad = expert_back_call(
                picks[layer, j],
                slot_shares[layer, j],
                blocks,
                kept[j],
                pairs[j],
                downs[j],
                returned,
            )
            pair_grads.append(pair_grad)
            down_grads.append(down_grad)
        return (returned, pair_grads, down_grads)

    def leave_back(cotangent, d_ffn_normed, after_attention, attended, enter_halves, leave_halves):
        ffn_back = jax.vjp(rms_norm, after_attention, gains_of(enter_halves)[1])[1]
        d_after, grad_gain = ffn_back(d_ffn_normed)
        d_after = d_after + cotangent.astype(f32)
        d_attended, own, other = project_back(d_after.astype(bf16), leave_halves)
        grads = [dot("qa,qb->ab", attended, part, bf16) for part in (own, other)]
        return (d_after, grad_gain, d_attended.astype(bf16), grads)

    def attend_back(queries, key_value_all, d_attended):
        d_queries, d_keys, d_values = attend_back_call(
            block_ids, queries, key_value_all, d_attended
        )
        d_key_value = jnp.concatenate([d_keys, d_values], axis=1).reshape(n_ctx, rows, 2 * kw)
        return (d_queries, collect(d_key_value).astype(bf16))

    def enter_back(d_queries, d_key_value, d_after, grad_gain_ffn, layer_input, normed, halves):
        blank = jnp.zeros((rows, gap), bf16)
        d_entered = jnp.concatenate([d_queries, d_key_value, blank], axis=1)
        d_normed, own, other = project_back(d_entered, halves)
        attn_back = jax.vjp(rms_norm, layer_input, gains_of(halves)[0])[1]
        d_input, grad_gain = attn_back(d_normed)
        gain_columns = jnp.stack([grad_gain, grad_gain_ffn], axis=1)
        gain_columns = jnp.pad(gain_columns, ((0, 0), (enter_cut - gap, gap - 2)))
        own, other = (dot("qa,qb->ab", normed, part) for part in (own, other))
        own = own + on_core(0.0, gain_columns)
        other = other + on_core(gain_columns, 0.0)
        return (d_input + d_after, [own.astype(bf16), other.astype(bf16)])

    deep_first = gather_deep(dense_shards[0])
    pair_first, down_first = deal_units(0, after(unit_stack, lent))
    deep_second = gather_deep(after(dense_shards[1], deep_first))
    pair_second, down_second = deal_units(1, after(unit_stack, pair_first))
    pair_first, down_first = after((pair_first, down_first), deep_first)
    pair_first, down_first = (gather_units(pair_first), gather_units(down_first))
    enter_own = gather_square(deep_first[:, :enter_cut])
    enter_first = (enter_own, swap(enter_own, "section", 1))
    leave_own = gather_square(after(deep_first[:, enter_cut:], enter_own))
    leave_first = (leave_own, swap(leave_own, "section", 1))

    first_in = at(tokens, core)[0].astype(f32)
    first_normed, first_queries, key_value = enter(first_in, enter_first)
    first_kv = jnp.concatenate(spread(key_value))
    dense_own = gather_square(after(deep_second, (leave_own, first_queries)))
    first_attended = attend_call(block_ids, first_queries, first_kv)
    first_mid = first_in + project(first_attended, leave_first)
    ffn_normed = rms_norm(first_mid, gains_of(enter_first)[1]).astype(bf16)
    pair_second, down_second = after((pair_second, down_second), first_attended)
    pair_second, down_second = (gather_units(pair_second), gather_units(down_second))
    blocks = spread(ffn_normed)
    first_pairs, first_downs = (pair_units(pair_first), pair_units(down_first))
    returned, first_kept = experts(0, blocks, first_pairs, first_downs)
    dense_other = swap(after(dense_own, ffn_normed), "section", 1)
    enter_second = (dense_own[:, :enter_cut], dense_other[:, :enter_cut])
    leave_second = (dense_own[:, enter_cut:], dense_other[:, enter_cut:])
    first_out = first_mid + collect(returned)
    first_sent = first_out.astype(bf16)

    second_in = first_sent.astype(f32)
    second_normed, second_queries, key_value = enter(second_in, enter_second)
    second_kv = jnp.concatenate(spread(key_value))
    second_attended = attend_call(block_ids, second_queries, second_kv)
    second_mid = second_in + project(second_attended, leave_second)
    ffn_normed = rms_norm(second_mid, gains_of(enter_second)[1]).astype(bf16)
    second_pairs, second_downs = (pair_units(pair_second), pair_units(down_second))
    blocks = spread(ffn_normed)
    cotangent = after(at(out_grad, core)[0], blocks)
    cot_blocks = spread(cotangent)
    returned, second_kept = experts(1, blocks, second_pairs, second_downs)
    second_sent = (second_mid + collect(returned)).astype(bf16)

    returned, pair_grads, down_grads = experts_back(
        1, cot_blocks, second_pairs, second_downs, second_kept
    )
    pair_totals, down_totals = (trade_units(pair_grads), trade_units(down_grads))
    d_after, grad_gain, d_attended, grads = leave_back(
        cotangent, collect(returned), second_mid, second_attended, enter_second, leave_second
    )
    leave_total = trade_dense(*grads)
    d_attended, pair_totals, down_totals = lax.optimization_barrier(
        (d_attended, pair_totals, down_totals)
    )
    second_pair_grads = reduce_units(pair_totals, shard_rows)
    second_down_grads = reduce_units(down_totals, down_rows)
    d_queries, d_key_value = attend_back(second_queries, second_kv, d_attended)
    d_key_value, leave_total = lax.optimization_barrier((d_key_value, leave_total))
    leave_total = reduce_square(leave_total)
    second_entry, grads = enter_back(
        d_queries, d_key_value, d_after, grad_gain, second_in, second_normed, enter_second
    )
    enter_total = trade_dense(*grads)

    cotangent = second_entry.astype(bf16)
    blocks = spread(cotangent)
    blocks, enter_total, leave_total = lax.optimization_barrier((blocks, enter_total, leave_total))
    enter_total = reduce_square(enter_total)
    returned, pair_grads, down_grads = experts_back(
        0, blocks, first_pairs, first_downs, first_kept
    )
    pair_totals, down_totals = (trade_units(pair_grads), trade_units(down_grads))
    d_ffn_normed, enter_total, second_pair_grads, second_down_grads = lax.optimization_barrier(
        (collect(returned), enter_total, second_pair_grads, second_down_grads)
    )
    second_leave_grad = reduce_deep(leave_total)
    second_enter_grad = reduce_deep(enter_total)
    second_pair_grads = scatter_units(second_pair_grads)
    second_down_grads = scatter_units(second_down_grads)
    d_after, grad_gain, d_attended, grads = leave_back(
        cotangent, d_ffn_normed, first_mid, first_attended, enter_first, leave_first
    )
    leave_total = trade_dense(*grads)
    d_attended, pair_totals, down_totals = lax.optimization_barrier(
        (d_attended, pair_totals, down_totals)
    )
    first_pair_grads = reduce_units(pair_totals, shard_rows)
    first_down_grads = reduce_units(down_totals, down_rows)
    d_queries, d_key_value = attend_back(first_queries, first_kv, d_attended)
    d_key_value, leave_total, second_leave_grad, second_enter_grad = lax.optimization_barrier(
        (d_key_value, leave_total, second_leave_grad, second_enter_grad)
    )
    leave_total = reduce_square(leave_total)
    first_entry, grads = enter_back(
        d_queries, d_key_value, d_after, grad_gain, first_in, first_normed, enter_first
    )
    first_enter_grad = reduce_deep(reduce_square(trade_dense(*grads)))
    first_leave_grad = reduce_deep(leave_total)
    first_pair_grads = scatter_units(first_pair_grads)
    first_down_grads = scatter_units(first_down_grads)

    def keep_own(first, second):
        other = swap(on_core(second, first), "section", 1)
        return own_other(on_core(first, second), other)

    layer_out = jnp.stack(keep_own(first_sent, second_sent))
    input_grads = jnp.stack(keep_own(first_entry, second_entry))
    enter_grad = jnp.concatenate(keep_own(first_enter_grad, second_enter_grad), axis=1)
    grad_out = jnp.concatenate(keep_own(first_leave_grad, second_leave_grad), axis=1)
    grad_gains = enter_grad[:, qw + 2 * kw :]

    def keep_experts(first, second):
        former, latter = keep_own(first, second)
        parts, deep = (former.shape[0], former.shape[3])
        if pieces == 1:
            return jnp.stack([former, latter], axis=2).reshape(parts, EXPERTS, deep, -1).astype(f32)
        whole = jnp.stack([former[:, :, 0], latter[:, :, 0]], axis=3)
        return whole.reshape(parts, EXPERTS, deep, -1).astype(f32)

    grad_down = keep_experts(first_down_grads, second_down_grads)[0]
    grad_gate, grad_up = keep_experts(first_pair_grads, second_pair_grads)
    return (
        layer_out[None, :, None],
        input_grads[None, :, None],
        grad_gains[:, 0][None],
        enter_grad[:, :qw][None],
        enter_grad[:, qw : qw + kw][None],
        enter_grad[:, qw + kw : qw + 2 * kw][None],
        grad_out[None],
        grad_gains[:, 1][None],
        grad_gate[None],
        grad_up[None],
        grad_down[None],
    )


def solution(mesh):
    rows_placed = P(None, "fsdp", "ctx", None)
    kept_placed = P("section", None, "fsdp", "ctx", None)
    gain_placed = P("section", ("ctx", "fsdp"))
    dense_placed = P("section", ("ctx", "fsdp"), None)
    expert_placed = P("section", None, ("ctx", "fsdp"), None)
    dense_all = (dense_placed,) * 4
    expert_all = (expert_placed,) * 3
    layer_placed = (gain_placed,) + dense_all + (gain_placed,) + expert_all
    return jax.shard_map(
        body,
        mesh=mesh,
        in_specs=(rows_placed, P(), kept_placed, kept_placed) + layer_placed + (rows_placed,),
        out_specs=(kept_placed, kept_placed) + layer_placed,
        check_vma=False,
    )
```

```python
import functools

import jax
import jax.numpy as jnp
from jax import lax
from jax.experimental import pallas as pl
from jax.experimental.pallas import tpu as pltpu
from jax.sharding import PartitionSpec as P

QH = 12
KVH = 2
HD = 128
GROUP = QH // KVH
TOP = 4
EXPERTS = 8
bf16 = jnp.bfloat16
f32 = jnp.float32


epsilon = 1e-06
masked_out = -1e30
gap = 256


def swap(value, axis, bit):
    count = lax.axis_size(axis)
    return lax.ppermute(value, axis, [(source, source ^ bit) for source in range(count)])


def tie(*values):
    return lax.optimization_barrier(values)


def after(value, earlier):
    return tie(value, earlier)[0]


def at(value, index, axis=0):
    return lax.dynamic_index_in_dim(value, index, axis, keepdims=False)


def rms_norm(rows_in, gain):
    return rows_in * lax.rsqrt(jnp.mean(rows_in * rows_in, axis=-1, keepdims=True) + epsilon) * gain


def dot(spec, left, right, kind=f32):
    return jnp.einsum(spec, left, right, preferred_element_type=kind)


TINY = pl.CostEstimate(flops=1000, bytes_accessed=1000, transcendentals=0)


def kernel_params():
    return pltpu.CompilerParams(vmem_limit_bytes=56 * 1024 * 1024)


def nt(left, right):
    return lax.dot_general(left, right, (((1,), (1,)), ((), ())), preferred_element_type=f32)


def nn(left, right):
    return jnp.dot(left, right, preferred_element_type=f32)


def head_rows(ref):
    return jnp.concatenate([ref[:, i * HD : (i + 1) * HD] for i in range(GROUP)], axis=0)


def softmax_rows(ids_ref, queries, keys, half, own):
    scores = nt(queries, keys) * HD ** (-0.5)
    tall, wide = scores.shape
    row = lax.broadcasted_iota(jnp.int32, (half, 1), 0)
    row = jnp.concatenate([row] * (tall // half), axis=0) + ids_ref[own] * half
    lane = lax.broadcasted_iota(jnp.int32, (1, half), 1)
    column = [lane + ids_ref[block] * half for block in range(wide // half)]
    column = jnp.concatenate(column, axis=1)
    scores = jnp.where(row >= column, scores, masked_out)
    shifted = jnp.exp(scores - jnp.max(scores, axis=1, keepdims=True))
    return shifted / jnp.sum(shifted, axis=1, keepdims=True)


def attend_kernel(ids_ref, query_ref, key_ref, value_ref, out_ref):
    half = query_ref.shape[0]
    probs = softmax_rows(ids_ref, head_rows(query_ref), key_ref[...], half, pl.program_id(1))
    out = nn(probs.astype(bf16), value_ref[...]).astype(bf16)
    for i in range(GROUP):
        out_ref[:, i * HD : (i + 1) * HD] = out[i * half : (i + 1) * half]


def attend_specs(rows, seq_len):
    half = rows // 2
    by_head = pl.BlockSpec((half, GROUP * HD), lambda g, h, ids: (h, g))
    keys = pl.BlockSpec((seq_len, HD), lambda g, h, ids: (0, g))
    values = pl.BlockSpec((seq_len, HD), lambda g, h, ids: (0, KVH + g))
    return by_head, keys, values


def attend_call(ids, queries, key_value):
    rows, seq_len = (queries.shape[0], key_value.shape[0])
    by_head, keys, values = attend_specs(rows, seq_len)
    return pl.pallas_call(
        attend_kernel,
        grid_spec=pltpu.PrefetchScalarGridSpec(
            num_scalar_prefetch=1,
            grid=(KVH, 2),
            in_specs=[by_head, keys, values],
            out_specs=by_head,
        ),
        out_shape=jax.ShapeDtypeStruct(queries.shape, bf16),
        compiler_params=kernel_params(),
        cost_estimate=TINY,
        name="attend",
    )(ids, queries, key_value, key_value)


def attend_back_kernel(ids_ref, query_ref, key_ref, value_ref, cot_ref, dq_ref, dk_ref, dv_ref):
    half = query_ref.shape[0]
    own = pl.program_id(1)
    queries, cot = (head_rows(query_ref), head_rows(cot_ref))
    probs = softmax_rows(ids_ref, queries, key_ref[...], half, own)
    d_probs = nt(cot, value_ref[...])
    inner = jnp.sum(probs * d_probs, axis=1, keepdims=True)
    d_scores = (probs * (d_probs - inner)).astype(bf16)
    d_queries = (nn(d_scores, key_ref[...]) * HD ** (-0.5)).astype(bf16)
    for i in range(GROUP):
        dq_ref[:, i * HD : (i + 1) * HD] = d_queries[i * half : (i + 1) * half]
    d_keys = nn(d_scores.T, queries) * HD ** (-0.5)
    d_values = nn(probs.astype(bf16).T, cot)

    @pl.when(own == 0)
    def _():
        dk_ref[...] = d_keys
        dv_ref[...] = d_values

    @pl.when(own != 0)
    def _():
        dk_ref[...] += d_keys
        dv_ref[...] += d_values


def attend_back_call(ids, queries, key_value, cot):
    rows, seq_len = (queries.shape[0], key_value.shape[0])
    by_head, keys, values = attend_specs(rows, seq_len)
    summed = jax.ShapeDtypeStruct((seq_len, KVH * HD), f32)
    return pl.pallas_call(
        attend_back_kernel,
        grid_spec=pltpu.PrefetchScalarGridSpec(
            num_scalar_prefetch=1,
            grid=(KVH, 2),
            in_specs=[by_head, keys, values, by_head],
            out_specs=[by_head, keys, keys],
        ),
        out_shape=[jax.ShapeDtypeStruct(queries.shape, bf16), summed, summed],
        compiler_params=kernel_params(),
        cost_estimate=TINY,
        name="attend_back",
    )(ids, queries, key_value, key_value, cot)


def gelu_parts(gate):
    root = 0.7978845608028654
    inner = root * (gate + 0.044715 * gate * gate * gate)
    bent = jnp.tanh(inner)
    value = 0.5 * gate * (1.0 + bent)
    slope = root * (1.0 + 3.0 * 0.044715 * gate * gate)
    return value, 0.5 * (1.0 + bent) + 0.5 * gate * (1.0 - bent * bent) * slope


def give_back(pick_ref, total_ref, share_ref, before, out):
    blocks, capacity, _ = pick_ref.shape
    for d in range(blocks):
        part = total_ref[d * capacity : (d + 1) * capacity, :]
        if share_ref is not None:
            part = part * share_ref[d]
        back = nn(pick_ref[d].T, part.astype(bf16))
        if before:
            back = back + before[d][...]
        out[d][...] = back.astype(out[d].dtype)


def expert_kernel(blocks, adds, pick_ref, share_ref, gate_ref, up_ref, down_ref, *refs):
    rows, refs = (refs[:blocks], refs[blocks:])
    before, refs = (refs[: blocks * adds], refs[blocks * adds :])
    out, (picked_ref, gate_pre_ref, up_pre_ref, total_ref) = (refs[:blocks], refs[blocks:])
    step = pl.program_id(0)
    capacity = pick_ref.shape[1]

    @pl.when(step == 0)
    def _():
        for d in range(blocks):
            block = nn(pick_ref[d], rows[d][...]).astype(bf16)
            picked_ref[d * capacity : (d + 1) * capacity, :] = block

    gate_pre = nn(picked_ref[...], gate_ref[...])
    up_pre = nn(picked_ref[...], up_ref[...])
    gate_pre_ref[...] = gate_pre
    up_pre_ref[...] = up_pre
    active = (gelu_parts(gate_pre)[0] * up_pre).astype(bf16)
    part = nn(active, down_ref[...])

    @pl.when(step == 0)
    def _():
        total_ref[...] = part

    @pl.when(step != 0)
    def _():
        total_ref[...] += part

    @pl.when(step == pl.num_programs(0) - 1)
    def _():
        give_back(pick_ref, total_ref, share_ref, before, out)


def whole_spec(shape):
    return pl.BlockSpec(shape, lambda step: (0,) * len(shape))


def expert_call(picks, shares, rows, pair, down, before):
    blocks, capacity, _ = picks.shape
    width, hidden = (rows[0].shape[1], down.shape[0])
    cut = 256
    tall = blocks * capacity
    columns = pl.BlockSpec((tall, cut), lambda step: (0, step))
    row_specs = [whole_spec(block.shape) for block in rows]
    kind = bf16 if before else f32
    result = pl.pallas_call(
        functools.partial(expert_kernel, blocks, 1 if before else 0),
        grid=(hidden // cut,),
        in_specs=[
            whole_spec(picks.shape),
            whole_spec(shares.shape),
            pl.BlockSpec((width, cut), lambda step: (0, step)),
            pl.BlockSpec((width, cut), lambda step: (0, hidden // cut + step)),
            pl.BlockSpec((cut, width), lambda step: (step, 0)),
        ]
        + row_specs * (2 if before else 1),
        out_specs=row_specs + [whole_spec((tall, width)), columns, columns],
        out_shape=[jax.ShapeDtypeStruct(block.shape, kind) for block in rows]
        + [
            jax.ShapeDtypeStruct((tall, width), bf16),
            jax.ShapeDtypeStruct((tall, hidden), f32),
            jax.ShapeDtypeStruct((tall, hidden), f32),
        ],
        scratch_shapes=[pltpu.VMEM((tall, width), f32)],
        compiler_params=kernel_params(),
        cost_estimate=TINY,
        name="expert",
    )(picks, shares, pair, pair, down, *rows, *before)
    return (result[:blocks], result[blocks:])


def expert_back_kernel(
    blocks, adds, pick_ref, share_ref, picked_ref, gate_pre_ref, up_pre_ref,
    gate_ref, up_ref, down_ref, *refs
):
    rows, refs = (refs[:blocks], refs[blocks:])
    before, refs = (refs[: blocks * adds], refs[blocks * adds :])
    out, refs = (refs[:blocks], refs[blocks:])
    pair_ref, down_grad_ref, slots_ref, turned_ref, total_ref = refs
    capacity = pick_ref.shape[1]
    step = pl.program_id(0)

    @pl.when(step == 0)
    def _():
        for d in range(blocks):
            block = nn(pick_ref[d], rows[d][...]) * share_ref[d]
            slots_ref[d * capacity : (d + 1) * capacity, :] = block.astype(bf16)
        turned_ref[...] = picked_ref[...].T

    d_active = nt(slots_ref[...], down_ref[...])
    value, slope = gelu_parts(gate_pre_ref[...])
    up_pre = up_pre_ref[...]
    active = (value * up_pre).astype(bf16)
    d_gate = (d_active * up_pre * slope).astype(bf16)
    d_up = (d_active * value).astype(bf16)
    down_grad_ref[...] = nn(active.T, slots_ref[...]).astype(bf16)
    pair_ref[0] = nn(turned_ref[...], d_gate).astype(bf16)
    pair_ref[1] = nn(turned_ref[...], d_up).astype(bf16)
    part = nt(d_gate, gate_ref[...]) + nt(d_up, up_ref[...])

    @pl.when(step == 0)
    def _():
        total_ref[...] = part

    @pl.when(step != 0)
    def _():
        total_ref[...] += part

    @pl.when(step == pl.num_programs(0) - 1)
    def _():
        give_back(pick_ref, total_ref, None, before, out)


def expert_back_call(picks, shares, rows, kept, pair, down, before):
    blocks, capacity, _ = picks.shape
    width, hidden = (rows[0].shape[1], down.shape[0])
    cut = 256
    tall = blocks * capacity
    columns = pl.BlockSpec((tall, cut), lambda step: (0, step))
    row_specs = [whole_spec(block.shape) for block in rows]
    kind = bf16 if before else f32
    result = pl.pallas_call(
        functools.partial(expert_back_kernel, blocks, 1 if before else 0),
        grid=(hidden // cut,),
        in_specs=[
            whole_spec(picks.shape),
            whole_spec(shares.shape),
            whole_spec((tall, width)),
            columns,
            columns,
            pl.BlockSpec((width, cut), lambda step: (0, step)),
            pl.BlockSpec((width, cut), lambda step: (0, hidden // cut + step)),
            pl.BlockSpec((cut, width), lambda step: (step, 0)),
        ]
        + row_specs * (2 if before else 1),
        out_specs=row_specs
        + [
            pl.BlockSpec((2, width, cut), lambda step: (0, 0, step)),
            pl.BlockSpec((cut, width), lambda step: (step, 0)),
        ],
        out_shape=[jax.ShapeDtypeStruct(block.shape, kind) for block in rows]
        + [
            jax.ShapeDtypeStruct((2, width, hidden), bf16),
            jax.ShapeDtypeStruct((hidden, width), bf16),
        ],
        scratch_shapes=[
            pltpu.VMEM((tall, width), bf16),
            pltpu.VMEM((width, tall), bf16),
            pltpu.VMEM((tall, width), f32),
        ],
        compiler_params=kernel_params(),
        cost_estimate=TINY,
        name="expert_back",
    )(picks, shares, *kept, pair, pair, down, *rows, *before)
    return (result[:blocks], result[blocks], result[blocks + 1])


def place_kernel(count, index_ref, *refs):
    step = pl.program_id(0)
    for bit in range(count):

        @pl.when(step == bit)
        def _():
            refs[count][0] = refs[bit][...]


def place_call(blocks, index):
    count = len(blocks)
    height, wide = blocks[0].shape
    result = pl.pallas_call(
        functools.partial(place_kernel, count),
        grid_spec=pltpu.PrefetchScalarGridSpec(
            num_scalar_prefetch=1,
            grid=(count,),
            in_specs=[pl.BlockSpec((height, wide), lambda step, at: (0, 0))] * count,
            out_specs=pl.BlockSpec((1, height, wide), lambda step, at: (at[0] ^ step, 0, 0)),
        ),
        out_shape=jax.ShapeDtypeStruct((count, height, wide), blocks[0].dtype),
        compiler_params=kernel_params(),
        cost_estimate=TINY,
        name="place",
    )(index.astype(jnp.int32).reshape(1), *blocks)
    return result.reshape(count * height, wide)


def order_kernel(count, order_ref, *refs):
    step = pl.program_id(0)
    for i in range(count):

        @pl.when(step == i)
        def _():
            refs[count][0, 0] = refs[i][0, 0]


def order_call(blocks, order, unit):
    count = len(blocks)
    n_ctx, _, tall, wide = blocks[0].shape

    def source(i):
        return pl.BlockSpec(
            (1, 1, tall, wide), lambda step, c, at: (jnp.where(step == i, c, 0), unit, 0, 0)
        )

    result = pl.pallas_call(
        functools.partial(order_kernel, count),
        grid_spec=pltpu.PrefetchScalarGridSpec(
            num_scalar_prefetch=1,
            grid=(count, n_ctx),
            in_specs=[source(i) for i in range(count)],
            out_specs=pl.BlockSpec((1, 1, tall, wide), lambda step, c, at: (c, at[step], 0, 0)),
        ),
        out_shape=jax.ShapeDtypeStruct((n_ctx, count, tall, wide), bf16),
        compiler_params=kernel_params(),
        cost_estimate=TINY,
        name="order",
    )(order.astype(jnp.int32), *blocks)
    return result.reshape(-1, wide)


def deal_kernel(count, deep, index_ref, *refs):
    step = pl.program_id(0)
    top_ref, rest_ref = refs[count:]
    for bit in range(count):

        @pl.when(step == bit)
        def _():
            top_ref[0] = refs[bit][:, :deep]
            rest_ref[0] = refs[bit][:, deep:]


def deal_call(blocks, deep, index):
    count = len(blocks)
    units, tall, wide = blocks[0].shape
    target = lambda step, at: (at[0] ^ step, 0, 0, 0)
    return pl.pallas_call(
        functools.partial(deal_kernel, count, deep),
        grid_spec=pltpu.PrefetchScalarGridSpec(
            num_scalar_prefetch=1,
            grid=(count,),
            in_specs=[pl.BlockSpec((units, tall, wide), lambda step, at: (0, 0, 0))] * count,
            out_specs=[
                pl.BlockSpec((1, units, deep, wide), target),
                pl.BlockSpec((1, units, tall - deep, wide), target),
            ],
        ),
        out_shape=[
            jax.ShapeDtypeStruct((count, units, deep, wide), bf16),
            jax.ShapeDtypeStruct((count, units, tall - deep, wide), bf16),
        ],
        compiler_params=kernel_params(),
        cost_estimate=TINY,
        name="deal",
    )(index.astype(jnp.int32).reshape(1), *blocks)


def body(
    tokens,
    block_of,
    routes,
    combine,
    attn_norm,
    w_query,
    w_key,
    w_value,
    w_out,
    ffn_norm,
    w_gate,
    w_up,
    w_down,
    out_grad,
):
    rows = tokens.shape[2]
    width = tokens.shape[3]
    half = rows // 2
    n_ctx = lax.axis_size("ctx")
    n_fsdp = lax.axis_size("fsdp")
    core, place, depth = (
        lax.axis_index(axis).astype(jnp.uint32) for axis in ("section", "ctx", "fsdp")
    )
    seq_len = rows * n_ctx
    capacity = rows * TOP * 5 // (4 * EXPERTS)
    score_scale = HD ** (-0.5)
    own_experts = EXPERTS // n_ctx
    hidden = w_gate.shape[3]
    shard_rows = w_query.shape[1]
    down_rows = w_down.shape[2]
    qw = w_query.shape[2]
    kw = w_key.shape[2]
    pieces = max(1, 2 * n_ctx // EXPERTS)
    per_core = max(1, EXPERTS // (2 * n_ctx))

    def on_core(former, latter):
        return jnp.where(core == 0, former, latter)

    def own_other(low, high):
        return (on_core(low, high), on_core(high, low))

    def to_units(shard):
        count, deep, wide = shard.shape
        if pieces == 1:
            return shard
        cut = shard.reshape(count, deep, pieces, wide // pieces).transpose(0, 2, 1, 3)
        return cut.reshape(2 * n_ctx, deep, wide // pieces)

    def spread(value):
        return [value] + [swap(value, "ctx", bit) for bit in range(1, n_ctx)]

    def collect(blocks):
        total = blocks[0].astype(f32)
        for bit in range(1, n_ctx):
            total = total + swap(blocks[bit].astype(bf16), "ctx", bit).astype(f32)
        return total

    info = jnp.concatenate([routes.astype(f32), combine], axis=-1)[0, :, 0].transpose(0, 2, 1)
    info_own, info_other = (at(info, core), swap(at(info, 1 - core), "section", 1))
    info = jnp.stack(own_other(info_own, info_other))
    info = jnp.stack([info] + [swap(info, "ctx", bit) for bit in range(1, n_ctx)], axis=1)

    gain_columns = jnp.stack([attn_norm[0], ffn_norm[0]], axis=1)
    gain_columns = jnp.pad(gain_columns, ((0, 0), (0, gap - 2)))
    enter_shard = jnp.concatenate([w_query[0], w_key[0], w_value[0], gain_columns], axis=1)
    enter_cut = enter_shard.shape[1] // 2
    leave_cut = w_out.shape[2] // 2
    low_shard = jnp.concatenate([enter_shard[:, :enter_cut], w_out[0, :, :leave_cut]], axis=1)
    high_shard = jnp.concatenate([enter_shard[:, enter_cut:], w_out[0, :, leave_cut:]], axis=1)
    lent = swap(on_core(high_shard, low_shard), "section", 1)
    dense_shards = (on_core(low_shard, lent), on_core(lent, high_shard))

    def gather_deep(shard):
        return place_call([shard] + [swap(shard, "fsdp", bit) for bit in range(1, n_fsdp)], depth)

    def gather_square(deep):
        return place_call(spread(deep), place)

    unit_stack = jnp.concatenate(
        [
            jnp.concatenate([to_units(w_gate[0]), to_units(w_up[0])], axis=2),
            to_units(w_down[0]),
        ],
        axis=1,
    )
    unit_stack = unit_stack.reshape((n_ctx, 2, per_core) + unit_stack.shape[1:])

    units_lent = swap(at(unit_stack, 1 - core, 1), "section", 1)
    unit_stacks = own_other(at(unit_stack, core, 1), units_lent)

    def deal_units(stack):
        blocks = [at(stack, place)]
        blocks += [swap(at(stack, place ^ bit), "ctx", bit) for bit in range(1, n_ctx)]
        return deal_call(blocks, shard_rows, place)

    ring = list(range(0, n_fsdp, 2)) + list(range(1, n_fsdp, 2))[::-1]
    ring_steps = [(ring[i], ring[(i + 1) % n_fsdp]) for i in range(n_fsdp)]
    ring_table = [[ring[ring.index(z) - i] for i in range(n_fsdp)] for z in range(n_fsdp)]
    behind_here = at(jnp.array(ring_table, jnp.uint32), depth)

    def ring_send(moved):
        return [blocks + [lax.ppermute(blocks[-1], "fsdp", ring_steps)] for blocks in moved]

    def order_units(moved):
        return [
            [order_call(blocks, behind_here, unit) for unit in range(per_core)] for blocks in moved
        ]

    def pair_units(mine):
        other = [swap(part, "section", 1) for part in mine]
        if pieces == 1:
            return list(mine) + other
        low, high = own_other(mine[0], other[0])
        if mine[0].shape[0] == width:
            cut = hidden // 2
            parts = [low[:, :cut], high[:, :cut], low[:, cut:], high[:, cut:]]
            return [jnp.concatenate(parts, axis=1)]
        return [jnp.concatenate([low, high], axis=1)]

    def cut_units(grads):
        if pieces == 1:
            return (grads[:per_core], grads[per_core:])
        own, other = own_other(*jnp.split(grads[0], 2, axis=-1))
        return ([own], [other])

    def ring_part(terms, behind):
        spot = behind_here[behind % n_fsdp]
        return sum(at(term, spot, 2).astype(f32) for term in terms)

    def ring_start(own, received, deep):
        terms = [part.reshape(-1, n_ctx, n_fsdp, deep, part.shape[-1]) for part in (own, received)]
        return (terms, ring_part(terms, 1).astype(bf16))

    def ring_step(state, step):
        return [
            (terms, (lax.ppermute(moving, "fsdp", ring_steps).astype(f32)
                     + ring_part(terms, step + 1)).astype(bf16))
            for terms, moving in state
        ]

    def ring_rest(state, first):
        for step in range(first, n_fsdp):
            state = ring_step(state, step)
        return [moving for _, moving in state]

    def scatter_units(moved):
        return [
            lax.all_to_all(jnp.stack(part, axis=2), "ctx", 1, 1)
            for part in (moved[:per_core], moved[per_core:])
        ]

    def reduce_square(own, received):
        own, received = (part.reshape(n_ctx, n_fsdp * shard_rows, -1) for part in (own, received))

        def part(bit):
            return at(own, place ^ bit).astype(f32) + at(received, place ^ bit).astype(f32)

        total = part(0)
        for bit in range(1, n_ctx):
            total = total + swap(part(bit).astype(bf16), "ctx", bit).astype(f32)
        return total.astype(bf16)

    def reduce_deep(mine):
        mine = mine.reshape(n_fsdp, shard_rows, -1)
        total = at(mine, depth).astype(f32)
        for bit in range(1, n_fsdp):
            total = total + swap(at(mine, depth ^ bit), "fsdp", bit).astype(f32)
        return total

    if pieces == 1:
        units_here = jnp.arange(per_core, dtype=jnp.uint32)
        units_here = jnp.concatenate(
            [core * per_core + units_here, (1 - core) * per_core + units_here]
        )
    else:
        units_here = jnp.zeros((1,), jnp.uint32)
    named = (place * own_experts + units_here).astype(f32)
    matches = info[:, None, :, :TOP] == named[None, :, None, None, None]
    hits = jnp.any(matches, axis=3)
    shares = jnp.sum(jnp.where(matches, info[:, None, :, TOP:], 0.0), axis=3)
    earlier = jnp.arange(rows)[:, None] < jnp.arange(rows)[None, :]
    rank = dot("ledr,rq->ledq", hits.astype(bf16), earlier.astype(bf16))
    slots = jnp.arange(capacity, dtype=f32)
    picks = hits[:, :, :, None, :] & (rank[:, :, :, None, :] == slots[:, None])
    slot_shares = jnp.sum(jnp.where(picks, shares[:, :, :, None, :], 0.0), axis=-1, keepdims=True)
    picks = picks.astype(bf16)

    order = place.astype(jnp.int32) ^ jnp.arange(n_ctx, dtype=jnp.int32)
    block_ids = jnp.take(block_of.reshape(n_ctx, 2), order, axis=0)
    block_ids = block_ids.reshape(-1)

    def project(value, halves):
        own, other = (dot("qa,ab->qb", value, part) for part in halves)
        return jnp.concatenate(own_other(own, other), axis=1)

    def project_back(value, halves):
        cut = value.shape[1] // 2
        own, other = own_other(value[:, :cut], value[:, cut:])
        total = dot("qb,ab->qa", own, halves[0]) + dot("qb,ab->qa", other, halves[1])
        return (total, own, other)

    def gains_of(halves):
        pair = on_core(halves[1][:, -gap : 2 - gap], halves[0][:, -gap : 2 - gap]).astype(f32)
        return (pair[:, 0], pair[:, 1])

    def enter(layer_input, halves):
        normed = rms_norm(layer_input, gains_of(halves)[0]).astype(bf16)
        entered = project(normed, halves).astype(bf16)
        return (normed, entered[:, :qw], entered[:, qw : qw + 2 * kw])

    def experts(layer, blocks, pairs, downs):
        returned, kept = ([], {})
        for j in range(own_experts):
            returned, kept[j] = expert_call(
                picks[layer, j], slot_shares[layer, j], blocks, pairs[j], downs[j], returned
            )
        return (returned, kept)

    def experts_back(layer, blocks, pairs, downs, kept):
        returned, grads = ([], {})
        for j in reversed(range(own_experts)):
            returned, *grads[j] = expert_back_call(
                picks[layer, j],
                slot_shares[layer, j],
                blocks,
                kept[j],
                pairs[j],
                downs[j],
                returned,
            )
        own, other = ([], [])
        for kind in range(2):
            mine, lended = cut_units([grads[j][kind] for j in range(own_experts)])
            own, other = (own + mine, other + lended)
        received = [swap(part, "section", 1) for part in other]
        *returned, own, received = tie(*returned, own, received)
        deep = [shard_rows] * per_core + [down_rows] * per_core
        state = [ring_start(a, b, d) for a, b, d in zip(own, received, deep)]
        return (returned, state)

    def leave_back(cotangent, d_ffn_normed, after_attention, attended, enter_halves, leave_halves):
        ffn_back = jax.vjp(rms_norm, after_attention, gains_of(enter_halves)[1])[1]
        d_after, grad_gain = ffn_back(d_ffn_normed)
        d_after = d_after + cotangent.astype(f32)
        d_attended, own, other = project_back(d_after.astype(bf16), leave_halves)
        grads = [dot("qa,qb->ab", attended, part, bf16) for part in (own, other)]
        return (d_after, grad_gain, d_attended.astype(bf16), grads)

    def attend_back(queries, key_value_all, d_attended):
        d_queries, d_keys, d_values = attend_back_call(
            block_ids, queries, key_value_all, d_attended
        )
        d_key_value = jnp.concatenate([d_keys, d_values], axis=1).reshape(n_ctx, rows, 2 * kw)
        return (d_queries, collect(d_key_value).astype(bf16))

    def enter_back(d_queries, d_key_value, d_after, grad_gain_ffn, layer_input, normed, halves):
        blank = jnp.zeros((rows, gap), bf16)
        d_entered = jnp.concatenate([d_queries, d_key_value, blank], axis=1)
        d_normed, own, other = project_back(d_entered, halves)
        attn_back = jax.vjp(rms_norm, layer_input, gains_of(halves)[0])[1]
        d_input, grad_gain = attn_back(d_normed)
        gain_columns = jnp.stack([grad_gain, grad_gain_ffn], axis=1)
        gain_columns = jnp.pad(gain_columns, ((0, 0), (enter_cut - gap, gap - 2)))
        own, other = (dot("qa,qb->ab", normed, part) for part in (own, other))
        own = own + on_core(0.0, gain_columns)
        other = other + on_core(gain_columns, 0.0)
        return (d_input + d_after, [own.astype(bf16), other.astype(bf16)])

    deep_first = gather_deep(dense_shards[0])
    dealt_first = deal_units(unit_stacks[0])
    deep_first, dealt_first, picks, stack_second = tie(
        deep_first, dealt_first, picks, unit_stacks[1]
    )
    enter_own = gather_square(deep_first[:, :enter_cut])
    units_moved = ring_send([[part] for part in dealt_first])
    enter_own, units_moved, deep_first, dealt_second = tie(
        enter_own, units_moved, deep_first, deal_units(stack_second)
    )
    enter_first = (enter_own, swap(enter_own, "section", 1))

    first_in = after(at(tokens, core)[0].astype(f32), slot_shares)
    first_normed, first_queries, key_value = enter(first_in, enter_first)
    first_kv, units_moved, deep_first, shard_second = tie(
        jnp.concatenate(spread(key_value)), ring_send(units_moved), deep_first, dense_shards[1]
    )
    leave_own = gather_square(deep_first[:, enter_cut:])
    leave_first = (leave_own, swap(leave_own, "section", 1))
    first_attended = attend_call(block_ids, first_queries, first_kv)
    first_mid = first_in + project(first_attended, leave_first)
    ffn_normed = rms_norm(first_mid, gains_of(enter_first)[1]).astype(bf16)
    for _ in range(3, n_fsdp):
        units_moved = ring_send(units_moved)
    ffn_normed, units_moved, deep_second, dealt_second = tie(
        ffn_normed, units_moved, gather_deep(shard_second), dealt_second
    )
    first_pairs, first_downs = (pair_units(part) for part in order_units(units_moved))
    blocks, deep_second, units_moved = tie(
        spread(ffn_normed), deep_second, ring_send([[part] for part in dealt_second])
    )
    enter_own = gather_square(deep_second[:, :enter_cut])
    returned, first_kept = experts(0, blocks, first_pairs, first_downs)
    returned, enter_own, deep_second, units_moved = tie(
        returned, enter_own, deep_second, ring_send(units_moved)
    )
    first_out = first_mid + collect(returned)
    for _ in range(3, n_fsdp):
        units_moved = ring_send(units_moved)
    first_out, enter_other, deep_second, units_moved = tie(
        first_out, swap(enter_own, "section", 1), deep_second, units_moved
    )
    enter_second = (enter_own, enter_other)
    first_sent = first_out.astype(bf16)

    second_in = first_sent.astype(f32)
    second_normed, second_queries, key_value = enter(second_in, enter_second)
    leave_own = gather_square(deep_second[:, enter_cut:])
    leave_second = (leave_own, swap(leave_own, "section", 1))
    second_kv = jnp.concatenate(spread(key_value))
    second_attended = attend_call(block_ids, second_queries, second_kv)
    second_mid = second_in + project(second_attended, leave_second)
    ffn_normed = rms_norm(second_mid, gains_of(enter_second)[1]).astype(bf16)
    second_pairs, second_downs = (pair_units(part) for part in order_units(units_moved))
    blocks = spread(ffn_normed)
    cotangent = after(at(out_grad, core)[0], blocks)
    cot_blocks = spread(cotangent)
    second_returned, second_kept = experts(1, blocks, second_pairs, second_downs)

    returned, units_moving = experts_back(1, cot_blocks, second_pairs, second_downs, second_kept)
    d_ffn_normed, units_moving = tie(collect(returned), ring_step(units_moving, 1))
    second_sent = (second_mid + collect(after(second_returned, d_ffn_normed))).astype(bf16)
    d_after, grad_gain, d_attended, grads = leave_back(
        cotangent, d_ffn_normed, second_mid, second_attended, enter_second, leave_second
    )
    leave_grads = (grads[0], swap(grads[1], "section", 1))
    d_queries, d_key_value = attend_back(second_queries, second_kv, d_attended)
    d_key_value, units_moving, leave_grads, second_sent = tie(
        d_key_value, ring_step(units_moving, 2), leave_grads, second_sent
    )
    second_entry, grads = enter_back(
        d_queries, d_key_value, d_after, grad_gain, second_in, second_normed, enter_second
    )
    enter_grads = (grads[0], swap(grads[1], "section", 1))

    cotangent = second_entry.astype(bf16)
    *blocks, enter_grads, units_moving = tie(
        *spread(cotangent), enter_grads, ring_rest(units_moving, 3)
    )
    second_experts = scatter_units(units_moving)
    dense_moving = [reduce_square(*enter_grads), reduce_square(*leave_grads)]
    returned, units_moving = experts_back(0, blocks, first_pairs, first_downs, first_kept)
    returned, second_experts, dense_moving = tie(returned, second_experts, dense_moving)
    d_ffn_normed, units_moving = tie(collect(returned), ring_step(units_moving, 1))
    second_dense = [reduce_deep(part) for part in dense_moving]
    d_after, grad_gain, d_attended, grads = leave_back(
        cotangent, d_ffn_normed, first_mid, first_attended, enter_first, leave_first
    )
    leave_grads = (grads[0], swap(grads[1], "section", 1))
    d_queries, d_key_value = attend_back(first_queries, first_kv, d_attended)
    d_key_value, units_moving, leave_grads, second_dense = tie(
        d_key_value, ring_step(units_moving, 2), leave_grads, second_dense
    )
    leave_moving = reduce_square(*leave_grads)
    first_entry, grads = enter_back(
        d_queries, d_key_value, d_after, grad_gain, first_in, first_normed, enter_first
    )
    enter_moving = reduce_square(grads[0], swap(grads[1], "section", 1))
    first_experts = scatter_units(ring_rest(units_moving, 3))
    first_dense = [reduce_deep(enter_moving), reduce_deep(leave_moving)]

    def keep_own(first, second):
        other = swap(on_core(second, first), "section", 1)
        return own_other(on_core(first, second), other)

    layer_out = jnp.stack(keep_own(first_sent, second_sent))
    input_grads = jnp.stack(keep_own(first_entry, second_entry))
    enter_grad = jnp.concatenate(keep_own(first_dense[0], second_dense[0]), axis=1)
    grad_out = jnp.concatenate(keep_own(first_dense[1], second_dense[1]), axis=1)
    grad_gains = enter_grad[:, qw + 2 * kw :]

    def keep_experts(first, second):
        former, latter = keep_own(first, second)
        parts, deep = (former.shape[0], former.shape[3])
        if pieces == 1:
            return jnp.stack([former, latter], axis=2).reshape(parts, EXPERTS, deep, -1).astype(f32)
        whole = jnp.stack([former[:, :, 0], latter[:, :, 0]], axis=3)
        return whole.reshape(parts, EXPERTS, deep, -1).astype(f32)

    grad_gate, grad_up = keep_experts(first_experts[0], second_experts[0])
    grad_down = keep_experts(first_experts[1], second_experts[1])[0]
    return (
        layer_out[None, :, None],
        input_grads[None, :, None],
        grad_gains[:, 0][None],
        enter_grad[:, :qw][None],
        enter_grad[:, qw : qw + kw][None],
        enter_grad[:, qw + kw : qw + 2 * kw][None],
        grad_out[None],
        grad_gains[:, 1][None],
        grad_gate[None],
        grad_up[None],
        grad_down[None],
    )


def solution(mesh):
    rows_placed = P(None, "fsdp", "ctx", None)
    kept_placed = P("section", None, "fsdp", "ctx", None)
    gain_placed = P("section", ("ctx", "fsdp"))
    dense_placed = P("section", ("ctx", "fsdp"), None)
    expert_placed = P("section", None, ("ctx", "fsdp"), None)
    dense_all = (dense_placed,) * 4
    expert_all = (expert_placed,) * 3
    layer_placed = (gain_placed,) + dense_all + (gain_placed,) + expert_all
    return jax.shard_map(
        body,
        mesh=mesh,
        in_specs=(rows_placed, P(), kept_placed, kept_placed) + layer_placed + (rows_placed,),
        out_specs=(kept_placed, kept_placed) + layer_placed,
        check_vma=False,
    )
```

```python
import functools

import jax
import jax.numpy as jnp
from jax import lax
from jax.experimental import pallas as pl
from jax.experimental.pallas import tpu as pltpu
from jax.sharding import PartitionSpec as P

QH = 12
KVH = 2
HD = 128
GROUP = QH // KVH
TOP = 4
EXPERTS = 8
bf16 = jnp.bfloat16
f32 = jnp.float32


epsilon = 1e-06
masked_out = -1e30
gap = 256


def swap(value, axis, bit):
    count = lax.axis_size(axis)
    return lax.ppermute(value, axis, [(source, source ^ bit) for source in range(count)])


def tie(*values):
    return lax.optimization_barrier(values)


def after(value, earlier):
    return tie(value, earlier)[0]


def at(value, index, axis=0):
    return lax.dynamic_index_in_dim(value, index, axis, keepdims=False)


def rms_norm(rows_in, gain):
    return rows_in * lax.rsqrt(jnp.mean(rows_in * rows_in, axis=-1, keepdims=True) + epsilon) * gain


def dot(spec, left, right, kind=f32):
    return jnp.einsum(spec, left, right, preferred_element_type=kind)


TINY = pl.CostEstimate(flops=1000, bytes_accessed=1000, transcendentals=0)


def kernel_params():
    return pltpu.CompilerParams(vmem_limit_bytes=56 * 1024 * 1024)


def nt(left, right):
    return lax.dot_general(left, right, (((1,), (1,)), ((), ())), preferred_element_type=f32)


def nn(left, right):
    return jnp.dot(left, right, preferred_element_type=f32)


def head_rows(ref):
    return jnp.concatenate([ref[:, i * HD : (i + 1) * HD] for i in range(GROUP)], axis=0)


def softmax_rows(ids_ref, queries, keys, half, own):
    scores = nt(queries, keys) * HD ** (-0.5)
    tall, wide = scores.shape
    row = lax.broadcasted_iota(jnp.int32, (half, 1), 0)
    row = jnp.concatenate([row] * (tall // half), axis=0) + ids_ref[own] * half
    lane = lax.broadcasted_iota(jnp.int32, (1, half), 1)
    column = [lane + ids_ref[block] * half for block in range(wide // half)]
    column = jnp.concatenate(column, axis=1)
    scores = jnp.where(row >= column, scores, masked_out)
    shifted = jnp.exp(scores - jnp.max(scores, axis=1, keepdims=True))
    return shifted / jnp.sum(shifted, axis=1, keepdims=True)


def attend_kernel(ids_ref, query_ref, key_ref, value_ref, out_ref):
    half = query_ref.shape[0]
    probs = softmax_rows(ids_ref, head_rows(query_ref), key_ref[...], half, pl.program_id(1))
    out = nn(probs.astype(bf16), value_ref[...]).astype(bf16)
    for i in range(GROUP):
        out_ref[:, i * HD : (i + 1) * HD] = out[i * half : (i + 1) * half]


def attend_specs(rows, seq_len):
    half = rows // 2
    by_head = pl.BlockSpec((half, GROUP * HD), lambda g, h, ids: (h, g))
    keys = pl.BlockSpec((seq_len, HD), lambda g, h, ids: (0, g))
    values = pl.BlockSpec((seq_len, HD), lambda g, h, ids: (0, KVH + g))
    return by_head, keys, values


def attend_call(ids, queries, key_value):
    rows, seq_len = (queries.shape[0], key_value.shape[0])
    by_head, keys, values = attend_specs(rows, seq_len)
    return pl.pallas_call(
        attend_kernel,
        grid_spec=pltpu.PrefetchScalarGridSpec(
            num_scalar_prefetch=1,
            grid=(KVH, 2),
            in_specs=[by_head, keys, values],
            out_specs=by_head,
        ),
        out_shape=jax.ShapeDtypeStruct(queries.shape, bf16),
        compiler_params=kernel_params(),
        cost_estimate=TINY,
        name="attend",
    )(ids, queries, key_value, key_value)


def attend_back_kernel(ids_ref, query_ref, key_ref, value_ref, cot_ref, dq_ref, dk_ref, dv_ref):
    half = query_ref.shape[0]
    own = pl.program_id(1)
    queries, cot = (head_rows(query_ref), head_rows(cot_ref))
    probs = softmax_rows(ids_ref, queries, key_ref[...], half, own)
    d_probs = nt(cot, value_ref[...])
    inner = jnp.sum(probs * d_probs, axis=1, keepdims=True)
    d_scores = (probs * (d_probs - inner)).astype(bf16)
    d_queries = (nn(d_scores, key_ref[...]) * HD ** (-0.5)).astype(bf16)
    for i in range(GROUP):
        dq_ref[:, i * HD : (i + 1) * HD] = d_queries[i * half : (i + 1) * half]
    d_keys = nn(d_scores.T, queries) * HD ** (-0.5)
    d_values = nn(probs.astype(bf16).T, cot)

    @pl.when(own == 0)
    def _():
        dk_ref[...] = d_keys
        dv_ref[...] = d_values

    @pl.when(own != 0)
    def _():
        dk_ref[...] += d_keys
        dv_ref[...] += d_values


def attend_back_call(ids, queries, key_value, cot):
    rows, seq_len = (queries.shape[0], key_value.shape[0])
    by_head, keys, values = attend_specs(rows, seq_len)
    summed = jax.ShapeDtypeStruct((seq_len, KVH * HD), f32)
    return pl.pallas_call(
        attend_back_kernel,
        grid_spec=pltpu.PrefetchScalarGridSpec(
            num_scalar_prefetch=1,
            grid=(KVH, 2),
            in_specs=[by_head, keys, values, by_head],
            out_specs=[by_head, keys, keys],
        ),
        out_shape=[jax.ShapeDtypeStruct(queries.shape, bf16), summed, summed],
        compiler_params=kernel_params(),
        cost_estimate=TINY,
        name="attend_back",
    )(ids, queries, key_value, key_value, cot)


def gelu_parts(gate):
    root = 0.7978845608028654
    inner = root * (gate + 0.044715 * gate * gate * gate)
    bent = jnp.tanh(inner)
    value = 0.5 * gate * (1.0 + bent)
    slope = root * (1.0 + 3.0 * 0.044715 * gate * gate)
    return value, 0.5 * (1.0 + bent) + 0.5 * gate * (1.0 - bent * bent) * slope


def give_back(pick_ref, total_ref, share_ref, before, out):
    blocks, capacity, _ = pick_ref.shape
    for d in range(blocks):
        part = total_ref[d * capacity : (d + 1) * capacity, :]
        if share_ref is not None:
            part = part * share_ref[d]
        back = nn(pick_ref[d].T, part.astype(bf16))
        if before:
            back = back + before[d][...]
        out[d][...] = back.astype(out[d].dtype)


def flat(ref):
    value = ref[...]
    return value.reshape(-1, value.shape[-1])


def add_up(total_ref, part, step):
    @pl.when(step == 0)
    def _():
        total_ref[...] = part

    @pl.when(step != 0)
    def _():
        total_ref[...] += part


def expert_kernel(blocks, adds, pick_ref, share_ref, gate_ref, up_ref, down_ref, *refs):
    rows, refs = (refs[:blocks], refs[blocks:])
    before, refs = (refs[: blocks * adds], refs[blocks * adds :])
    out, (picked_ref, gate_pre_ref, up_pre_ref, total_ref) = (refs[:blocks], refs[blocks:])
    step = pl.program_id(0)
    capacity = pick_ref.shape[1]

    @pl.when(step == 0)
    def _():
        for d in range(blocks):
            block = nn(pick_ref[d], rows[d][...]).astype(bf16)
            picked_ref[d * capacity : (d + 1) * capacity, :] = block

    gate_pre = nn(picked_ref[...], flat(gate_ref))
    up_pre = nn(picked_ref[...], flat(up_ref))
    gate_pre_ref[...] = gate_pre
    up_pre_ref[...] = up_pre
    active = (gelu_parts(gate_pre)[0] * up_pre).astype(bf16)
    add_up(total_ref, nn(active, flat(down_ref)), step)

    @pl.when(step == pl.num_programs(0) - 1)
    def _():
        give_back(pick_ref, total_ref, share_ref, before, out)


def whole_spec(shape):
    return pl.BlockSpec(
        shape, lambda step: (0,) * len(shape), pipeline_mode=pl.Buffered(buffer_count=1)
    )


def weight_operands(weights, deep, cut):
    if len(weights) == 1:
        unit = weights[0]
        shards, tall, width = unit.shape
        specs = [
            pl.BlockSpec((shards, deep, cut), lambda step: (0, 0, 2 * step)),
            pl.BlockSpec((shards, deep, cut), lambda step: (0, 0, 2 * step + 1)),
            pl.BlockSpec(
                (shards // 2, tall - deep, width), lambda step: (step, deep // (tall - deep), 0)
            ),
        ]
        return specs, [unit, unit, unit]
    pair, down = weights
    specs = [
        pl.BlockSpec((pair.shape[0], cut), lambda step: (0, 2 * step)),
        pl.BlockSpec((pair.shape[0], cut), lambda step: (0, 2 * step + 1)),
        pl.BlockSpec((cut, down.shape[1]), lambda step: (step, 0)),
    ]
    return specs, [pair, pair, down]


def expert_call(picks, shares, rows, weights, deep, hidden, before):
    blocks, capacity, _ = picks.shape
    width, cut, tall = (rows[0].shape[1], hidden // 2, blocks * capacity)
    columns = pl.BlockSpec((tall, cut), lambda step: (0, step))
    row_specs = [whole_spec(block.shape) for block in rows]
    specs, operands = weight_operands(weights, deep, cut)
    result = pl.pallas_call(
        functools.partial(expert_kernel, blocks, 1 if before else 0),
        grid=(2,),
        in_specs=[whole_spec(picks.shape), whole_spec(shares.shape)]
        + specs
        + row_specs * (2 if before else 1),
        out_specs=row_specs + [whole_spec((tall, width)), columns, columns],
        out_shape=[jax.ShapeDtypeStruct(block.shape, bf16) for block in rows]
        + [
            jax.ShapeDtypeStruct((tall, width), bf16),
            jax.ShapeDtypeStruct((tall, hidden), f32),
            jax.ShapeDtypeStruct((tall, hidden), f32),
        ],
        scratch_shapes=[pltpu.VMEM((tall, width), f32)],
        compiler_params=kernel_params(),
        cost_estimate=TINY,
        name="expert",
    )(picks, shares, *operands, *rows, *before)
    return (result[:blocks], result[blocks:])


def expert_back_kernel(
    blocks, adds, deep, pick_ref, share_ref, picked_ref, gate_pre_ref, up_pre_ref,
    gate_ref, up_ref, down_ref, *refs
):
    rows, refs = (refs[:blocks], refs[blocks:])
    before, refs = (refs[: blocks * adds], refs[blocks * adds :])
    out, refs = (refs[:blocks], refs[blocks:])
    grad_refs, (slots_ref, turned_ref, total_ref) = (refs[:-3], refs[-3:])
    step = pl.program_id(0)
    capacity, cut = (pick_ref.shape[1], gate_pre_ref.shape[1])

    @pl.when(step == 0)
    def _():
        for d in range(blocks):
            block = nn(pick_ref[d], rows[d][...]) * share_ref[d]
            slots_ref[d * capacity : (d + 1) * capacity, :] = block.astype(bf16)
        turned_ref[...] = picked_ref[...].T

    d_active = nt(slots_ref[...], flat(down_ref))
    value, slope = gelu_parts(gate_pre_ref[...])
    up_pre = up_pre_ref[...]
    active = (value * up_pre).astype(bf16)
    d_gate = (d_active * up_pre * slope).astype(bf16)
    d_up = (d_active * value).astype(bf16)
    grad_down = nn(active.T, slots_ref[...]).astype(bf16)
    grad_gate = nn(turned_ref[...], d_gate).astype(bf16)
    grad_up = nn(turned_ref[...], d_up).astype(bf16)
    if len(grad_refs) == 1:
        unit_ref = grad_refs[0]
        shards, tall, width = unit_ref.shape
        for side in range(2):

            @pl.when(step == side)
            def _():
                left, some = (2 * side * cut, shards // 2)
                unit_ref[:, :deep, left : left + cut] = grad_gate.reshape(shards, deep, cut)
                left = left + cut
                unit_ref[:, :deep, left : left + cut] = grad_up.reshape(shards, deep, cut)
                rest = grad_down.reshape(some, tall - deep, width)
                unit_ref[side * some : (side + 1) * some, deep:, :] = rest
    else:
        grad_refs[0][:, :cut] = grad_gate
        grad_refs[0][:, cut:] = grad_up
        grad_refs[1][...] = grad_down
    part = nt(d_gate, flat(gate_ref)) + nt(d_up, flat(up_ref))
    add_up(total_ref, part, step)

    @pl.when(step == pl.num_programs(0) - 1)
    def _():
        give_back(pick_ref, total_ref, None, before, out)


def expert_back_call(picks, shares, rows, kept, weights, deep, hidden, before):
    blocks, capacity, _ = picks.shape
    width, cut, tall = (rows[0].shape[1], hidden // 2, blocks * capacity)
    columns = pl.BlockSpec((tall, cut), lambda step: (0, step))
    row_specs = [whole_spec(block.shape) for block in rows]
    specs, operands = weight_operands(weights, deep, cut)
    grad_shapes = [jax.ShapeDtypeStruct(part.shape, bf16) for part in weights]
    if len(weights) == 1:
        grad_specs = [whole_spec(weights[0].shape)]
    else:
        grad_specs = [
            pl.BlockSpec((width, 2 * cut), lambda step: (0, step)),
            pl.BlockSpec((cut, width), lambda step: (step, 0)),
        ]
    result = pl.pallas_call(
        functools.partial(expert_back_kernel, blocks, 1 if before else 0, deep),
        grid=(2,),
        in_specs=[
            whole_spec(picks.shape),
            whole_spec(shares.shape),
            whole_spec((tall, width)),
            columns,
            columns,
        ]
        + specs
        + row_specs * (2 if before else 1),
        out_specs=row_specs + grad_specs,
        out_shape=[jax.ShapeDtypeStruct(block.shape, bf16) for block in rows] + grad_shapes,
        scratch_shapes=[
            pltpu.VMEM((tall, width), bf16),
            pltpu.VMEM((width, tall), bf16),
            pltpu.VMEM((tall, width), f32),
        ],
        compiler_params=kernel_params(),
        cost_estimate=TINY,
        name="expert_back",
    )(picks, shares, *kept, *operands, *rows, *before)
    return (result[:blocks], result[blocks:])


def place_kernel(count, index_ref, *refs):
    step = pl.program_id(0)
    for bit in range(count):

        @pl.when(step == bit)
        def _():
            refs[count][0] = refs[bit][...]


def place_call(blocks, index):
    count = len(blocks)
    shape = blocks[0].shape
    zeros = (0,) * len(shape)
    return pl.pallas_call(
        functools.partial(place_kernel, count),
        grid_spec=pltpu.PrefetchScalarGridSpec(
            num_scalar_prefetch=1,
            grid=(count,),
            in_specs=[pl.BlockSpec(shape, lambda step, at: zeros)] * count,
            out_specs=pl.BlockSpec((1,) + shape, lambda step, at: (at[0] ^ step,) + zeros),
        ),
        out_shape=jax.ShapeDtypeStruct((count,) + shape, blocks[0].dtype),
        compiler_params=kernel_params(),
        cost_estimate=TINY,
        name="place",
    )(index.astype(jnp.int32).reshape(1), *blocks)


def order_kernel(count, order_ref, *refs):
    step = pl.program_id(0)
    for i in range(count):

        @pl.when(step == i)
        def _():
            refs[count][:, 0] = refs[i][:, 0]


def order_call(blocks, order, unit):
    count = len(blocks)
    n_ctx, _, tall, wide = blocks[0].shape
    shape = (n_ctx, 1, tall, wide)
    source = pl.BlockSpec(
        shape, lambda step, at: (0, unit, 0, 0), pipeline_mode=pl.Buffered(buffer_count=1)
    )
    result = pl.pallas_call(
        functools.partial(order_kernel, count),
        grid_spec=pltpu.PrefetchScalarGridSpec(
            num_scalar_prefetch=1,
            grid=(count,),
            in_specs=[source] * count,
            out_specs=pl.BlockSpec(shape, lambda step, at: (0, at[step], 0, 0)),
        ),
        out_shape=jax.ShapeDtypeStruct((n_ctx, count, tall, wide), bf16),
        compiler_params=kernel_params(),
        cost_estimate=TINY,
        name="order",
    )(order.astype(jnp.int32), *blocks)
    return result.reshape(n_ctx * count, tall, wide)


def finish_kernel(deep, index_ref, own_ref, other_ref, gate_ref, up_ref, down_ref):
    side = pl.program_id(1)
    wide = gate_ref.shape[2] // 2

    def write(source):
        for half in range(2):
            left, target = (2 * half * wide, slice(half * wide, (half + 1) * wide))
            gate_ref[:, :, target] = source[0, :, :deep, left : left + wide].astype(f32)
            left = left + wide
            up_ref[:, :, target] = source[0, :, :deep, left : left + wide].astype(f32)
        down_ref[...] = source[0, :, deep:, :].astype(f32)

    @pl.when(side == index_ref[1])
    def _():
        write(own_ref)

    @pl.when(side != index_ref[1])
    def _():
        write(other_ref)


def finish_call(own, other, deep, hidden, place, core):
    n_ctx, units, tall, width = own.shape
    experts = 2 * n_ctx * units
    source = pl.BlockSpec((1, units, tall, width), lambda bit, side, at: (bit, 0, 0, 0))
    target = lambda bit, side, at: (2 * (at[0] ^ bit) + side, 0, 0)
    return pl.pallas_call(
        functools.partial(finish_kernel, deep),
        grid_spec=pltpu.PrefetchScalarGridSpec(
            num_scalar_prefetch=1,
            grid=(n_ctx, 2),
            in_specs=[source, source],
            out_specs=[
                pl.BlockSpec((units, deep, hidden), target),
                pl.BlockSpec((units, deep, hidden), target),
                pl.BlockSpec((units, tall - deep, width), target),
            ],
        ),
        out_shape=[
            jax.ShapeDtypeStruct((experts, deep, hidden), f32),
            jax.ShapeDtypeStruct((experts, deep, hidden), f32),
            jax.ShapeDtypeStruct((experts, tall - deep, width), f32),
        ],
        compiler_params=kernel_params(),
        cost_estimate=TINY,
        name="finish",
    )(jnp.stack([place, core]).astype(jnp.int32), own, other)


def body(
    tokens,
    block_of,
    routes,
    combine,
    attn_norm,
    w_query,
    w_key,
    w_value,
    w_out,
    ffn_norm,
    w_gate,
    w_up,
    w_down,
    out_grad,
):
    rows = tokens.shape[2]
    width = tokens.shape[3]
    half = rows // 2
    n_ctx = lax.axis_size("ctx")
    n_fsdp = lax.axis_size("fsdp")
    core, place, depth = (
        lax.axis_index(axis).astype(jnp.uint32) for axis in ("section", "ctx", "fsdp")
    )
    seq_len = rows * n_ctx
    capacity = rows * TOP * 5 // (4 * EXPERTS)
    score_scale = HD ** (-0.5)
    own_experts = EXPERTS // n_ctx
    hidden = w_gate.shape[3]
    shard_rows = w_query.shape[1]
    down_rows = w_down.shape[2]
    qw = w_query.shape[2]
    kw = w_key.shape[2]
    pieces = max(1, 2 * n_ctx // EXPERTS)
    per_core = max(1, EXPERTS // (2 * n_ctx))
    unit_rows = shard_rows + down_rows
    aligned = shard_rows % 16 == 0 and down_rows % 16 == 0

    def on_core(former, latter):
        return jnp.where(core == 0, former, latter)

    def own_other(low, high):
        return (on_core(low, high), on_core(high, low))

    def spread(value):
        return [value] + [swap(value, "ctx", bit) for bit in range(1, n_ctx)]

    def collect(blocks):
        total = blocks[0].astype(f32)
        for bit in range(1, n_ctx):
            total = total + swap(blocks[bit].astype(bf16), "ctx", bit).astype(f32)
        return total

    info = jnp.concatenate([routes.astype(f32), combine], axis=-1)[0, :, 0].transpose(0, 2, 1)
    info_own, info_other = (at(info, core), swap(at(info, 1 - core), "section", 1))
    info = jnp.stack(own_other(info_own, info_other))
    info = jnp.stack([info] + [swap(info, "ctx", bit) for bit in range(1, n_ctx)], axis=1)

    gain_columns = jnp.stack([attn_norm[0], ffn_norm[0]], axis=1)
    gain_columns = jnp.pad(gain_columns, ((0, 0), (0, gap - 2)))
    enter_shard = jnp.concatenate([w_query[0], w_key[0], w_value[0], gain_columns], axis=1)
    enter_cut = enter_shard.shape[1] // 2
    leave_cut = w_out.shape[2] // 2
    low_shard = jnp.concatenate([enter_shard[:, :enter_cut], w_out[0, :, :leave_cut]], axis=1)
    high_shard = jnp.concatenate([enter_shard[:, enter_cut:], w_out[0, :, leave_cut:]], axis=1)
    lent = swap(on_core(high_shard, low_shard), "section", 1)
    dense_shards = (on_core(low_shard, lent), on_core(lent, high_shard))

    def gather_deep(shard):
        blocks = [shard] + [swap(shard, "fsdp", bit) for bit in range(1, n_fsdp)]
        return place_call(blocks, depth).reshape(-1, shard.shape[1])

    def join_square(blocks):
        return place_call(blocks, place).reshape(-1, blocks[0].shape[1])

    def gather_square(deep):
        return join_square(spread(deep))

    cut = hidden // 2
    unit_stack = jnp.concatenate(
        [
            jnp.concatenate(
                [w_gate[0, ..., :cut], w_up[0, ..., :cut], w_gate[0, ..., cut:], w_up[0, ..., cut:]],
                axis=2,
            ),
            w_down[0],
        ],
        axis=1,
    )
    if pieces == 2:
        unit_stack = jnp.stack(jnp.split(unit_stack, 2, axis=2), axis=1)
    unit_stack = unit_stack.reshape(n_ctx, 2, per_core, unit_rows, width // pieces)
    units_lent = swap(at(unit_stack, 1 - core, 1), "section", 1)
    unit_stacks = own_other(at(unit_stack, core, 1), units_lent)

    def deal_units(stack):
        blocks = [at(stack, place)]
        blocks += [swap(at(stack, place ^ bit), "ctx", bit) for bit in range(1, n_ctx)]
        return place_call(blocks, place)

    ring = list(range(0, n_fsdp, 2)) + list(range(1, n_fsdp, 2))[::-1]
    ring_steps = [(ring[i], ring[(i + 1) % n_fsdp]) for i in range(n_fsdp)]
    ring_table = [[ring[ring.index(z) - i] for i in range(n_fsdp)] for z in range(n_fsdp)]
    behind_here = at(jnp.array(ring_table, jnp.uint32), depth)

    def ring_send(blocks):
        return blocks + [lax.ppermute(blocks[-1], "fsdp", ring_steps)]

    def own_units(blocks):
        return [order_call(blocks, behind_here, unit) for unit in range(per_core)]

    def pair_units(mine):
        other = [swap(part, "section", 1) for part in mine]
        units = list(mine) + other
        if pieces == 2:
            units = [jnp.concatenate(own_other(mine[0], other[0]), axis=2)]
        if aligned:
            return [[unit] for unit in units]
        return [
            [unit[:, :shard_rows].reshape(-1, width), unit[:, shard_rows:].reshape(-1, width)]
            for unit in units
        ]

    def cut_units(grads):
        if aligned:
            units = [unit for (unit,) in grads]
        else:
            units = [
                jnp.concatenate(
                    [part.reshape(n_ctx * n_fsdp, -1, width) for part in parts], axis=1
                )
                for parts in grads
            ]
        if pieces == 1:
            return (units[:per_core], units[per_core:])
        own, other = own_other(*jnp.split(units[0], 2, axis=2))
        return ([own], [other])

    def ring_part(terms, behind):
        spot = behind_here[behind % n_fsdp]
        return sum(at(term, spot, 1).astype(f32) for term in terms)

    def ring_start(own, received):
        terms = [part.reshape((n_ctx, n_fsdp) + part.shape[1:]) for part in (own, received)]
        return (terms, ring_part(terms, 1).astype(bf16))

    def ring_step(state, step):
        return [
            (terms, (lax.ppermute(moving, "fsdp", ring_steps).astype(f32)
                     + ring_part(terms, step + 1)).astype(bf16))
            for terms, moving in state
        ]

    def ring_rest(state, first):
        for step in range(first, n_fsdp):
            state = ring_step(state, step)
        return [moving for _, moving in state]

    def scatter_units(moved):
        whole = jnp.stack(moved, axis=1)
        blocks = [at(whole, place)]
        blocks += [swap(at(whole, place ^ bit), "ctx", bit) for bit in range(1, n_ctx)]
        return jnp.stack(blocks)

    def reduce_square(*pairs):
        pairs = [[part.reshape(n_ctx, -1, part.shape[1]) for part in pair] for pair in pairs]

        def part(bit):
            sums = [
                at(own, place ^ bit).astype(f32) + at(received, place ^ bit).astype(f32)
                for own, received in pairs
            ]
            return jnp.concatenate(sums, axis=1)

        total = part(0)
        for bit in range(1, n_ctx):
            total = total + swap(part(bit).astype(bf16), "ctx", bit).astype(f32)
        return total.astype(bf16)

    def reduce_deep(mine):
        mine = mine.reshape(n_fsdp, shard_rows, -1)
        total = at(mine, depth).astype(f32)
        for bit in range(1, n_fsdp):
            total = total + swap(at(mine, depth ^ bit), "fsdp", bit).astype(f32)
        return total

    if pieces == 1:
        units_here = jnp.arange(per_core, dtype=jnp.uint32)
        units_here = jnp.concatenate(
            [core * per_core + units_here, (1 - core) * per_core + units_here]
        )
    else:
        units_here = jnp.zeros((1,), jnp.uint32)
    named = (place * own_experts + units_here).astype(f32)
    matches = info[:, None, :, :TOP] == named[None, :, None, None, None]
    hits = jnp.any(matches, axis=3)
    shares = jnp.sum(jnp.where(matches, info[:, None, :, TOP:], 0.0), axis=3)
    earlier = jnp.arange(rows)[:, None] < jnp.arange(rows)[None, :]
    rank = dot("ledr,rq->ledq", hits.astype(bf16), earlier.astype(bf16))
    slots = jnp.arange(capacity, dtype=f32)
    picks = hits[:, :, :, None, :] & (rank[:, :, :, None, :] == slots[:, None])
    slot_shares = jnp.sum(jnp.where(picks, shares[:, :, :, None, :], 0.0), axis=-1, keepdims=True)
    picks = picks.astype(bf16)

    order = place.astype(jnp.int32) ^ jnp.arange(n_ctx, dtype=jnp.int32)
    block_ids = jnp.take(block_of.reshape(n_ctx, 2), order, axis=0)
    block_ids = block_ids.reshape(-1)

    def project(value, halves):
        own, other = (dot("qa,ab->qb", value, part) for part in halves)
        return jnp.concatenate(own_other(own, other), axis=1)

    def project_back(value, halves):
        cut = value.shape[1] // 2
        own, other = own_other(value[:, :cut], value[:, cut:])
        total = dot("qb,ab->qa", own, halves[0]) + dot("qb,ab->qa", other, halves[1])
        return (total, own, other)

    def gains_of(halves):
        pair = on_core(halves[1][:, -gap : 2 - gap], halves[0][:, -gap : 2 - gap]).astype(f32)
        return (pair[:, 0], pair[:, 1])

    def enter(normed, halves):
        entered = project(normed, halves).astype(bf16)
        return (entered[:, :qw], entered[:, qw : qw + 2 * kw])

    def experts(layer, blocks, weights):
        returned, kept = ([], {})
        for j in range(own_experts):
            returned, kept[j] = expert_call(
                picks[layer, j],
                slot_shares[layer, j],
                blocks,
                weights[j],
                shard_rows,
                hidden,
                returned,
            )
        return (returned, kept)

    def experts_back(layer, blocks, weights, kept):
        returned, grads = ([], {})
        for j in reversed(range(own_experts)):
            returned, grads[j] = expert_back_call(
                picks[layer, j],
                slot_shares[layer, j],
                blocks,
                kept[j],
                weights[j],
                shard_rows,
                hidden,
                returned,
            )
        own, other = cut_units([grads[j] for j in range(own_experts)])
        received = [swap(part, "section", 1) for part in other]
        return (returned, own, received)

    def leave_back(cotangent, d_ffn_normed, after_attention, attended, enter_halves, leave_halves):
        ffn_back = jax.vjp(rms_norm, after_attention, gains_of(enter_halves)[1])[1]
        d_after, grad_gain = ffn_back(d_ffn_normed)
        d_after = d_after + cotangent.astype(f32)
        d_attended, own, other = project_back(d_after.astype(bf16), leave_halves)
        grads = [dot("qa,qb->ab", attended, part, bf16) for part in (own, other)]
        return (d_after, grad_gain, d_attended.astype(bf16), grads)

    def attend_back(queries, key_value_all, d_attended):
        d_queries, d_keys, d_values = attend_back_call(
            block_ids, queries, key_value_all, d_attended
        )
        d_key_value = jnp.concatenate([d_keys, d_values], axis=1).reshape(n_ctx, rows, 2 * kw)
        return (d_queries, collect(d_key_value).astype(bf16))

    def enter_back(d_queries, d_key_value, d_after, grad_gain_ffn, layer_input, normed, halves):
        blank = jnp.zeros((rows, gap), bf16)
        d_entered = jnp.concatenate([d_queries, d_key_value, blank], axis=1)
        d_normed, own, other = project_back(d_entered, halves)
        attn_back = jax.vjp(rms_norm, layer_input, gains_of(halves)[0])[1]
        d_input, grad_gain = attn_back(d_normed)
        gain_columns = jnp.stack([grad_gain, grad_gain_ffn], axis=1)
        gain_columns = jnp.pad(gain_columns, ((0, 0), (enter_cut - gap, gap - 2)))
        own, other = (dot("qa,qb->ab", normed, part) for part in (own, other))
        own = own + on_core(0.0, gain_columns)
        other = other + on_core(gain_columns, 0.0)
        return (d_input + d_after, [own.astype(bf16), other.astype(bf16)])

    deep = gather_deep(jnp.concatenate(dense_shards, axis=1))
    dealt_first, dealt_second = (deal_units(stack) for stack in unit_stacks)
    deep, dealt_first, dealt_second, picks = tie(deep, dealt_first, dealt_second, picks)
    deep_first, deep_second = jnp.split(deep, 2, axis=1)
    dense_blocks, units_moved = tie(spread(deep_first), ring_send([dealt_first]))
    dense_own = join_square(dense_blocks)
    dense_other = swap(dense_own, "section", 1)
    enter_first = (dense_own[:, :enter_cut], dense_other[:, :enter_cut])
    leave_first = (dense_own[:, enter_cut:], dense_other[:, enter_cut:])

    first_in = after(at(tokens, core)[0].astype(f32), slot_shares)
    first_normed = rms_norm(first_in, gains_of(enter_first)[0]).astype(bf16)
    first_queries, key_value = enter(first_normed, enter_first)
    first_kv, units_moved, deep_second = tie(
        jnp.concatenate(spread(key_value)), ring_send(units_moved), deep_second
    )
    enter_blocks = spread(deep_second[:, :enter_cut])
    first_attended = attend_call(block_ids, first_queries, first_kv)
    first_mid = first_in + project(first_attended, leave_first)
    ffn_normed = rms_norm(first_mid, gains_of(enter_first)[1]).astype(bf16)
    for _ in range(3, n_fsdp):
        units_moved = ring_send(units_moved)
    ffn_normed, units_moved, deep_second, enter_blocks = tie(
        ffn_normed, units_moved, deep_second, enter_blocks
    )
    enter_own = join_square(enter_blocks)
    first_units = own_units(units_moved)
    blocks, units_moved, deep_second = tie(
        spread(ffn_normed), ring_send([dealt_second]), deep_second
    )
    enter_second = (enter_own, swap(enter_own, "section", 1))
    leave_blocks = spread(deep_second[:, enter_cut:])
    first_weights = pair_units(first_units)
    returned, first_kept = experts(0, blocks, first_weights)
    returned, units_moved, leave_blocks = tie(returned, ring_send(units_moved), leave_blocks)
    leave_own = join_square(leave_blocks)
    leave_second = (leave_own, swap(leave_own, "section", 1))
    first_out = first_mid + collect(returned)
    for _ in range(3, n_fsdp):
        units_moved = ring_send(units_moved)
    first_out, units_moved = tie(first_out, units_moved)
    first_sent = first_out.astype(bf16)

    second_in = first_sent.astype(f32)
    second_normed = rms_norm(second_in, gains_of(enter_second)[0]).astype(bf16)
    second_queries, key_value = enter(second_normed, enter_second)
    second_kv = jnp.concatenate(spread(key_value))
    second_attended = attend_call(block_ids, second_queries, second_kv)
    second_mid = second_in + project(second_attended, leave_second)
    ffn_normed = rms_norm(second_mid, gains_of(enter_second)[1]).astype(bf16)
    second_weights = pair_units(own_units(units_moved))
    blocks = spread(ffn_normed)
    cotangent = after(at(out_grad, core)[0], blocks)
    cot_blocks = spread(cotangent)
    returned, second_kept = experts(1, blocks, second_weights)
    cot_blocks, returned = tie(cot_blocks, returned)
    second_out = second_mid + collect(returned)

    returned, own, received = experts_back(1, cot_blocks, second_weights, second_kept)
    returned, own, received, second_out = tie(returned, own, received, second_out)
    second_sent = second_out.astype(bf16)
    units_moving = [ring_start(*pair) for pair in zip(own, received)]
    d_after, grad_gain, d_attended, grads = leave_back(
        cotangent, collect(returned), second_mid, second_attended, enter_second, leave_second
    )
    d_attended, units_moving = tie(d_attended, ring_step(units_moving, 1))
    leave_grads = (grads[0], swap(grads[1], "section", 1))
    d_queries, d_key_value = attend_back(second_queries, second_kv, d_attended)
    d_key_value, leave_grads, units_moving = tie(
        d_key_value, leave_grads, ring_step(units_moving, 2)
    )
    second_entry, grads = enter_back(
        d_queries, d_key_value, d_after, grad_gain, second_in, second_normed, enter_second
    )
    units_moving = ring_rest(units_moving, 3)
    enter_grads = (grads[0], swap(grads[1], "section", 1))

    cotangent = second_entry.astype(bf16)
    blocks, enter_grads, second_moved = tie(spread(cotangent), enter_grads, units_moving)
    dense_moving = reduce_square(enter_grads, leave_grads)
    returned, own, received = experts_back(0, blocks, first_weights, first_kept)
    returned, own, received, dense_moving = tie(returned, own, received, dense_moving)
    units_moving = [ring_start(*pair) for pair in zip(own, received)]
    d_after, grad_gain, d_attended, grads = leave_back(
        cotangent, collect(returned), first_mid, first_attended, enter_first, leave_first
    )
    d_attended, units_moving, dense_moving, second_moved = tie(
        d_attended, ring_step(units_moving, 1), dense_moving, second_moved
    )
    second_scattered = scatter_units(second_moved)
    second_dense = reduce_deep(dense_moving)
    leave_grads = (grads[0], swap(grads[1], "section", 1))
    d_queries, d_key_value = attend_back(first_queries, first_kv, d_attended)
    d_key_value, leave_grads, units_moving = tie(
        d_key_value, leave_grads, ring_step(units_moving, 2)
    )
    leave_moving = reduce_square(leave_grads)
    first_entry, grads = enter_back(
        d_queries, d_key_value, d_after, grad_gain, first_in, first_normed, enter_first
    )
    grads, second_dense, second_scattered, leave_moving = tie(
        grads, second_dense, second_scattered, leave_moving
    )
    enter_moving = reduce_square((grads[0], swap(grads[1], "section", 1)))
    first_scattered = scatter_units(ring_rest(units_moving, 3))
    first_dense = jnp.concatenate([reduce_deep(enter_moving), reduce_deep(leave_moving)], axis=1)

    def keep_own(first, second):
        other = swap(on_core(second, first), "section", 1)
        return own_other(on_core(first, second), other)

    layer_out = jnp.stack(keep_own(first_sent, second_sent))
    input_grads = jnp.stack(keep_own(first_entry, second_entry))
    low_dense, high_dense = keep_own(first_dense, second_dense)
    enter_grad = jnp.concatenate([low_dense[:, :enter_cut], high_dense[:, :enter_cut]], axis=1)
    grad_out = jnp.concatenate([low_dense[:, enter_cut:], high_dense[:, enter_cut:]], axis=1)
    grad_gains = enter_grad[:, qw + 2 * kw :]
    mine = on_core(first_scattered, second_scattered)
    other = swap(on_core(second_scattered, first_scattered), "section", 1)
    if aligned and pieces == 1:
        grad_gate, grad_up, grad_down = finish_call(mine, other, shard_rows, hidden, place, core)
    else:
        sides = [jnp.take(part, order, axis=0) for part in own_other(mine, other)]
        if pieces == 1:
            whole = jnp.stack(sides, axis=1).reshape(EXPERTS, unit_rows, width)
        else:
            whole = jnp.concatenate([side[:, 0] for side in sides], axis=2)
        pairs = whole[:, :shard_rows].astype(f32).reshape(EXPERTS, shard_rows, 2, 2, cut)
        grad_gate = pairs[:, :, :, 0].reshape(EXPERTS, shard_rows, hidden)
        grad_up = pairs[:, :, :, 1].reshape(EXPERTS, shard_rows, hidden)
        grad_down = whole[:, shard_rows:].astype(f32)
    return (
        layer_out[None, :, None],
        input_grads[None, :, None],
        grad_gains[:, 0][None],
        enter_grad[:, :qw][None],
        enter_grad[:, qw : qw + kw][None],
        enter_grad[:, qw + kw : qw + 2 * kw][None],
        grad_out[None],
        grad_gains[:, 1][None],
        grad_gate[None],
        grad_up[None],
        grad_down[None],
    )


def solution(mesh):
    rows_placed = P(None, "fsdp", "ctx", None)
    kept_placed = P("section", None, "fsdp", "ctx", None)
    gain_placed = P("section", ("ctx", "fsdp"))
    dense_placed = P("section", ("ctx", "fsdp"), None)
    expert_placed = P("section", None, ("ctx", "fsdp"), None)
    dense_all = (dense_placed,) * 4
    expert_all = (expert_placed,) * 3
    layer_placed = (gain_placed,) + dense_all + (gain_placed,) + expert_all
    return jax.shard_map(
        body,
        mesh=mesh,
        in_specs=(rows_placed, P(), kept_placed, kept_placed) + layer_placed + (rows_placed,),
        out_specs=(kept_placed, kept_placed) + layer_placed,
        check_vma=False,
    )
```

```python
import functools

import jax
import jax.numpy as jnp
from jax import lax
from jax.experimental import pallas as pl
from jax.experimental.pallas import tpu as pltpu
from jax.sharding import PartitionSpec as P

QH = 12
KVH = 2
HD = 128
GROUP = QH // KVH
TOP = 4
EXPERTS = 8
bf16 = jnp.bfloat16
f32 = jnp.float32


epsilon = 1e-06
masked_out = -1e30
gap = 256


def swap(value, axis, bit):
    count = lax.axis_size(axis)
    return lax.ppermute(value, axis, [(source, source ^ bit) for source in range(count)])


def tie(*values):
    return lax.optimization_barrier(values)


def after(value, earlier):
    return tie(value, earlier)[0]


def at(value, index, axis=0):
    return lax.dynamic_index_in_dim(value, index, axis, keepdims=False)


def dot(spec, left, right, kind=f32):
    return jnp.einsum(spec, left, right, preferred_element_type=kind)


def cost(micros):
    return pl.CostEstimate(
        flops=int(micros * 1e9), bytes_accessed=int(micros * 3e6), transcendentals=0
    )


def kernel_params():
    return pltpu.CompilerParams(vmem_limit_bytes=56 * 1024 * 1024)


def nt(left, right):
    return lax.dot_general(left, right, (((1,), (1,)), ((), ())), preferred_element_type=f32)


def nn(left, right):
    return jnp.dot(left, right, preferred_element_type=f32)


def head_rows(ref):
    return jnp.concatenate([ref[:, i * HD : (i + 1) * HD] for i in range(GROUP)], axis=0)


def softmax_rows(ids_ref, queries, keys, half, own):
    scores = nt(queries, keys) * HD ** (-0.5)
    tall, wide = scores.shape
    row = lax.broadcasted_iota(jnp.int32, (half, 1), 0)
    row = jnp.concatenate([row] * (tall // half), axis=0) + ids_ref[own] * half
    lane = lax.broadcasted_iota(jnp.int32, (1, half), 1)
    column = [lane + ids_ref[block] * half for block in range(wide // half)]
    column = jnp.concatenate(column, axis=1)
    scores = jnp.where(row >= column, scores, masked_out)
    shifted = jnp.exp(scores - jnp.max(scores, axis=1, keepdims=True))
    return shifted / jnp.sum(shifted, axis=1, keepdims=True)


def attend_kernel(ids_ref, query_ref, key_ref, value_ref, out_ref):
    half = query_ref.shape[0]
    probs = softmax_rows(ids_ref, head_rows(query_ref), key_ref[...], half, pl.program_id(1))
    out = nn(probs.astype(bf16), value_ref[...]).astype(bf16)
    for i in range(GROUP):
        out_ref[:, i * HD : (i + 1) * HD] = out[i * half : (i + 1) * half]


def attend_specs(rows, seq_len):
    half = rows // 2
    by_head = pl.BlockSpec((half, GROUP * HD), lambda g, h, ids: (h, g))
    keys = pl.BlockSpec((seq_len, HD), lambda g, h, ids: (0, g))
    values = pl.BlockSpec((seq_len, HD), lambda g, h, ids: (0, KVH + g))
    return by_head, keys, values


def attend_call(ids, queries, key_value):
    rows, seq_len = (queries.shape[0], key_value.shape[0])
    by_head, keys, values = attend_specs(rows, seq_len)
    return pl.pallas_call(
        attend_kernel,
        grid_spec=pltpu.PrefetchScalarGridSpec(
            num_scalar_prefetch=1,
            grid=(KVH, 2),
            in_specs=[by_head, keys, values],
            out_specs=by_head,
        ),
        out_shape=jax.ShapeDtypeStruct((rows, QH * HD), bf16),
        compiler_params=kernel_params(),
        cost_estimate=cost(12),
        name="attend",
    )(ids, queries, key_value, key_value)


def attend_back_kernel(ids_ref, query_ref, key_ref, value_ref, cot_ref, dq_ref, *refs):
    out, (dk_ref, dv_ref) = (refs[:-2], refs[-2:])
    half = query_ref.shape[0]
    group, own = (pl.program_id(0), pl.program_id(1))
    queries, cot = (head_rows(query_ref), head_rows(cot_ref))
    probs = softmax_rows(ids_ref, queries, key_ref[...], half, own)
    d_probs = nt(cot, value_ref[...])
    inner = jnp.sum(probs * d_probs, axis=1, keepdims=True)
    d_scores = (probs * (d_probs - inner)).astype(bf16)
    d_queries = (nn(d_scores, key_ref[...]) * HD ** (-0.5)).astype(bf16)
    for i in range(GROUP):
        dq_ref[:, i * HD : (i + 1) * HD] = d_queries[i * half : (i + 1) * half]
    d_keys = nn(d_scores.T, queries) * HD ** (-0.5)
    d_values = nn(probs.astype(bf16).T, cot)

    @pl.when(own == 0)
    def _():
        dk_ref[...] = d_keys
        dv_ref[...] = d_values

    @pl.when(own != 0)
    def _():
        rows = 2 * half
        for block, ref in enumerate(out):
            part = slice(block * rows, (block + 1) * rows)
            for first, total, last in ((0, dk_ref, d_keys), (KVH * HD, dv_ref, d_values)):
                columns = pl.ds(pl.multiple_of(first + group * HD, HD), HD)
                ref[:, columns] = (total[part, :] + last[part]).astype(bf16)


def attend_back_call(ids, queries, key_value, cot):
    rows, seq_len = (queries.shape[0], key_value.shape[0])
    by_head, keys, values = attend_specs(rows, seq_len)
    blocks = seq_len // rows
    wide = 2 * KVH * HD
    result = pl.pallas_call(
        attend_back_kernel,
        grid_spec=pltpu.PrefetchScalarGridSpec(
            num_scalar_prefetch=1,
            grid=(KVH, 2),
            in_specs=[by_head, keys, values, by_head],
            out_specs=[by_head] + [pl.BlockSpec((rows, wide), lambda g, h, ids: (0, 0))] * blocks,
            scratch_shapes=[pltpu.VMEM((seq_len, HD), f32)] * 2,
        ),
        out_shape=[jax.ShapeDtypeStruct((rows, QH * HD), bf16)]
        + [jax.ShapeDtypeStruct((rows, wide), bf16)] * blocks,
        compiler_params=kernel_params(),
        cost_estimate=cost(16),
        name="attend_back",
    )(ids, queries, key_value, key_value, cot)
    return (result[0], result[1:])


def gelu_parts(gate):
    root = 0.7978845608028654
    inner = root * (gate + 0.044715 * gate * gate * gate)
    bent = jnp.tanh(inner)
    value = 0.5 * gate * (1.0 + bent)
    slope = root * (1.0 + 3.0 * 0.044715 * gate * gate)
    return value, 0.5 * (1.0 + bent) + 0.5 * gate * (1.0 - bent * bent) * slope


def give_back(pick_ref, total_ref, share_ref, before, out):
    blocks, capacity, _ = pick_ref.shape
    for d in range(blocks):
        part = total_ref[d * capacity : (d + 1) * capacity, :]
        if share_ref is not None:
            part = part * share_ref[d]
        back = nn(pick_ref[d].T, part.astype(bf16))
        if before:
            back = back + before[d][...]
        out[d][...] = back.astype(out[d].dtype)


def flat(ref):
    value = ref[...]
    return value.reshape(-1, value.shape[-1])


def add_up(total_ref, part, step):
    @pl.when(step == 0)
    def _():
        total_ref[...] = part

    @pl.when(step != 0)
    def _():
        total_ref[...] += part


def expert_kernel(blocks, adds, pick_ref, share_ref, gate_ref, up_ref, down_ref, *refs):
    rows, refs = (refs[:blocks], refs[blocks:])
    before, refs = (refs[: blocks * adds], refs[blocks * adds :])
    out, (picked_ref, gate_pre_ref, up_pre_ref, total_ref) = (refs[:blocks], refs[blocks:])
    step = pl.program_id(0)
    capacity = pick_ref.shape[1]

    @pl.when(step == 0)
    def _():
        for d in range(blocks):
            block = nn(pick_ref[d], rows[d][...]).astype(bf16)
            picked_ref[d * capacity : (d + 1) * capacity, :] = block

    gate_pre = nn(picked_ref[...], flat(gate_ref))
    up_pre = nn(picked_ref[...], flat(up_ref))
    gate_pre_ref[...] = gate_pre
    up_pre_ref[...] = up_pre
    active = (gelu_parts(gate_pre)[0] * up_pre).astype(bf16)
    add_up(total_ref, nn(active, flat(down_ref)), step)

    @pl.when(step == pl.num_programs(0) - 1)
    def _():
        give_back(pick_ref, total_ref, share_ref, before, out)


def whole_spec(shape):
    return pl.BlockSpec(
        shape, lambda step: (0,) * len(shape), pipeline_mode=pl.Buffered(buffer_count=1)
    )


def weight_operands(weights, deep, cut):
    if len(weights) == 1:
        unit = weights[0]
        shards, tall, width = unit.shape
        specs = [
            pl.BlockSpec((shards, deep, cut), lambda step: (0, 0, 2 * step)),
            pl.BlockSpec((shards, deep, cut), lambda step: (0, 0, 2 * step + 1)),
            pl.BlockSpec(
                (shards // 2, tall - deep, width), lambda step: (step, deep // (tall - deep), 0)
            ),
        ]
        return specs, [unit, unit, unit]
    pair, down = weights
    specs = [
        pl.BlockSpec((pair.shape[0], cut), lambda step: (0, 2 * step)),
        pl.BlockSpec((pair.shape[0], cut), lambda step: (0, 2 * step + 1)),
        pl.BlockSpec((cut, down.shape[1]), lambda step: (step, 0)),
    ]
    return specs, [pair, pair, down]


def expert_call(picks, shares, rows, weights, deep, hidden, before):
    blocks, capacity, _ = picks.shape
    width, cut, tall = (rows[0].shape[1], hidden // 2, blocks * capacity)
    columns = pl.BlockSpec((tall, cut), lambda step: (0, step))
    row_specs = [whole_spec(block.shape) for block in rows]
    specs, operands = weight_operands(weights, deep, cut)
    result = pl.pallas_call(
        functools.partial(expert_kernel, blocks, 1 if before else 0),
        grid=(2,),
        in_specs=[whole_spec(picks.shape), whole_spec(shares.shape)]
        + specs
        + row_specs * (2 if before else 1),
        out_specs=row_specs + [whole_spec((tall, width)), columns, columns],
        out_shape=[jax.ShapeDtypeStruct(block.shape, bf16) for block in rows]
        + [
            jax.ShapeDtypeStruct((tall, width), bf16),
            jax.ShapeDtypeStruct((tall, hidden), f32),
            jax.ShapeDtypeStruct((tall, hidden), f32),
        ],
        scratch_shapes=[pltpu.VMEM((tall, width), f32)],
        compiler_params=kernel_params(),
        cost_estimate=cost(15),
        name="expert",
    )(picks, shares, *operands, *rows, *before)
    return (result[:blocks], result[blocks:])


def expert_back_kernel(
    blocks, adds, deep, pick_ref, share_ref, picked_ref, gate_pre_ref, up_pre_ref,
    gate_ref, up_ref, down_ref, *refs
):
    rows, refs = (refs[:blocks], refs[blocks:])
    before, refs = (refs[: blocks * adds], refs[blocks * adds :])
    out, refs = (refs[:blocks], refs[blocks:])
    grad_refs, (slots_ref, turned_ref, total_ref) = (refs[:-3], refs[-3:])
    step = pl.program_id(0)
    capacity, cut = (pick_ref.shape[1], gate_pre_ref.shape[1])

    @pl.when(step == 0)
    def _():
        for d in range(blocks):
            block = nn(pick_ref[d], rows[d][...]) * share_ref[d]
            slots_ref[d * capacity : (d + 1) * capacity, :] = block.astype(bf16)
        turned_ref[...] = picked_ref[...].T

    d_active = nt(slots_ref[...], flat(down_ref))
    value, slope = gelu_parts(gate_pre_ref[...])
    up_pre = up_pre_ref[...]
    active = (value * up_pre).astype(bf16)
    d_gate = (d_active * up_pre * slope).astype(bf16)
    d_up = (d_active * value).astype(bf16)
    grad_down = nn(active.T, slots_ref[...]).astype(bf16)
    grad_gate = nn(turned_ref[...], d_gate).astype(bf16)
    grad_up = nn(turned_ref[...], d_up).astype(bf16)
    if len(grad_refs) == 1:
        unit_ref = grad_refs[0]
        shards, tall, width = unit_ref.shape
        for side in range(2):

            @pl.when(step == side)
            def _():
                left, some = (2 * side * cut, shards // 2)
                unit_ref[:, :deep, left : left + cut] = grad_gate.reshape(shards, deep, cut)
                left = left + cut
                unit_ref[:, :deep, left : left + cut] = grad_up.reshape(shards, deep, cut)
                rest = grad_down.reshape(some, tall - deep, width)
                unit_ref[side * some : (side + 1) * some, deep:, :] = rest
    else:
        grad_refs[0][:, :cut] = grad_gate
        grad_refs[0][:, cut:] = grad_up
        grad_refs[1][...] = grad_down
    part = nt(d_gate, flat(gate_ref)) + nt(d_up, flat(up_ref))
    add_up(total_ref, part, step)

    @pl.when(step == pl.num_programs(0) - 1)
    def _():
        give_back(pick_ref, total_ref, None, before, out)


def expert_back_call(picks, shares, rows, kept, weights, deep, hidden, before):
    blocks, capacity, _ = picks.shape
    width, cut, tall = (rows[0].shape[1], hidden // 2, blocks * capacity)
    columns = pl.BlockSpec((tall, cut), lambda step: (0, step))
    row_specs = [whole_spec(block.shape) for block in rows]
    specs, operands = weight_operands(weights, deep, cut)
    grad_shapes = [jax.ShapeDtypeStruct(part.shape, bf16) for part in weights]
    if len(weights) == 1:
        grad_specs = [whole_spec(weights[0].shape)]
    else:
        grad_specs = [
            pl.BlockSpec((width, 2 * cut), lambda step: (0, step)),
            pl.BlockSpec((cut, width), lambda step: (step, 0)),
        ]
    result = pl.pallas_call(
        functools.partial(expert_back_kernel, blocks, 1 if before else 0, deep),
        grid=(2,),
        in_specs=[
            whole_spec(picks.shape),
            whole_spec(shares.shape),
            whole_spec((tall, width)),
            columns,
            columns,
        ]
        + specs
        + row_specs * (2 if before else 1),
        out_specs=row_specs + grad_specs,
        out_shape=[jax.ShapeDtypeStruct(block.shape, bf16) for block in rows] + grad_shapes,
        scratch_shapes=[
            pltpu.VMEM((tall, width), bf16),
            pltpu.VMEM((width, tall), bf16),
            pltpu.VMEM((tall, width), f32),
        ],
        compiler_params=kernel_params(),
        cost_estimate=cost(25),
        name="expert_back",
    )(picks, shares, *kept, *operands, *rows, *before)
    return (result[:blocks], result[blocks:])


def norm_parts(value):
    scale = lax.rsqrt(jnp.mean(value * value, axis=1, keepdims=True) + epsilon)
    return scale, value * scale


def norm_back(grad, gain, value):
    scale, scaled = norm_parts(value)
    grown = grad * gain
    back = scale * (grown - scaled * jnp.mean(scaled * grown, axis=1, keepdims=True))
    return back, (grad * scaled).astype(bf16)


def add_all(refs):
    total = refs[0][...].astype(f32)
    for ref in refs[1:]:
        total = total + ref[...].astype(f32)
    return total


def side_offsets(core_ref, steps, cut):
    step, core = (pl.program_id(0), core_ref[0])
    own = pl.multiple_of((core * steps + step) * cut, cut)
    other = pl.multiple_of(((1 - core) * steps + step) * cut, cut)
    return own, other


def dense_call(kernel, core, steps, whole, halves, out, scratch, name):
    cut = halves[0].shape[1] // steps

    def keep(shape):
        return pl.BlockSpec(
            shape, lambda step, core: (0,) * len(shape), pipeline_mode=pl.Buffered(buffer_count=1)
        )

    def tile(tall):
        return pl.BlockSpec((tall, cut), lambda step, core: (0, step))

    return pl.pallas_call(
        kernel,
        grid_spec=pltpu.PrefetchScalarGridSpec(
            num_scalar_prefetch=1,
            grid=(steps,),
            in_specs=[keep(part.shape) for part in whole] + [tile(halves[0].shape[0])] * 2,
            out_specs=[
                tile(part.shape[0]) if tiled else keep(part.shape) for part, tiled in out
            ],
            scratch_shapes=scratch,
        ),
        out_shape=[part for part, _ in out],
        compiler_params=kernel_params(),
        cost_estimate=cost(4 * steps if name.endswith("back") else 2 * steps),
        name=name,
    )(core.astype(jnp.int32).reshape(1), *whole, *halves)


def shape_of(kind, *shape):
    return jax.ShapeDtypeStruct(shape, kind)


def enter_kernel(steps, terms, core_ref, gain_ref, *refs):
    parts, (own_ref, other_ref, sent_ref, normed_ref, out_ref) = (refs[:terms], refs[terms:])
    own, other = side_offsets(core_ref, steps, own_ref.shape[1])

    @pl.when(pl.program_id(0) == 0)
    def _():
        sent = add_all(parts).astype(bf16)
        sent_ref[...] = sent
        normed_ref[...] = (norm_parts(sent.astype(f32))[1] * gain_ref[...]).astype(bf16)

    cut = own_ref.shape[1]
    out_ref[:, pl.ds(own, cut)] = nn(normed_ref[...], own_ref[...]).astype(bf16)
    out_ref[:, pl.ds(other, cut)] = nn(normed_ref[...], other_ref[...]).astype(bf16)


def enter_call(core, parts, gain, halves):
    rows, width = parts[0].shape
    return dense_call(
        functools.partial(enter_kernel, 3, len(parts)),
        core,
        3,
        [gain] + parts,
        halves,
        [
            (shape_of(bf16, rows, width), False),
            (shape_of(bf16, rows, width), False),
            (shape_of(bf16, rows, 2 * halves[0].shape[1]), False),
        ],
        [],
        "enter",
    )


def leave_kernel(steps, core_ref, gain_ref, rows_ref, attended_ref, own_ref, other_ref,
                 mid_ref, normed_ref):
    cut = own_ref.shape[1]
    for start, ref in zip(side_offsets(core_ref, steps, cut), (own_ref, other_ref)):
        part = pl.ds(start, cut)
        mid_ref[:, part] = rows_ref[:, part].astype(f32) + nn(attended_ref[...], ref[...])

    @pl.when(pl.program_id(0) == steps - 1)
    def _():
        normed_ref[...] = (norm_parts(mid_ref[...])[1] * gain_ref[...]).astype(bf16)


def leave_call(core, rows_in, attended, gain, halves):
    rows, width = rows_in.shape
    return dense_call(
        functools.partial(leave_kernel, 2),
        core,
        2,
        [gain, rows_in, attended],
        halves,
        [(shape_of(f32, rows, width), False), (shape_of(bf16, rows, width), False)],
        [],
        "leave",
    )


def leave_back_kernel(steps, terms, core_ref, gain_ref, mid_ref, cot_ref, attended_ref, *refs):
    parts, refs = (refs[:terms], refs[terms:])
    own_ref, other_ref, after_ref, term_ref, d_attended_ref, *refs = refs
    own_grad_ref, other_grad_ref, branch_ref, turned_ref, total_ref = refs
    step, cut = (pl.program_id(0), own_ref.shape[1])

    @pl.when(step == 0)
    def _():
        back, term_ref[...] = norm_back(add_all(parts), gain_ref[...], mid_ref[...])
        back = back + cot_ref[...].astype(f32)
        after_ref[...] = back
        branch_ref[...] = back.astype(bf16)
        turned_ref[...] = attended_ref[...].T

    own, other = side_offsets(core_ref, steps, cut)
    d_own, d_other = (branch_ref[:, pl.ds(own, cut)], branch_ref[:, pl.ds(other, cut)])
    own_grad_ref[...] = nn(turned_ref[...], d_own).astype(bf16)
    other_grad_ref[...] = nn(turned_ref[...], d_other).astype(bf16)
    add_up(total_ref, nt(d_own, own_ref[...]) + nt(d_other, other_ref[...]), step)

    @pl.when(step == steps - 1)
    def _():
        d_attended_ref[...] = total_ref[...].astype(bf16)


def leave_back_call(core, parts, gain, mid, cotangent, attended, halves):
    rows, width = mid.shape
    half = (halves[0].shape[0], halves[0].shape[1])
    return dense_call(
        functools.partial(leave_back_kernel, 2, len(parts)),
        core,
        2,
        [gain, mid, cotangent, attended] + parts,
        halves,
        [
            (shape_of(f32, rows, width), False),
            (shape_of(bf16, rows, width), False),
            (shape_of(bf16, rows, width), False),
            (shape_of(bf16, *half), True),
            (shape_of(bf16, *half), True),
        ],
        [
            pltpu.VMEM((rows, width), bf16),
            pltpu.VMEM((width, rows), bf16),
            pltpu.VMEM((rows, width), f32),
        ],
        "leave_back",
    )


def enter_back_kernel(steps, terms, core_ref, gain_ref, rows_ref, normed_ref, after_ref, term_ref,
                      dq_ref, *refs):
    parts, refs = (refs[:terms], refs[terms:])
    own_ref, other_ref, entry_ref, sent_ref, own_grad_ref, other_grad_ref, *refs = refs
    entered_ref, turned_ref, total_ref = refs
    step, cut = (pl.program_id(0), own_ref.shape[1])
    rows, qw = dq_ref.shape

    @pl.when(step == 0)
    def _():
        entered_ref[:, :qw] = dq_ref[...]
        wide = parts[0].shape[1]
        entered_ref[:, qw : qw + wide] = add_all(parts).astype(bf16)
        entered_ref[:, qw + wide :] = jnp.zeros((rows, gap), bf16)
        turned_ref[...] = normed_ref[...].T

    own, other = side_offsets(core_ref, steps, cut)
    d_own, d_other = (entered_ref[:, pl.ds(own, cut)], entered_ref[:, pl.ds(other, cut)])
    own_grad_ref[...] = nn(turned_ref[...], d_own).astype(bf16)
    other_grad_ref[...] = nn(turned_ref[...], d_other).astype(bf16)
    add_up(total_ref, nt(d_own, own_ref[...]) + nt(d_other, other_ref[...]), step)

    @pl.when(step == steps - 1)
    def _():
        back, attn_term = norm_back(total_ref[...], gain_ref[...], rows_ref[...].astype(f32))
        back = back + after_ref[...]
        entry_ref[...] = back
        sent_ref[...] = back.astype(bf16)
        lane = lax.broadcasted_iota(jnp.int32, (rows, 128), 1)
        sums = nn(attn_term.T, (lane == 0).astype(bf16))
        sums = (sums + nn(term_ref[...].T, (lane == 1).astype(bf16))).astype(bf16)
        left = cut - gap

        @pl.when(core_ref[0] == 0)
        def _():
            other_grad_ref[:, left : left + 128] = sums

        @pl.when(core_ref[0] != 0)
        def _():
            own_grad_ref[:, left : left + 128] = sums


def enter_back_call(core, dq, parts, gain, rows_in, normed, after, term, halves):
    rows, width = rows_in.shape
    return dense_call(
        functools.partial(enter_back_kernel, 3, len(parts)),
        core,
        3,
        [gain, rows_in, normed, after, term, dq] + parts,
        halves,
        [
            (shape_of(f32, rows, width), False),
            (shape_of(bf16, rows, width), False),
            (shape_of(bf16, *halves[0].shape), True),
            (shape_of(bf16, *halves[0].shape), True),
        ],
        [
            pltpu.VMEM((rows, 2 * halves[0].shape[1]), bf16),
            pltpu.VMEM((width, rows), bf16),
            pltpu.VMEM((rows, width), f32),
        ],
        "enter_back",
    )


def place_kernel(count, joined, index_ref, *refs):
    step = pl.program_id(0)
    for bit in range(count):

        @pl.when(step == bit)
        def _():
            if joined:
                refs[count][...] = refs[bit][...]
            else:
                refs[count][0] = refs[bit][...]


def place_call(blocks, index):
    count = len(blocks)
    shape = blocks[0].shape
    zeros = (0,) * len(shape)
    joined = len(shape) == 2 and shape[0] % 16 == 0
    if joined:
        out_spec = pl.BlockSpec(shape, lambda step, at: (at[0] ^ step, 0))
        out_shape = (count * shape[0], shape[1])
    else:
        out_spec = pl.BlockSpec((1,) + shape, lambda step, at: (at[0] ^ step,) + zeros)
        out_shape = (count,) + shape
    return pl.pallas_call(
        functools.partial(place_kernel, count, joined),
        grid_spec=pltpu.PrefetchScalarGridSpec(
            num_scalar_prefetch=1,
            grid=(count,),
            in_specs=[pl.BlockSpec(shape, lambda step, at: zeros)] * count,
            out_specs=out_spec,
        ),
        out_shape=jax.ShapeDtypeStruct(out_shape, blocks[0].dtype),
        compiler_params=kernel_params(),
        cost_estimate=cost(2),
        name="place",
    )(index.astype(jnp.int32).reshape(1), *blocks)


def order_kernel(count, order_ref, *refs):
    step = pl.program_id(0)
    for i in range(count):

        @pl.when(step == i)
        def _():
            refs[count][:, 0] = refs[i][:, 0]


def order_call(blocks, order, unit):
    count = len(blocks)
    n_ctx, _, tall, wide = blocks[0].shape
    shape = (n_ctx, 1, tall, wide)
    source = pl.BlockSpec(
        shape, lambda step, at: (0, unit, 0, 0), pipeline_mode=pl.Buffered(buffer_count=1)
    )
    result = pl.pallas_call(
        functools.partial(order_kernel, count),
        grid_spec=pltpu.PrefetchScalarGridSpec(
            num_scalar_prefetch=1,
            grid=(count,),
            in_specs=[source] * count,
            out_specs=pl.BlockSpec(shape, lambda step, at: (0, at[step], 0, 0)),
        ),
        out_shape=jax.ShapeDtypeStruct((n_ctx, count, tall, wide), bf16),
        compiler_params=kernel_params(),
        cost_estimate=cost(4),
        name="order",
    )(order.astype(jnp.int32), *blocks)
    return result.reshape(n_ctx * count, tall, wide)


def finish_kernel(deep, index_ref, own_ref, other_ref, gate_ref, up_ref, down_ref):
    side = pl.program_id(1)
    wide = gate_ref.shape[2] // 2

    def write(source):
        for half in range(2):
            left, target = (2 * half * wide, slice(half * wide, (half + 1) * wide))
            gate_ref[:, :, target] = source[0, :, :deep, left : left + wide].astype(f32)
            left = left + wide
            up_ref[:, :, target] = source[0, :, :deep, left : left + wide].astype(f32)
        down_ref[...] = source[0, :, deep:, :].astype(f32)

    @pl.when(side == index_ref[1])
    def _():
        write(own_ref)

    @pl.when(side != index_ref[1])
    def _():
        write(other_ref)


def finish_call(own, other, deep, hidden, place, core):
    n_ctx, units, tall, width = own.shape
    experts = 2 * n_ctx * units
    source = pl.BlockSpec((1, units, tall, width), lambda bit, side, at: (bit, 0, 0, 0))
    target = lambda bit, side, at: (2 * (at[0] ^ bit) + side, 0, 0)
    return pl.pallas_call(
        functools.partial(finish_kernel, deep),
        grid_spec=pltpu.PrefetchScalarGridSpec(
            num_scalar_prefetch=1,
            grid=(n_ctx, 2),
            in_specs=[source, source],
            out_specs=[
                pl.BlockSpec((units, deep, hidden), target),
                pl.BlockSpec((units, deep, hidden), target),
                pl.BlockSpec((units, tall - deep, width), target),
            ],
        ),
        out_shape=[
            jax.ShapeDtypeStruct((experts, deep, hidden), f32),
            jax.ShapeDtypeStruct((experts, deep, hidden), f32),
            jax.ShapeDtypeStruct((experts, tall - deep, width), f32),
        ],
        compiler_params=kernel_params(),
        cost_estimate=cost(8),
        name="finish",
    )(jnp.stack([place, core]).astype(jnp.int32), own, other)


def body(
    tokens,
    block_of,
    routes,
    combine,
    attn_norm,
    w_query,
    w_key,
    w_value,
    w_out,
    ffn_norm,
    w_gate,
    w_up,
    w_down,
    out_grad,
):
    rows = tokens.shape[2]
    width = tokens.shape[3]
    half = rows // 2
    n_ctx = lax.axis_size("ctx")
    n_fsdp = lax.axis_size("fsdp")
    core, place, depth = (
        lax.axis_index(axis).astype(jnp.uint32) for axis in ("section", "ctx", "fsdp")
    )
    seq_len = rows * n_ctx
    capacity = rows * TOP * 5 // (4 * EXPERTS)
    score_scale = HD ** (-0.5)
    own_experts = EXPERTS // n_ctx
    hidden = w_gate.shape[3]
    shard_rows = w_query.shape[1]
    down_rows = w_down.shape[2]
    qw = w_query.shape[2]
    kw = w_key.shape[2]
    pieces = max(1, 2 * n_ctx // EXPERTS)
    per_core = max(1, EXPERTS // (2 * n_ctx))
    unit_rows = shard_rows + down_rows
    aligned = shard_rows % 16 == 0 and down_rows % 16 == 0

    def on_core(former, latter):
        return jnp.where(core == 0, former, latter)

    def own_other(low, high):
        return (on_core(low, high), on_core(high, low))

    def spread(value):
        return [value] + [swap(value, "ctx", bit) for bit in range(1, n_ctx)]

    def gather_back(blocks):
        return [blocks[0]] + [swap(blocks[bit], "ctx", bit) for bit in range(1, n_ctx)]

    info = jnp.concatenate([routes.astype(f32), combine], axis=-1)[0, :, 0].transpose(0, 2, 1)
    info_own, info_other = (at(info, core), swap(at(info, 1 - core), "section", 1))
    info = jnp.stack(own_other(info_own, info_other))
    info = jnp.stack([info] + [swap(info, "ctx", bit) for bit in range(1, n_ctx)], axis=1)

    gain_columns = jnp.stack([attn_norm[0], ffn_norm[0]], axis=1)
    gain_columns = jnp.pad(gain_columns, ((0, 0), (0, gap - 2)))
    enter_shard = jnp.concatenate([w_query[0], w_key[0], w_value[0], gain_columns], axis=1)
    enter_cut = enter_shard.shape[1] // 2
    leave_cut = w_out.shape[2] // 2
    low_shard = jnp.concatenate([enter_shard[:, :enter_cut], w_out[0, :, :leave_cut]], axis=1)
    high_shard = jnp.concatenate([enter_shard[:, enter_cut:], w_out[0, :, leave_cut:]], axis=1)
    lent = swap(on_core(high_shard, low_shard), "section", 1)
    dense_shards = (on_core(low_shard, lent), on_core(lent, high_shard))

    def gather_deep(shard):
        blocks = [shard] + [swap(shard, "fsdp", bit) for bit in range(1, n_fsdp)]
        return place_call(blocks, depth).reshape(-1, shard.shape[1])

    def join_square(blocks):
        return place_call(blocks, place).reshape(-1, blocks[0].shape[1])

    def gather_square(deep):
        return join_square(spread(deep))

    cut = hidden // 2
    unit_stack = jnp.concatenate(
        [
            jnp.concatenate(
                [w_gate[0, ..., :cut], w_up[0, ..., :cut], w_gate[0, ..., cut:], w_up[0, ..., cut:]],
                axis=2,
            ),
            w_down[0],
        ],
        axis=1,
    )
    if pieces == 2:
        unit_stack = jnp.stack(jnp.split(unit_stack, 2, axis=2), axis=1)
    unit_stack = unit_stack.reshape(n_ctx, 2, per_core, unit_rows, width // pieces)
    units_lent = swap(at(unit_stack, 1 - core, 1), "section", 1)
    unit_stacks = own_other(at(unit_stack, core, 1), units_lent)

    def deal_units(stack):
        blocks = [at(stack, place)]
        blocks += [swap(at(stack, place ^ bit), "ctx", bit) for bit in range(1, n_ctx)]
        return place_call(blocks, place)

    ring = list(range(0, n_fsdp, 2)) + list(range(1, n_fsdp, 2))[::-1]
    ring_steps = [(ring[i], ring[(i + 1) % n_fsdp]) for i in range(n_fsdp)]
    ring_table = [[ring[ring.index(z) - i] for i in range(n_fsdp)] for z in range(n_fsdp)]
    behind_here = at(jnp.array(ring_table, jnp.uint32), depth)

    def ring_send(moved):
        return [blocks + [lax.ppermute(blocks[-1], "fsdp", ring_steps)] for blocks in moved]

    def own_units(blocks):
        return [order_call(blocks, behind_here, unit) for unit in range(per_core)]

    def pair_units(mine):
        other = [swap(part, "section", 1) for part in mine]
        units = list(mine) + other
        if pieces == 2:
            units = [jnp.concatenate(own_other(mine[0], other[0]), axis=2)]
        if aligned:
            return [[unit] for unit in units]
        return [
            [unit[:, :shard_rows].reshape(-1, width), unit[:, shard_rows:].reshape(-1, width)]
            for unit in units
        ]

    def cut_units(grads):
        if aligned:
            units = [unit for (unit,) in grads]
        else:
            units = [
                jnp.concatenate(
                    [part.reshape(n_ctx * n_fsdp, -1, width) for part in parts], axis=1
                )
                for parts in grads
            ]
        if pieces == 1:
            return (units[:per_core], units[per_core:])
        own, other = own_other(*jnp.split(units[0], 2, axis=2))
        return ([own], [other])

    def ring_part(terms, behind):
        spot = behind_here[behind % n_fsdp]
        return sum(at(term, spot, 1).astype(f32) for term in terms)

    def ring_start(own, received):
        terms = [part.reshape((n_ctx, n_fsdp) + part.shape[1:]) for part in (own, received)]
        return (terms, ring_part(terms, 1).astype(bf16))

    def ring_step(state, step):
        return [
            (terms, (lax.ppermute(moving, "fsdp", ring_steps).astype(f32)
                     + ring_part(terms, step + 1)).astype(bf16))
            for terms, moving in state
        ]

    def ring_rest(state, first):
        for step in range(first, n_fsdp):
            state = ring_step(state, step)
        return [moving for _, moving in state]

    def scatter_units(moved):
        whole = jnp.stack(moved, axis=1)
        blocks = [at(whole, place)]
        blocks += [swap(at(whole, place ^ bit), "ctx", bit) for bit in range(1, n_ctx)]
        return jnp.stack(blocks)

    def trade_square(own, received):
        own, received = (part.reshape(n_ctx, -1, part.shape[1]) for part in (own, received))

        def part(bit):
            return at(own, place ^ bit).astype(f32) + at(received, place ^ bit).astype(f32)

        return [part(0)] + [swap(part(bit).astype(bf16), "ctx", bit) for bit in range(1, n_ctx)]

    def sum_square(parts):
        return sum(part.astype(f32) for part in parts).astype(bf16)

    def reduce_deep(mine):
        mine = mine.reshape(n_fsdp, shard_rows, -1)
        total = at(mine, depth).astype(f32)
        for bit in range(1, n_fsdp):
            total = total + swap(at(mine, depth ^ bit), "fsdp", bit).astype(f32)
        return total

    if pieces == 1:
        units_here = jnp.arange(per_core, dtype=jnp.uint32)
        units_here = jnp.concatenate(
            [core * per_core + units_here, (1 - core) * per_core + units_here]
        )
    else:
        units_here = jnp.zeros((1,), jnp.uint32)
    named = (place * own_experts + units_here).astype(f32)
    matches = info[:, None, :, :TOP] == named[None, :, None, None, None]
    hits = jnp.any(matches, axis=3)
    shares = jnp.sum(jnp.where(matches, info[:, None, :, TOP:], 0.0), axis=3)
    earlier = jnp.arange(rows)[:, None] < jnp.arange(rows)[None, :]
    rank = dot("ledr,rq->ledq", hits.astype(bf16), earlier.astype(bf16))
    slots = jnp.arange(capacity, dtype=f32)
    picks = hits[:, :, :, None, :] & (rank[:, :, :, None, :] == slots[:, None])
    slot_shares = jnp.sum(jnp.where(picks, shares[:, :, :, None, :], 0.0), axis=-1, keepdims=True)
    picks = picks.astype(bf16)

    order = place.astype(jnp.int32) ^ jnp.arange(n_ctx, dtype=jnp.int32)
    block_ids = jnp.take(block_of.reshape(n_ctx, 2), order, axis=0)
    block_ids = block_ids.reshape(-1)

    def gains_of(halves):
        pair = on_core(halves[1][:, -gap : 2 - gap], halves[0][:, -gap : 2 - gap])
        pair = pair.astype(f32).T
        return (pair[:1], pair[1:])

    def experts(layer, blocks, weights):
        returned, kept = ([], {})
        for j in range(own_experts):
            returned, kept[j] = expert_call(
                picks[layer, j],
                slot_shares[layer, j],
                blocks,
                weights[j],
                shard_rows,
                hidden,
                returned,
            )
        return (returned, kept)

    def experts_back(layer, blocks, weights, kept, beside):
        returned, grads, arrived = ([], {}, [])
        for j in reversed(range(own_experts)):
            returned, grads[j] = expert_back_call(
                picks[layer, j],
                slot_shares[layer, j],
                blocks,
                kept[j],
                weights[j],
                shard_rows,
                hidden,
                returned,
            )
            if beside:
                returned, grads[j], sent = tie(returned, grads[j], beside.pop(0)())
                arrived.append(sent)
        arrived += [send() for send in beside]
        own, other = cut_units([grads[j] for j in range(own_experts)])
        received = [swap(part, "section", 1) for part in other]
        return (returned, own, received, arrived)

    def keep_own(first, second):
        other = swap(on_core(second, first), "section", 1)
        return own_other(on_core(first, second), other)

    deep_first = gather_deep(dense_shards[0])
    dealt_first, dealt_second = (deal_units(stack) for stack in unit_stacks)
    deep_first, dealt_first, dealt_second, picks, shard_second = tie(
        deep_first, dealt_first, dealt_second, picks, dense_shards[1]
    )
    moved = [[dealt_first], [shard_second[None, None]]]
    dense_blocks, moved = tie(spread(deep_first[:, :enter_cut]), ring_send(moved))
    enter_own = join_square(dense_blocks)
    enter_first = (enter_own, swap(enter_own, "section", 1))

    first_gains = gains_of(enter_first)
    first_in = after(at(tokens, core)[0], slot_shares)
    _, first_normed, first_entered = enter_call(core, [first_in], first_gains[0], enter_first)
    key_value = first_entered[:, qw : qw + 2 * kw]
    first_kv, moved, deep_first = tie(
        jnp.concatenate(spread(key_value)), ring_send(moved), deep_first
    )
    leave_blocks = spread(deep_first[:, enter_cut:])
    first_attended = attend_call(block_ids, first_entered, first_kv)
    first_attended, leave_blocks = tie(first_attended, leave_blocks)
    leave_own = join_square(leave_blocks)
    leave_first = (leave_own, swap(leave_own, "section", 1))
    for _ in range(2, n_fsdp - 1):
        moved = ring_send(moved)
    first_mid, ffn_normed = leave_call(core, first_in, first_attended, first_gains[1], leave_first)
    ffn_normed, moved, dealt_second = tie(ffn_normed, moved, dealt_second)
    first_units = own_units(moved[0])
    deep_second = order_call(moved[1], behind_here, 0).reshape(-1, low_shard.shape[1])
    blocks, deep_second, dealt_second = tie(spread(ffn_normed), deep_second, dealt_second)
    enter_blocks = spread(deep_second[:, :enter_cut])
    first_weights = pair_units(first_units)
    returned, first_kept = experts(0, blocks, first_weights)
    returned, moved, enter_blocks, deep_second = tie(
        returned, ring_send([[dealt_second]]), enter_blocks, deep_second
    )
    enter_own = join_square(enter_blocks)
    enter_second = (enter_own, swap(enter_own, "section", 1))
    returned, moved, deep_second = tie(gather_back(returned), ring_send(moved), deep_second)

    second_gains = gains_of(enter_second)
    second_in, second_normed, second_entered = enter_call(
        core, [first_mid] + returned, second_gains[0], enter_second
    )
    key_value = second_entered[:, qw : qw + 2 * kw]
    for _ in range(3, n_fsdp):
        moved = ring_send(moved)
    second_kv, moved, deep_second = tie(jnp.concatenate(spread(key_value)), moved, deep_second)
    leave_blocks = spread(deep_second[:, enter_cut:])
    second_attended = attend_call(block_ids, second_entered, second_kv)
    second_attended, leave_blocks = tie(second_attended, leave_blocks)
    leave_own = join_square(leave_blocks)
    leave_second = (leave_own, swap(leave_own, "section", 1))
    second_mid, ffn_normed = leave_call(
        core, second_in, second_attended, second_gains[1], leave_second
    )
    second_weights = pair_units(own_units(moved[0]))
    blocks = spread(ffn_normed)
    cotangent = after(at(out_grad, core)[0], blocks)
    cot_blocks = spread(cotangent)
    returned, second_kept = experts(1, blocks, second_weights)
    cot_blocks, returned = tie(cot_blocks, returned)
    second_parts = gather_back(returned)

    returned, own, received, _ = experts_back(1, cot_blocks, second_weights, second_kept, [])
    returned, own, received, second_parts = tie(returned, own, received, second_parts)
    second_out = second_mid + sum(part.astype(f32) for part in second_parts)
    layer_outs = keep_own(second_in, second_out.astype(bf16))
    units_moving = [ring_start(*pair) for pair in zip(own, received)]
    after_rows, term, d_attended, *grads = leave_back_call(
        core,
        gather_back(returned),
        second_gains[1],
        second_mid,
        cotangent,
        second_attended,
        leave_second,
    )
    d_attended, units_moving = tie(d_attended, ring_step(units_moving, 1))
    leave_grads = (grads[0], swap(grads[1], "section", 1))
    d_queries, d_key_value = attend_back_call(block_ids, second_entered, second_kv, d_attended)
    d_key_value, leave_grads, units_moving = tie(
        gather_back(d_key_value), leave_grads, ring_step(units_moving, 2)
    )
    second_entry, cotangent, *grads = enter_back_call(
        core,
        d_queries,
        d_key_value,
        second_gains[0],
        second_in,
        second_normed,
        after_rows,
        term,
        enter_second,
    )
    cotangent, grads = tie(cotangent, grads)
    units_moving = ring_rest(units_moving, 3)
    enter_grads = (grads[0], swap(grads[1], "section", 1))

    blocks, enter_grads, second_moved = tie(spread(cotangent), enter_grads, units_moving)
    leave_grads, layer_outs = after((leave_grads, layer_outs), blocks)
    beside = [lambda: trade_square(*leave_grads), lambda: trade_square(*enter_grads)]
    returned, own, received, arrived = experts_back(0, blocks, first_weights, first_kept, beside)
    returned, own, received = tie(returned, own, received)
    units_moving = [ring_start(*pair) for pair in zip(own, received)]
    after_rows, term, d_attended, *grads = leave_back_call(
        core,
        gather_back(returned),
        first_gains[1],
        first_mid,
        cotangent,
        first_attended,
        leave_first,
    )
    d_attended, units_moving, arrived, second_moved = tie(
        d_attended, ring_step(units_moving, 1), arrived, second_moved
    )
    second_scattered = scatter_units(second_moved)
    leave_moving, enter_moving = (sum_square(parts) for parts in arrived)
    second_moving = jnp.concatenate([enter_moving, leave_moving], axis=1)
    leave_grads = (grads[0], swap(grads[1], "section", 1))
    d_queries, d_key_value = attend_back_call(block_ids, first_entered, first_kv, d_attended)
    d_key_value, leave_grads, units_moving, second_scattered, layer_outs = tie(
        gather_back(d_key_value),
        leave_grads,
        ring_step(units_moving, 2),
        second_scattered,
        layer_outs,
    )
    leave_parts = trade_square(*leave_grads)
    first_entry, _, *grads = enter_back_call(
        core,
        d_queries,
        d_key_value,
        first_gains[0],
        first_in,
        first_normed,
        after_rows,
        term,
        enter_first,
    )
    enter_grads, leave_parts, second_moving = tie(
        (grads[0], swap(grads[1], "section", 1)), leave_parts, second_moving
    )
    enter_parts, second_dense = tie(trade_square(*enter_grads), reduce_deep(second_moving))
    first_moving = [sum_square(parts) for parts in (enter_parts, leave_parts)]
    first_dense = reduce_deep(jnp.concatenate(first_moving, axis=1))
    first_scattered = scatter_units(ring_rest(units_moving, 3))

    layer_out = jnp.stack(layer_outs)
    input_grads = jnp.stack(keep_own(first_entry, second_entry))
    low_dense, high_dense = keep_own(first_dense, second_dense)
    enter_grad = jnp.concatenate([low_dense[:, :enter_cut], high_dense[:, :enter_cut]], axis=1)
    grad_out = jnp.concatenate([low_dense[:, enter_cut:], high_dense[:, enter_cut:]], axis=1)
    grad_gains = enter_grad[:, qw + 2 * kw :]
    mine = on_core(first_scattered, second_scattered)
    other = swap(on_core(second_scattered, first_scattered), "section", 1)
    if aligned and pieces == 1:
        grad_gate, grad_up, grad_down = finish_call(mine, other, shard_rows, hidden, place, core)
    else:
        sides = [jnp.take(part, order, axis=0) for part in own_other(mine, other)]
        if pieces == 1:
            whole = jnp.stack(sides, axis=1).reshape(EXPERTS, unit_rows, width)
        else:
            whole = jnp.concatenate([side[:, 0] for side in sides], axis=2)
        pairs = whole[:, :shard_rows].astype(f32).reshape(EXPERTS, shard_rows, 2, 2, cut)
        grad_gate = pairs[:, :, :, 0].reshape(EXPERTS, shard_rows, hidden)
        grad_up = pairs[:, :, :, 1].reshape(EXPERTS, shard_rows, hidden)
        grad_down = whole[:, shard_rows:].astype(f32)
    return (
        layer_out[None, :, None],
        input_grads[None, :, None],
        grad_gains[:, 0][None],
        enter_grad[:, :qw][None],
        enter_grad[:, qw : qw + kw][None],
        enter_grad[:, qw + kw : qw + 2 * kw][None],
        grad_out[None],
        grad_gains[:, 1][None],
        grad_gate[None],
        grad_up[None],
        grad_down[None],
    )


def solution(mesh):
    rows_placed = P(None, "fsdp", "ctx", None)
    kept_placed = P("section", None, "fsdp", "ctx", None)
    gain_placed = P("section", ("ctx", "fsdp"))
    dense_placed = P("section", ("ctx", "fsdp"), None)
    expert_placed = P("section", None, ("ctx", "fsdp"), None)
    dense_all = (dense_placed,) * 4
    expert_all = (expert_placed,) * 3
    layer_placed = (gain_placed,) + dense_all + (gain_placed,) + expert_all
    return jax.shard_map(
        body,
        mesh=mesh,
        in_specs=(rows_placed, P(), kept_placed, kept_placed) + layer_placed + (rows_placed,),
        out_specs=(kept_placed, kept_placed) + layer_placed,
        check_vma=False,
    )
```

```python
import functools

import jax
import jax.numpy as jnp
from jax import lax
from jax.experimental import pallas as pl
from jax.experimental.pallas import tpu as pltpu
from jax.sharding import PartitionSpec as P

QH = 12
KVH = 2
HD = 128
GROUP = QH // KVH
TOP = 4
EXPERTS = 8
bf16 = jnp.bfloat16
f32 = jnp.float32


epsilon = 1e-06
masked_out = -1e30
gap = 256


def swap(value, axis, bit):
    count = lax.axis_size(axis)
    return lax.ppermute(value, axis, [(source, source ^ bit) for source in range(count)])


def tie(*values):
    return lax.optimization_barrier(values)


def after(value, earlier):
    return tie(value, earlier)[0]


def at(value, index, axis=0):
    return lax.dynamic_index_in_dim(value, index, axis, keepdims=False)


def dot(spec, left, right, kind=f32):
    return jnp.einsum(spec, left, right, preferred_element_type=kind)


def cost(micros):
    return pl.CostEstimate(
        flops=int(micros * 1e9), bytes_accessed=int(micros * 3e6), transcendentals=0
    )


def kernel_params():
    return pltpu.CompilerParams(vmem_limit_bytes=56 * 1024 * 1024)


def nt(left, right):
    return lax.dot_general(left, right, (((1,), (1,)), ((), ())), preferred_element_type=f32)


def nn(left, right):
    return jnp.dot(left, right, preferred_element_type=f32)


def head_rows(ref):
    return jnp.concatenate([ref[:, i * HD : (i + 1) * HD] for i in range(GROUP)], axis=0)


def softmax_rows(ids_ref, queries, keys, half, own):
    scores = nt(queries, keys) * HD ** (-0.5)
    tall, wide = scores.shape
    row = lax.broadcasted_iota(jnp.int32, (half, 1), 0)
    row = jnp.concatenate([row] * (tall // half), axis=0) + ids_ref[own] * half
    lane = lax.broadcasted_iota(jnp.int32, (1, half), 1)
    column = [lane + ids_ref[block] * half for block in range(wide // half)]
    column = jnp.concatenate(column, axis=1)
    scores = jnp.where(row >= column, scores, masked_out)
    shifted = jnp.exp(scores - jnp.max(scores, axis=1, keepdims=True))
    return shifted / jnp.sum(shifted, axis=1, keepdims=True)


def attend_kernel(ids_ref, query_ref, key_ref, value_ref, out_ref):
    half = query_ref.shape[0]
    probs = softmax_rows(ids_ref, head_rows(query_ref), key_ref[...], half, pl.program_id(1))
    out = nn(probs.astype(bf16), value_ref[...]).astype(bf16)
    for i in range(GROUP):
        out_ref[:, i * HD : (i + 1) * HD] = out[i * half : (i + 1) * half]


def attend_specs(rows, seq_len):
    half = rows // 2
    by_head = pl.BlockSpec((half, GROUP * HD), lambda g, h, ids: (h, g))
    keys = pl.BlockSpec((seq_len, HD), lambda g, h, ids: (0, g))
    values = pl.BlockSpec((seq_len, HD), lambda g, h, ids: (0, KVH + g))
    return by_head, keys, values


def attend_call(ids, queries, key_value):
    rows, seq_len = (queries.shape[0], key_value.shape[0])
    by_head, keys, values = attend_specs(rows, seq_len)
    return pl.pallas_call(
        attend_kernel,
        grid_spec=pltpu.PrefetchScalarGridSpec(
            num_scalar_prefetch=1,
            grid=(KVH, 2),
            in_specs=[by_head, keys, values],
            out_specs=by_head,
        ),
        out_shape=jax.ShapeDtypeStruct((rows, QH * HD), bf16),
        compiler_params=kernel_params(),
        cost_estimate=cost(12),
        name="attend",
    )(ids, queries, key_value, key_value)


def attend_back_kernel(ids_ref, query_ref, key_ref, value_ref, cot_ref, dq_ref, *refs):
    out, (dk_ref, dv_ref) = (refs[:-2], refs[-2:])
    half = query_ref.shape[0]
    group, own = (pl.program_id(0), pl.program_id(1))
    queries, cot = (head_rows(query_ref), head_rows(cot_ref))
    probs = softmax_rows(ids_ref, queries, key_ref[...], half, own)
    d_probs = nt(cot, value_ref[...])
    inner = jnp.sum(probs * d_probs, axis=1, keepdims=True)
    d_scores = (probs * (d_probs - inner)).astype(bf16)
    d_queries = (nn(d_scores, key_ref[...]) * HD ** (-0.5)).astype(bf16)
    for i in range(GROUP):
        dq_ref[:, i * HD : (i + 1) * HD] = d_queries[i * half : (i + 1) * half]
    d_keys = nn(d_scores.T, queries) * HD ** (-0.5)
    d_values = nn(probs.astype(bf16).T, cot)

    @pl.when(own == 0)
    def _():
        dk_ref[...] = d_keys
        dv_ref[...] = d_values

    @pl.when(own != 0)
    def _():
        rows = 2 * half
        for block, ref in enumerate(out):
            part = slice(block * rows, (block + 1) * rows)
            for first, total, last in ((0, dk_ref, d_keys), (KVH * HD, dv_ref, d_values)):
                columns = pl.ds(pl.multiple_of(first + group * HD, HD), HD)
                ref[:, columns] = (total[part, :] + last[part]).astype(bf16)


def attend_back_call(ids, queries, key_value, cot):
    rows, seq_len = (queries.shape[0], key_value.shape[0])
    by_head, keys, values = attend_specs(rows, seq_len)
    blocks = seq_len // rows
    wide = 2 * KVH * HD
    result = pl.pallas_call(
        attend_back_kernel,
        grid_spec=pltpu.PrefetchScalarGridSpec(
            num_scalar_prefetch=1,
            grid=(KVH, 2),
            in_specs=[by_head, keys, values, by_head],
            out_specs=[by_head] + [pl.BlockSpec((rows, wide), lambda g, h, ids: (0, 0))] * blocks,
            scratch_shapes=[pltpu.VMEM((seq_len, HD), f32)] * 2,
        ),
        out_shape=[jax.ShapeDtypeStruct((rows, QH * HD), bf16)]
        + [jax.ShapeDtypeStruct((rows, wide), bf16)] * blocks,
        compiler_params=kernel_params(),
        cost_estimate=cost(1),
        name="attend_back",
    )(ids, queries, key_value, key_value, cot)
    return (result[0], result[1:])


def gelu_parts(gate):
    root = 0.7978845608028654
    inner = root * (gate + 0.044715 * gate * gate * gate)
    bent = jnp.tanh(inner)
    value = 0.5 * gate * (1.0 + bent)
    slope = root * (1.0 + 3.0 * 0.044715 * gate * gate)
    return value, 0.5 * (1.0 + bent) + 0.5 * gate * (1.0 - bent * bent) * slope


def give_back(pick_ref, total_ref, share_ref, before, out):
    blocks, capacity, _ = pick_ref.shape
    for d in range(blocks):
        part = total_ref[d * capacity : (d + 1) * capacity, :]
        if share_ref is not None:
            part = part * share_ref[d]
        back = nn(pick_ref[d].T, part.astype(bf16))
        if before:
            back = back + before[d][...]
        out[d][...] = back.astype(out[d].dtype)


def flat(ref):
    value = ref[...]
    return value.reshape(-1, value.shape[-1])


def add_up(total_ref, part, step):
    @pl.when(step == 0)
    def _():
        total_ref[...] = part

    @pl.when(step != 0)
    def _():
        total_ref[...] += part


def expert_kernel(blocks, adds, pick_ref, share_ref, gate_ref, up_ref, down_ref, *refs):
    rows, refs = (refs[:blocks], refs[blocks:])
    before, refs = (refs[: blocks * adds], refs[blocks * adds :])
    out, (picked_ref, gate_pre_ref, up_pre_ref, total_ref) = (refs[:blocks], refs[blocks:])
    step = pl.program_id(0)
    capacity = pick_ref.shape[1]

    @pl.when(step == 0)
    def _():
        for d in range(blocks):
            block = nn(pick_ref[d], rows[d][...]).astype(bf16)
            picked_ref[d * capacity : (d + 1) * capacity, :] = block

    gate_pre = nn(picked_ref[...], flat(gate_ref))
    up_pre = nn(picked_ref[...], flat(up_ref))
    gate_pre_ref[...] = gate_pre
    up_pre_ref[...] = up_pre
    active = (gelu_parts(gate_pre)[0] * up_pre).astype(bf16)
    add_up(total_ref, nn(active, flat(down_ref)), step)

    @pl.when(step == pl.num_programs(0) - 1)
    def _():
        give_back(pick_ref, total_ref, share_ref, before, out)


def whole_spec(shape):
    return pl.BlockSpec(
        shape, lambda step: (0,) * len(shape), pipeline_mode=pl.Buffered(buffer_count=1)
    )


def weight_operands(weights, deep, cut):
    if len(weights) == 1:
        unit = weights[0]
        shards, tall, width = unit.shape
        specs = [
            pl.BlockSpec((shards, deep, cut), lambda step: (0, 0, 2 * step)),
            pl.BlockSpec((shards, deep, cut), lambda step: (0, 0, 2 * step + 1)),
            pl.BlockSpec(
                (shards // 2, tall - deep, width), lambda step: (step, deep // (tall - deep), 0)
            ),
        ]
        return specs, [unit, unit, unit]
    pair, down = weights
    specs = [
        pl.BlockSpec((pair.shape[0], cut), lambda step: (0, 2 * step)),
        pl.BlockSpec((pair.shape[0], cut), lambda step: (0, 2 * step + 1)),
        pl.BlockSpec((cut, down.shape[1]), lambda step: (step, 0)),
    ]
    return specs, [pair, pair, down]


def expert_call(picks, shares, rows, weights, deep, hidden, before):
    blocks, capacity, _ = picks.shape
    width, cut, tall = (rows[0].shape[1], hidden // 2, blocks * capacity)
    columns = pl.BlockSpec((tall, cut), lambda step: (0, step))
    row_specs = [whole_spec(block.shape) for block in rows]
    specs, operands = weight_operands(weights, deep, cut)
    result = pl.pallas_call(
        functools.partial(expert_kernel, blocks, 1 if before else 0),
        grid=(2,),
        in_specs=[whole_spec(picks.shape), whole_spec(shares.shape)]
        + specs
        + row_specs * (2 if before else 1),
        out_specs=row_specs + [whole_spec((tall, width)), columns, columns],
        out_shape=[jax.ShapeDtypeStruct(block.shape, bf16) for block in rows]
        + [
            jax.ShapeDtypeStruct((tall, width), bf16),
            jax.ShapeDtypeStruct((tall, hidden), f32),
            jax.ShapeDtypeStruct((tall, hidden), f32),
        ],
        scratch_shapes=[pltpu.VMEM((tall, width), f32)],
        compiler_params=kernel_params(),
        cost_estimate=cost(15),
        name="expert",
    )(picks, shares, *operands, *rows, *before)
    return (result[:blocks], result[blocks:])


def expert_back_kernel(
    blocks, adds, deep, pick_ref, share_ref, picked_ref, gate_pre_ref, up_pre_ref,
    gate_ref, up_ref, down_ref, *refs
):
    rows, refs = (refs[:blocks], refs[blocks:])
    before, refs = (refs[: blocks * adds], refs[blocks * adds :])
    out, refs = (refs[:blocks], refs[blocks:])
    grad_refs, (slots_ref, turned_ref, total_ref) = (refs[:-3], refs[-3:])
    step = pl.program_id(0)
    capacity, cut = (pick_ref.shape[1], gate_pre_ref.shape[1])

    @pl.when(step == 0)
    def _():
        for d in range(blocks):
            block = nn(pick_ref[d], rows[d][...]) * share_ref[d]
            slots_ref[d * capacity : (d + 1) * capacity, :] = block.astype(bf16)
        turned_ref[...] = picked_ref[...].T

    d_active = nt(slots_ref[...], flat(down_ref))
    value, slope = gelu_parts(gate_pre_ref[...])
    up_pre = up_pre_ref[...]
    active = (value * up_pre).astype(bf16)
    d_gate = (d_active * up_pre * slope).astype(bf16)
    d_up = (d_active * value).astype(bf16)
    grad_down = nn(active.T, slots_ref[...]).astype(bf16)
    grad_gate = nn(turned_ref[...], d_gate).astype(bf16)
    grad_up = nn(turned_ref[...], d_up).astype(bf16)
    if len(grad_refs) == 1:
        unit_ref = grad_refs[0]
        shards, tall, width = unit_ref.shape
        for side in range(2):

            @pl.when(step == side)
            def _():
                left, some = (2 * side * cut, shards // 2)
                unit_ref[:, :deep, left : left + cut] = grad_gate.reshape(shards, deep, cut)
                left = left + cut
                unit_ref[:, :deep, left : left + cut] = grad_up.reshape(shards, deep, cut)
                rest = grad_down.reshape(some, tall - deep, width)
                unit_ref[side * some : (side + 1) * some, deep:, :] = rest
    else:
        grad_refs[0][:, :cut] = grad_gate
        grad_refs[0][:, cut:] = grad_up
        grad_refs[1][...] = grad_down
    part = nt(d_gate, flat(gate_ref)) + nt(d_up, flat(up_ref))
    add_up(total_ref, part, step)

    @pl.when(step == pl.num_programs(0) - 1)
    def _():
        give_back(pick_ref, total_ref, None, before, out)


def expert_back_call(picks, shares, rows, kept, weights, deep, hidden, before):
    blocks, capacity, _ = picks.shape
    width, cut, tall = (rows[0].shape[1], hidden // 2, blocks * capacity)
    columns = pl.BlockSpec((tall, cut), lambda step: (0, step))
    row_specs = [whole_spec(block.shape) for block in rows]
    specs, operands = weight_operands(weights, deep, cut)
    grad_shapes = [jax.ShapeDtypeStruct(part.shape, bf16) for part in weights]
    if len(weights) == 1:
        grad_specs = [whole_spec(weights[0].shape)]
    else:
        grad_specs = [
            pl.BlockSpec((width, 2 * cut), lambda step: (0, step)),
            pl.BlockSpec((cut, width), lambda step: (step, 0)),
        ]
    result = pl.pallas_call(
        functools.partial(expert_back_kernel, blocks, 1 if before else 0, deep),
        grid=(2,),
        in_specs=[
            whole_spec(picks.shape),
            whole_spec(shares.shape),
            whole_spec((tall, width)),
            columns,
            columns,
        ]
        + specs
        + row_specs * (2 if before else 1),
        out_specs=row_specs + grad_specs,
        out_shape=[jax.ShapeDtypeStruct(block.shape, bf16) for block in rows] + grad_shapes,
        scratch_shapes=[
            pltpu.VMEM((tall, width), bf16),
            pltpu.VMEM((width, tall), bf16),
            pltpu.VMEM((tall, width), f32),
        ],
        compiler_params=kernel_params(),
        cost_estimate=cost(25),
        name="expert_back",
    )(picks, shares, *kept, *operands, *rows, *before)
    return (result[:blocks], result[blocks:])


def norm_parts(value):
    scale = lax.rsqrt(jnp.mean(value * value, axis=1, keepdims=True) + epsilon)
    return scale, value * scale


def norm_back(grad, gain, value):
    scale, scaled = norm_parts(value)
    grown = grad * gain
    back = scale * (grown - scaled * jnp.mean(scaled * grown, axis=1, keepdims=True))
    return back, (grad * scaled).astype(bf16)


def add_all(refs):
    total = refs[0][...].astype(f32)
    for ref in refs[1:]:
        total = total + ref[...].astype(f32)
    return total


def side_offsets(core_ref, steps, cut):
    step, core = (pl.program_id(0), core_ref[0])
    own = pl.multiple_of((core * steps + step) * cut, cut)
    other = pl.multiple_of(((1 - core) * steps + step) * cut, cut)
    return own, other


def dense_call(kernel, core, steps, whole, halves, out, scratch, name, micros):
    cut = halves[0].shape[1] // steps

    def keep(shape):
        return pl.BlockSpec(
            shape, lambda step, core: (0,) * len(shape), pipeline_mode=pl.Buffered(buffer_count=1)
        )

    def tile(tall):
        return pl.BlockSpec((tall, cut), lambda step, core: (0, step))

    return pl.pallas_call(
        kernel,
        grid_spec=pltpu.PrefetchScalarGridSpec(
            num_scalar_prefetch=1,
            grid=(steps,),
            in_specs=[keep(part.shape) for part in whole] + [tile(halves[0].shape[0])] * 2,
            out_specs=[
                tile(part.shape[0]) if tiled else keep(part.shape) for part, tiled in out
            ],
            scratch_shapes=scratch,
        ),
        out_shape=[part for part, _ in out],
        compiler_params=kernel_params(),
        cost_estimate=cost(micros),
        name=name,
    )(core.astype(jnp.int32).reshape(1), *whole, *halves)


def shape_of(kind, *shape):
    return jax.ShapeDtypeStruct(shape, kind)


def enter_kernel(steps, terms, core_ref, gain_ref, *refs):
    parts, (own_ref, other_ref, sent_ref, normed_ref, out_ref) = (refs[:terms], refs[terms:])
    own, other = side_offsets(core_ref, steps, own_ref.shape[1])

    @pl.when(pl.program_id(0) == 0)
    def _():
        sent = add_all(parts).astype(bf16)
        sent_ref[...] = sent
        normed_ref[...] = (norm_parts(sent.astype(f32))[1] * gain_ref[...]).astype(bf16)

    cut = own_ref.shape[1]
    out_ref[:, pl.ds(own, cut)] = nn(normed_ref[...], own_ref[...]).astype(bf16)
    out_ref[:, pl.ds(other, cut)] = nn(normed_ref[...], other_ref[...]).astype(bf16)


def enter_call(core, parts, gain, halves):
    rows, width = parts[0].shape
    return dense_call(
        functools.partial(enter_kernel, 3, len(parts)),
        core,
        3,
        [gain] + parts,
        halves,
        [
            (shape_of(bf16, rows, width), False),
            (shape_of(bf16, rows, width), False),
            (shape_of(bf16, rows, 2 * halves[0].shape[1]), False),
        ],
        [],
        "enter",
        6,
    )


def leave_kernel(steps, core_ref, gain_ref, rows_ref, attended_ref, own_ref, other_ref,
                 mid_ref, normed_ref):
    cut = own_ref.shape[1]
    for start, ref in zip(side_offsets(core_ref, steps, cut), (own_ref, other_ref)):
        part = pl.ds(start, cut)
        mid_ref[:, part] = rows_ref[:, part].astype(f32) + nn(attended_ref[...], ref[...])

    @pl.when(pl.program_id(0) == steps - 1)
    def _():
        normed_ref[...] = (norm_parts(mid_ref[...])[1] * gain_ref[...]).astype(bf16)


def leave_call(core, rows_in, attended, gain, halves):
    rows, width = rows_in.shape
    return dense_call(
        functools.partial(leave_kernel, 2),
        core,
        2,
        [gain, rows_in, attended],
        halves,
        [(shape_of(f32, rows, width), False), (shape_of(bf16, rows, width), False)],
        [],
        "leave",
        5,
    )


def leave_back_kernel(steps, terms, core_ref, gain_ref, mid_ref, cot_ref, attended_ref, *refs):
    parts, refs = (refs[:terms], refs[terms:])
    own_ref, other_ref, after_ref, term_ref, d_attended_ref, *refs = refs
    own_grad_ref, other_grad_ref, branch_ref, turned_ref, total_ref = refs
    step, cut = (pl.program_id(0), own_ref.shape[1])

    @pl.when(step == 0)
    def _():
        back, term_ref[...] = norm_back(add_all(parts), gain_ref[...], mid_ref[...])
        back = back + cot_ref[...].astype(f32)
        after_ref[...] = back
        branch_ref[...] = back.astype(bf16)
        turned_ref[...] = attended_ref[...].T

    own, other = side_offsets(core_ref, steps, cut)
    d_own, d_other = (branch_ref[:, pl.ds(own, cut)], branch_ref[:, pl.ds(other, cut)])
    own_grad_ref[...] = nn(turned_ref[...], d_own).astype(bf16)
    other_grad_ref[...] = nn(turned_ref[...], d_other).astype(bf16)
    add_up(total_ref, nt(d_own, own_ref[...]) + nt(d_other, other_ref[...]), step)

    @pl.when(step == steps - 1)
    def _():
        d_attended_ref[...] = total_ref[...].astype(bf16)


def leave_back_call(core, parts, gain, mid, cotangent, attended, halves):
    rows, width = mid.shape
    half = (halves[0].shape[0], halves[0].shape[1])
    return dense_call(
        functools.partial(leave_back_kernel, 2, len(parts)),
        core,
        2,
        [gain, mid, cotangent, attended] + parts,
        halves,
        [
            (shape_of(f32, rows, width), False),
            (shape_of(bf16, rows, width), False),
            (shape_of(bf16, rows, width), False),
            (shape_of(bf16, *half), True),
            (shape_of(bf16, *half), True),
        ],
        [
            pltpu.VMEM((rows, width), bf16),
            pltpu.VMEM((width, rows), bf16),
            pltpu.VMEM((rows, width), f32),
        ],
        "leave_back",
        8,
    )


def enter_back_kernel(steps, terms, core_ref, gain_ref, rows_ref, normed_ref, after_ref, term_ref,
                      dq_ref, *refs):
    parts, refs = (refs[:terms], refs[terms:])
    own_ref, other_ref, entry_ref, sent_ref, own_grad_ref, other_grad_ref, *refs = refs
    entered_ref, turned_ref, total_ref = refs
    step, cut = (pl.program_id(0), own_ref.shape[1])
    rows, qw = dq_ref.shape

    @pl.when(step == 0)
    def _():
        entered_ref[:, :qw] = dq_ref[...]
        wide = parts[0].shape[1]
        entered_ref[:, qw : qw + wide] = add_all(parts).astype(bf16)
        entered_ref[:, qw + wide :] = jnp.zeros((rows, gap), bf16)
        turned_ref[...] = normed_ref[...].T

    own, other = side_offsets(core_ref, steps, cut)
    d_own, d_other = (entered_ref[:, pl.ds(own, cut)], entered_ref[:, pl.ds(other, cut)])
    own_grad_ref[...] = nn(turned_ref[...], d_own).astype(bf16)
    other_grad_ref[...] = nn(turned_ref[...], d_other).astype(bf16)
    add_up(total_ref, nt(d_own, own_ref[...]) + nt(d_other, other_ref[...]), step)

    @pl.when(step == steps - 1)
    def _():
        back, attn_term = norm_back(total_ref[...], gain_ref[...], rows_ref[...].astype(f32))
        back = back + after_ref[...]
        entry_ref[...] = back
        sent_ref[...] = back.astype(bf16)
        lane = lax.broadcasted_iota(jnp.int32, (rows, 128), 1)
        sums = nn(attn_term.T, (lane == 0).astype(bf16))
        sums = (sums + nn(term_ref[...].T, (lane == 1).astype(bf16))).astype(bf16)
        left = cut - gap

        @pl.when(core_ref[0] == 0)
        def _():
            other_grad_ref[:, left : left + 128] = sums

        @pl.when(core_ref[0] != 0)
        def _():
            own_grad_ref[:, left : left + 128] = sums


def enter_back_call(core, dq, parts, gain, rows_in, normed, after, term, halves):
    rows, width = rows_in.shape
    return dense_call(
        functools.partial(enter_back_kernel, 3, len(parts)),
        core,
        3,
        [gain, rows_in, normed, after, term, dq] + parts,
        halves,
        [
            (shape_of(f32, rows, width), False),
            (shape_of(bf16, rows, width), False),
            (shape_of(bf16, *halves[0].shape), True),
            (shape_of(bf16, *halves[0].shape), True),
        ],
        [
            pltpu.VMEM((rows, 2 * halves[0].shape[1]), bf16),
            pltpu.VMEM((width, rows), bf16),
            pltpu.VMEM((rows, width), f32),
        ],
        "enter_back",
        1,
    )


def place_kernel(count, joined, index_ref, *refs):
    step = pl.program_id(0)
    for bit in range(count):

        @pl.when(step == bit)
        def _():
            if joined:
                refs[count][...] = refs[bit][...]
            else:
                refs[count][0] = refs[bit][...]


def place_call(blocks, index):
    count = len(blocks)
    shape = blocks[0].shape
    zeros = (0,) * len(shape)
    joined = len(shape) == 2 and shape[0] % 16 == 0
    if joined:
        out_spec = pl.BlockSpec(shape, lambda step, at: (at[0] ^ step, 0))
        out_shape = (count * shape[0], shape[1])
    else:
        out_spec = pl.BlockSpec((1,) + shape, lambda step, at: (at[0] ^ step,) + zeros)
        out_shape = (count,) + shape
    return pl.pallas_call(
        functools.partial(place_kernel, count, joined),
        grid_spec=pltpu.PrefetchScalarGridSpec(
            num_scalar_prefetch=1,
            grid=(count,),
            in_specs=[pl.BlockSpec(shape, lambda step, at: zeros)] * count,
            out_specs=out_spec,
        ),
        out_shape=jax.ShapeDtypeStruct(out_shape, blocks[0].dtype),
        compiler_params=kernel_params(),
        cost_estimate=cost(2),
        name="place",
    )(index.astype(jnp.int32).reshape(1), *blocks)


def order_kernel(count, order_ref, *refs):
    step = pl.program_id(0)
    for i in range(count):

        @pl.when(step == i)
        def _():
            refs[count][:, 0] = refs[i][:, 0]


def order_call(blocks, order, unit):
    count = len(blocks)
    n_ctx, _, tall, wide = blocks[0].shape
    shape = (n_ctx, 1, tall, wide)
    source = pl.BlockSpec(
        shape, lambda step, at: (0, unit, 0, 0), pipeline_mode=pl.Buffered(buffer_count=1)
    )
    result = pl.pallas_call(
        functools.partial(order_kernel, count),
        grid_spec=pltpu.PrefetchScalarGridSpec(
            num_scalar_prefetch=1,
            grid=(count,),
            in_specs=[source] * count,
            out_specs=pl.BlockSpec(shape, lambda step, at: (0, at[step], 0, 0)),
        ),
        out_shape=jax.ShapeDtypeStruct((n_ctx, count, tall, wide), bf16),
        compiler_params=kernel_params(),
        cost_estimate=cost(4),
        name="order",
    )(order.astype(jnp.int32), *blocks)
    return result.reshape(n_ctx * count, tall, wide)


def finish_kernel(deep, index_ref, own_ref, other_ref, gate_ref, up_ref, down_ref):
    side = pl.program_id(1)
    wide = gate_ref.shape[2] // 2

    def write(source):
        for half in range(2):
            left, target = (2 * half * wide, slice(half * wide, (half + 1) * wide))
            gate_ref[:, :, target] = source[0, :, :deep, left : left + wide].astype(f32)
            left = left + wide
            up_ref[:, :, target] = source[0, :, :deep, left : left + wide].astype(f32)
        down_ref[...] = source[0, :, deep:, :].astype(f32)

    @pl.when(side == index_ref[1])
    def _():
        write(own_ref)

    @pl.when(side != index_ref[1])
    def _():
        write(other_ref)


def finish_call(own, other, deep, hidden, place, core):
    n_ctx, units, tall, width = own.shape
    experts = 2 * n_ctx * units
    source = pl.BlockSpec((1, units, tall, width), lambda bit, side, at: (bit, 0, 0, 0))
    target = lambda bit, side, at: (2 * (at[0] ^ bit) + side, 0, 0)
    return pl.pallas_call(
        functools.partial(finish_kernel, deep),
        grid_spec=pltpu.PrefetchScalarGridSpec(
            num_scalar_prefetch=1,
            grid=(n_ctx, 2),
            in_specs=[source, source],
            out_specs=[
                pl.BlockSpec((units, deep, hidden), target),
                pl.BlockSpec((units, deep, hidden), target),
                pl.BlockSpec((units, tall - deep, width), target),
            ],
        ),
        out_shape=[
            jax.ShapeDtypeStruct((experts, deep, hidden), f32),
            jax.ShapeDtypeStruct((experts, deep, hidden), f32),
            jax.ShapeDtypeStruct((experts, tall - deep, width), f32),
        ],
        compiler_params=kernel_params(),
        cost_estimate=cost(8),
        name="finish",
    )(jnp.stack([place, core]).astype(jnp.int32), own, other)


def body(
    tokens,
    block_of,
    routes,
    combine,
    attn_norm,
    w_query,
    w_key,
    w_value,
    w_out,
    ffn_norm,
    w_gate,
    w_up,
    w_down,
    out_grad,
):
    rows = tokens.shape[2]
    width = tokens.shape[3]
    half = rows // 2
    n_ctx = lax.axis_size("ctx")
    n_fsdp = lax.axis_size("fsdp")
    core, place, depth = (
        lax.axis_index(axis).astype(jnp.uint32) for axis in ("section", "ctx", "fsdp")
    )
    seq_len = rows * n_ctx
    capacity = rows * TOP * 5 // (4 * EXPERTS)
    score_scale = HD ** (-0.5)
    own_experts = EXPERTS // n_ctx
    hidden = w_gate.shape[3]
    shard_rows = w_query.shape[1]
    down_rows = w_down.shape[2]
    qw = w_query.shape[2]
    kw = w_key.shape[2]
    pieces = max(1, 2 * n_ctx // EXPERTS)
    per_core = max(1, EXPERTS // (2 * n_ctx))
    unit_rows = shard_rows + down_rows
    aligned = shard_rows % 16 == 0 and down_rows % 16 == 0

    def on_core(former, latter):
        return jnp.where(core == 0, former, latter)

    def own_other(low, high):
        return (on_core(low, high), on_core(high, low))

    early, late = (range(1, n_ctx // 2 + 1), range(n_ctx // 2 + 1, n_ctx))

    def send(value, bits):
        return [swap(value, "ctx", bit) for bit in bits]

    def spread(value):
        return [value] + send(value, early) + send(value, late)

    def gather_back(blocks):
        return [blocks[0]] + [swap(blocks[bit], "ctx", bit) for bit in range(1, n_ctx)]

    info = jnp.concatenate([routes.astype(f32), combine], axis=-1)[0, :, 0].transpose(0, 2, 1)
    info_own, info_other = (at(info, core), swap(at(info, 1 - core), "section", 1))
    info = jnp.stack(own_other(info_own, info_other))
    info = jnp.stack([info] + [swap(info, "ctx", bit) for bit in range(1, n_ctx)], axis=1)

    gain_columns = jnp.stack([attn_norm[0], ffn_norm[0]], axis=1)
    gain_columns = jnp.pad(gain_columns, ((0, 0), (0, gap - 2)))
    enter_shard = jnp.concatenate([w_query[0], w_key[0], w_value[0], gain_columns], axis=1)
    enter_cut = enter_shard.shape[1] // 2
    leave_cut = w_out.shape[2] // 2
    low_shard = jnp.concatenate([enter_shard[:, :enter_cut], w_out[0, :, :leave_cut]], axis=1)
    high_shard = jnp.concatenate([enter_shard[:, enter_cut:], w_out[0, :, leave_cut:]], axis=1)
    lent = swap(on_core(high_shard, low_shard), "section", 1)
    dense_shards = (on_core(low_shard, lent), on_core(lent, high_shard))

    def gather_deep(shard):
        blocks = [shard] + [swap(shard, "fsdp", bit) for bit in range(1, n_fsdp)]
        return place_call(blocks, depth).reshape(-1, shard.shape[1])

    def join_square(blocks):
        return place_call(blocks, place).reshape(-1, blocks[0].shape[1])

    def gather_square(deep):
        return join_square(spread(deep))

    cut = hidden // 2
    unit_stack = jnp.concatenate(
        [
            jnp.concatenate(
                [w_gate[0, ..., :cut], w_up[0, ..., :cut], w_gate[0, ..., cut:], w_up[0, ..., cut:]],
                axis=2,
            ),
            w_down[0],
        ],
        axis=1,
    )
    if pieces == 2:
        unit_stack = jnp.stack(jnp.split(unit_stack, 2, axis=2), axis=1)
    unit_stack = unit_stack.reshape(n_ctx, 2, per_core, unit_rows, width // pieces)
    units_lent = swap(at(unit_stack, 1 - core, 1), "section", 1)
    unit_stacks = own_other(at(unit_stack, core, 1), units_lent)

    def deal_units(stack):
        blocks = [at(stack, place)]
        blocks += [swap(at(stack, place ^ bit), "ctx", bit) for bit in range(1, n_ctx)]
        return place_call(blocks, place)

    ring = list(range(0, n_fsdp, 2)) + list(range(1, n_fsdp, 2))[::-1]
    ring_steps = [(ring[i], ring[(i + 1) % n_fsdp]) for i in range(n_fsdp)]
    ring_table = [[ring[ring.index(z) - i] for i in range(n_fsdp)] for z in range(n_fsdp)]
    behind_here = at(jnp.array(ring_table, jnp.uint32), depth)

    def ring_send(moved):
        return [blocks + [lax.ppermute(blocks[-1], "fsdp", ring_steps)] for blocks in moved]

    def own_units(blocks):
        return [order_call(blocks, behind_here, unit) for unit in range(per_core)]

    def pair_units(mine):
        other = [swap(part, "section", 1) for part in mine]
        units = list(mine) + other
        if pieces == 2:
            units = [jnp.concatenate(own_other(mine[0], other[0]), axis=2)]
        if aligned:
            return [[unit] for unit in units]
        return [
            [unit[:, :shard_rows].reshape(-1, width), unit[:, shard_rows:].reshape(-1, width)]
            for unit in units
        ]

    def cut_units(grads):
        if aligned:
            units = [unit for (unit,) in grads]
        else:
            units = [
                jnp.concatenate(
                    [part.reshape(n_ctx * n_fsdp, -1, width) for part in parts], axis=1
                )
                for parts in grads
            ]
        if pieces == 1:
            return (units[:per_core], units[per_core:])
        own, other = own_other(*jnp.split(units[0], 2, axis=2))
        return ([own], [other])

    def ring_part(terms, behind):
        spot = behind_here[behind % n_fsdp]
        return sum(at(term, spot, 1).astype(f32) for term in terms)

    def ring_start(own, received):
        terms = [part.reshape((n_ctx, n_fsdp) + part.shape[1:]) for part in (own, received)]
        return (terms, ring_part(terms, 1).astype(bf16))

    def ring_step(state, step):
        return [
            (terms, (lax.ppermute(moving, "fsdp", ring_steps).astype(f32)
                     + ring_part(terms, step + 1)).astype(bf16))
            for terms, moving in state
        ]

    def ring_rest(state, first):
        for step in range(first, n_fsdp):
            state = ring_step(state, step)
        return [moving for _, moving in state]

    def scatter_units(moved):
        whole = jnp.stack(moved, axis=1)
        blocks = [at(whole, place)]
        blocks += [swap(at(whole, place ^ bit), "ctx", bit) for bit in range(1, n_ctx)]
        return jnp.stack(blocks)

    def trade_square(own, received, bits):
        own, received = (part.reshape(n_ctx, -1, part.shape[1]) for part in (own, received))

        def part(bit):
            return at(own, place ^ bit).astype(f32) + at(received, place ^ bit).astype(f32)

        return [part(bit) if bit == 0 else swap(part(bit).astype(bf16), "ctx", bit) for bit in bits]

    def sum_square(parts):
        return sum(part.astype(f32) for part in parts).astype(bf16)

    def reduce_deep(mine):
        mine = mine.reshape(n_fsdp, shard_rows, -1)
        total = at(mine, depth).astype(f32)
        for bit in range(1, n_fsdp):
            total = total + swap(at(mine, depth ^ bit), "fsdp", bit).astype(f32)
        return total

    if pieces == 1:
        units_here = jnp.arange(per_core, dtype=jnp.uint32)
        units_here = jnp.concatenate(
            [core * per_core + units_here, (1 - core) * per_core + units_here]
        )
    else:
        units_here = jnp.zeros((1,), jnp.uint32)
    named = (place * own_experts + units_here).astype(f32)
    matches = info[:, None, :, :TOP] == named[None, :, None, None, None]
    hits = jnp.any(matches, axis=3)
    shares = jnp.sum(jnp.where(matches, info[:, None, :, TOP:], 0.0), axis=3)
    earlier = jnp.arange(rows)[:, None] < jnp.arange(rows)[None, :]
    rank = dot("ledr,rq->ledq", hits.astype(bf16), earlier.astype(bf16))
    slots = jnp.arange(capacity, dtype=f32)
    picks = hits[:, :, :, None, :] & (rank[:, :, :, None, :] == slots[:, None])
    slot_shares = jnp.sum(jnp.where(picks, shares[:, :, :, None, :], 0.0), axis=-1, keepdims=True)
    picks = picks.astype(bf16)

    order = place.astype(jnp.int32) ^ jnp.arange(n_ctx, dtype=jnp.int32)
    block_ids = jnp.take(block_of.reshape(n_ctx, 2), order, axis=0)
    block_ids = block_ids.reshape(-1)

    def gains_of(halves):
        pair = on_core(halves[1][:, -gap : 2 - gap], halves[0][:, -gap : 2 - gap])
        pair = pair.astype(f32).T
        return (pair[:1], pair[1:])

    def experts(layer, blocks, weights):
        returned, kept = ([], {})
        for j in range(own_experts):
            returned, kept[j] = expert_call(
                picks[layer, j],
                slot_shares[layer, j],
                blocks,
                weights[j],
                shard_rows,
                hidden,
                returned,
            )
        return (returned, kept)

    def experts_back(layer, blocks, weights, kept, beside):
        returned, grads, arrived = ([], {}, [])
        for j in reversed(range(own_experts)):
            returned, grads[j] = expert_back_call(
                picks[layer, j],
                slot_shares[layer, j],
                blocks,
                kept[j],
                weights[j],
                shard_rows,
                hidden,
                returned,
            )
            if beside:
                sent = beside.pop(0)()
                returned, grads[j], later = tie(returned, grads[j], sent)
                if isinstance(sent, dict):
                    sent.update(later)
                arrived.append(later)
        arrived += [send() for send in beside]
        own, other = cut_units([grads[j] for j in range(own_experts)])
        received = [swap(part, "section", 1) for part in other]
        return (returned, own, received, arrived)

    def keep_own(first, second):
        other = swap(on_core(second, first), "section", 1)
        return own_other(on_core(first, second), other)

    deep_first = gather_deep(dense_shards[0])
    dealt_first, dealt_second = (deal_units(stack) for stack in unit_stacks)
    deep_first, dealt_first, dealt_second, picks, shard_second = tie(
        deep_first, dealt_first, dealt_second, picks, dense_shards[1]
    )
    dense_blocks, moved, deep_first = tie(
        spread(deep_first[:, :enter_cut]), ring_send([[dealt_first]]), deep_first
    )
    leave_shard = deep_first[:, enter_cut:]
    leave_blocks = [leave_shard] + send(leave_shard, early)
    enter_own = join_square(dense_blocks)
    enter_first = (enter_own, swap(enter_own, "section", 1))

    first_gains = gains_of(enter_first)
    first_in = after(at(tokens, core)[0], slot_shares)
    _, first_normed, first_entered = enter_call(core, [first_in], first_gains[0], enter_first)
    first_entered, leave_blocks = tie(first_entered, leave_blocks)
    key_value = first_entered[:, qw : qw + 2 * kw]
    first_kv, moved, leave_shard = tie(
        jnp.concatenate(spread(key_value)), ring_send(moved), leave_shard
    )
    first_attended = attend_call(block_ids, first_entered, first_kv)
    for _ in range(2, n_fsdp - 1):
        moved = ring_send(moved)
    first_attended, leave_blocks, moved, shard_second, dealt_second = tie(
        first_attended, leave_blocks + send(leave_shard, late), moved, shard_second, dealt_second
    )
    leave_own = join_square(leave_blocks)
    leave_first = (leave_own, swap(leave_own, "section", 1))
    first_mid, ffn_normed = leave_call(core, first_in, first_attended, first_gains[1], leave_first)
    first_units = own_units(moved[0])
    ffn_normed, shard_second = tie(ffn_normed, shard_second)
    blocks, deep_second, dealt_second, first_units = tie(
        spread(ffn_normed), gather_deep(shard_second), dealt_second, first_units
    )
    enter_blocks = spread(deep_second[:, :enter_cut])
    first_weights = pair_units(first_units)
    returned, first_kept = experts(0, blocks, first_weights)
    returned, moved, enter_blocks, deep_second = tie(
        returned, ring_send([[dealt_second]]), enter_blocks, deep_second
    )
    enter_own = join_square(enter_blocks)
    enter_second = (enter_own, swap(enter_own, "section", 1))
    returned, moved, deep_second = tie(gather_back(returned), ring_send(moved), deep_second)
    leave_shard = deep_second[:, enter_cut:]
    leave_blocks = [leave_shard] + send(leave_shard, early)

    second_gains = gains_of(enter_second)
    second_in, second_normed, second_entered = enter_call(
        core, [first_mid] + returned, second_gains[0], enter_second
    )
    second_entered, leave_blocks = tie(second_entered, leave_blocks)
    key_value = second_entered[:, qw : qw + 2 * kw]
    for _ in range(3, n_fsdp):
        moved = ring_send(moved)
    second_kv, moved, leave_shard = tie(jnp.concatenate(spread(key_value)), moved, leave_shard)
    second_attended = attend_call(block_ids, second_entered, second_kv)
    second_attended, leave_blocks = tie(second_attended, leave_blocks + send(leave_shard, late))
    leave_own = join_square(leave_blocks)
    leave_second = (leave_own, swap(leave_own, "section", 1))
    second_mid, ffn_normed = leave_call(
        core, second_in, second_attended, second_gains[1], leave_second
    )
    second_weights = pair_units(own_units(moved[0]))
    blocks = spread(ffn_normed)
    cotangent = after(at(out_grad, core)[0], blocks)
    cot_blocks = spread(cotangent)
    returned, second_kept = experts(1, blocks, second_weights)
    cot_blocks, returned = tie(cot_blocks, returned)

    second_returned = returned
    beside = [
        lambda: [swap(second_returned[bit], "ctx", bit) for bit in early],
        lambda: [swap(second_returned[bit], "ctx", bit) for bit in late],
    ]
    returned, own, received, arrived = experts_back(
        1, cot_blocks, second_weights, second_kept, beside
    )
    returned, own, received, arrived = tie(returned, own, received, arrived)
    second_parts = [second_returned[0]] + [part for parts in arrived for part in parts]
    second_out = second_mid + sum(part.astype(f32) for part in second_parts)
    layer_outs = keep_own(second_in, second_out.astype(bf16))
    units_moving = [ring_start(*pair) for pair in zip(own, received)]
    after_rows, term, d_attended, *grads = leave_back_call(
        core,
        gather_back(returned),
        second_gains[1],
        second_mid,
        cotangent,
        second_attended,
        leave_second,
    )
    d_attended, units_moving = tie(d_attended, ring_step(units_moving, 1))
    leave_grads = (grads[0], swap(grads[1], "section", 1))
    d_queries, d_key_value = attend_back_call(block_ids, second_entered, second_kv, d_attended)
    units_moving = ring_step(units_moving, 2)
    d_key_value, leave_grads = tie(gather_back(d_key_value), leave_grads)
    leave_parts = trade_square(*leave_grads, early)
    second_entry, cotangent, *grads = enter_back_call(
        core,
        d_queries,
        d_key_value,
        second_gains[0],
        second_in,
        second_normed,
        after_rows,
        term,
        enter_second,
    )
    cotangent, grads, units_moving, leave_parts = tie(
        cotangent, grads, units_moving, leave_parts
    )
    units_moving = ring_rest(units_moving, 3)
    enter_grads = (grads[0], swap(grads[1], "section", 1))

    blocks, enter_grads, second_moved = tie(spread(cotangent), enter_grads, units_moving)
    leave_grads, layer_outs = after((leave_grads, layer_outs), blocks)
    arrived = {}

    def beside_other():
        arrived["leave"] = trade_square(*leave_grads, late)
        arrived["enter"] = trade_square(*enter_grads, early)
        return arrived

    def beside_own():
        parts = trade_square(*leave_grads, [0]) + leave_parts + arrived["leave"]
        return (trade_square(*enter_grads, late), reduce_deep(sum_square(parts)))

    beside = [beside_other, beside_own]
    returned, own, received, (arrived, last) = experts_back(
        0, blocks, first_weights, first_kept, beside
    )
    returned, own, received = tie(returned, own, received)
    units_moving = [ring_start(*pair) for pair in zip(own, received)]
    after_rows, term, d_attended, *grads = leave_back_call(
        core,
        gather_back(returned),
        first_gains[1],
        first_mid,
        cotangent,
        first_attended,
        leave_first,
    )
    d_attended, units_moving, second_moved = tie(
        d_attended, ring_step(units_moving, 1), second_moved
    )
    second_scattered = scatter_units(second_moved)
    second_leave = last[1]
    second_moving = sum_square(trade_square(*enter_grads, [0]) + arrived["enter"] + last[0])
    leave_grads = (grads[0], swap(grads[1], "section", 1))
    d_queries, d_key_value = attend_back_call(block_ids, first_entered, first_kv, d_attended)
    units_moving = ring_step(units_moving, 2)
    d_key_value, leave_grads, second_scattered, layer_outs = tie(
        gather_back(d_key_value), leave_grads, second_scattered, layer_outs
    )
    leave_parts = trade_square(*leave_grads, early)
    first_entry, _, *grads = enter_back_call(
        core,
        d_queries,
        d_key_value,
        first_gains[0],
        first_in,
        first_normed,
        after_rows,
        term,
        enter_first,
    )
    grads, units_moving, leave_parts, leave_grads = tie(
        grads, units_moving, leave_parts, leave_grads
    )
    units_moving = ring_rest(units_moving, 3)
    leave_parts = trade_square(*leave_grads, [0]) + leave_parts
    enter_grads, leave_parts, second_moving = tie(
        (grads[0], swap(grads[1], "section", 1)),
        leave_parts + trade_square(*leave_grads, late),
        second_moving,
    )
    enter_parts, units_moving, second_moving = tie(
        trade_square(*enter_grads, range(n_ctx)), units_moving, second_moving
    )
    first_moving = [sum_square(parts) for parts in (enter_parts, leave_parts)]
    first_moving = jnp.concatenate(first_moving, axis=1)
    dense = reduce_deep(jnp.concatenate([first_moving, second_moving], axis=1))
    first_dense = dense[:, : enter_cut + leave_cut]
    second_dense = dense[:, enter_cut + leave_cut :]
    second_dense = jnp.concatenate([second_dense, second_leave], axis=1)
    first_scattered = scatter_units(units_moving)

    layer_out = jnp.stack(layer_outs)
    input_grads = jnp.stack(keep_own(first_entry, second_entry))
    low_dense, high_dense = keep_own(first_dense, second_dense)
    enter_grad = jnp.concatenate([low_dense[:, :enter_cut], high_dense[:, :enter_cut]], axis=1)
    grad_out = jnp.concatenate([low_dense[:, enter_cut:], high_dense[:, enter_cut:]], axis=1)
    grad_gains = enter_grad[:, qw + 2 * kw :]
    mine = on_core(first_scattered, second_scattered)
    other = swap(on_core(second_scattered, first_scattered), "section", 1)
    if aligned and pieces == 1:
        grad_gate, grad_up, grad_down = finish_call(mine, other, shard_rows, hidden, place, core)
    else:
        sides = [jnp.take(part, order, axis=0) for part in own_other(mine, other)]
        if pieces == 1:
            whole = jnp.stack(sides, axis=1).reshape(EXPERTS, unit_rows, width)
        else:
            whole = jnp.concatenate([side[:, 0] for side in sides], axis=2)
        pairs = whole[:, :shard_rows].astype(f32).reshape(EXPERTS, shard_rows, 2, 2, cut)
        grad_gate = pairs[:, :, :, 0].reshape(EXPERTS, shard_rows, hidden)
        grad_up = pairs[:, :, :, 1].reshape(EXPERTS, shard_rows, hidden)
        grad_down = whole[:, shard_rows:].astype(f32)
    return (
        layer_out[None, :, None],
        input_grads[None, :, None],
        grad_gains[:, 0][None],
        enter_grad[:, :qw][None],
        enter_grad[:, qw : qw + kw][None],
        enter_grad[:, qw + kw : qw + 2 * kw][None],
        grad_out[None],
        grad_gains[:, 1][None],
        grad_gate[None],
        grad_up[None],
        grad_down[None],
    )


def solution(mesh):
    rows_placed = P(None, "fsdp", "ctx", None)
    kept_placed = P("section", None, "fsdp", "ctx", None)
    gain_placed = P("section", ("ctx", "fsdp"))
    dense_placed = P("section", ("ctx", "fsdp"), None)
    expert_placed = P("section", None, ("ctx", "fsdp"), None)
    dense_all = (dense_placed,) * 4
    expert_all = (expert_placed,) * 3
    layer_placed = (gain_placed,) + dense_all + (gain_placed,) + expert_all
    return jax.shard_map(
        body,
        mesh=mesh,
        in_specs=(rows_placed, P(), kept_placed, kept_placed) + layer_placed + (rows_placed,),
        out_specs=(kept_placed, kept_placed) + layer_placed,
        check_vma=False,
    )
```

```python
import functools

import jax
import jax.numpy as jnp
from jax import lax
from jax.experimental import pallas as pl
from jax.experimental.pallas import tpu as pltpu
from jax.sharding import PartitionSpec as P

QH = 12
KVH = 2
HD = 128
GROUP = QH // KVH
TOP = 4
EXPERTS = 8
bf16 = jnp.bfloat16
f32 = jnp.float32


epsilon = 1e-06
masked_out = -1e30
gap = 256


def swap(value, axis, bit):
    count = lax.axis_size(axis)
    return lax.ppermute(value, axis, [(source, source ^ bit) for source in range(count)])


def tie(*values):
    return lax.optimization_barrier(values)


def after(value, earlier):
    return tie(value, earlier)[0]


def at(value, index, axis=0):
    return lax.dynamic_index_in_dim(value, index, axis, keepdims=False)


def dot(spec, left, right, kind=f32):
    return jnp.einsum(spec, left, right, preferred_element_type=kind)


def cost(micros):
    return pl.CostEstimate(
        flops=int(micros * 1e9), bytes_accessed=int(micros * 3e6), transcendentals=0
    )


def kernel_params():
    return pltpu.CompilerParams(vmem_limit_bytes=56 * 1024 * 1024)


def nt(left, right):
    return lax.dot_general(left, right, (((1,), (1,)), ((), ())), preferred_element_type=f32)


def nn(left, right):
    return jnp.dot(left, right, preferred_element_type=f32)


def head_rows(ref):
    return jnp.concatenate([ref[:, i * HD : (i + 1) * HD] for i in range(GROUP)], axis=0)


def softmax_rows(ids_ref, queries, keys, half, own):
    scores = nt(queries, keys) * HD ** (-0.5)
    tall, wide = scores.shape
    row = lax.broadcasted_iota(jnp.int32, (half, 1), 0)
    row = jnp.concatenate([row] * (tall // half), axis=0) + ids_ref[own] * half
    lane = lax.broadcasted_iota(jnp.int32, (1, half), 1)
    column = [lane + ids_ref[block] * half for block in range(wide // half)]
    column = jnp.concatenate(column, axis=1)
    scores = jnp.where(row >= column, scores, masked_out)
    shifted = jnp.exp(scores - jnp.max(scores, axis=1, keepdims=True))
    return shifted / jnp.sum(shifted, axis=1, keepdims=True)


def attend_kernel(ids_ref, query_ref, key_ref, value_ref, out_ref):
    half = query_ref.shape[0]
    probs = softmax_rows(ids_ref, head_rows(query_ref), key_ref[...], half, pl.program_id(1))
    out = nn(probs.astype(bf16), value_ref[...]).astype(bf16)
    for i in range(GROUP):
        out_ref[:, i * HD : (i + 1) * HD] = out[i * half : (i + 1) * half]


def attend_specs(rows, seq_len):
    half = rows // 2
    by_head = pl.BlockSpec((half, GROUP * HD), lambda g, h, ids: (h, g))
    keys = pl.BlockSpec((seq_len, HD), lambda g, h, ids: (0, g))
    values = pl.BlockSpec((seq_len, HD), lambda g, h, ids: (0, KVH + g))
    return by_head, keys, values


def attend_call(ids, queries, key_value):
    rows, seq_len = (queries.shape[0], key_value.shape[0])
    by_head, keys, values = attend_specs(rows, seq_len)
    return pl.pallas_call(
        attend_kernel,
        grid_spec=pltpu.PrefetchScalarGridSpec(
            num_scalar_prefetch=1,
            grid=(KVH, 2),
            in_specs=[by_head, keys, values],
            out_specs=by_head,
        ),
        out_shape=jax.ShapeDtypeStruct((rows, QH * HD), bf16),
        compiler_params=kernel_params(),
        cost_estimate=cost(1),
        name="attend",
    )(ids, queries, key_value, key_value)


def attend_back_kernel(ids_ref, query_ref, key_ref, value_ref, cot_ref, dq_ref, *refs):
    out, (dk_ref, dv_ref) = (refs[:-2], refs[-2:])
    half = query_ref.shape[0]
    group, own = (pl.program_id(0), pl.program_id(1))
    queries, cot = (head_rows(query_ref), head_rows(cot_ref))
    probs = softmax_rows(ids_ref, queries, key_ref[...], half, own)
    d_probs = nt(cot, value_ref[...])
    inner = jnp.sum(probs * d_probs, axis=1, keepdims=True)
    d_scores = (probs * (d_probs - inner)).astype(bf16)
    d_queries = (nn(d_scores, key_ref[...]) * HD ** (-0.5)).astype(bf16)
    for i in range(GROUP):
        dq_ref[:, i * HD : (i + 1) * HD] = d_queries[i * half : (i + 1) * half]
    d_keys = nn(d_scores.T, queries) * HD ** (-0.5)
    d_values = nn(probs.astype(bf16).T, cot)

    @pl.when(own == 0)
    def _():
        dk_ref[...] = d_keys
        dv_ref[...] = d_values

    @pl.when(own != 0)
    def _():
        rows = 2 * half
        for block, ref in enumerate(out):
            part = slice(block * rows, (block + 1) * rows)
            for first, total, last in ((0, dk_ref, d_keys), (KVH * HD, dv_ref, d_values)):
                columns = pl.ds(pl.multiple_of(first + group * HD, HD), HD)
                ref[:, columns] = (total[part, :] + last[part]).astype(bf16)


def attend_back_call(ids, queries, key_value, cot):
    rows, seq_len = (queries.shape[0], key_value.shape[0])
    by_head, keys, values = attend_specs(rows, seq_len)
    blocks = seq_len // rows
    wide = 2 * KVH * HD
    result = pl.pallas_call(
        attend_back_kernel,
        grid_spec=pltpu.PrefetchScalarGridSpec(
            num_scalar_prefetch=1,
            grid=(KVH, 2),
            in_specs=[by_head, keys, values, by_head],
            out_specs=[by_head] + [pl.BlockSpec((rows, wide), lambda g, h, ids: (0, 0))] * blocks,
            scratch_shapes=[pltpu.VMEM((seq_len, HD), f32)] * 2,
        ),
        out_shape=[jax.ShapeDtypeStruct((rows, QH * HD), bf16)]
        + [jax.ShapeDtypeStruct((rows, wide), bf16)] * blocks,
        compiler_params=kernel_params(),
        cost_estimate=cost(1),
        name="attend_back",
    )(ids, queries, key_value, key_value, cot)
    return (result[0], result[1:])


def gelu_parts(gate):
    root = 0.7978845608028654
    inner = root * (gate + 0.044715 * gate * gate * gate)
    bent = jnp.tanh(inner)
    value = 0.5 * gate * (1.0 + bent)
    slope = root * (1.0 + 3.0 * 0.044715 * gate * gate)
    return value, 0.5 * (1.0 + bent) + 0.5 * gate * (1.0 - bent * bent) * slope


def give_back(pick_ref, total_ref, share_ref, before, out):
    blocks, capacity, _ = pick_ref.shape
    for d in range(blocks):
        part = total_ref[d * capacity : (d + 1) * capacity, :]
        if share_ref is not None:
            part = part * share_ref[d]
        back = nn(pick_ref[d].T, part.astype(bf16))
        if before:
            back = back + before[d][...]
        out[d][...] = back.astype(out[d].dtype)


def flat(ref):
    value = ref[...]
    return value.reshape(-1, value.shape[-1])


def add_up(total_ref, part, step):
    @pl.when(step == 0)
    def _():
        total_ref[...] = part

    @pl.when(step != 0)
    def _():
        total_ref[...] += part


def expert_kernel(blocks, adds, pick_ref, share_ref, gate_ref, up_ref, down_ref, *refs):
    rows, refs = (refs[:blocks], refs[blocks:])
    before, refs = (refs[: blocks * adds], refs[blocks * adds :])
    out, (picked_ref, gate_pre_ref, up_pre_ref, total_ref) = (refs[:blocks], refs[blocks:])
    step = pl.program_id(0)
    capacity = pick_ref.shape[1]

    @pl.when(step == 0)
    def _():
        for d in range(blocks):
            block = nn(pick_ref[d], rows[d][...]).astype(bf16)
            picked_ref[d * capacity : (d + 1) * capacity, :] = block

    gate_pre = nn(picked_ref[...], flat(gate_ref))
    up_pre = nn(picked_ref[...], flat(up_ref))
    gate_pre_ref[...] = gate_pre
    up_pre_ref[...] = up_pre
    active = (gelu_parts(gate_pre)[0] * up_pre).astype(bf16)
    add_up(total_ref, nn(active, flat(down_ref)), step)

    @pl.when(step == pl.num_programs(0) - 1)
    def _():
        give_back(pick_ref, total_ref, share_ref, before, out)


def whole_spec(shape):
    return pl.BlockSpec(
        shape, lambda step: (0,) * len(shape), pipeline_mode=pl.Buffered(buffer_count=1)
    )


def weight_operands(weights, deep, cut):
    if len(weights) == 1:
        unit = weights[0]
        shards, tall, width = unit.shape
        specs = [
            pl.BlockSpec((shards, deep, cut), lambda step: (0, 0, 2 * step)),
            pl.BlockSpec((shards, deep, cut), lambda step: (0, 0, 2 * step + 1)),
            pl.BlockSpec(
                (shards // 2, tall - deep, width), lambda step: (step, deep // (tall - deep), 0)
            ),
        ]
        return specs, [unit, unit, unit]
    pair, down = weights
    specs = [
        pl.BlockSpec((pair.shape[0], cut), lambda step: (0, 2 * step)),
        pl.BlockSpec((pair.shape[0], cut), lambda step: (0, 2 * step + 1)),
        pl.BlockSpec((cut, down.shape[1]), lambda step: (step, 0)),
    ]
    return specs, [pair, pair, down]


def expert_call(picks, shares, rows, weights, deep, hidden, before, micros):
    blocks, capacity, _ = picks.shape
    width, cut, tall = (rows[0].shape[1], hidden // 2, blocks * capacity)
    columns = pl.BlockSpec((tall, cut), lambda step: (0, step))
    row_specs = [whole_spec(block.shape) for block in rows]
    specs, operands = weight_operands(weights, deep, cut)
    result = pl.pallas_call(
        functools.partial(expert_kernel, blocks, 1 if before else 0),
        grid=(2,),
        in_specs=[whole_spec(picks.shape), whole_spec(shares.shape)]
        + specs
        + row_specs * (2 if before else 1),
        out_specs=row_specs + [whole_spec((tall, width)), columns, columns],
        out_shape=[jax.ShapeDtypeStruct(block.shape, bf16) for block in rows]
        + [
            jax.ShapeDtypeStruct((tall, width), bf16),
            jax.ShapeDtypeStruct((tall, hidden), f32),
            jax.ShapeDtypeStruct((tall, hidden), f32),
        ],
        scratch_shapes=[pltpu.VMEM((tall, width), f32)],
        compiler_params=kernel_params(),
        cost_estimate=cost(micros),
        name="expert",
    )(picks, shares, *operands, *rows, *before)
    return (list(result[:blocks]), list(result[blocks:]))


def expert_back_kernel(
    blocks, adds, sums, deep, pick_ref, share_ref, picked_ref, gate_pre_ref, up_pre_ref,
    gate_ref, up_ref, down_ref, *refs
):
    rows, refs = (refs[:blocks], refs[blocks:])
    before, refs = (refs[: blocks * adds], refs[blocks * adds :])
    sum_refs, refs = (refs[:sums], refs[sums:])
    out, refs = (refs[:blocks], refs[blocks:])
    grad_refs, (slots_ref, turned_ref, total_ref) = (refs[:-3], refs[-3:])
    step = pl.program_id(0)
    capacity, cut = (pick_ref.shape[1], gate_pre_ref.shape[1])

    @pl.when(step == 0)
    def _():
        for d in range(blocks):
            block = nn(pick_ref[d], rows[d][...]) * share_ref[d]
            slots_ref[d * capacity : (d + 1) * capacity, :] = block.astype(bf16)
        turned_ref[...] = picked_ref[...].T

    d_active = nt(slots_ref[...], flat(down_ref))
    value, slope = gelu_parts(gate_pre_ref[...])
    up_pre = up_pre_ref[...]
    active = (value * up_pre).astype(bf16)
    d_gate = (d_active * up_pre * slope).astype(bf16)
    d_up = (d_active * value).astype(bf16)
    grad_down = nn(active.T, slots_ref[...])
    grad_gate = nn(turned_ref[...], d_gate)
    grad_up = nn(turned_ref[...], d_up)
    if len(grad_refs) == 1:
        unit_ref = grad_refs[0]
        shards, tall, width = unit_ref.shape

        def write(place, value):
            if sums:
                value = value + sum_refs[0][place].astype(f32)
            unit_ref[place] = value.astype(bf16)

        for side in range(2):

            @pl.when(step == side)
            def _():
                left, some = (2 * side * cut, shards // 2)
                top, every = (slice(0, deep), slice(0, shards))
                write((every, top, slice(left, left + cut)), grad_gate.reshape(shards, deep, cut))
                left = left + cut
                write((every, top, slice(left, left + cut)), grad_up.reshape(shards, deep, cut))
                place = (slice(side * some, (side + 1) * some), slice(deep, tall), slice(0, width))
                write(place, grad_down.reshape(some, tall - deep, width))
    else:
        pair = jnp.concatenate([grad_gate, grad_up], axis=1)
        for ref, total, value in zip(grad_refs, sum_refs or (None, None), (pair, grad_down)):
            if total is not None:
                value = value + total[...].astype(f32)
            ref[...] = value.astype(bf16)
    part = nt(d_gate, flat(gate_ref)) + nt(d_up, flat(up_ref))
    add_up(total_ref, part, step)

    @pl.when(step == pl.num_programs(0) - 1)
    def _():
        give_back(pick_ref, total_ref, None, before, out)


def expert_back_call(picks, shares, rows, kept, weights, deep, hidden, before, grads, micros):
    blocks, capacity, _ = picks.shape
    width, cut, tall = (rows[0].shape[1], hidden // 2, blocks * capacity)
    columns = pl.BlockSpec((tall, cut), lambda step: (0, step))
    row_specs = [whole_spec(block.shape) for block in rows]
    specs, operands = weight_operands(weights, deep, cut)
    grad_shapes = [jax.ShapeDtypeStruct(part.shape, bf16) for part in weights]
    if len(weights) == 1:
        grad_specs = [whole_spec(weights[0].shape)]
    else:
        grad_specs = [
            pl.BlockSpec((width, 2 * cut), lambda step: (0, step)),
            pl.BlockSpec((cut, width), lambda step: (step, 0)),
        ]
    result = pl.pallas_call(
        functools.partial(expert_back_kernel, blocks, 1 if before else 0, len(grads), deep),
        grid=(2,),
        in_specs=[
            whole_spec(picks.shape),
            whole_spec(shares.shape),
            whole_spec((tall, width)),
            columns,
            columns,
        ]
        + specs
        + row_specs * (2 if before else 1)
        + grad_specs[: len(grads)],
        out_specs=row_specs + grad_specs,
        out_shape=[jax.ShapeDtypeStruct(block.shape, bf16) for block in rows] + grad_shapes,
        scratch_shapes=[
            pltpu.VMEM((tall, width), bf16),
            pltpu.VMEM((width, tall), bf16),
            pltpu.VMEM((tall, width), f32),
        ],
        compiler_params=kernel_params(),
        cost_estimate=cost(micros),
        name="expert_back",
    )(picks, shares, *kept, *operands, *rows, *before, *grads)
    return (list(result[:blocks]), list(result[blocks:]))


def norm_parts(value):
    scale = lax.rsqrt(jnp.mean(value * value, axis=1, keepdims=True) + epsilon)
    return scale, value * scale


def norm_back(grad, gain, value):
    scale, scaled = norm_parts(value)
    grown = grad * gain
    back = scale * (grown - scaled * jnp.mean(scaled * grown, axis=1, keepdims=True))
    return back, (grad * scaled).astype(bf16)


def add_all(refs):
    total = refs[0][...].astype(f32)
    for ref in refs[1:]:
        total = total + ref[...].astype(f32)
    return total


def side_offsets(core_ref, steps, cut):
    step, core = (pl.program_id(0), core_ref[0])
    own = pl.multiple_of((core * steps + step) * cut, cut)
    other = pl.multiple_of(((1 - core) * steps + step) * cut, cut)
    return own, other


def dense_call(kernel, core, steps, whole, halves, out, scratch, name, micros):
    cut = halves[0].shape[1] // steps

    def keep(shape):
        return pl.BlockSpec(
            shape, lambda step, core: (0,) * len(shape), pipeline_mode=pl.Buffered(buffer_count=1)
        )

    def tile(tall):
        return pl.BlockSpec((tall, cut), lambda step, core: (0, step))

    return pl.pallas_call(
        kernel,
        grid_spec=pltpu.PrefetchScalarGridSpec(
            num_scalar_prefetch=1,
            grid=(steps,),
            in_specs=[keep(part.shape) for part in whole] + [tile(halves[0].shape[0])] * 2,
            out_specs=[
                tile(part.shape[0]) if tiled else keep(part.shape) for part, tiled in out
            ],
            scratch_shapes=scratch,
        ),
        out_shape=[part for part, _ in out],
        compiler_params=kernel_params(),
        cost_estimate=cost(micros),
        name=name,
    )(core.astype(jnp.int32).reshape(1), *whole, *halves)


def shape_of(kind, *shape):
    return jax.ShapeDtypeStruct(shape, kind)


def enter_kernel(steps, terms, core_ref, gain_ref, *refs):
    parts, (own_ref, other_ref, sent_ref, normed_ref, out_ref) = (refs[:terms], refs[terms:])
    own, other = side_offsets(core_ref, steps, own_ref.shape[1])

    @pl.when(pl.program_id(0) == 0)
    def _():
        sent = add_all(parts).astype(bf16)
        sent_ref[...] = sent
        normed_ref[...] = (norm_parts(sent.astype(f32))[1] * gain_ref[...]).astype(bf16)

    cut = own_ref.shape[1]
    out_ref[:, pl.ds(own, cut)] = nn(normed_ref[...], own_ref[...]).astype(bf16)
    out_ref[:, pl.ds(other, cut)] = nn(normed_ref[...], other_ref[...]).astype(bf16)


def enter_call(core, parts, gain, halves):
    rows, width = parts[0].shape
    return dense_call(
        functools.partial(enter_kernel, 3, len(parts)),
        core,
        3,
        [gain] + parts,
        halves,
        [
            (shape_of(bf16, rows, width), False),
            (shape_of(bf16, rows, width), False),
            (shape_of(bf16, rows, 2 * halves[0].shape[1]), False),
        ],
        [],
        "enter",
        6,
    )


def leave_kernel(steps, core_ref, gain_ref, rows_ref, attended_ref, own_ref, other_ref,
                 mid_ref, normed_ref):
    cut = own_ref.shape[1]
    for start, ref in zip(side_offsets(core_ref, steps, cut), (own_ref, other_ref)):
        part = pl.ds(start, cut)
        mid_ref[:, part] = rows_ref[:, part].astype(f32) + nn(attended_ref[...], ref[...])

    @pl.when(pl.program_id(0) == steps - 1)
    def _():
        normed_ref[...] = (norm_parts(mid_ref[...])[1] * gain_ref[...]).astype(bf16)


def leave_call(core, rows_in, attended, gain, halves):
    rows, width = rows_in.shape
    return dense_call(
        functools.partial(leave_kernel, 2),
        core,
        2,
        [gain, rows_in, attended],
        halves,
        [(shape_of(f32, rows, width), False), (shape_of(bf16, rows, width), False)],
        [],
        "leave",
        5,
    )


def leave_back_kernel(steps, terms, core_ref, gain_ref, mid_ref, cot_ref, attended_ref, *refs):
    parts, refs = (refs[:terms], refs[terms:])
    own_ref, other_ref, after_ref, term_ref, d_attended_ref, *refs = refs
    own_grad_ref, other_grad_ref, branch_ref, turned_ref, total_ref = refs
    step, cut = (pl.program_id(0), own_ref.shape[1])

    @pl.when(step == 0)
    def _():
        back, term_ref[...] = norm_back(add_all(parts), gain_ref[...], mid_ref[...])
        back = back + cot_ref[...].astype(f32)
        after_ref[...] = back
        branch_ref[...] = back.astype(bf16)
        turned_ref[...] = attended_ref[...].T

    own, other = side_offsets(core_ref, steps, cut)
    d_own, d_other = (branch_ref[:, pl.ds(own, cut)], branch_ref[:, pl.ds(other, cut)])
    own_grad_ref[...] = nn(turned_ref[...], d_own).astype(bf16)
    other_grad_ref[...] = nn(turned_ref[...], d_other).astype(bf16)
    add_up(total_ref, nt(d_own, own_ref[...]) + nt(d_other, other_ref[...]), step)

    @pl.when(step == steps - 1)
    def _():
        d_attended_ref[...] = total_ref[...].astype(bf16)


def leave_back_call(core, parts, gain, mid, cotangent, attended, halves):
    rows, width = mid.shape
    half = (halves[0].shape[0], halves[0].shape[1])
    return dense_call(
        functools.partial(leave_back_kernel, 2, len(parts)),
        core,
        2,
        [gain, mid, cotangent, attended] + parts,
        halves,
        [
            (shape_of(f32, rows, width), False),
            (shape_of(bf16, rows, width), False),
            (shape_of(bf16, rows, width), False),
            (shape_of(bf16, *half), True),
            (shape_of(bf16, *half), True),
        ],
        [
            pltpu.VMEM((rows, width), bf16),
            pltpu.VMEM((width, rows), bf16),
            pltpu.VMEM((rows, width), f32),
        ],
        "leave_back",
        8,
    )


def enter_back_kernel(steps, terms, core_ref, gain_ref, rows_ref, normed_ref, after_ref, term_ref,
                      dq_ref, *refs):
    parts, refs = (refs[:terms], refs[terms:])
    own_ref, other_ref, entry_ref, sent_ref, own_grad_ref, other_grad_ref, *refs = refs
    entered_ref, turned_ref, total_ref = refs
    step, cut = (pl.program_id(0), own_ref.shape[1])
    rows, qw = dq_ref.shape

    @pl.when(step == 0)
    def _():
        entered_ref[:, :qw] = dq_ref[...]
        wide = parts[0].shape[1]
        entered_ref[:, qw : qw + wide] = add_all(parts).astype(bf16)
        entered_ref[:, qw + wide :] = jnp.zeros((rows, gap), bf16)
        turned_ref[...] = normed_ref[...].T

    own, other = side_offsets(core_ref, steps, cut)
    d_own, d_other = (entered_ref[:, pl.ds(own, cut)], entered_ref[:, pl.ds(other, cut)])
    own_grad_ref[...] = nn(turned_ref[...], d_own).astype(bf16)
    other_grad_ref[...] = nn(turned_ref[...], d_other).astype(bf16)
    add_up(total_ref, nt(d_own, own_ref[...]) + nt(d_other, other_ref[...]), step)

    @pl.when(step == steps - 1)
    def _():
        back, attn_term = norm_back(total_ref[...], gain_ref[...], rows_ref[...].astype(f32))
        back = back + after_ref[...]
        entry_ref[...] = back
        sent_ref[...] = back.astype(bf16)
        lane = lax.broadcasted_iota(jnp.int32, (rows, 128), 1)
        sums = nn(attn_term.T, (lane == 0).astype(bf16))
        sums = (sums + nn(term_ref[...].T, (lane == 1).astype(bf16))).astype(bf16)
        left = cut - gap

        @pl.when(core_ref[0] == 0)
        def _():
            other_grad_ref[:, left : left + 128] = sums

        @pl.when(core_ref[0] != 0)
        def _():
            own_grad_ref[:, left : left + 128] = sums


def enter_back_call(core, dq, parts, gain, rows_in, normed, after, term, halves):
    rows, width = rows_in.shape
    return dense_call(
        functools.partial(enter_back_kernel, 3, len(parts)),
        core,
        3,
        [gain, rows_in, normed, after, term, dq] + parts,
        halves,
        [
            (shape_of(f32, rows, width), False),
            (shape_of(bf16, rows, width), False),
            (shape_of(bf16, *halves[0].shape), True),
            (shape_of(bf16, *halves[0].shape), True),
        ],
        [
            pltpu.VMEM((rows, 2 * halves[0].shape[1]), bf16),
            pltpu.VMEM((width, rows), bf16),
            pltpu.VMEM((rows, width), f32),
        ],
        "enter_back",
        1,
    )


def place_kernel(count, joined, index_ref, *refs):
    step = pl.program_id(0)
    for bit in range(count):

        @pl.when(step == bit)
        def _():
            if joined:
                refs[count][...] = refs[bit][...]
            else:
                refs[count][0] = refs[bit][...]


def place_call(blocks, index):
    count = len(blocks)
    shape = blocks[0].shape
    zeros = (0,) * len(shape)
    joined = len(shape) == 2 and shape[0] % 16 == 0
    if joined:
        out_spec = pl.BlockSpec(shape, lambda step, at: (at[0] ^ step, 0))
        out_shape = (count * shape[0], shape[1])
    else:
        out_spec = pl.BlockSpec((1,) + shape, lambda step, at: (at[0] ^ step,) + zeros)
        out_shape = (count,) + shape
    return pl.pallas_call(
        functools.partial(place_kernel, count, joined),
        grid_spec=pltpu.PrefetchScalarGridSpec(
            num_scalar_prefetch=1,
            grid=(count,),
            in_specs=[pl.BlockSpec(shape, lambda step, at: zeros)] * count,
            out_specs=out_spec,
        ),
        out_shape=jax.ShapeDtypeStruct(out_shape, blocks[0].dtype),
        compiler_params=kernel_params(),
        cost_estimate=cost(2),
        name="place",
    )(index.astype(jnp.int32).reshape(1), *blocks)


def order_kernel(count, order_ref, *refs):
    step = pl.program_id(0)
    for i in range(count):

        @pl.when(step == i)
        def _():
            refs[count][:, 0] = refs[i][:, 0]


def order_call(blocks, order, unit):
    count = len(blocks)
    n_ctx, _, tall, wide = blocks[0].shape
    shape = (n_ctx, 1, tall, wide)
    source = pl.BlockSpec(
        shape, lambda step, at: (0, unit, 0, 0), pipeline_mode=pl.Buffered(buffer_count=1)
    )
    result = pl.pallas_call(
        functools.partial(order_kernel, count),
        grid_spec=pltpu.PrefetchScalarGridSpec(
            num_scalar_prefetch=1,
            grid=(count,),
            in_specs=[source] * count,
            out_specs=pl.BlockSpec(shape, lambda step, at: (0, at[step], 0, 0)),
        ),
        out_shape=jax.ShapeDtypeStruct((n_ctx, count, tall, wide), bf16),
        compiler_params=kernel_params(),
        cost_estimate=cost(4),
        name="order",
    )(order.astype(jnp.int32), *blocks)
    return result.reshape(n_ctx * count, tall, wide)


def finish_kernel(deep, index_ref, own_ref, other_ref, gate_ref, up_ref, down_ref):
    side = pl.program_id(1)
    wide = gate_ref.shape[2] // 2

    def write(source):
        for half in range(2):
            left, target = (2 * half * wide, slice(half * wide, (half + 1) * wide))
            gate_ref[:, :, target] = source[0, :, :deep, left : left + wide].astype(f32)
            left = left + wide
            up_ref[:, :, target] = source[0, :, :deep, left : left + wide].astype(f32)
        down_ref[...] = source[0, :, deep:, :].astype(f32)

    @pl.when(side == index_ref[1])
    def _():
        write(own_ref)

    @pl.when(side != index_ref[1])
    def _():
        write(other_ref)


def finish_call(own, other, deep, hidden, place, core):
    n_ctx, units, tall, width = own.shape
    experts = 2 * n_ctx * units
    source = pl.BlockSpec((1, units, tall, width), lambda bit, side, at: (bit, 0, 0, 0))
    target = lambda bit, side, at: (2 * (at[0] ^ bit) + side, 0, 0)
    return pl.pallas_call(
        functools.partial(finish_kernel, deep),
        grid_spec=pltpu.PrefetchScalarGridSpec(
            num_scalar_prefetch=1,
            grid=(n_ctx, 2),
            in_specs=[source, source],
            out_specs=[
                pl.BlockSpec((units, deep, hidden), target),
                pl.BlockSpec((units, deep, hidden), target),
                pl.BlockSpec((units, tall - deep, width), target),
            ],
        ),
        out_shape=[
            jax.ShapeDtypeStruct((experts, deep, hidden), f32),
            jax.ShapeDtypeStruct((experts, deep, hidden), f32),
            jax.ShapeDtypeStruct((experts, tall - deep, width), f32),
        ],
        compiler_params=kernel_params(),
        cost_estimate=cost(8),
        name="finish",
    )(jnp.stack([place, core]).astype(jnp.int32), own, other)


def body(
    tokens,
    block_of,
    routes,
    combine,
    attn_norm,
    w_query,
    w_key,
    w_value,
    w_out,
    ffn_norm,
    w_gate,
    w_up,
    w_down,
    out_grad,
):
    rows = tokens.shape[2]
    width = tokens.shape[3]
    half = rows // 2
    n_ctx = lax.axis_size("ctx")
    n_fsdp = lax.axis_size("fsdp")
    core, place, depth = (
        lax.axis_index(axis).astype(jnp.uint32) for axis in ("section", "ctx", "fsdp")
    )
    seq_len = rows * n_ctx
    capacity = rows * TOP * 5 // (4 * EXPERTS)
    score_scale = HD ** (-0.5)
    own_experts = EXPERTS // n_ctx
    hidden = w_gate.shape[3]
    shard_rows = w_query.shape[1]
    down_rows = w_down.shape[2]
    qw = w_query.shape[2]
    kw = w_key.shape[2]
    pieces = max(1, 2 * n_ctx // EXPERTS)
    per_core = max(1, EXPERTS // (2 * n_ctx))
    unit_rows = shard_rows + down_rows
    aligned = shard_rows % 16 == 0 and down_rows % 16 == 0

    def on_core(former, latter):
        return jnp.where(core == 0, former, latter)

    def own_other(low, high):
        return (on_core(low, high), on_core(high, low))

    early, late = (range(1, n_ctx // 2 + 1), range(n_ctx // 2 + 1, n_ctx))

    def send(value, bits):
        return [swap(value, "ctx", bit) for bit in bits]

    def spread(value):
        return [value] + send(value, early) + send(value, late)

    def gather_back(blocks):
        return [blocks[0]] + [swap(blocks[bit], "ctx", bit) for bit in range(1, n_ctx)]

    info = jnp.concatenate([routes.astype(f32), combine], axis=-1)[0, :, 0].transpose(0, 2, 1)
    info_own, info_other = (at(info, core), swap(at(info, 1 - core), "section", 1))
    info = jnp.stack(own_other(info_own, info_other))
    info = jnp.stack([info] + [swap(info, "ctx", bit) for bit in range(1, n_ctx)], axis=1)

    gain_columns = jnp.stack([attn_norm[0], ffn_norm[0]], axis=1)
    gain_columns = jnp.pad(gain_columns, ((0, 0), (0, gap - 2)))
    enter_shard = jnp.concatenate([w_query[0], w_key[0], w_value[0], gain_columns], axis=1)
    enter_cut = enter_shard.shape[1] // 2
    leave_cut = w_out.shape[2] // 2
    low_shard = jnp.concatenate([enter_shard[:, :enter_cut], w_out[0, :, :leave_cut]], axis=1)
    high_shard = jnp.concatenate([enter_shard[:, enter_cut:], w_out[0, :, leave_cut:]], axis=1)
    lent = swap(on_core(high_shard, low_shard), "section", 1)
    dense_shards = (on_core(low_shard, lent), on_core(lent, high_shard))

    def gather_deep(shard):
        blocks = [shard] + [swap(shard, "fsdp", bit) for bit in range(1, n_fsdp)]
        return place_call(blocks, depth).reshape(-1, shard.shape[1])

    def join_square(blocks):
        return place_call(blocks, place).reshape(-1, blocks[0].shape[1])

    def gather_square(deep):
        return join_square(spread(deep))

    cut = hidden // 2
    unit_stack = jnp.concatenate(
        [
            jnp.concatenate(
                [w_gate[0, ..., :cut], w_up[0, ..., :cut], w_gate[0, ..., cut:], w_up[0, ..., cut:]],
                axis=2,
            ),
            w_down[0],
        ],
        axis=1,
    )
    if pieces == 2:
        unit_stack = jnp.stack(jnp.split(unit_stack, 2, axis=2), axis=1)
    unit_stack = unit_stack.reshape(n_ctx, 2, per_core, unit_rows, width // pieces)
    units_lent = swap(at(unit_stack, 1 - core, 1), "section", 1)
    unit_stacks = own_other(at(unit_stack, core, 1), units_lent)

    def deal_units(stack):
        blocks = [at(stack, place)]
        blocks += [swap(at(stack, place ^ bit), "ctx", bit) for bit in range(1, n_ctx)]
        return place_call(blocks, place)

    ring = list(range(0, n_fsdp, 2)) + list(range(1, n_fsdp, 2))[::-1]
    ring_steps = [(ring[i], ring[(i + 1) % n_fsdp]) for i in range(n_fsdp)]
    ring_table = [[ring[ring.index(z) - i] for i in range(n_fsdp)] for z in range(n_fsdp)]
    behind_here = at(jnp.array(ring_table, jnp.uint32), depth)

    def ring_send(moved):
        return [blocks + [lax.ppermute(blocks[-1], "fsdp", ring_steps)] for blocks in moved]

    def own_units(blocks):
        return [order_call(blocks, behind_here, unit) for unit in range(per_core)]

    def pair_units(mine):
        other = [swap(part, "section", 1) for part in mine]
        units = list(mine) + other
        if pieces == 2:
            units = [jnp.concatenate(own_other(mine[0], other[0]), axis=2)]
        if aligned:
            return [[unit] for unit in units]
        return [
            [unit[:, :shard_rows].reshape(-1, width), unit[:, shard_rows:].reshape(-1, width)]
            for unit in units
        ]

    def cut_units(grads):
        if aligned:
            units = [unit for (unit,) in grads]
        else:
            units = [
                jnp.concatenate(
                    [part.reshape(n_ctx * n_fsdp, -1, width) for part in parts], axis=1
                )
                for parts in grads
            ]
        if pieces == 1:
            return (units[:per_core], units[per_core:])
        own, other = own_other(*jnp.split(units[0], 2, axis=2))
        return ([own], [other])

    def ring_part(terms, behind):
        spot = behind_here[behind % n_fsdp]
        return sum(at(term, spot, 1).astype(f32) for term in terms)

    def ring_start(own, received):
        terms = [part.reshape((n_ctx, n_fsdp) + part.shape[1:]) for part in (own, received)]
        return (terms, ring_part(terms, 1).astype(bf16))

    def ring_step(state, step):
        return [
            (terms, (lax.ppermute(moving, "fsdp", ring_steps).astype(f32)
                     + ring_part(terms, step + 1)).astype(bf16))
            for terms, moving in state
        ]

    def ring_rest(state, first):
        for step in range(first, n_fsdp):
            state = ring_step(state, step)
        return [moving for _, moving in state]

    def scatter_units(moved):
        whole = jnp.stack(moved, axis=1)
        blocks = [at(whole, place)]
        blocks += [swap(at(whole, place ^ bit), "ctx", bit) for bit in range(1, n_ctx)]
        return jnp.stack(blocks)

    def trade_square(own, received, bits):
        own, received = (part.reshape(n_ctx, -1, part.shape[1]) for part in (own, received))

        def part(bit):
            return at(own, place ^ bit).astype(f32) + at(received, place ^ bit).astype(f32)

        return [part(bit) if bit == 0 else swap(part(bit).astype(bf16), "ctx", bit) for bit in bits]

    def sum_square(parts):
        return sum(part.astype(f32) for part in parts).astype(bf16)

    def reduce_deep(mine):
        mine = mine.reshape(n_fsdp, shard_rows, -1)
        total = at(mine, depth).astype(f32)
        for bit in range(1, n_fsdp):
            total = total + swap(at(mine, depth ^ bit), "fsdp", bit).astype(f32)
        return total

    if pieces == 1:
        units_here = jnp.arange(per_core, dtype=jnp.uint32)
        units_here = jnp.concatenate(
            [core * per_core + units_here, (1 - core) * per_core + units_here]
        )
    else:
        units_here = jnp.zeros((1,), jnp.uint32)
    named = (place * own_experts + units_here).astype(f32)
    matches = info[:, None, :, :TOP] == named[None, :, None, None, None]
    hits = jnp.any(matches, axis=3)
    shares = jnp.sum(jnp.where(matches, info[:, None, :, TOP:], 0.0), axis=3)
    earlier = jnp.arange(rows)[:, None] < jnp.arange(rows)[None, :]
    rank = dot("ledr,rq->ledq", hits.astype(bf16), earlier.astype(bf16))
    slots = jnp.arange(capacity, dtype=f32)
    picks = hits[:, :, :, None, :] & (rank[:, :, :, None, :] == slots[:, None])
    slot_shares = jnp.sum(jnp.where(picks, shares[:, :, :, None, :], 0.0), axis=-1, keepdims=True)
    picks = picks.astype(bf16)

    order = place.astype(jnp.int32) ^ jnp.arange(n_ctx, dtype=jnp.int32)
    block_ids = jnp.take(block_of.reshape(n_ctx, 2), order, axis=0)
    block_ids = block_ids.reshape(-1)

    def gains_of(halves):
        pair = on_core(halves[1][:, -gap : 2 - gap], halves[0][:, -gap : 2 - gap])
        pair = pair.astype(f32).T
        return (pair[:1], pair[1:])

    near = 1 + len(early)
    parts = (slice(0, near), slice(near, n_ctx))

    def experts(layer, blocks, weights, answer):
        kept, arrived = ({}, [])
        back = {}
        for index, part in enumerate(parts):
            rows_here = blocks[part]
            if index:
                back[0], rows_here = tie(back[0], rows_here)
                arrived = [swap(block, "ctx", bit) for bit, block in zip(early, back[0][1:])]
            back[index] = []
            for j in range(own_experts):
                back[index], kept[index, j] = expert_call(
                    picks[layer, j, part],
                    slot_shares[layer, j, part],
                    rows_here,
                    weights[j],
                    shard_rows,
                    hidden,
                    back[index],
                    3 if index == 0 else 1,
                )
        if not answer:
            return (back[0] + back[1], kept)
        back[1], arrived = tie(back[1], arrived)
        arrived += [swap(block, "ctx", bit) for bit, block in zip(late, back[1])]
        return (back[0][:1] + arrived, kept)

    def experts_back(layer, blocks, weights, kept, beside, hold):
        sent, arrived = ([], [])
        back = {}
        grads = {j: [] for j in range(own_experts)}
        for index, part in enumerate(parts):
            rows_here = blocks[part]
            if index:
                back[0], rows_here = tie(back[0], rows_here)
                arrived = [swap(block, "ctx", bit) for bit, block in zip(early, back[0][1:])]
            back[index] = []
            for j in reversed(range(own_experts)):
                back[index], grads[j] = expert_back_call(
                    picks[layer, j, part],
                    slot_shares[layer, j, part],
                    rows_here,
                    kept[index, j],
                    weights[j],
                    shard_rows,
                    hidden,
                    back[index],
                    grads[j],
                    20 if index == 0 else 1,
                )
                if beside:
                    found = beside.pop(0)(*sent)
                    if hold:
                        back[index], grads[j], found = tie(back[index], grads[j], found)
                    else:
                        grads[j], found = tie(grads[j], found)
                    sent.append(found)
        for send_more in beside:
            sent.append(send_more(*sent))
        back[1], arrived, grads = tie(back[1], arrived, grads)
        arrived += [swap(block, "ctx", bit) for bit, block in zip(late, back[1])]
        own, other = cut_units([grads[j] for j in range(own_experts)])
        received = [swap(part, "section", 1) for part in other]
        return (back[0][:1] + arrived, own, received, sent)

    def keep_own(first, second):
        other = swap(on_core(second, first), "section", 1)
        return own_other(on_core(first, second), other)

    deep = gather_deep(jnp.concatenate(dense_shards, axis=1))
    dealt_first, dealt_second = (deal_units(stack) for stack in unit_stacks)
    deep, dealt_first, dealt_second, picks = tie(deep, dealt_first, dealt_second, picks)
    deep_first, deep_second = jnp.split(deep, 2, axis=1)
    dense_blocks, moved, leave_shard, deep_second = tie(
        spread(deep_first[:, :enter_cut]),
        ring_send([[dealt_first]]),
        deep_first[:, enter_cut:],
        deep_second,
    )
    leave_blocks = [leave_shard] + send(leave_shard, early)
    enter_own = join_square(dense_blocks)
    enter_first = (enter_own, swap(enter_own, "section", 1))

    first_gains = gains_of(enter_first)
    first_in = after(at(tokens, core)[0], slot_shares)
    _, first_normed, first_entered = enter_call(core, [first_in], first_gains[0], enter_first)
    first_entered, leave_blocks = tie(first_entered, leave_blocks)
    key_value = first_entered[:, qw : qw + 2 * kw]
    first_kv, moved, leave_shard, deep_second = tie(
        jnp.concatenate(spread(key_value)), ring_send(moved), leave_shard, deep_second
    )
    enter_shard = deep_second[:, :enter_cut]
    enter_blocks = [enter_shard] + send(enter_shard, early)
    first_attended = attend_call(block_ids, first_entered, first_kv)
    for _ in range(2, n_fsdp - 1):
        moved = ring_send(moved)
    first_attended, leave_blocks, dealt_second, moved, enter_blocks, enter_shard = tie(
        first_attended,
        leave_blocks + send(leave_shard, late),
        dealt_second,
        moved,
        enter_blocks,
        enter_shard,
    )
    leave_own = join_square(leave_blocks)
    leave_first = (leave_own, swap(leave_own, "section", 1))
    first_mid, ffn_normed = leave_call(core, first_in, first_attended, first_gains[1], leave_first)
    first_units = own_units(moved[0])
    ffn_normed, enter_blocks = tie(ffn_normed, enter_blocks + send(enter_shard, late))
    blocks = spread(ffn_normed)
    blocks[:near], dealt_second, first_units, enter_blocks, deep_second = tie(
        blocks[:near], dealt_second, first_units, enter_blocks, deep_second
    )
    enter_own = join_square(enter_blocks)
    enter_second = (enter_own, swap(enter_own, "section", 1))
    first_weights = pair_units(first_units)
    returned, first_kept = experts(0, blocks, first_weights, True)
    returned[:near], moved = tie(returned[:near], ring_send([[dealt_second]]))
    returned, moved, deep_second = tie(returned, ring_send(moved), deep_second)
    leave_shard = deep_second[:, enter_cut:]
    leave_blocks = [leave_shard] + send(leave_shard, early)

    second_gains = gains_of(enter_second)
    second_in, second_normed, second_entered = enter_call(
        core, [first_mid] + returned, second_gains[0], enter_second
    )
    second_entered, leave_blocks = tie(second_entered, leave_blocks)
    key_value = second_entered[:, qw : qw + 2 * kw]
    for _ in range(3, n_fsdp):
        moved = ring_send(moved)
    second_kv, leave_shard = tie(jnp.concatenate(spread(key_value)), leave_shard)
    second_attended = attend_call(block_ids, second_entered, second_kv)
    second_attended, leave_blocks, moved = tie(
        second_attended, leave_blocks + send(leave_shard, late), moved
    )
    leave_own = join_square(leave_blocks)
    leave_second = (leave_own, swap(leave_own, "section", 1))
    second_mid, ffn_normed = leave_call(
        core, second_in, second_attended, second_gains[1], leave_second
    )
    second_weights = pair_units(own_units(moved[0]))
    blocks = spread(ffn_normed)
    cotangent = after(at(out_grad, core)[0], blocks[:near])
    cot_blocks = spread(cotangent)
    second_returned, second_kept = experts(1, blocks, second_weights, False)
    cot_blocks, second_returned = tie(cot_blocks, second_returned)

    beside = [
        lambda *_: [swap(second_returned[bit], "ctx", bit) for bit in early],
        lambda *_: [swap(second_returned[bit], "ctx", bit) for bit in late],
    ]
    returned, own, received, arrived = experts_back(
        1, cot_blocks, second_weights, second_kept, beside, True
    )
    second_parts = [second_returned[0]] + [part for parts in arrived for part in parts]
    second_out = second_mid + sum(part.astype(f32) for part in second_parts)
    units_moving = [ring_start(*pair) for pair in zip(own, received)]
    after_rows, term, d_attended, *grads = leave_back_call(
        core,
        returned,
        second_gains[1],
        second_mid,
        cotangent,
        second_attended,
        leave_second,
    )
    d_attended, units_moving = tie(d_attended, ring_step(units_moving, 1))
    leave_grads = (grads[0], swap(grads[1], "section", 1))
    d_queries, d_key_value = attend_back_call(block_ids, second_entered, second_kv, d_attended)
    units_moving = ring_step(units_moving, 2)
    d_queries, d_key_value, leave_grads = tie(d_queries, d_key_value, leave_grads)
    d_key_value = gather_back(d_key_value)
    leave_parts = trade_square(*leave_grads, range(n_ctx))
    second_entry, cotangent, *grads = enter_back_call(
        core,
        d_queries,
        d_key_value,
        second_gains[0],
        second_in,
        second_normed,
        after_rows,
        term,
        enter_second,
    )
    cotangent, grads, units_moving, leave_parts = tie(
        cotangent, grads, units_moving, leave_parts
    )
    units_moving = ring_rest(units_moving, 3)
    enter_grads = (grads[0], swap(grads[1], "section", 1))

    blocks = spread(cotangent)
    blocks[:near], enter_grads = tie(blocks[:near], enter_grads)
    second_moved = units_moving
    layer_rows, leave_parts, second_moved = after(
        ((second_in, second_out.astype(bf16)), leave_parts, second_moved), blocks[:near]
    )
    beside = [
        lambda: (keep_own(*layer_rows), reduce_deep(sum_square(leave_parts))),
        lambda _: trade_square(*enter_grads, early),
    ]
    returned, own, received, (first, enter_parts) = experts_back(
        0, blocks, first_weights, first_kept, beside, True
    )
    layer_outs, second_leave = first
    returned, enter_grads = tie(returned, enter_grads)
    enter_parts = trade_square(*enter_grads, [0]) + enter_parts + trade_square(*enter_grads, late)
    units_moving = [ring_start(*pair) for pair in zip(own, received)]
    after_rows, term, d_attended, *grads = leave_back_call(
        core,
        returned,
        first_gains[1],
        first_mid,
        cotangent,
        first_attended,
        leave_first,
    )
    d_attended, units_moving, second_moved = tie(
        d_attended, ring_step(units_moving, 1), second_moved
    )
    leave_grads = (grads[0], swap(grads[1], "section", 1))
    d_queries, d_key_value = attend_back_call(block_ids, first_entered, first_kv, d_attended)
    units_moving = ring_step(units_moving, 2)
    d_queries, d_key_value, enter_parts = tie(d_queries, d_key_value, enter_parts)
    d_key_value, leave_grads = tie(gather_back(d_key_value), leave_grads)
    second_moving = sum_square(enter_parts)
    leave_parts = trade_square(*leave_grads, early)
    first_entry, _, *grads = enter_back_call(
        core,
        d_queries,
        d_key_value,
        first_gains[0],
        first_in,
        first_normed,
        after_rows,
        term,
        enter_first,
    )
    grads, units_moving, leave_parts, leave_grads = tie(
        grads, units_moving, leave_parts, leave_grads
    )
    units_moving = ring_rest(units_moving, 3)
    leave_parts = trade_square(*leave_grads, [0]) + leave_parts
    enter_grads, leave_parts = tie(
        (grads[0], swap(grads[1], "section", 1)), leave_parts + trade_square(*leave_grads, late)
    )
    enter_parts, units_moving = tie(trade_square(*enter_grads, range(n_ctx)), units_moving)
    first_moving = [sum_square(parts) for parts in (enter_parts, leave_parts)]
    dense = reduce_deep(jnp.concatenate(first_moving + [second_moving], axis=1))
    first_dense = dense[:, : enter_cut + leave_cut]
    second_dense = jnp.concatenate([dense[:, enter_cut + leave_cut :], second_leave], axis=1)
    scattered = scatter_units(units_moving + second_moved)
    first_scattered, second_scattered = (scattered[:, :per_core], scattered[:, per_core:])

    layer_out = jnp.stack(layer_outs)
    input_grads = jnp.stack(keep_own(first_entry, second_entry))
    low_dense, high_dense = keep_own(first_dense, second_dense)
    enter_grad = jnp.concatenate([low_dense[:, :enter_cut], high_dense[:, :enter_cut]], axis=1)
    grad_out = jnp.concatenate([low_dense[:, enter_cut:], high_dense[:, enter_cut:]], axis=1)
    grad_gains = enter_grad[:, qw + 2 * kw :]
    mine = on_core(first_scattered, second_scattered)
    other = swap(on_core(second_scattered, first_scattered), "section", 1)
    if aligned and pieces == 1:
        grad_gate, grad_up, grad_down = finish_call(mine, other, shard_rows, hidden, place, core)
    else:
        sides = [jnp.take(part, order, axis=0) for part in own_other(mine, other)]
        if pieces == 1:
            whole = jnp.stack(sides, axis=1).reshape(EXPERTS, unit_rows, width)
        else:
            whole = jnp.concatenate([side[:, 0] for side in sides], axis=2)
        pairs = whole[:, :shard_rows].astype(f32).reshape(EXPERTS, shard_rows, 2, 2, cut)
        grad_gate = pairs[:, :, :, 0].reshape(EXPERTS, shard_rows, hidden)
        grad_up = pairs[:, :, :, 1].reshape(EXPERTS, shard_rows, hidden)
        grad_down = whole[:, shard_rows:].astype(f32)
    return (
        layer_out[None, :, None],
        input_grads[None, :, None],
        grad_gains[:, 0][None],
        enter_grad[:, :qw][None],
        enter_grad[:, qw : qw + kw][None],
        enter_grad[:, qw + kw : qw + 2 * kw][None],
        grad_out[None],
        grad_gains[:, 1][None],
        grad_gate[None],
        grad_up[None],
        grad_down[None],
    )


def solution(mesh):
    rows_placed = P(None, "fsdp", "ctx", None)
    kept_placed = P("section", None, "fsdp", "ctx", None)
    gain_placed = P("section", ("ctx", "fsdp"))
    dense_placed = P("section", ("ctx", "fsdp"), None)
    expert_placed = P("section", None, ("ctx", "fsdp"), None)
    dense_all = (dense_placed,) * 4
    expert_all = (expert_placed,) * 3
    layer_placed = (gain_placed,) + dense_all + (gain_placed,) + expert_all
    return jax.shard_map(
        body,
        mesh=mesh,
        in_specs=(rows_placed, P(), kept_placed, kept_placed) + layer_placed + (rows_placed,),
        out_specs=(kept_placed, kept_placed) + layer_placed,
        check_vma=False,
    )
```

```python
import functools

import jax
import jax.numpy as jnp
from jax import lax
from jax.experimental import pallas as pl
from jax.experimental.pallas import tpu as pltpu
from jax.sharding import PartitionSpec as P

QH = 12
KVH = 2
HD = 128
GROUP = QH // KVH
TOP = 4
EXPERTS = 8
bf16 = jnp.bfloat16
f32 = jnp.float32


epsilon = 1e-06
masked_out = -1e30
gap = 256


def swap(value, axis, bit):
    count = lax.axis_size(axis)
    return lax.ppermute(value, axis, [(source, source ^ bit) for source in range(count)])


def tie(*values):
    return lax.optimization_barrier(values)


def after(value, earlier):
    return tie(value, earlier)[0]


def at(value, index, axis=0):
    return lax.dynamic_index_in_dim(value, index, axis, keepdims=False)


def dot(spec, left, right, kind=f32):
    return jnp.einsum(spec, left, right, preferred_element_type=kind)


def cost(micros):
    return pl.CostEstimate(
        flops=int(micros * 1e9), bytes_accessed=int(micros * 3e6), transcendentals=0
    )


def kernel_params():
    return pltpu.CompilerParams(vmem_limit_bytes=56 * 1024 * 1024)


def nt(left, right):
    return lax.dot_general(left, right, (((1,), (1,)), ((), ())), preferred_element_type=f32)


def nn(left, right):
    return jnp.dot(left, right, preferred_element_type=f32)


def head_rows(ref):
    return jnp.concatenate([ref[:, i * HD : (i + 1) * HD] for i in range(GROUP)], axis=0)


def softmax_rows(ids_ref, queries, keys, half, own):
    scores = nt(queries, keys) * HD ** (-0.5)
    tall, wide = scores.shape
    row = lax.broadcasted_iota(jnp.int32, (half, 1), 0)
    row = jnp.concatenate([row] * (tall // half), axis=0) + ids_ref[own] * half
    lane = lax.broadcasted_iota(jnp.int32, (1, half), 1)
    column = [lane + ids_ref[block] * half for block in range(wide // half)]
    column = jnp.concatenate(column, axis=1)
    scores = jnp.where(row >= column, scores, masked_out)
    shifted = jnp.exp(scores - jnp.max(scores, axis=1, keepdims=True))
    return shifted / jnp.sum(shifted, axis=1, keepdims=True)


def attend_kernel(ids_ref, query_ref, key_ref, value_ref, out_ref):
    half = query_ref.shape[0]
    probs = softmax_rows(ids_ref, head_rows(query_ref), key_ref[...], half, pl.program_id(1))
    out = nn(probs.astype(bf16), value_ref[...]).astype(bf16)
    for i in range(GROUP):
        out_ref[:, i * HD : (i + 1) * HD] = out[i * half : (i + 1) * half]


def attend_specs(rows, seq_len):
    half = rows // 2
    by_head = pl.BlockSpec((half, GROUP * HD), lambda g, h, ids: (h, g))
    keys = pl.BlockSpec((seq_len, HD), lambda g, h, ids: (0, g))
    values = pl.BlockSpec((seq_len, HD), lambda g, h, ids: (0, KVH + g))
    return by_head, keys, values


def attend_call(ids, queries, key_value):
    rows, seq_len = (queries.shape[0], key_value.shape[0])
    by_head, keys, values = attend_specs(rows, seq_len)
    return pl.pallas_call(
        attend_kernel,
        grid_spec=pltpu.PrefetchScalarGridSpec(
            num_scalar_prefetch=1,
            grid=(KVH, 2),
            in_specs=[by_head, keys, values],
            out_specs=by_head,
        ),
        out_shape=jax.ShapeDtypeStruct((rows, QH * HD), bf16),
        compiler_params=kernel_params(),
        cost_estimate=cost(1),
        name="attend",
    )(ids, queries, key_value, key_value)


def attend_back_kernel(ids_ref, query_ref, key_ref, value_ref, cot_ref, dq_ref, *refs):
    out, (dk_ref, dv_ref) = (refs[:-2], refs[-2:])
    half = query_ref.shape[0]
    group, own = (pl.program_id(0), pl.program_id(1))
    queries, cot = (head_rows(query_ref), head_rows(cot_ref))
    probs = softmax_rows(ids_ref, queries, key_ref[...], half, own)
    d_probs = nt(cot, value_ref[...])
    inner = jnp.sum(probs * d_probs, axis=1, keepdims=True)
    d_scores = (probs * (d_probs - inner)).astype(bf16)
    d_queries = (nn(d_scores, key_ref[...]) * HD ** (-0.5)).astype(bf16)
    for i in range(GROUP):
        dq_ref[:, i * HD : (i + 1) * HD] = d_queries[i * half : (i + 1) * half]
    d_keys = nn(d_scores.T, queries) * HD ** (-0.5)
    d_values = nn(probs.astype(bf16).T, cot)

    @pl.when(own == 0)
    def _():
        dk_ref[...] = d_keys
        dv_ref[...] = d_values

    @pl.when(own != 0)
    def _():
        rows = 2 * half
        for block, ref in enumerate(out):
            part = slice(block * rows, (block + 1) * rows)
            for first, total, last in ((0, dk_ref, d_keys), (KVH * HD, dv_ref, d_values)):
                columns = pl.ds(pl.multiple_of(first + group * HD, HD), HD)
                ref[:, columns] = (total[part, :] + last[part]).astype(bf16)


def attend_back_call(ids, queries, key_value, cot):
    rows, seq_len = (queries.shape[0], key_value.shape[0])
    by_head, keys, values = attend_specs(rows, seq_len)
    blocks = seq_len // rows
    wide = 2 * KVH * HD
    result = pl.pallas_call(
        attend_back_kernel,
        grid_spec=pltpu.PrefetchScalarGridSpec(
            num_scalar_prefetch=1,
            grid=(KVH, 2),
            in_specs=[by_head, keys, values, by_head],
            out_specs=[by_head] + [pl.BlockSpec((rows, wide), lambda g, h, ids: (0, 0))] * blocks,
            scratch_shapes=[pltpu.VMEM((seq_len, HD), f32)] * 2,
        ),
        out_shape=[jax.ShapeDtypeStruct((rows, QH * HD), bf16)]
        + [jax.ShapeDtypeStruct((rows, wide), bf16)] * blocks,
        compiler_params=kernel_params(),
        cost_estimate=cost(1),
        name="attend_back",
    )(ids, queries, key_value, key_value, cot)
    return (result[0], result[1:])


def gelu_parts(gate):
    root = 0.7978845608028654
    inner = root * (gate + 0.044715 * gate * gate * gate)
    bent = jnp.tanh(inner)
    value = 0.5 * gate * (1.0 + bent)
    slope = root * (1.0 + 3.0 * 0.044715 * gate * gate)
    return value, 0.5 * (1.0 + bent) + 0.5 * gate * (1.0 - bent * bent) * slope


def give_back(pick_ref, total_ref, share_ref, before, out):
    blocks, capacity, _ = pick_ref.shape
    for d in range(blocks):
        part = total_ref[d * capacity : (d + 1) * capacity, :]
        if share_ref is not None:
            part = part * share_ref[d]
        back = nn(pick_ref[d].T, part.astype(bf16))
        if before:
            back = back + before[d][...]
        out[d][...] = back.astype(out[d].dtype)


def flat(ref):
    value = ref[...]
    return value.reshape(-1, value.shape[-1])


def add_up(total_ref, part, step):
    @pl.when(step == 0)
    def _():
        total_ref[...] = part

    @pl.when(step != 0)
    def _():
        total_ref[...] += part


def expert_kernel(blocks, adds, pick_ref, share_ref, gate_ref, up_ref, down_ref, *refs):
    rows, refs = (refs[:blocks], refs[blocks:])
    before, refs = (refs[: blocks * adds], refs[blocks * adds :])
    out, (picked_ref, gate_pre_ref, up_pre_ref, total_ref) = (refs[:blocks], refs[blocks:])
    step = pl.program_id(0)
    capacity = pick_ref.shape[1]

    @pl.when(step == 0)
    def _():
        for d in range(blocks):
            block = nn(pick_ref[d], rows[d][...]).astype(bf16)
            picked_ref[d * capacity : (d + 1) * capacity, :] = block

    gate_pre = nn(picked_ref[...], flat(gate_ref))
    up_pre = nn(picked_ref[...], flat(up_ref))
    gate_pre_ref[...] = gate_pre
    up_pre_ref[...] = up_pre
    active = (gelu_parts(gate_pre)[0] * up_pre).astype(bf16)
    add_up(total_ref, nn(active, flat(down_ref)), step)

    @pl.when(step == pl.num_programs(0) - 1)
    def _():
        give_back(pick_ref, total_ref, share_ref, before, out)


def whole_spec(shape):
    return pl.BlockSpec(
        shape, lambda step: (0,) * len(shape), pipeline_mode=pl.Buffered(buffer_count=1)
    )


def weight_operands(weights, deep, cut):
    if len(weights) == 1:
        unit = weights[0]
        shards, tall, width = unit.shape
        specs = [
            pl.BlockSpec((shards, deep, cut), lambda step: (0, 0, 2 * step)),
            pl.BlockSpec((shards, deep, cut), lambda step: (0, 0, 2 * step + 1)),
            pl.BlockSpec(
                (shards // 2, tall - deep, width), lambda step: (step, deep // (tall - deep), 0)
            ),
        ]
        return specs, [unit, unit, unit]
    pair, down = weights
    specs = [
        pl.BlockSpec((pair.shape[0], cut), lambda step: (0, 2 * step)),
        pl.BlockSpec((pair.shape[0], cut), lambda step: (0, 2 * step + 1)),
        pl.BlockSpec((cut, down.shape[1]), lambda step: (step, 0)),
    ]
    return specs, [pair, pair, down]


def expert_call(picks, shares, rows, weights, deep, hidden, before, micros):
    blocks, capacity, _ = picks.shape
    width, cut, tall = (rows[0].shape[1], hidden // 2, blocks * capacity)
    columns = pl.BlockSpec((tall, cut), lambda step: (0, step))
    row_specs = [whole_spec(block.shape) for block in rows]
    specs, operands = weight_operands(weights, deep, cut)
    result = pl.pallas_call(
        functools.partial(expert_kernel, blocks, 1 if before else 0),
        grid=(2,),
        in_specs=[whole_spec(picks.shape), whole_spec(shares.shape)]
        + specs
        + row_specs * (2 if before else 1),
        out_specs=row_specs + [whole_spec((tall, width)), columns, columns],
        out_shape=[jax.ShapeDtypeStruct(block.shape, bf16) for block in rows]
        + [
            jax.ShapeDtypeStruct((tall, width), bf16),
            jax.ShapeDtypeStruct((tall, hidden), f32),
            jax.ShapeDtypeStruct((tall, hidden), f32),
        ],
        scratch_shapes=[pltpu.VMEM((tall, width), f32)],
        compiler_params=kernel_params(),
        cost_estimate=cost(micros),
        name="expert",
    )(picks, shares, *operands, *rows, *before)
    return (list(result[:blocks]), list(result[blocks:]))


def expert_back_kernel(
    blocks, adds, pick_ref, share_ref, gate_pre_ref, up_pre_ref, gate_ref, up_ref, down_ref, *refs
):
    rows, refs = (refs[:blocks], refs[blocks:])
    before, refs = (refs[: blocks * adds], refs[blocks * adds :])
    out, refs = (refs[:blocks], refs[blocks:])
    slots_ref, d_gate_ref, d_up_ref, active_ref, total_ref = refs
    step = pl.program_id(0)
    capacity = pick_ref.shape[1]

    @pl.when(step == 0)
    def _():
        for d in range(blocks):
            block = nn(pick_ref[d], rows[d][...]) * share_ref[d]
            slots_ref[d * capacity : (d + 1) * capacity, :] = block.astype(bf16)

    d_active = nt(slots_ref[...], flat(down_ref))
    value, slope = gelu_parts(gate_pre_ref[...])
    up_pre = up_pre_ref[...]
    d_gate = (d_active * up_pre * slope).astype(bf16)
    d_up = (d_active * value).astype(bf16)
    active_ref[...] = (value * up_pre).astype(bf16)
    d_gate_ref[...] = d_gate
    d_up_ref[...] = d_up
    add_up(total_ref, nt(d_gate, flat(gate_ref)) + nt(d_up, flat(up_ref)), step)

    @pl.when(step == pl.num_programs(0) - 1)
    def _():
        give_back(pick_ref, total_ref, None, before, out)


def expert_back_call(picks, shares, rows, kept, weights, deep, before, micros):
    _, gate_pre, up_pre = kept
    blocks, capacity, _ = picks.shape
    width, (tall, hidden) = (rows[0].shape[1], gate_pre.shape)
    cut = hidden // 2
    columns = pl.BlockSpec((tall, cut), lambda step: (0, step))
    row_specs = [whole_spec(block.shape) for block in rows]
    specs, operands = weight_operands(weights, deep, cut)
    result = pl.pallas_call(
        functools.partial(expert_back_kernel, blocks, 1 if before else 0),
        grid=(2,),
        in_specs=[whole_spec(picks.shape), whole_spec(shares.shape), columns, columns]
        + specs
        + row_specs * (2 if before else 1),
        out_specs=row_specs + [whole_spec((tall, width)), columns, columns, columns],
        out_shape=[jax.ShapeDtypeStruct(block.shape, bf16) for block in rows]
        + [jax.ShapeDtypeStruct((tall, width), bf16)]
        + [jax.ShapeDtypeStruct((tall, hidden), bf16)] * 3,
        scratch_shapes=[pltpu.VMEM((tall, width), f32)],
        compiler_params=kernel_params(),
        cost_estimate=cost(micros),
        name="expert_back",
    )(picks, shares, gate_pre, up_pre, *operands, *rows, *before)
    return (list(result[:blocks]), list(result[blocks:]))


def expert_grads_kernel(parts, deep, *refs):
    picked, slots, d_gate, d_up, active = (refs[i * parts : (i + 1) * parts] for i in range(5))
    grad_refs, turned_ref = (refs[5 * parts : -1], refs[-1])
    step = pl.program_id(0)

    def below(some):
        return jnp.concatenate([ref[...] for ref in some], axis=0)

    @pl.when(step == 0)
    def _():
        turned_ref[...] = below(picked).T

    grad_gate = nn(turned_ref[...], below(d_gate)).astype(bf16)
    grad_up = nn(turned_ref[...], below(d_up)).astype(bf16)
    grad_down = nn(below(active).T, below(slots)).astype(bf16)
    cut = grad_gate.shape[1]
    if len(grad_refs) == 1:
        unit_ref = grad_refs[0]
        shards, tall, width = unit_ref.shape
        for side in range(2):

            @pl.when(step == side)
            def _():
                left, some = (2 * side * cut, shards // 2)
                unit_ref[:, :deep, left : left + cut] = grad_gate.reshape(shards, deep, cut)
                left = left + cut
                unit_ref[:, :deep, left : left + cut] = grad_up.reshape(shards, deep, cut)
                rest = grad_down.reshape(some, tall - deep, width)
                unit_ref[side * some : (side + 1) * some, deep:, :] = rest
    else:
        grad_refs[0][:, :cut] = grad_gate
        grad_refs[0][:, cut:] = grad_up
        grad_refs[1][...] = grad_down


def expert_grads_call(picked, saved, weights, deep):
    slots, d_gate, d_up, active = zip(*saved)
    width, hidden = (picked[0].shape[1], d_gate[0].shape[1])
    cut = hidden // 2
    columns = [pl.BlockSpec((part.shape[0], cut), lambda step: (0, step)) for part in picked]
    if len(weights) == 1:
        grad_specs = [whole_spec(weights[0].shape)]
    else:
        grad_specs = [
            pl.BlockSpec((width, 2 * cut), lambda step: (0, step)),
            pl.BlockSpec((cut, width), lambda step: (step, 0)),
        ]
    return list(
        pl.pallas_call(
            functools.partial(expert_grads_kernel, len(picked), deep),
            grid=(2,),
            in_specs=[whole_spec(part.shape) for part in picked] * 2 + columns * 3,
            out_specs=grad_specs,
            out_shape=[jax.ShapeDtypeStruct(part.shape, bf16) for part in weights],
            scratch_shapes=[pltpu.VMEM((width, sum(part.shape[0] for part in picked)), bf16)],
            compiler_params=kernel_params(),
            cost_estimate=cost(1),
            name="expert_grads",
        )(*picked, *slots, *d_gate, *d_up, *active)
    )


def norm_parts(value):
    scale = lax.rsqrt(jnp.mean(value * value, axis=1, keepdims=True) + epsilon)
    return scale, value * scale


def norm_back(grad, gain, value):
    scale, scaled = norm_parts(value)
    grown = grad * gain
    back = scale * (grown - scaled * jnp.mean(scaled * grown, axis=1, keepdims=True))
    return back, (grad * scaled).astype(bf16)


def add_all(refs):
    total = refs[0][...].astype(f32)
    for ref in refs[1:]:
        total = total + ref[...].astype(f32)
    return total


def side_offsets(core_ref, steps, cut):
    step, core = (pl.program_id(0), core_ref[0])
    own = pl.multiple_of((core * steps + step) * cut, cut)
    other = pl.multiple_of(((1 - core) * steps + step) * cut, cut)
    return own, other


def dense_call(kernel, core, steps, whole, halves, out, scratch, name, micros):
    cut = halves[0].shape[1] // steps

    def keep(shape):
        return pl.BlockSpec(
            shape, lambda step, core: (0,) * len(shape), pipeline_mode=pl.Buffered(buffer_count=1)
        )

    def tile(tall):
        return pl.BlockSpec((tall, cut), lambda step, core: (0, step))

    return pl.pallas_call(
        kernel,
        grid_spec=pltpu.PrefetchScalarGridSpec(
            num_scalar_prefetch=1,
            grid=(steps,),
            in_specs=[keep(part.shape) for part in whole] + [tile(halves[0].shape[0])] * 2,
            out_specs=[
                tile(part.shape[0]) if tiled else keep(part.shape) for part, tiled in out
            ],
            scratch_shapes=scratch,
        ),
        out_shape=[part for part, _ in out],
        compiler_params=kernel_params(),
        cost_estimate=cost(micros),
        name=name,
    )(core.astype(jnp.int32).reshape(1), *whole, *halves)


def shape_of(kind, *shape):
    return jax.ShapeDtypeStruct(shape, kind)


def enter_kernel(steps, terms, core_ref, gain_ref, *refs):
    parts, (own_ref, other_ref, sent_ref, normed_ref, out_ref) = (refs[:terms], refs[terms:])
    own, other = side_offsets(core_ref, steps, own_ref.shape[1])

    @pl.when(pl.program_id(0) == 0)
    def _():
        sent = add_all(parts).astype(bf16)
        sent_ref[...] = sent
        normed_ref[...] = (norm_parts(sent.astype(f32))[1] * gain_ref[...]).astype(bf16)

    cut = own_ref.shape[1]
    out_ref[:, pl.ds(own, cut)] = nn(normed_ref[...], own_ref[...]).astype(bf16)
    out_ref[:, pl.ds(other, cut)] = nn(normed_ref[...], other_ref[...]).astype(bf16)


def enter_call(core, parts, gain, halves):
    rows, width = parts[0].shape
    return dense_call(
        functools.partial(enter_kernel, 3, len(parts)),
        core,
        3,
        [gain] + parts,
        halves,
        [
            (shape_of(bf16, rows, width), False),
            (shape_of(bf16, rows, width), False),
            (shape_of(bf16, rows, 2 * halves[0].shape[1]), False),
        ],
        [],
        "enter",
        6,
    )


def leave_kernel(steps, core_ref, gain_ref, rows_ref, attended_ref, own_ref, other_ref,
                 mid_ref, normed_ref):
    cut = own_ref.shape[1]
    for start, ref in zip(side_offsets(core_ref, steps, cut), (own_ref, other_ref)):
        part = pl.ds(start, cut)
        mid_ref[:, part] = rows_ref[:, part].astype(f32) + nn(attended_ref[...], ref[...])

    @pl.when(pl.program_id(0) == steps - 1)
    def _():
        normed_ref[...] = (norm_parts(mid_ref[...])[1] * gain_ref[...]).astype(bf16)


def leave_call(core, rows_in, attended, gain, halves):
    rows, width = rows_in.shape
    return dense_call(
        functools.partial(leave_kernel, 2),
        core,
        2,
        [gain, rows_in, attended],
        halves,
        [(shape_of(f32, rows, width), False), (shape_of(bf16, rows, width), False)],
        [],
        "leave",
        5,
    )


def leave_back_kernel(steps, terms, core_ref, gain_ref, mid_ref, cot_ref, attended_ref, *refs):
    parts, refs = (refs[:terms], refs[terms:])
    own_ref, other_ref, after_ref, term_ref, d_attended_ref, *refs = refs
    own_grad_ref, other_grad_ref, branch_ref, turned_ref, total_ref = refs
    step, cut = (pl.program_id(0), own_ref.shape[1])

    @pl.when(step == 0)
    def _():
        back, term_ref[...] = norm_back(add_all(parts), gain_ref[...], mid_ref[...])
        back = back + cot_ref[...].astype(f32)
        after_ref[...] = back
        branch_ref[...] = back.astype(bf16)
        turned_ref[...] = attended_ref[...].T

    own, other = side_offsets(core_ref, steps, cut)
    d_own, d_other = (branch_ref[:, pl.ds(own, cut)], branch_ref[:, pl.ds(other, cut)])
    own_grad_ref[...] = nn(turned_ref[...], d_own).astype(bf16)
    other_grad_ref[...] = nn(turned_ref[...], d_other).astype(bf16)
    add_up(total_ref, nt(d_own, own_ref[...]) + nt(d_other, other_ref[...]), step)

    @pl.when(step == steps - 1)
    def _():
        d_attended_ref[...] = total_ref[...].astype(bf16)


def leave_back_call(core, parts, gain, mid, cotangent, attended, halves):
    rows, width = mid.shape
    half = (halves[0].shape[0], halves[0].shape[1])
    return dense_call(
        functools.partial(leave_back_kernel, 2, len(parts)),
        core,
        2,
        [gain, mid, cotangent, attended] + parts,
        halves,
        [
            (shape_of(f32, rows, width), False),
            (shape_of(bf16, rows, width), False),
            (shape_of(bf16, rows, width), False),
            (shape_of(bf16, *half), True),
            (shape_of(bf16, *half), True),
        ],
        [
            pltpu.VMEM((rows, width), bf16),
            pltpu.VMEM((width, rows), bf16),
            pltpu.VMEM((rows, width), f32),
        ],
        "leave_back",
        8,
    )


def enter_back_kernel(steps, terms, core_ref, gain_ref, rows_ref, normed_ref, after_ref, term_ref,
                      dq_ref, *refs):
    parts, refs = (refs[:terms], refs[terms:])
    own_ref, other_ref, entry_ref, sent_ref, own_grad_ref, other_grad_ref, *refs = refs
    entered_ref, turned_ref, total_ref = refs
    step, cut = (pl.program_id(0), own_ref.shape[1])
    rows, qw = dq_ref.shape

    @pl.when(step == 0)
    def _():
        entered_ref[:, :qw] = dq_ref[...]
        wide = parts[0].shape[1]
        entered_ref[:, qw : qw + wide] = add_all(parts).astype(bf16)
        entered_ref[:, qw + wide :] = jnp.zeros((rows, gap), bf16)
        turned_ref[...] = normed_ref[...].T

    own, other = side_offsets(core_ref, steps, cut)
    d_own, d_other = (entered_ref[:, pl.ds(own, cut)], entered_ref[:, pl.ds(other, cut)])
    own_grad_ref[...] = nn(turned_ref[...], d_own).astype(bf16)
    other_grad_ref[...] = nn(turned_ref[...], d_other).astype(bf16)
    add_up(total_ref, nt(d_own, own_ref[...]) + nt(d_other, other_ref[...]), step)

    @pl.when(step == steps - 1)
    def _():
        back, attn_term = norm_back(total_ref[...], gain_ref[...], rows_ref[...].astype(f32))
        back = back + after_ref[...]
        entry_ref[...] = back
        sent_ref[...] = back.astype(bf16)
        lane = lax.broadcasted_iota(jnp.int32, (rows, 128), 1)
        sums = nn(attn_term.T, (lane == 0).astype(bf16))
        sums = (sums + nn(term_ref[...].T, (lane == 1).astype(bf16))).astype(bf16)
        left = cut - gap

        @pl.when(core_ref[0] == 0)
        def _():
            other_grad_ref[:, left : left + 128] = sums

        @pl.when(core_ref[0] != 0)
        def _():
            own_grad_ref[:, left : left + 128] = sums


def enter_back_call(core, dq, parts, gain, rows_in, normed, after, term, halves):
    rows, width = rows_in.shape
    return dense_call(
        functools.partial(enter_back_kernel, 3, len(parts)),
        core,
        3,
        [gain, rows_in, normed, after, term, dq] + parts,
        halves,
        [
            (shape_of(f32, rows, width), False),
            (shape_of(bf16, rows, width), False),
            (shape_of(bf16, *halves[0].shape), True),
            (shape_of(bf16, *halves[0].shape), True),
        ],
        [
            pltpu.VMEM((rows, 2 * halves[0].shape[1]), bf16),
            pltpu.VMEM((width, rows), bf16),
            pltpu.VMEM((rows, width), f32),
        ],
        "enter_back",
        1,
    )


def place_kernel(count, joined, index_ref, *refs):
    step = pl.program_id(0)
    for bit in range(count):

        @pl.when(step == bit)
        def _():
            if joined:
                refs[count][...] = refs[bit][...]
            else:
                refs[count][0] = refs[bit][...]


def place_call(blocks, index):
    count = len(blocks)
    shape = blocks[0].shape
    zeros = (0,) * len(shape)
    joined = len(shape) == 2 and shape[0] % 16 == 0
    if joined:
        out_spec = pl.BlockSpec(shape, lambda step, at: (at[0] ^ step, 0))
        out_shape = (count * shape[0], shape[1])
    else:
        out_spec = pl.BlockSpec((1,) + shape, lambda step, at: (at[0] ^ step,) + zeros)
        out_shape = (count,) + shape
    return pl.pallas_call(
        functools.partial(place_kernel, count, joined),
        grid_spec=pltpu.PrefetchScalarGridSpec(
            num_scalar_prefetch=1,
            grid=(count,),
            in_specs=[pl.BlockSpec(shape, lambda step, at: zeros)] * count,
            out_specs=out_spec,
        ),
        out_shape=jax.ShapeDtypeStruct(out_shape, blocks[0].dtype),
        compiler_params=kernel_params(),
        cost_estimate=cost(2),
        name="place",
    )(index.astype(jnp.int32).reshape(1), *blocks)


def order_kernel(count, order_ref, *refs):
    step = pl.program_id(0)
    for i in range(count):

        @pl.when(step == i)
        def _():
            refs[count][:, 0] = refs[i][:, 0]


def order_call(blocks, order, unit):
    count = len(blocks)
    n_ctx, _, tall, wide = blocks[0].shape
    shape = (n_ctx, 1, tall, wide)
    source = pl.BlockSpec(
        shape, lambda step, at: (0, unit, 0, 0), pipeline_mode=pl.Buffered(buffer_count=1)
    )
    result = pl.pallas_call(
        functools.partial(order_kernel, count),
        grid_spec=pltpu.PrefetchScalarGridSpec(
            num_scalar_prefetch=1,
            grid=(count,),
            in_specs=[source] * count,
            out_specs=pl.BlockSpec(shape, lambda step, at: (0, at[step], 0, 0)),
        ),
        out_shape=jax.ShapeDtypeStruct((n_ctx, count, tall, wide), bf16),
        compiler_params=kernel_params(),
        cost_estimate=cost(4),
        name="order",
    )(order.astype(jnp.int32), *blocks)
    return result.reshape(n_ctx * count, tall, wide)


def finish_kernel(deep, index_ref, own_ref, other_ref, gate_ref, up_ref, down_ref):
    side = pl.program_id(1)
    wide = gate_ref.shape[2] // 2

    def write(source):
        for half in range(2):
            left, target = (2 * half * wide, slice(half * wide, (half + 1) * wide))
            gate_ref[:, :, target] = source[0, :, :deep, left : left + wide].astype(f32)
            left = left + wide
            up_ref[:, :, target] = source[0, :, :deep, left : left + wide].astype(f32)
        down_ref[...] = source[0, :, deep:, :].astype(f32)

    @pl.when(side == index_ref[1])
    def _():
        write(own_ref)

    @pl.when(side != index_ref[1])
    def _():
        write(other_ref)


def finish_call(own, other, deep, hidden, place, core):
    n_ctx, units, tall, width = own.shape
    experts = 2 * n_ctx * units
    source = pl.BlockSpec((1, units, tall, width), lambda bit, side, at: (bit, 0, 0, 0))
    target = lambda bit, side, at: (2 * (at[0] ^ bit) + side, 0, 0)
    return pl.pallas_call(
        functools.partial(finish_kernel, deep),
        grid_spec=pltpu.PrefetchScalarGridSpec(
            num_scalar_prefetch=1,
            grid=(n_ctx, 2),
            in_specs=[source, source],
            out_specs=[
                pl.BlockSpec((units, deep, hidden), target),
                pl.BlockSpec((units, deep, hidden), target),
                pl.BlockSpec((units, tall - deep, width), target),
            ],
        ),
        out_shape=[
            jax.ShapeDtypeStruct((experts, deep, hidden), f32),
            jax.ShapeDtypeStruct((experts, deep, hidden), f32),
            jax.ShapeDtypeStruct((experts, tall - deep, width), f32),
        ],
        compiler_params=kernel_params(),
        cost_estimate=cost(8),
        name="finish",
    )(jnp.stack([place, core]).astype(jnp.int32), own, other)


def body(
    tokens,
    block_of,
    routes,
    combine,
    attn_norm,
    w_query,
    w_key,
    w_value,
    w_out,
    ffn_norm,
    w_gate,
    w_up,
    w_down,
    out_grad,
):
    rows = tokens.shape[2]
    width = tokens.shape[3]
    half = rows // 2
    n_ctx = lax.axis_size("ctx")
    n_fsdp = lax.axis_size("fsdp")
    core, place, depth = (
        lax.axis_index(axis).astype(jnp.uint32) for axis in ("section", "ctx", "fsdp")
    )
    seq_len = rows * n_ctx
    capacity = rows * TOP * 5 // (4 * EXPERTS)
    score_scale = HD ** (-0.5)
    own_experts = EXPERTS // n_ctx
    hidden = w_gate.shape[3]
    shard_rows = w_query.shape[1]
    down_rows = w_down.shape[2]
    qw = w_query.shape[2]
    kw = w_key.shape[2]
    pieces = max(1, 2 * n_ctx // EXPERTS)
    per_core = max(1, EXPERTS // (2 * n_ctx))
    unit_rows = shard_rows + down_rows
    aligned = shard_rows % 16 == 0 and down_rows % 16 == 0

    def on_core(former, latter):
        return jnp.where(core == 0, former, latter)

    def own_other(low, high):
        return (on_core(low, high), on_core(high, low))

    early, late = (range(1, n_ctx // 2 + 1), range(n_ctx // 2 + 1, n_ctx))

    def send(value, bits):
        return [swap(value, "ctx", bit) for bit in bits]

    def spread(value):
        return [value] + send(value, early) + send(value, late)

    def gather_back(blocks):
        return [blocks[0]] + [swap(blocks[bit], "ctx", bit) for bit in range(1, n_ctx)]

    info = jnp.concatenate([routes.astype(f32), combine], axis=-1)[0, :, 0].transpose(0, 2, 1)
    info_own, info_other = (at(info, core), swap(at(info, 1 - core), "section", 1))
    info = jnp.stack(own_other(info_own, info_other))
    info = jnp.stack([info] + [swap(info, "ctx", bit) for bit in range(1, n_ctx)], axis=1)

    gain_columns = jnp.stack([attn_norm[0], ffn_norm[0]], axis=1)
    gain_columns = jnp.pad(gain_columns, ((0, 0), (0, gap - 2)))
    enter_shard = jnp.concatenate([w_query[0], w_key[0], w_value[0], gain_columns], axis=1)
    enter_cut = enter_shard.shape[1] // 2
    leave_cut = w_out.shape[2] // 2
    low_shard = jnp.concatenate([enter_shard[:, :enter_cut], w_out[0, :, :leave_cut]], axis=1)
    high_shard = jnp.concatenate([enter_shard[:, enter_cut:], w_out[0, :, leave_cut:]], axis=1)
    lent = swap(on_core(high_shard, low_shard), "section", 1)
    dense_shards = (on_core(low_shard, lent), on_core(lent, high_shard))

    def gather_deep(shard):
        blocks = [shard] + [swap(shard, "fsdp", bit) for bit in range(1, n_fsdp)]
        return place_call(blocks, depth).reshape(-1, shard.shape[1])

    def join_square(blocks):
        return place_call(blocks, place).reshape(-1, blocks[0].shape[1])

    def gather_square(deep):
        return join_square(spread(deep))

    cut = hidden // 2
    unit_stack = jnp.concatenate(
        [
            jnp.concatenate(
                [w_gate[0, ..., :cut], w_up[0, ..., :cut], w_gate[0, ..., cut:], w_up[0, ..., cut:]],
                axis=2,
            ),
            w_down[0],
        ],
        axis=1,
    )
    if pieces == 2:
        unit_stack = jnp.stack(jnp.split(unit_stack, 2, axis=2), axis=1)
    unit_stack = unit_stack.reshape(n_ctx, 2, per_core, unit_rows, width // pieces)
    units_lent = swap(at(unit_stack, 1 - core, 1), "section", 1)
    unit_stacks = jnp.stack(own_other(at(unit_stack, core, 1), units_lent), axis=1)

    def deal_units(stack):
        blocks = [at(stack, place)]
        blocks += [swap(at(stack, place ^ bit), "ctx", bit) for bit in range(1, n_ctx)]
        dealt = place_call(blocks, place)
        return (dealt[:, 0], dealt[:, 1])

    ring = list(range(0, n_fsdp, 2)) + list(range(1, n_fsdp, 2))[::-1]
    ring_steps = [(ring[i], ring[(i + 1) % n_fsdp]) for i in range(n_fsdp)]
    ring_table = [[ring[ring.index(z) - i] for i in range(n_fsdp)] for z in range(n_fsdp)]
    behind_here = at(jnp.array(ring_table, jnp.uint32), depth)

    def ring_send(moved):
        return [blocks + [lax.ppermute(blocks[-1], "fsdp", ring_steps)] for blocks in moved]

    def own_units(blocks):
        return [order_call(blocks, behind_here, unit) for unit in range(per_core)]

    def pair_units(mine):
        other = [swap(part, "section", 1) for part in mine]
        units = list(mine) + other
        if pieces == 2:
            units = [jnp.concatenate(own_other(mine[0], other[0]), axis=2)]
        if aligned:
            return [[unit] for unit in units]
        return [
            [unit[:, :shard_rows].reshape(-1, width), unit[:, shard_rows:].reshape(-1, width)]
            for unit in units
        ]

    def cut_units(grads):
        if aligned:
            units = [unit for (unit,) in grads]
        else:
            units = [
                jnp.concatenate(
                    [part.reshape(n_ctx * n_fsdp, -1, width) for part in parts], axis=1
                )
                for parts in grads
            ]
        if pieces == 1:
            return (units[:per_core], units[per_core:])
        own, other = own_other(*jnp.split(units[0], 2, axis=2))
        return ([own], [other])

    def ring_part(terms, behind):
        spot = behind_here[behind % n_fsdp]
        return sum(at(term, spot, 1).astype(f32) for term in terms)

    def ring_start(own, received):
        terms = [part.reshape((n_ctx, n_fsdp) + part.shape[1:]) for part in (own, received)]
        return (terms, ring_part(terms, 1).astype(bf16))

    def ring_move(state):
        return [(terms, lax.ppermute(moving, "fsdp", ring_steps)) for terms, moving in state]

    def ring_add(state, step):
        return [
            (terms, (moved.astype(f32) + ring_part(terms, step + 1)).astype(bf16))
            for terms, moved in state
        ]

    def ring_step(state, step):
        return ring_add(ring_move(state), step)

    def ring_last(state):
        state = ring_add(state, 2)
        for step in range(3, n_fsdp - 1):
            state = ring_step(state, step)
        return ring_move(state)

    def ring_rest(state, first):
        for step in range(first, n_fsdp):
            state = ring_step(state, step)
        return [moving for _, moving in state]

    def scatter_units(moved):
        whole = jnp.stack(moved, axis=1)
        blocks = [at(whole, place)]
        blocks += [swap(at(whole, place ^ bit), "ctx", bit) for bit in range(1, n_ctx)]
        return jnp.stack(blocks)

    def trade_square(own, received, bits):
        own, received = (part.reshape(n_ctx, -1, part.shape[1]) for part in (own, received))

        def part(bit):
            return at(own, place ^ bit).astype(f32) + at(received, place ^ bit).astype(f32)

        return [part(bit) if bit == 0 else swap(part(bit).astype(bf16), "ctx", bit) for bit in bits]

    def sum_square(parts):
        return sum(part.astype(f32) for part in parts).astype(bf16)

    def reduce_deep(mine):
        mine = mine.reshape(n_fsdp, shard_rows, -1)
        total = at(mine, depth).astype(f32)
        for bit in range(1, n_fsdp):
            total = total + swap(at(mine, depth ^ bit), "fsdp", bit).astype(f32)
        return total

    if pieces == 1:
        units_here = jnp.arange(per_core, dtype=jnp.uint32)
        units_here = jnp.concatenate(
            [core * per_core + units_here, (1 - core) * per_core + units_here]
        )
    else:
        units_here = jnp.zeros((1,), jnp.uint32)
    named = (place * own_experts + units_here).astype(f32)
    matches = info[:, None, :, :TOP] == named[None, :, None, None, None]
    hits = jnp.any(matches, axis=3)
    shares = jnp.sum(jnp.where(matches, info[:, None, :, TOP:], 0.0), axis=3)
    earlier = jnp.arange(rows)[:, None] < jnp.arange(rows)[None, :]
    rank = dot("ledr,rq->ledq", hits.astype(bf16), earlier.astype(bf16))
    slots = jnp.arange(capacity, dtype=f32)
    picks = hits[:, :, :, None, :] & (rank[:, :, :, None, :] == slots[:, None])
    slot_shares = jnp.sum(jnp.where(picks, shares[:, :, :, None, :], 0.0), axis=-1, keepdims=True)
    picks = picks.astype(bf16)

    order = place.astype(jnp.int32) ^ jnp.arange(n_ctx, dtype=jnp.int32)
    block_ids = jnp.take(block_of.reshape(n_ctx, 2), order, axis=0)
    block_ids = block_ids.reshape(-1)

    def gains_of(halves):
        pair = on_core(halves[1][:, -gap : 2 - gap], halves[0][:, -gap : 2 - gap])
        pair = pair.astype(f32).T
        return (pair[:1], pair[1:])

    near = 1 + len(early)
    parts = (slice(0, near), slice(near, n_ctx))

    def experts(layer, blocks, weights, answer, beside=lambda: []):
        kept, arrived = ({}, [])
        back = {}
        for index, part in enumerate(parts):
            rows_here = blocks[part]
            if index:
                back[0], rows_here = tie(back[0], rows_here)
                arrived = [swap(block, "ctx", bit) for bit, block in zip(early, back[0][1:])]
            back[index] = []
            for j in range(own_experts):
                back[index], kept[index, j] = expert_call(
                    picks[layer, j, part],
                    slot_shares[layer, j, part],
                    rows_here,
                    weights[j],
                    shard_rows,
                    hidden,
                    back[index],
                    3 if index == 0 else 1,
                )
        if not answer:
            return (back[0] + back[1], kept)
        back[1], arrived, found = tie(back[1], arrived, beside())
        arrived += [swap(block, "ctx", bit) for bit, block in zip(late, back[1])]
        return (back[0][:1] + arrived, kept, found)

    def experts_back(layer, blocks, weights, kept, beside, beside_later):
        back, saved = ({}, {})
        for index, part in enumerate(parts):
            rows_here = blocks[part]
            if index:
                back[0], rows_here, found = tie(back[0], rows_here, beside())
                arrived = [swap(block, "ctx", bit) for bit, block in zip(early, back[0][1:])]
            back[index] = []
            for j in range(own_experts):
                back[index], saved[index, j] = expert_back_call(
                    picks[layer, j, part],
                    slot_shares[layer, j, part],
                    rows_here,
                    kept[index, j],
                    weights[j],
                    shard_rows,
                    back[index],
                    4 if index == 0 else 1,
                )
        back[1], arrived, saved = tie(back[1], arrived, saved)
        arrived += [swap(block, "ctx", bit) for bit, block in zip(late, back[1])]
        grads = {}
        for j in reversed(range(own_experts)):
            picked = [kept[index, j][0] for index in range(2)]
            both = [saved[index, j] for index in range(2)]
            grads[j] = expert_grads_call(picked, both, weights[j], shard_rows)
        arrived, grads, later = tie(arrived, grads, beside_later(found))
        own, other = cut_units([grads[j] for j in range(own_experts)])
        received = [swap(part, "section", 1) for part in other]
        return (back[0][:1] + arrived, own, received, found, later)

    def keep_own(first, second):
        other = swap(on_core(second, first), "section", 1)
        return own_other(on_core(first, second), other)

    dense_first, dense_second = dense_shards
    deep = gather_deep(jnp.concatenate([dense_first, dense_second[:, :enter_cut]], axis=1))
    dealt_first, dealt_second = deal_units(unit_stacks)
    deep, dealt_first, dealt_second, picks, dense_second = tie(
        deep, dealt_first, dealt_second, picks, dense_second
    )
    dense_blocks, moved, leave_shard, enter_shard = tie(
        spread(deep[:, :enter_cut]),
        ring_send([[dealt_first]]),
        deep[:, enter_cut : enter_cut + leave_cut],
        deep[:, enter_cut + leave_cut :],
    )
    leave_blocks = [leave_shard] + send(leave_shard, early)
    enter_own = join_square(dense_blocks)
    enter_first = (enter_own, swap(enter_own, "section", 1))

    first_gains = gains_of(enter_first)
    first_in = after(at(tokens, core)[0], slot_shares)
    _, first_normed, first_entered = enter_call(core, [first_in], first_gains[0], enter_first)
    first_entered, leave_blocks = tie(first_entered, leave_blocks)
    key_value = first_entered[:, qw : qw + 2 * kw]
    first_kv, moved, leave_shard, enter_shard = tie(
        jnp.concatenate(spread(key_value)), ring_send(moved), leave_shard, enter_shard
    )
    enter_blocks = [enter_shard] + send(enter_shard, early)
    first_attended = attend_call(block_ids, first_entered, first_kv)
    for _ in range(2, n_fsdp - 1):
        moved = ring_send(moved)
    first_attended, leave_blocks, dealt_second, moved, enter_blocks, enter_shard, dense_second = tie(
        first_attended,
        leave_blocks + send(leave_shard, late),
        dealt_second,
        moved,
        enter_blocks,
        enter_shard,
        dense_second,
    )
    leave_own = join_square(leave_blocks)
    leave_first = (leave_own, swap(leave_own, "section", 1))
    first_mid, ffn_normed = leave_call(core, first_in, first_attended, first_gains[1], leave_first)
    first_units = own_units(moved[0])
    ffn_normed, enter_blocks, dense_second = tie(
        ffn_normed, enter_blocks + send(enter_shard, late), dense_second
    )
    blocks = spread(ffn_normed)
    blocks[:near], moved, first_units, enter_blocks, leave_shard = tie(
        blocks[:near],
        ring_send([[dealt_second]]),
        first_units,
        enter_blocks,
        dense_second[:, enter_cut:],
    )
    enter_own = join_square(enter_blocks)
    enter_second = (enter_own, swap(enter_own, "section", 1))
    first_weights = pair_units(first_units)
    returned, first_kept, (moved, leave_shard) = experts(
        0, blocks, first_weights, True, lambda: (ring_send(moved), after(leave_shard, moved))
    )
    returned, moved, leave_shard = tie(returned, moved, gather_deep(leave_shard))
    moved = ring_send(moved)
    leave_blocks = [leave_shard] + send(leave_shard, early)

    second_gains = gains_of(enter_second)
    second_in, second_normed, second_entered = enter_call(
        core, [first_mid] + returned, second_gains[0], enter_second
    )
    second_entered, leave_blocks, moved = tie(second_entered, leave_blocks, moved)
    key_value = second_entered[:, qw : qw + 2 * kw]
    for _ in range(4, n_fsdp):
        moved = ring_send(moved)
    second_kv, leave_shard = tie(jnp.concatenate(spread(key_value)), leave_shard)
    second_attended = attend_call(block_ids, second_entered, second_kv)
    second_attended, leave_blocks, moved = tie(
        second_attended, leave_blocks + send(leave_shard, late), moved
    )
    leave_own = join_square(leave_blocks)
    leave_second = (leave_own, swap(leave_own, "section", 1))
    second_mid, ffn_normed = leave_call(
        core, second_in, second_attended, second_gains[1], leave_second
    )
    second_weights = pair_units(own_units(moved[0]))
    blocks = spread(ffn_normed)
    second_returned, second_kept = experts(1, blocks, second_weights, False)
    cotangent = after(at(out_grad, core)[0], second_returned[:near])
    cot_blocks = spread(cotangent)
    cot_blocks[:near], second_returned[near:] = tie(cot_blocks[:near], second_returned[near:])

    returned, own, received, second_returned, _ = experts_back(
        1, cot_blocks, second_weights, second_kept, lambda: second_returned, lambda found: ()
    )
    units_moving = [ring_start(*pair) for pair in zip(own, received)]
    returned, second_returned = tie(returned, second_returned)
    second_parts = gather_back(second_returned)
    after_rows, term, d_attended, *grads = leave_back_call(
        core,
        returned,
        second_gains[1],
        second_mid,
        cotangent,
        second_attended,
        leave_second,
    )
    leave_grads = (grads[0], swap(grads[1], "section", 1))
    d_queries, d_key_value = attend_back_call(block_ids, second_entered, second_kv, d_attended)
    d_queries, d_key_value, leave_grads, second_parts = tie(
        d_queries, d_key_value, leave_grads, second_parts
    )
    second_out = second_mid + sum(part.astype(f32) for part in second_parts)
    d_key_value = gather_back(d_key_value)
    leave_parts = trade_square(*leave_grads, [0, *early])
    second_entry, cotangent, *grads = enter_back_call(
        core,
        d_queries,
        d_key_value,
        second_gains[0],
        second_in,
        second_normed,
        after_rows,
        term,
        enter_second,
    )
    cotangent, grads, units_moving, leave_parts, layer_rows = tie(
        cotangent,
        grads,
        ring_move(units_moving),
        leave_parts,
        (second_in, second_out.astype(bf16)),
    )
    units_moving = ring_add(units_moving, 1)
    enter_grads = (grads[0], swap(grads[1], "section", 1))

    blocks = spread(cotangent)
    blocks[:near], enter_grads = tie(blocks[:near], enter_grads)
    returned, own, received, (_, layer_outs), units_moving = experts_back(
        0,
        blocks,
        first_weights,
        first_kept,
        lambda: (ring_move(units_moving), keep_own(*after(layer_rows, blocks[:near]))),
        lambda found: ring_last(found[0]),
    )
    returned, leave_grads, enter_grads = tie(returned, leave_grads, enter_grads)
    second_moved = [moving for _, moving in ring_add(units_moving, n_fsdp - 1)]
    units_moving = [ring_start(*pair) for pair in zip(own, received)]
    leave_parts = leave_parts + trade_square(*leave_grads, late)
    after_rows, term, d_attended, *grads = leave_back_call(
        core,
        returned,
        first_gains[1],
        first_mid,
        cotangent,
        first_attended,
        leave_first,
    )
    d_attended, enter_grads = tie(d_attended, enter_grads)
    enter_parts = trade_square(*enter_grads, [0, *early])
    leave_grads = (grads[0], swap(grads[1], "section", 1))
    d_queries, d_key_value = attend_back_call(block_ids, first_entered, first_kv, d_attended)
    d_queries, d_key_value, leave_grads, enter_parts, enter_grads, leave_parts = tie(
        d_queries, d_key_value, leave_grads, enter_parts, enter_grads, leave_parts
    )
    d_key_value, enter_grads, leave_grads = tie(
        gather_back(d_key_value), enter_grads, leave_grads
    )
    enter_parts = enter_parts + trade_square(*enter_grads, late)
    first_entry, _, *grads = enter_back_call(
        core,
        d_queries,
        d_key_value,
        first_gains[0],
        first_in,
        first_normed,
        after_rows,
        term,
        enter_first,
    )
    grads, units_moving, enter_parts, leave_grads = tie(
        grads, ring_move(units_moving), enter_parts, leave_grads
    )
    second_moving = [sum_square(parts) for parts in (enter_parts, leave_parts)]
    units_moving = ring_move(ring_add(units_moving, 1))
    enter_grads = (grads[0], swap(grads[1], "section", 1))
    leave_parts = trade_square(*leave_grads, range(n_ctx))
    enter_parts, leave_parts, units_moving = tie(
        trade_square(*enter_grads, range(n_ctx)), leave_parts, units_moving
    )
    units_moving = ring_add(units_moving, 2)
    first_moving = [sum_square(parts) for parts in (enter_parts, leave_parts)]
    dense = reduce_deep(jnp.concatenate(first_moving + second_moving, axis=1))
    first_dense, second_dense = jnp.split(dense, 2, axis=1)
    scattered = scatter_units(ring_rest(units_moving, 3) + second_moved)
    first_scattered, second_scattered = (scattered[:, :per_core], scattered[:, per_core:])

    layer_out = jnp.stack(layer_outs)
    input_grads = jnp.stack(keep_own(first_entry, second_entry))
    low_dense, high_dense = keep_own(first_dense, second_dense)
    enter_grad = jnp.concatenate([low_dense[:, :enter_cut], high_dense[:, :enter_cut]], axis=1)
    grad_out = jnp.concatenate([low_dense[:, enter_cut:], high_dense[:, enter_cut:]], axis=1)
    grad_gains = enter_grad[:, qw + 2 * kw :]
    mine = on_core(first_scattered, second_scattered)
    other = swap(on_core(second_scattered, first_scattered), "section", 1)
    if aligned and pieces == 1:
        grad_gate, grad_up, grad_down = finish_call(mine, other, shard_rows, hidden, place, core)
    else:
        sides = [jnp.take(part, order, axis=0) for part in own_other(mine, other)]
        if pieces == 1:
            whole = jnp.stack(sides, axis=1).reshape(EXPERTS, unit_rows, width)
        else:
            whole = jnp.concatenate([side[:, 0] for side in sides], axis=2)
        pairs = whole[:, :shard_rows].astype(f32).reshape(EXPERTS, shard_rows, 2, 2, cut)
        grad_gate = pairs[:, :, :, 0].reshape(EXPERTS, shard_rows, hidden)
        grad_up = pairs[:, :, :, 1].reshape(EXPERTS, shard_rows, hidden)
        grad_down = whole[:, shard_rows:].astype(f32)
    return (
        layer_out[None, :, None],
        input_grads[None, :, None],
        grad_gains[:, 0][None],
        enter_grad[:, :qw][None],
        enter_grad[:, qw : qw + kw][None],
        enter_grad[:, qw + kw : qw + 2 * kw][None],
        grad_out[None],
        grad_gains[:, 1][None],
        grad_gate[None],
        grad_up[None],
        grad_down[None],
    )


def solution(mesh):
    rows_placed = P(None, "fsdp", "ctx", None)
    kept_placed = P("section", None, "fsdp", "ctx", None)
    gain_placed = P("section", ("ctx", "fsdp"))
    dense_placed = P("section", ("ctx", "fsdp"), None)
    expert_placed = P("section", None, ("ctx", "fsdp"), None)
    dense_all = (dense_placed,) * 4
    expert_all = (expert_placed,) * 3
    layer_placed = (gain_placed,) + dense_all + (gain_placed,) + expert_all
    return jax.shard_map(
        body,
        mesh=mesh,
        in_specs=(rows_placed, P(), kept_placed, kept_placed) + layer_placed + (rows_placed,),
        out_specs=(kept_placed, kept_placed) + layer_placed,
        check_vma=False,
    )
```

```python
import functools

import jax
import jax.numpy as jnp
from jax import lax
from jax.experimental import pallas as pl
from jax.experimental.pallas import tpu as pltpu
from jax.sharding import PartitionSpec as P

QH = 12
KVH = 2
HD = 128
GROUP = QH // KVH
TOP = 4
EXPERTS = 8
bf16 = jnp.bfloat16
f32 = jnp.float32


epsilon = 1e-06
masked_out = -1e30
gap = 256


def swap(value, axis, bit):
    count = lax.axis_size(axis)
    return lax.ppermute(value, axis, [(source, source ^ bit) for source in range(count)])


def tie(*values):
    return lax.optimization_barrier(values)


def after(value, earlier):
    return tie(value, earlier)[0]


def at(value, index, axis=0):
    return lax.dynamic_index_in_dim(value, index, axis, keepdims=False)


def dot(spec, left, right, kind=f32):
    return jnp.einsum(spec, left, right, preferred_element_type=kind)


def cost(micros):
    return pl.CostEstimate(
        flops=int(micros * 1e9), bytes_accessed=int(micros * 3e6), transcendentals=0
    )


def kernel_params():
    return pltpu.CompilerParams(vmem_limit_bytes=56 * 1024 * 1024)


def nt(left, right):
    return lax.dot_general(left, right, (((1,), (1,)), ((), ())), preferred_element_type=f32)


def nn(left, right):
    return jnp.dot(left, right, preferred_element_type=f32)


def head_rows(ref):
    return jnp.concatenate([ref[:, i * HD : (i + 1) * HD] for i in range(GROUP)], axis=0)


def softmax_rows(ids_ref, queries, keys, half, own):
    scores = nt(queries, keys) * HD ** (-0.5)
    tall, wide = scores.shape
    row = lax.broadcasted_iota(jnp.int32, (half, 1), 0)
    row = jnp.concatenate([row] * (tall // half), axis=0) + ids_ref[own] * half
    lane = lax.broadcasted_iota(jnp.int32, (1, half), 1)
    column = [lane + ids_ref[block] * half for block in range(wide // half)]
    column = jnp.concatenate(column, axis=1)
    scores = jnp.where(row >= column, scores, masked_out)
    shifted = jnp.exp(scores - jnp.max(scores, axis=1, keepdims=True))
    return shifted / jnp.sum(shifted, axis=1, keepdims=True)


def attend_kernel(ids_ref, query_ref, key_ref, value_ref, out_ref):
    half = query_ref.shape[0]
    probs = softmax_rows(ids_ref, head_rows(query_ref), key_ref[...], half, pl.program_id(1))
    out = nn(probs.astype(bf16), value_ref[...]).astype(bf16)
    for i in range(GROUP):
        out_ref[:, i * HD : (i + 1) * HD] = out[i * half : (i + 1) * half]


def attend_specs(rows, seq_len):
    half = rows // 2
    by_head = pl.BlockSpec((half, GROUP * HD), lambda g, h, ids: (h, g))
    keys = pl.BlockSpec((seq_len, HD), lambda g, h, ids: (0, g))
    values = pl.BlockSpec((seq_len, HD), lambda g, h, ids: (0, KVH + g))
    return by_head, keys, values


def attend_call(ids, queries, key_value):
    rows, seq_len = (queries.shape[0], key_value.shape[0])
    by_head, keys, values = attend_specs(rows, seq_len)
    return pl.pallas_call(
        attend_kernel,
        grid_spec=pltpu.PrefetchScalarGridSpec(
            num_scalar_prefetch=1,
            grid=(KVH, 2),
            in_specs=[by_head, keys, values],
            out_specs=by_head,
        ),
        out_shape=jax.ShapeDtypeStruct((rows, QH * HD), bf16),
        compiler_params=kernel_params(),
        cost_estimate=cost(1),
        name="attend",
    )(ids, queries, key_value, key_value)


def attend_back_kernel(ids_ref, query_ref, key_ref, value_ref, cot_ref, dq_ref, *refs):
    out, (dk_ref, dv_ref) = (refs[:-2], refs[-2:])
    half = query_ref.shape[0]
    group, own = (pl.program_id(0), pl.program_id(1))
    queries, cot = (head_rows(query_ref), head_rows(cot_ref))
    probs = softmax_rows(ids_ref, queries, key_ref[...], half, own)
    d_probs = nt(cot, value_ref[...])
    inner = jnp.sum(probs * d_probs, axis=1, keepdims=True)
    d_scores = (probs * (d_probs - inner)).astype(bf16)
    d_queries = (nn(d_scores, key_ref[...]) * HD ** (-0.5)).astype(bf16)
    for i in range(GROUP):
        dq_ref[:, i * HD : (i + 1) * HD] = d_queries[i * half : (i + 1) * half]
    d_keys = nn(d_scores.T, queries) * HD ** (-0.5)
    d_values = nn(probs.astype(bf16).T, cot)

    @pl.when(own == 0)
    def _():
        dk_ref[...] = d_keys
        dv_ref[...] = d_values

    @pl.when(own != 0)
    def _():
        rows = 2 * half
        for block, ref in enumerate(out):
            part = slice(block * rows, (block + 1) * rows)
            for first, total, last in ((0, dk_ref, d_keys), (KVH * HD, dv_ref, d_values)):
                columns = pl.ds(pl.multiple_of(first + group * HD, HD), HD)
                ref[:, columns] = (total[part, :] + last[part]).astype(bf16)


def attend_back_call(ids, queries, key_value, cot):
    rows, seq_len = (queries.shape[0], key_value.shape[0])
    by_head, keys, values = attend_specs(rows, seq_len)
    blocks = seq_len // rows
    wide = 2 * KVH * HD
    result = pl.pallas_call(
        attend_back_kernel,
        grid_spec=pltpu.PrefetchScalarGridSpec(
            num_scalar_prefetch=1,
            grid=(KVH, 2),
            in_specs=[by_head, keys, values, by_head],
            out_specs=[by_head] + [pl.BlockSpec((rows, wide), lambda g, h, ids: (0, 0))] * blocks,
            scratch_shapes=[pltpu.VMEM((seq_len, HD), f32)] * 2,
        ),
        out_shape=[jax.ShapeDtypeStruct((rows, QH * HD), bf16)]
        + [jax.ShapeDtypeStruct((rows, wide), bf16)] * blocks,
        compiler_params=kernel_params(),
        cost_estimate=cost(1),
        name="attend_back",
    )(ids, queries, key_value, key_value, cot)
    return (result[0], result[1:])


def gelu_parts(gate):
    root = 0.7978845608028654
    inner = root * (gate + 0.044715 * gate * gate * gate)
    bent = jnp.tanh(inner)
    value = 0.5 * gate * (1.0 + bent)
    slope = root * (1.0 + 3.0 * 0.044715 * gate * gate)
    return value, 0.5 * (1.0 + bent) + 0.5 * gate * (1.0 - bent * bent) * slope


def give_back(pick_ref, total_ref, share_ref, before, out):
    blocks, capacity, _ = pick_ref.shape
    for d in range(blocks):
        part = total_ref[d * capacity : (d + 1) * capacity, :]
        if share_ref is not None:
            part = part * share_ref[d]
        back = nn(pick_ref[d].T, part.astype(bf16))
        if before:
            back = back + before[d][...]
        out[d][...] = back.astype(out[d].dtype)


def flat(ref):
    value = ref[...]
    return value.reshape(-1, value.shape[-1])


def add_up(total_ref, part, step):
    @pl.when(step == 0)
    def _():
        total_ref[...] = part

    @pl.when(step != 0)
    def _():
        total_ref[...] += part


def expert_kernel(blocks, adds, pick_ref, share_ref, gate_ref, up_ref, down_ref, *refs):
    rows, refs = (refs[:blocks], refs[blocks:])
    before, refs = (refs[: blocks * adds], refs[blocks * adds :])
    out, (picked_ref, gate_pre_ref, up_pre_ref, total_ref) = (refs[:blocks], refs[blocks:])
    step = pl.program_id(0)
    capacity = pick_ref.shape[1]

    @pl.when(step == 0)
    def _():
        for d in range(blocks):
            block = nn(pick_ref[d], rows[d][...]).astype(bf16)
            picked_ref[d * capacity : (d + 1) * capacity, :] = block

    gate_pre = nn(picked_ref[...], flat(gate_ref))
    up_pre = nn(picked_ref[...], flat(up_ref))
    gate_pre_ref[...] = gate_pre
    up_pre_ref[...] = up_pre
    active = (gelu_parts(gate_pre)[0] * up_pre).astype(bf16)
    add_up(total_ref, nn(active, flat(down_ref)), step)

    @pl.when(step == pl.num_programs(0) - 1)
    def _():
        give_back(pick_ref, total_ref, share_ref, before, out)


def whole_spec(shape):
    return pl.BlockSpec(
        shape, lambda step: (0,) * len(shape), pipeline_mode=pl.Buffered(buffer_count=1)
    )


def weight_operands(weights, deep, cut):
    if len(weights) == 1:
        unit = weights[0]
        shards, tall, width = unit.shape
        specs = [
            pl.BlockSpec((shards, deep, cut), lambda step: (0, 0, 2 * step)),
            pl.BlockSpec((shards, deep, cut), lambda step: (0, 0, 2 * step + 1)),
            pl.BlockSpec(
                (shards // 2, tall - deep, width), lambda step: (step, deep // (tall - deep), 0)
            ),
        ]
        return specs, [unit, unit, unit]
    pair, down = weights
    specs = [
        pl.BlockSpec((pair.shape[0], cut), lambda step: (0, 2 * step)),
        pl.BlockSpec((pair.shape[0], cut), lambda step: (0, 2 * step + 1)),
        pl.BlockSpec((cut, down.shape[1]), lambda step: (step, 0)),
    ]
    return specs, [pair, pair, down]


def expert_call(picks, shares, rows, weights, deep, hidden, before, micros):
    blocks, capacity, _ = picks.shape
    width, cut, tall = (rows[0].shape[1], hidden // 2, blocks * capacity)
    columns = pl.BlockSpec((tall, cut), lambda step: (0, step))
    row_specs = [whole_spec(block.shape) for block in rows]
    specs, operands = weight_operands(weights, deep, cut)
    result = pl.pallas_call(
        functools.partial(expert_kernel, blocks, 1 if before else 0),
        grid=(2,),
        in_specs=[whole_spec(picks.shape), whole_spec(shares.shape)]
        + specs
        + row_specs * (2 if before else 1),
        out_specs=row_specs + [whole_spec((tall, width)), columns, columns],
        out_shape=[jax.ShapeDtypeStruct(block.shape, bf16) for block in rows]
        + [
            jax.ShapeDtypeStruct((tall, width), bf16),
            jax.ShapeDtypeStruct((tall, hidden), f32),
            jax.ShapeDtypeStruct((tall, hidden), f32),
        ],
        scratch_shapes=[pltpu.VMEM((tall, width), f32)],
        compiler_params=kernel_params(),
        cost_estimate=cost(micros),
        name="expert",
    )(picks, shares, *operands, *rows, *before)
    return (list(result[:blocks]), list(result[blocks:]))


def expert_back_kernel(
    blocks, adds, pick_ref, share_ref, gate_pre_ref, up_pre_ref, gate_ref, up_ref, down_ref, *refs
):
    rows, refs = (refs[:blocks], refs[blocks:])
    before, refs = (refs[: blocks * adds], refs[blocks * adds :])
    out, refs = (refs[:blocks], refs[blocks:])
    slots_ref, d_gate_ref, d_up_ref, active_ref, total_ref = refs
    step = pl.program_id(0)
    capacity = pick_ref.shape[1]

    @pl.when(step == 0)
    def _():
        for d in range(blocks):
            block = nn(pick_ref[d], rows[d][...]) * share_ref[d]
            slots_ref[d * capacity : (d + 1) * capacity, :] = block.astype(bf16)

    d_active = nt(slots_ref[...], flat(down_ref))
    value, slope = gelu_parts(gate_pre_ref[...])
    up_pre = up_pre_ref[...]
    d_gate = (d_active * up_pre * slope).astype(bf16)
    d_up = (d_active * value).astype(bf16)
    active_ref[...] = (value * up_pre).astype(bf16)
    d_gate_ref[...] = d_gate
    d_up_ref[...] = d_up
    add_up(total_ref, nt(d_gate, flat(gate_ref)) + nt(d_up, flat(up_ref)), step)

    @pl.when(step == pl.num_programs(0) - 1)
    def _():
        give_back(pick_ref, total_ref, None, before, out)


def expert_back_call(picks, shares, rows, kept, weights, deep, before, micros):
    _, gate_pre, up_pre = kept
    blocks, capacity, _ = picks.shape
    width, (tall, hidden) = (rows[0].shape[1], gate_pre.shape)
    cut = hidden // 2
    columns = pl.BlockSpec((tall, cut), lambda step: (0, step))
    row_specs = [whole_spec(block.shape) for block in rows]
    specs, operands = weight_operands(weights, deep, cut)
    result = pl.pallas_call(
        functools.partial(expert_back_kernel, blocks, 1 if before else 0),
        grid=(2,),
        in_specs=[whole_spec(picks.shape), whole_spec(shares.shape), columns, columns]
        + specs
        + row_specs * (2 if before else 1),
        out_specs=row_specs + [whole_spec((tall, width)), columns, columns, columns],
        out_shape=[jax.ShapeDtypeStruct(block.shape, bf16) for block in rows]
        + [jax.ShapeDtypeStruct((tall, width), bf16)]
        + [jax.ShapeDtypeStruct((tall, hidden), bf16)] * 3,
        scratch_shapes=[pltpu.VMEM((tall, width), f32)],
        compiler_params=kernel_params(),
        cost_estimate=cost(micros),
        name="expert_back",
    )(picks, shares, gate_pre, up_pre, *operands, *rows, *before)
    return (list(result[:blocks]), list(result[blocks:]))


def expert_grads_kernel(parts, deep, *refs):
    picked, slots, d_gate, d_up, active = (refs[i * parts : (i + 1) * parts] for i in range(5))
    grad_refs, turned_ref = (refs[5 * parts : -1], refs[-1])
    step = pl.program_id(0)

    def below(some):
        return jnp.concatenate([ref[...] for ref in some], axis=0)

    @pl.when(step == 0)
    def _():
        turned_ref[...] = below(picked).T

    grad_gate = nn(turned_ref[...], below(d_gate)).astype(bf16)
    grad_up = nn(turned_ref[...], below(d_up)).astype(bf16)
    grad_down = nn(below(active).T, below(slots)).astype(bf16)
    cut = grad_gate.shape[1]
    if len(grad_refs) == 1:
        unit_ref = grad_refs[0]
        shards, tall, width = unit_ref.shape
        for side in range(2):

            @pl.when(step == side)
            def _():
                left, some = (2 * side * cut, shards // 2)
                unit_ref[:, :deep, left : left + cut] = grad_gate.reshape(shards, deep, cut)
                left = left + cut
                unit_ref[:, :deep, left : left + cut] = grad_up.reshape(shards, deep, cut)
                rest = grad_down.reshape(some, tall - deep, width)
                unit_ref[side * some : (side + 1) * some, deep:, :] = rest
    else:
        grad_refs[0][:, :cut] = grad_gate
        grad_refs[0][:, cut:] = grad_up
        grad_refs[1][...] = grad_down


def expert_grads_call(picked, saved, weights, deep):
    slots, d_gate, d_up, active = zip(*saved)
    width, hidden = (picked[0].shape[1], d_gate[0].shape[1])
    cut = hidden // 2
    columns = [pl.BlockSpec((part.shape[0], cut), lambda step: (0, step)) for part in picked]
    if len(weights) == 1:
        grad_specs = [whole_spec(weights[0].shape)]
    else:
        grad_specs = [
            pl.BlockSpec((width, 2 * cut), lambda step: (0, step)),
            pl.BlockSpec((cut, width), lambda step: (step, 0)),
        ]
    return list(
        pl.pallas_call(
            functools.partial(expert_grads_kernel, len(picked), deep),
            grid=(2,),
            in_specs=[whole_spec(part.shape) for part in picked] * 2 + columns * 3,
            out_specs=grad_specs,
            out_shape=[jax.ShapeDtypeStruct(part.shape, bf16) for part in weights],
            scratch_shapes=[pltpu.VMEM((width, sum(part.shape[0] for part in picked)), bf16)],
            compiler_params=kernel_params(),
            cost_estimate=cost(1),
            name="expert_grads",
        )(*picked, *slots, *d_gate, *d_up, *active)
    )


def norm_parts(value):
    scale = lax.rsqrt(jnp.mean(value * value, axis=1, keepdims=True) + epsilon)
    return scale, value * scale


def norm_back(grad, gain, value):
    scale, scaled = norm_parts(value)
    grown = grad * gain
    back = scale * (grown - scaled * jnp.mean(scaled * grown, axis=1, keepdims=True))
    return back, (grad * scaled).astype(bf16)


def add_all(refs):
    total = refs[0][...].astype(f32)
    for ref in refs[1:]:
        total = total + ref[...].astype(f32)
    return total


def side_offsets(core_ref, steps, cut):
    step, core = (pl.program_id(0), core_ref[0])
    own = pl.multiple_of((core * steps + step) * cut, cut)
    other = pl.multiple_of(((1 - core) * steps + step) * cut, cut)
    return own, other


def dense_call(kernel, core, steps, whole, halves, out, scratch, name, micros):
    cut = halves[0].shape[1] // steps

    def keep(shape):
        return pl.BlockSpec(
            shape, lambda step, core: (0,) * len(shape), pipeline_mode=pl.Buffered(buffer_count=1)
        )

    def tile(tall):
        return pl.BlockSpec((tall, cut), lambda step, core: (0, step))

    return pl.pallas_call(
        kernel,
        grid_spec=pltpu.PrefetchScalarGridSpec(
            num_scalar_prefetch=1,
            grid=(steps,),
            in_specs=[keep(part.shape) for part in whole] + [tile(halves[0].shape[0])] * 2,
            out_specs=[
                tile(part.shape[0]) if tiled else keep(part.shape) for part, tiled in out
            ],
            scratch_shapes=scratch,
        ),
        out_shape=[part for part, _ in out],
        compiler_params=kernel_params(),
        cost_estimate=cost(micros),
        name=name,
    )(core.astype(jnp.int32).reshape(1), *whole, *halves)


def shape_of(kind, *shape):
    return jax.ShapeDtypeStruct(shape, kind)


def enter_kernel(steps, terms, core_ref, gain_ref, *refs):
    parts, (own_ref, other_ref, sent_ref, normed_ref, out_ref) = (refs[:terms], refs[terms:])
    own, other = side_offsets(core_ref, steps, own_ref.shape[1])

    @pl.when(pl.program_id(0) == 0)
    def _():
        sent = add_all(parts).astype(bf16)
        sent_ref[...] = sent
        normed_ref[...] = (norm_parts(sent.astype(f32))[1] * gain_ref[...]).astype(bf16)

    cut = own_ref.shape[1]
    out_ref[:, pl.ds(own, cut)] = nn(normed_ref[...], own_ref[...]).astype(bf16)
    out_ref[:, pl.ds(other, cut)] = nn(normed_ref[...], other_ref[...]).astype(bf16)


def enter_call(core, parts, gain, halves):
    rows, width = parts[0].shape
    return dense_call(
        functools.partial(enter_kernel, 3, len(parts)),
        core,
        3,
        [gain] + parts,
        halves,
        [
            (shape_of(bf16, rows, width), False),
            (shape_of(bf16, rows, width), False),
            (shape_of(bf16, rows, 2 * halves[0].shape[1]), False),
        ],
        [],
        "enter",
        6,
    )


def leave_kernel(steps, core_ref, gain_ref, rows_ref, attended_ref, own_ref, other_ref,
                 mid_ref, normed_ref):
    cut = own_ref.shape[1]
    for start, ref in zip(side_offsets(core_ref, steps, cut), (own_ref, other_ref)):
        part = pl.ds(start, cut)
        mid_ref[:, part] = rows_ref[:, part].astype(f32) + nn(attended_ref[...], ref[...])

    @pl.when(pl.program_id(0) == steps - 1)
    def _():
        normed_ref[...] = (norm_parts(mid_ref[...])[1] * gain_ref[...]).astype(bf16)


def leave_call(core, rows_in, attended, gain, halves):
    rows, width = rows_in.shape
    return dense_call(
        functools.partial(leave_kernel, 2),
        core,
        2,
        [gain, rows_in, attended],
        halves,
        [(shape_of(f32, rows, width), False), (shape_of(bf16, rows, width), False)],
        [],
        "leave",
        5,
    )


def leave_back_kernel(steps, terms, core_ref, gain_ref, mid_ref, cot_ref, attended_ref, *refs):
    parts, refs = (refs[:terms], refs[terms:])
    own_ref, other_ref, after_ref, term_ref, d_attended_ref, *refs = refs
    own_grad_ref, other_grad_ref, branch_ref, turned_ref, total_ref = refs
    step, cut = (pl.program_id(0), own_ref.shape[1])

    @pl.when(step == 0)
    def _():
        back, term_ref[...] = norm_back(add_all(parts), gain_ref[...], mid_ref[...])
        back = back + cot_ref[...].astype(f32)
        after_ref[...] = back
        branch_ref[...] = back.astype(bf16)
        turned_ref[...] = attended_ref[...].T

    own, other = side_offsets(core_ref, steps, cut)
    d_own, d_other = (branch_ref[:, pl.ds(own, cut)], branch_ref[:, pl.ds(other, cut)])
    own_grad_ref[...] = nn(turned_ref[...], d_own).astype(bf16)
    other_grad_ref[...] = nn(turned_ref[...], d_other).astype(bf16)
    add_up(total_ref, nt(d_own, own_ref[...]) + nt(d_other, other_ref[...]), step)

    @pl.when(step == steps - 1)
    def _():
        d_attended_ref[...] = total_ref[...].astype(bf16)


def leave_back_call(core, parts, gain, mid, cotangent, attended, halves):
    rows, width = mid.shape
    half = (halves[0].shape[0], halves[0].shape[1])
    return dense_call(
        functools.partial(leave_back_kernel, 2, len(parts)),
        core,
        2,
        [gain, mid, cotangent, attended] + parts,
        halves,
        [
            (shape_of(f32, rows, width), False),
            (shape_of(bf16, rows, width), False),
            (shape_of(bf16, rows, width), False),
            (shape_of(bf16, *half), True),
            (shape_of(bf16, *half), True),
        ],
        [
            pltpu.VMEM((rows, width), bf16),
            pltpu.VMEM((width, rows), bf16),
            pltpu.VMEM((rows, width), f32),
        ],
        "leave_back",
        8,
    )


def enter_back_kernel(steps, terms, core_ref, gain_ref, rows_ref, normed_ref, after_ref, term_ref,
                      dq_ref, *refs):
    parts, refs = (refs[:terms], refs[terms:])
    own_ref, other_ref, entry_ref, sent_ref, own_grad_ref, other_grad_ref, *refs = refs
    entered_ref, turned_ref, total_ref = refs
    step, cut = (pl.program_id(0), own_ref.shape[1])
    rows, qw = dq_ref.shape

    @pl.when(step == 0)
    def _():
        entered_ref[:, :qw] = dq_ref[...]
        wide = parts[0].shape[1]
        entered_ref[:, qw : qw + wide] = add_all(parts).astype(bf16)
        entered_ref[:, qw + wide :] = jnp.zeros((rows, gap), bf16)
        turned_ref[...] = normed_ref[...].T

    own, other = side_offsets(core_ref, steps, cut)
    d_own, d_other = (entered_ref[:, pl.ds(own, cut)], entered_ref[:, pl.ds(other, cut)])
    own_grad_ref[...] = nn(turned_ref[...], d_own).astype(bf16)
    other_grad_ref[...] = nn(turned_ref[...], d_other).astype(bf16)
    add_up(total_ref, nt(d_own, own_ref[...]) + nt(d_other, other_ref[...]), step)

    @pl.when(step == steps - 1)
    def _():
        back, attn_term = norm_back(total_ref[...], gain_ref[...], rows_ref[...].astype(f32))
        back = back + after_ref[...]
        entry_ref[...] = back
        sent_ref[...] = back.astype(bf16)
        lane = lax.broadcasted_iota(jnp.int32, (rows, 128), 1)
        sums = nn(attn_term.T, (lane == 0).astype(bf16))
        sums = (sums + nn(term_ref[...].T, (lane == 1).astype(bf16))).astype(bf16)
        left = cut - gap

        @pl.when(core_ref[0] == 0)
        def _():
            other_grad_ref[:, left : left + 128] = sums

        @pl.when(core_ref[0] != 0)
        def _():
            own_grad_ref[:, left : left + 128] = sums


def enter_back_call(core, dq, parts, gain, rows_in, normed, after, term, halves):
    rows, width = rows_in.shape
    return dense_call(
        functools.partial(enter_back_kernel, 3, len(parts)),
        core,
        3,
        [gain, rows_in, normed, after, term, dq] + parts,
        halves,
        [
            (shape_of(f32, rows, width), False),
            (shape_of(bf16, rows, width), False),
            (shape_of(bf16, *halves[0].shape), True),
            (shape_of(bf16, *halves[0].shape), True),
        ],
        [
            pltpu.VMEM((rows, 2 * halves[0].shape[1]), bf16),
            pltpu.VMEM((width, rows), bf16),
            pltpu.VMEM((rows, width), f32),
        ],
        "enter_back",
        1,
    )


def place_kernel(count, joined, index_ref, *refs):
    step = pl.program_id(0)
    for bit in range(count):

        @pl.when(step == bit)
        def _():
            if joined:
                refs[count][...] = refs[bit][...]
            else:
                refs[count][0] = refs[bit][...]


def place_call(blocks, index):
    count = len(blocks)
    shape = blocks[0].shape
    zeros = (0,) * len(shape)
    joined = len(shape) == 2 and shape[0] % 16 == 0
    if joined:
        out_spec = pl.BlockSpec(shape, lambda step, at: (at[0] ^ step, 0))
        out_shape = (count * shape[0], shape[1])
    else:
        out_spec = pl.BlockSpec((1,) + shape, lambda step, at: (at[0] ^ step,) + zeros)
        out_shape = (count,) + shape
    return pl.pallas_call(
        functools.partial(place_kernel, count, joined),
        grid_spec=pltpu.PrefetchScalarGridSpec(
            num_scalar_prefetch=1,
            grid=(count,),
            in_specs=[pl.BlockSpec(shape, lambda step, at: zeros)] * count,
            out_specs=out_spec,
        ),
        out_shape=jax.ShapeDtypeStruct(out_shape, blocks[0].dtype),
        compiler_params=kernel_params(),
        cost_estimate=cost(2),
        name="place",
    )(index.astype(jnp.int32).reshape(1), *blocks)


def deal_kernel(count, index_ref, *refs):
    step = pl.program_id(0)
    for bit in range(count):

        @pl.when(step == bit)
        def _():
            for layer, ref in enumerate(refs[count:]):
                ref[0] = refs[bit][layer]


def deal_call(blocks, index):
    count = len(blocks)
    layers, *shape = blocks[0].shape
    shape = tuple(shape)
    zeros = (0,) * len(shape)
    return pl.pallas_call(
        functools.partial(deal_kernel, count),
        grid_spec=pltpu.PrefetchScalarGridSpec(
            num_scalar_prefetch=1,
            grid=(count,),
            in_specs=[pl.BlockSpec((layers,) + shape, lambda step, at: (0,) + zeros)] * count,
            out_specs=[pl.BlockSpec((1,) + shape, lambda step, at: (at[0] ^ step,) + zeros)]
            * layers,
        ),
        out_shape=[jax.ShapeDtypeStruct((count,) + shape, blocks[0].dtype)] * layers,
        compiler_params=kernel_params(),
        cost_estimate=cost(2),
        name="deal",
    )(index.astype(jnp.int32).reshape(1), *blocks)


def order_kernel(count, order_ref, *refs):
    step = pl.program_id(0)
    for i in range(count):

        @pl.when(step == i)
        def _():
            refs[count][:, 0] = refs[i][:, 0]


def order_call(blocks, order, unit):
    count = len(blocks)
    n_ctx, _, tall, wide = blocks[0].shape
    shape = (n_ctx, 1, tall, wide)
    source = pl.BlockSpec(
        shape, lambda step, at: (0, unit, 0, 0), pipeline_mode=pl.Buffered(buffer_count=1)
    )
    result = pl.pallas_call(
        functools.partial(order_kernel, count),
        grid_spec=pltpu.PrefetchScalarGridSpec(
            num_scalar_prefetch=1,
            grid=(count,),
            in_specs=[source] * count,
            out_specs=pl.BlockSpec(shape, lambda step, at: (0, at[step], 0, 0)),
        ),
        out_shape=jax.ShapeDtypeStruct((n_ctx, count, tall, wide), bf16),
        compiler_params=kernel_params(),
        cost_estimate=cost(4),
        name="order",
    )(order.astype(jnp.int32), *blocks)
    return result.reshape(n_ctx * count, tall, wide)


def finish_kernel(deep, index_ref, own_ref, other_ref, gate_ref, up_ref, down_ref):
    side = pl.program_id(1)
    wide = gate_ref.shape[2] // 2

    def write(source):
        for half in range(2):
            left, target = (2 * half * wide, slice(half * wide, (half + 1) * wide))
            gate_ref[:, :, target] = source[0, :, :deep, left : left + wide].astype(f32)
            left = left + wide
            up_ref[:, :, target] = source[0, :, :deep, left : left + wide].astype(f32)
        down_ref[...] = source[0, :, deep:, :].astype(f32)

    @pl.when(side == index_ref[1])
    def _():
        write(own_ref)

    @pl.when(side != index_ref[1])
    def _():
        write(other_ref)


def finish_call(own, other, deep, hidden, place, core):
    n_ctx, units, tall, width = own.shape
    experts = 2 * n_ctx * units
    source = pl.BlockSpec((1, units, tall, width), lambda bit, side, at: (bit, 0, 0, 0))
    target = lambda bit, side, at: (2 * (at[0] ^ bit) + side, 0, 0)
    return pl.pallas_call(
        functools.partial(finish_kernel, deep),
        grid_spec=pltpu.PrefetchScalarGridSpec(
            num_scalar_prefetch=1,
            grid=(n_ctx, 2),
            in_specs=[source, source],
            out_specs=[
                pl.BlockSpec((units, deep, hidden), target),
                pl.BlockSpec((units, deep, hidden), target),
                pl.BlockSpec((units, tall - deep, width), target),
            ],
        ),
        out_shape=[
            jax.ShapeDtypeStruct((experts, deep, hidden), f32),
            jax.ShapeDtypeStruct((experts, deep, hidden), f32),
            jax.ShapeDtypeStruct((experts, tall - deep, width), f32),
        ],
        compiler_params=kernel_params(),
        cost_estimate=cost(8),
        name="finish",
    )(jnp.stack([place, core]).astype(jnp.int32), own, other)


def body(
    tokens,
    block_of,
    routes,
    combine,
    attn_norm,
    w_query,
    w_key,
    w_value,
    w_out,
    ffn_norm,
    w_gate,
    w_up,
    w_down,
    out_grad,
):
    rows = tokens.shape[2]
    width = tokens.shape[3]
    half = rows // 2
    n_ctx = lax.axis_size("ctx")
    n_fsdp = lax.axis_size("fsdp")
    core, place, depth = (
        lax.axis_index(axis).astype(jnp.uint32) for axis in ("section", "ctx", "fsdp")
    )
    seq_len = rows * n_ctx
    capacity = rows * TOP * 5 // (4 * EXPERTS)
    score_scale = HD ** (-0.5)
    own_experts = EXPERTS // n_ctx
    hidden = w_gate.shape[3]
    shard_rows = w_query.shape[1]
    down_rows = w_down.shape[2]
    qw = w_query.shape[2]
    kw = w_key.shape[2]
    pieces = max(1, 2 * n_ctx // EXPERTS)
    per_core = max(1, EXPERTS // (2 * n_ctx))
    unit_rows = shard_rows + down_rows
    aligned = shard_rows % 16 == 0 and down_rows % 16 == 0

    def on_core(former, latter):
        return jnp.where(core == 0, former, latter)

    def own_other(low, high):
        return (on_core(low, high), on_core(high, low))

    early, late = (range(1, n_ctx // 2 + 1), range(n_ctx // 2 + 1, n_ctx))

    def send(value, bits):
        return [swap(value, "ctx", bit) for bit in bits]

    def spread(value):
        return [value] + send(value, early) + send(value, late)

    def spread_rows(value):
        near_blocks = send(value, early)
        value, near_blocks = tie(value, near_blocks)
        return [value] + near_blocks + send(value, late)

    def gather_back(blocks):
        return [blocks[0]] + [swap(blocks[bit], "ctx", bit) for bit in range(1, n_ctx)]

    info = jnp.concatenate([routes.astype(f32), combine], axis=-1)[0, :, 0].transpose(0, 2, 1)
    info_own, info_other = (at(info, core), swap(at(info, 1 - core), "section", 1))
    info = jnp.stack(own_other(info_own, info_other))
    info = jnp.stack([info] + [swap(info, "ctx", bit) for bit in range(1, n_ctx)], axis=1)

    gain_columns = jnp.stack([attn_norm[0], ffn_norm[0]], axis=1)
    gain_columns = jnp.pad(gain_columns, ((0, 0), (0, gap - 2)))
    enter_shard = jnp.concatenate([w_query[0], w_key[0], w_value[0], gain_columns], axis=1)
    enter_cut = enter_shard.shape[1] // 2
    leave_cut = w_out.shape[2] // 2
    low_shard = jnp.concatenate([enter_shard[:, :enter_cut], w_out[0, :, :leave_cut]], axis=1)
    high_shard = jnp.concatenate([enter_shard[:, enter_cut:], w_out[0, :, leave_cut:]], axis=1)
    lent = swap(on_core(high_shard, low_shard), "section", 1)
    dense_shards = (on_core(low_shard, lent), on_core(lent, high_shard))

    def gather_deep(shard):
        blocks = [shard] + [swap(shard, "fsdp", bit) for bit in range(1, n_fsdp)]
        return place_call(blocks, depth).reshape(-1, shard.shape[1])

    def join_square(blocks):
        return place_call(blocks, place).reshape(-1, blocks[0].shape[1])

    def gather_square(deep):
        return join_square(spread(deep))

    cut = hidden // 2
    unit_stack = jnp.concatenate(
        [
            jnp.concatenate(
                [w_gate[0, ..., :cut], w_up[0, ..., :cut], w_gate[0, ..., cut:], w_up[0, ..., cut:]],
                axis=2,
            ),
            w_down[0],
        ],
        axis=1,
    )
    if pieces == 2:
        unit_stack = jnp.stack(jnp.split(unit_stack, 2, axis=2), axis=1)
    unit_stack = unit_stack.reshape(n_ctx, 2, per_core, unit_rows, width // pieces)
    units_lent = swap(at(unit_stack, 1 - core, 1), "section", 1)
    unit_stacks = jnp.stack(own_other(at(unit_stack, core, 1), units_lent), axis=1)

    def deal_units(stack):
        blocks = [at(stack, place)]
        blocks += [swap(at(stack, place ^ bit), "ctx", bit) for bit in range(1, n_ctx)]
        return deal_call(blocks, place)

    ring = list(range(0, n_fsdp, 2)) + list(range(1, n_fsdp, 2))[::-1]
    ring_steps = [(ring[i], ring[(i + 1) % n_fsdp]) for i in range(n_fsdp)]
    ring_table = [[ring[ring.index(z) - i] for i in range(n_fsdp)] for z in range(n_fsdp)]
    behind_here = at(jnp.array(ring_table, jnp.uint32), depth)

    def ring_send(moved):
        return [blocks + [lax.ppermute(blocks[-1], "fsdp", ring_steps)] for blocks in moved]

    def own_units(blocks):
        return [order_call(blocks, behind_here, unit) for unit in range(per_core)]

    def pair_units(mine):
        other = [swap(part, "section", 1) for part in mine]
        units = list(mine) + other
        if pieces == 2:
            units = [jnp.concatenate(own_other(mine[0], other[0]), axis=2)]
        if aligned:
            return [[unit] for unit in units]
        return [
            [unit[:, :shard_rows].reshape(-1, width), unit[:, shard_rows:].reshape(-1, width)]
            for unit in units
        ]

    def cut_units(grads):
        if aligned:
            units = [unit for (unit,) in grads]
        else:
            units = [
                jnp.concatenate(
                    [part.reshape(n_ctx * n_fsdp, -1, width) for part in parts], axis=1
                )
                for parts in grads
            ]
        if pieces == 1:
            return (units[:per_core], units[per_core:])
        own, other = own_other(*jnp.split(units[0], 2, axis=2))
        return ([own], [other])

    def ring_part(terms, behind):
        spot = behind_here[behind % n_fsdp]
        return sum(at(term, spot, 1).astype(f32) for term in terms)

    def ring_start(own, received):
        terms = [part.reshape((n_ctx, n_fsdp) + part.shape[1:]) for part in (own, received)]
        return (terms, ring_part(terms, 1).astype(bf16))

    def ring_move(state):
        return [(terms, lax.ppermute(moving, "fsdp", ring_steps)) for terms, moving in state]

    def ring_add(state, step):
        return [
            (terms, (moved.astype(f32) + ring_part(terms, step + 1)).astype(bf16))
            for terms, moved in state
        ]

    def ring_step(state, step):
        return ring_add(ring_move(state), step)

    def ring_last(state):
        state = ring_add(state, 2)
        for step in range(3, n_fsdp - 1):
            state = ring_step(state, step)
        return ring_move(state)

    def ring_rest(state, first):
        for step in range(first, n_fsdp):
            state = ring_step(state, step)
        return [moving for _, moving in state]

    def scatter_units(moved):
        whole = jnp.stack(moved, axis=1)
        blocks = [at(whole, place)]
        blocks += [swap(at(whole, place ^ bit), "ctx", bit) for bit in range(1, n_ctx)]
        return jnp.stack(blocks)

    def trade_square(own, received, bits):
        own, received = (part.reshape(n_ctx, -1, part.shape[1]) for part in (own, received))

        def part(bit):
            return at(own, place ^ bit).astype(f32) + at(received, place ^ bit).astype(f32)

        return [part(bit) if bit == 0 else swap(part(bit).astype(bf16), "ctx", bit) for bit in bits]

    def sum_square(parts):
        return sum(part.astype(f32) for part in parts).astype(bf16)

    def reduce_deep(mine):
        mine = mine.reshape(n_fsdp, shard_rows, -1)
        total = at(mine, depth).astype(f32)
        for bit in range(1, n_fsdp):
            total = total + swap(at(mine, depth ^ bit), "fsdp", bit).astype(f32)
        return total

    if pieces == 1:
        units_here = jnp.arange(per_core, dtype=jnp.uint32)
        units_here = jnp.concatenate(
            [core * per_core + units_here, (1 - core) * per_core + units_here]
        )
    else:
        units_here = jnp.zeros((1,), jnp.uint32)
    named = (place * own_experts + units_here).astype(f32)
    matches = info[:, None, :, :TOP] == named[None, :, None, None, None]
    hits = jnp.any(matches, axis=3)
    shares = jnp.sum(jnp.where(matches, info[:, None, :, TOP:], 0.0), axis=3)
    earlier = jnp.arange(rows)[:, None] < jnp.arange(rows)[None, :]
    rank = dot("ledr,rq->ledq", hits.astype(bf16), earlier.astype(bf16))
    slots = jnp.arange(capacity, dtype=f32)
    picks = hits[:, :, :, None, :] & (rank[:, :, :, None, :] == slots[:, None])
    slot_shares = jnp.sum(jnp.where(picks, shares[:, :, :, None, :], 0.0), axis=-1, keepdims=True)
    picks = picks.astype(bf16)

    order = place.astype(jnp.int32) ^ jnp.arange(n_ctx, dtype=jnp.int32)
    block_ids = jnp.take(block_of.reshape(n_ctx, 2), order, axis=0)
    block_ids = block_ids.reshape(-1)

    def gains_of(halves):
        pair = on_core(halves[1][:, -gap : 2 - gap], halves[0][:, -gap : 2 - gap])
        pair = pair.astype(f32).T
        return (pair[:1], pair[1:])

    near = 1 + len(early)
    parts = (slice(0, near), slice(near, n_ctx))

    def experts(layer, blocks, weights, answer, beside=lambda: []):
        kept, arrived = ({}, [])
        back = {}
        for index, part in enumerate(parts):
            rows_here = blocks[part]
            if index:
                back[0], rows_here = tie(back[0], rows_here)
                arrived = [swap(block, "ctx", bit) for bit, block in zip(early, back[0][1:])]
            back[index] = []
            for j in range(own_experts):
                back[index], kept[index, j] = expert_call(
                    picks[layer, j, part],
                    slot_shares[layer, j, part],
                    rows_here,
                    weights[j],
                    shard_rows,
                    hidden,
                    back[index],
                    3 if index == 0 else 1,
                )
        if not answer:
            return (back[0] + back[1], kept)
        back[1], arrived, found = tie(back[1], arrived, beside())
        arrived += [swap(block, "ctx", bit) for bit, block in zip(late, back[1])]
        return (back[0][:1] + arrived, kept, found)

    def experts_back(layer, blocks, weights, kept, delay, beside_near, beside_far, beside_end):
        back, saved = ({}, {})
        for index, part in enumerate(parts):
            rows_here = blocks[part]
            if index:
                back[0], rows_here, found_near = tie(back[0], rows_here, beside_near())
                arrived = [swap(block, "ctx", bit) for bit, block in zip(early, back[0][1:])]
            back[index] = []
            for j in range(own_experts):
                back[index], saved[index, j] = expert_back_call(
                    picks[layer, j, part],
                    slot_shares[layer, j, part],
                    rows_here,
                    kept[index, j],
                    weights[j],
                    shard_rows,
                    back[index],
                    4 if index == 0 else 1,
                )
        back[1], arrived, saved, found_far = tie(back[1], arrived, saved, beside_far(found_near))
        arrived += [swap(block, "ctx", bit) for bit, block in zip(late, back[1])]

        def grads_of(j, saved):
            picked = [kept[index, j][0] for index in range(2)]
            both = [saved[index, j] for index in range(2)]
            return expert_grads_call(picked, both, weights[j], shard_rows)

        now = [j for j in reversed(range(own_experts)) if not delay or j >= per_core]
        grads = {j: grads_of(j, saved) for j in now}
        arrived, grads, found_end = tie(arrived, grads, beside_end(found_far))
        returned = back[0][:1] + arrived
        if len(now) == own_experts:
            own, other = cut_units([grads[j] for j in range(own_experts)])
            received = [swap(part, "section", 1) for part in other]
            return (returned, lambda earlier: (own, received), found_end)
        received = [swap(grads[j][0], "section", 1) for j in reversed(now)]

        def finish(earlier):
            ready = after(saved, earlier)
            return ([grads_of(j, ready)[0] for j in range(per_core)], received)

        return (returned, finish, found_end)

    def keep_own(first, second):
        other = swap(on_core(second, first), "section", 1)
        return own_other(on_core(first, second), other)

    dense_first, dense_second = dense_shards
    deep = gather_deep(jnp.concatenate([dense_first, dense_second[:, :enter_cut]], axis=1))
    dealt_first, dealt_second = deal_units(unit_stacks)
    deep, dealt_first, dealt_second, picks, dense_second = tie(
        deep, dealt_first, dealt_second, picks, dense_second
    )
    dense_blocks, moved, leave_shard, enter_shard = tie(
        spread(deep[:, :enter_cut]),
        ring_send([[dealt_first]]),
        deep[:, enter_cut : enter_cut + leave_cut],
        deep[:, enter_cut + leave_cut :],
    )
    leave_blocks = [leave_shard] + send(leave_shard, early)
    enter_own = join_square(dense_blocks)
    enter_first = (enter_own, swap(enter_own, "section", 1))

    first_gains = gains_of(enter_first)
    first_in = after(at(tokens, core)[0], slot_shares)
    _, first_normed, first_entered = enter_call(core, [first_in], first_gains[0], enter_first)
    first_entered, leave_blocks = tie(first_entered, leave_blocks)
    key_value = first_entered[:, qw : qw + 2 * kw]
    first_kv, moved, leave_shard, enter_shard = tie(
        jnp.concatenate(spread(key_value)), ring_send(moved), leave_shard, enter_shard
    )
    enter_blocks = [enter_shard] + send(enter_shard, early)
    first_attended = attend_call(block_ids, first_entered, first_kv)
    for _ in range(2, n_fsdp - 1):
        moved = ring_send(moved)
    first_attended, leave_blocks, dealt_second, moved, enter_blocks, enter_shard, dense_second = tie(
        first_attended,
        leave_blocks + send(leave_shard, late),
        dealt_second,
        moved,
        enter_blocks,
        enter_shard,
        dense_second,
    )
    leave_own = join_square(leave_blocks)
    leave_first = (leave_own, swap(leave_own, "section", 1))
    first_mid, ffn_normed = leave_call(core, first_in, first_attended, first_gains[1], leave_first)
    first_units = own_units(moved[0])
    blocks = spread_rows(ffn_normed)
    blocks[:near], moved, first_units, enter_shard, leave_shard = tie(
        blocks[:near],
        ring_send([[dealt_second]]),
        first_units,
        enter_shard,
        dense_second[:, enter_cut:],
    )
    first_weights = pair_units(first_units)
    returned, first_kept, (moved, leave_shard, enter_blocks) = experts(
        0,
        blocks,
        first_weights,
        True,
        lambda: (
            ring_send(moved),
            after(leave_shard, moved),
            enter_blocks + send(enter_shard, late),
        ),
    )
    enter_own = join_square(enter_blocks)
    enter_second = (enter_own, swap(enter_own, "section", 1))
    returned, moved, leave_shard = tie(returned, moved, gather_deep(leave_shard))
    moved = ring_send(moved)
    leave_blocks = [leave_shard] + send(leave_shard, early)

    second_gains = gains_of(enter_second)
    second_in, second_normed, second_entered = enter_call(
        core, [first_mid] + returned, second_gains[0], enter_second
    )
    second_entered, leave_blocks = tie(second_entered, leave_blocks)
    key_value = second_entered[:, qw : qw + 2 * kw]
    for _ in range(4, n_fsdp):
        moved = ring_send(moved)
    second_kv, leave_shard = tie(jnp.concatenate(spread(key_value)), leave_shard)
    second_attended = attend_call(block_ids, second_entered, second_kv)
    second_attended, leave_blocks, moved = tie(
        second_attended, leave_blocks + send(leave_shard, late), moved
    )
    leave_own = join_square(leave_blocks)
    leave_second = (leave_own, swap(leave_own, "section", 1))
    second_mid, ffn_normed = leave_call(
        core, second_in, second_attended, second_gains[1], leave_second
    )
    second_weights = pair_units(own_units(after(moved, ffn_normed)[0]))
    blocks = spread_rows(ffn_normed)
    second_returned, second_kept = experts(1, blocks, second_weights, False)
    cotangent = after(at(out_grad, core)[0], second_returned[:near])
    cot_blocks = spread_rows(cotangent)
    cot_blocks[:near], second_returned[near:] = tie(cot_blocks[:near], second_returned[near:])

    returned, finish, (second_returned, near_parts) = experts_back(
        1,
        cot_blocks,
        second_weights,
        second_kept,
        False,
        lambda: second_returned,
        lambda found: found,
        lambda found: (found, [swap(found[bit], "ctx", bit) for bit in early]),
    )
    far_parts = [swap(second_returned[bit], "ctx", bit) for bit in late]
    units_moving = [ring_start(*pair) for pair in zip(*finish(()))]
    after_rows, term, d_attended, *grads = leave_back_call(
        core,
        returned,
        second_gains[1],
        second_mid,
        cotangent,
        second_attended,
        leave_second,
    )
    leave_grads = (grads[0], swap(grads[1], "section", 1))
    d_queries, d_key_value = attend_back_call(block_ids, second_entered, second_kv, d_attended)
    d_queries, d_key_value, leave_grads, far_parts = tie(
        d_queries, d_key_value, leave_grads, far_parts
    )
    second_parts = second_returned[:1] + near_parts + far_parts
    second_out = second_mid + sum(part.astype(f32) for part in second_parts)
    d_key_value, units_moving = tie(gather_back(d_key_value), ring_move(units_moving))
    units_moving = ring_move(ring_add(units_moving, 1))
    leave_parts = trade_square(*leave_grads, range(n_ctx))
    second_entry, cotangent, *grads = enter_back_call(
        core,
        d_queries,
        d_key_value,
        second_gains[0],
        second_in,
        second_normed,
        after_rows,
        term,
        enter_second,
    )
    cotangent, grads, leave_parts, layer_rows = tie(
        cotangent, grads, leave_parts, (second_in, second_out.astype(bf16))
    )
    enter_grads = (grads[0], swap(grads[1], "section", 1))

    blocks = spread_rows(cotangent)
    blocks[:near], enter_grads, units_moving, layer_rows = tie(
        blocks[:near], enter_grads, units_moving, layer_rows
    )
    returned, finish, (units_moving, layer_outs, enter_parts) = experts_back(
        0,
        blocks,
        first_weights,
        first_kept,
        False,
        lambda: trade_square(*enter_grads, [0, *early]),
        lambda found: (ring_last(units_moving), keep_own(*layer_rows), found, enter_grads),
        lambda found: (found[0], found[1], found[2] + trade_square(*found[3], late)),
    )
    second_moved = [moving for _, moving in ring_add(units_moving, n_fsdp - 1)]
    second_moving = [sum_square(parts) for parts in (enter_parts, leave_parts)]
    own, received = finish(())
    after_rows, term, d_attended, *grads = leave_back_call(
        core,
        returned,
        first_gains[1],
        first_mid,
        cotangent,
        first_attended,
        leave_first,
    )
    units_moving = [ring_start(*pair) for pair in zip(own, received)]
    leave_grads = (grads[0], swap(grads[1], "section", 1))
    d_queries, d_key_value = attend_back_call(block_ids, first_entered, first_kv, d_attended)
    d_queries, d_key_value, leave_grads = tie(d_queries, d_key_value, leave_grads)
    leave_parts = trade_square(*leave_grads, range(n_ctx))
    d_key_value, units_moving = tie(gather_back(d_key_value), ring_move(units_moving))
    units_moving = ring_move(ring_add(units_moving, 1))
    first_entry, _, *grads = enter_back_call(
        core,
        d_queries,
        d_key_value,
        first_gains[0],
        first_in,
        first_normed,
        after_rows,
        term,
        enter_first,
    )
    grads, leave_parts = tie(grads, leave_parts)
    enter_grads = (grads[0], swap(grads[1], "section", 1))
    enter_parts, first_entry = tie(trade_square(*enter_grads, range(n_ctx)), first_entry)
    first_moving = [sum_square(parts) for parts in (enter_parts, leave_parts)]
    dense = reduce_deep(jnp.concatenate(first_moving + second_moving, axis=1))
    first_dense, second_dense = jnp.split(dense, 2, axis=1)
    scattered = scatter_units(ring_rest(ring_add(units_moving, 2), 3) + second_moved)
    first_scattered, second_scattered = (scattered[:, :per_core], scattered[:, per_core:])

    layer_out = jnp.stack(layer_outs)
    input_grads = jnp.stack(keep_own(first_entry, second_entry))
    low_dense, high_dense = keep_own(first_dense, second_dense)
    enter_grad = jnp.concatenate([low_dense[:, :enter_cut], high_dense[:, :enter_cut]], axis=1)
    grad_out = jnp.concatenate([low_dense[:, enter_cut:], high_dense[:, enter_cut:]], axis=1)
    grad_gains = enter_grad[:, qw + 2 * kw :]
    mine = on_core(first_scattered, second_scattered)
    other = swap(on_core(second_scattered, first_scattered), "section", 1)
    if aligned and pieces == 1:
        grad_gate, grad_up, grad_down = finish_call(mine, other, shard_rows, hidden, place, core)
    else:
        sides = [jnp.take(part, order, axis=0) for part in own_other(mine, other)]
        if pieces == 1:
            whole = jnp.stack(sides, axis=1).reshape(EXPERTS, unit_rows, width)
        else:
            whole = jnp.concatenate([side[:, 0] for side in sides], axis=2)
        pairs = whole[:, :shard_rows].astype(f32).reshape(EXPERTS, shard_rows, 2, 2, cut)
        grad_gate = pairs[:, :, :, 0].reshape(EXPERTS, shard_rows, hidden)
        grad_up = pairs[:, :, :, 1].reshape(EXPERTS, shard_rows, hidden)
        grad_down = whole[:, shard_rows:].astype(f32)
    return (
        layer_out[None, :, None],
        input_grads[None, :, None],
        grad_gains[:, 0][None],
        enter_grad[:, :qw][None],
        enter_grad[:, qw : qw + kw][None],
        enter_grad[:, qw + kw : qw + 2 * kw][None],
        grad_out[None],
        grad_gains[:, 1][None],
        grad_gate[None],
        grad_up[None],
        grad_down[None],
    )


def solution(mesh):
    rows_placed = P(None, "fsdp", "ctx", None)
    kept_placed = P("section", None, "fsdp", "ctx", None)
    gain_placed = P("section", ("ctx", "fsdp"))
    dense_placed = P("section", ("ctx", "fsdp"), None)
    expert_placed = P("section", None, ("ctx", "fsdp"), None)
    dense_all = (dense_placed,) * 4
    expert_all = (expert_placed,) * 3
    layer_placed = (gain_placed,) + dense_all + (gain_placed,) + expert_all
    return jax.shard_map(
        body,
        mesh=mesh,
        in_specs=(rows_placed, P(), kept_placed, kept_placed) + layer_placed + (rows_placed,),
        out_specs=(kept_placed, kept_placed) + layer_placed,
        check_vma=False,
    )
```

```python
import functools

import jax
import jax.numpy as jnp
from jax import lax
from jax.experimental import pallas as pl
from jax.experimental.pallas import tpu as pltpu
from jax.sharding import PartitionSpec as P

QH = 12
KVH = 2
HD = 128
GROUP = QH // KVH
TOP = 4
EXPERTS = 8
bf16 = jnp.bfloat16
f32 = jnp.float32


epsilon = 1e-06
masked_out = -1e30
gap = 256


def swap(value, axis, bit):
    count = lax.axis_size(axis)
    return lax.ppermute(value, axis, [(source, source ^ bit) for source in range(count)])


def tie(*values):
    return lax.optimization_barrier(values)


def after(value, earlier):
    return tie(value, earlier)[0]


def at(value, index, axis=0):
    return lax.dynamic_index_in_dim(value, index, axis, keepdims=False)


def dot(spec, left, right, kind=f32):
    return jnp.einsum(spec, left, right, preferred_element_type=kind)


def cost(micros):
    return pl.CostEstimate(
        flops=int(micros * 1e9), bytes_accessed=int(micros * 3e6), transcendentals=0
    )


def kernel_params():
    return pltpu.CompilerParams(vmem_limit_bytes=56 * 1024 * 1024)


def nt(left, right):
    return lax.dot_general(left, right, (((1,), (1,)), ((), ())), preferred_element_type=f32)


def nn(left, right):
    return jnp.dot(left, right, preferred_element_type=f32)


def head_rows(ref):
    return jnp.concatenate([ref[:, i * HD : (i + 1) * HD] for i in range(GROUP)], axis=0)


def softmax_rows(ids_ref, queries, keys, half, own):
    scores = nt(queries, keys) * HD ** (-0.5)
    tall, wide = scores.shape
    row = lax.broadcasted_iota(jnp.int32, (half, 1), 0)
    row = jnp.concatenate([row] * (tall // half), axis=0) + ids_ref[own] * half
    lane = lax.broadcasted_iota(jnp.int32, (1, half), 1)
    column = [lane + ids_ref[block] * half for block in range(wide // half)]
    column = jnp.concatenate(column, axis=1)
    scores = jnp.where(row >= column, scores, masked_out)
    shifted = jnp.exp(scores - jnp.max(scores, axis=1, keepdims=True))
    return shifted / jnp.sum(shifted, axis=1, keepdims=True)


def attend_kernel(ids_ref, query_ref, key_ref, value_ref, out_ref):
    half = query_ref.shape[0]
    probs = softmax_rows(ids_ref, head_rows(query_ref), key_ref[...], half, pl.program_id(1))
    out = nn(probs.astype(bf16), value_ref[...]).astype(bf16)
    for i in range(GROUP):
        out_ref[:, i * HD : (i + 1) * HD] = out[i * half : (i + 1) * half]


def attend_specs(rows, seq_len):
    half = rows // 2
    by_head = pl.BlockSpec((half, GROUP * HD), lambda g, h, ids: (h, g))
    keys = pl.BlockSpec((seq_len, HD), lambda g, h, ids: (0, g))
    values = pl.BlockSpec((seq_len, HD), lambda g, h, ids: (0, KVH + g))
    return by_head, keys, values


def attend_call(ids, queries, key_value):
    rows, seq_len = (queries.shape[0], key_value.shape[0])
    by_head, keys, values = attend_specs(rows, seq_len)
    return pl.pallas_call(
        attend_kernel,
        grid_spec=pltpu.PrefetchScalarGridSpec(
            num_scalar_prefetch=1,
            grid=(KVH, 2),
            in_specs=[by_head, keys, values],
            out_specs=by_head,
        ),
        out_shape=jax.ShapeDtypeStruct((rows, QH * HD), bf16),
        compiler_params=kernel_params(),
        cost_estimate=cost(1),
        name="attend",
    )(ids, queries, key_value, key_value)


def attend_back_kernel(ids_ref, query_ref, key_ref, value_ref, cot_ref, dq_ref, *refs):
    out, (dk_ref, dv_ref) = (refs[:-2], refs[-2:])
    half = query_ref.shape[0]
    group, own = (pl.program_id(0), pl.program_id(1))
    queries, cot = (head_rows(query_ref), head_rows(cot_ref))
    probs = softmax_rows(ids_ref, queries, key_ref[...], half, own)
    d_probs = nt(cot, value_ref[...])
    inner = jnp.sum(probs * d_probs, axis=1, keepdims=True)
    d_scores = (probs * (d_probs - inner)).astype(bf16)
    d_queries = (nn(d_scores, key_ref[...]) * HD ** (-0.5)).astype(bf16)
    for i in range(GROUP):
        dq_ref[:, i * HD : (i + 1) * HD] = d_queries[i * half : (i + 1) * half]
    d_keys = nn(d_scores.T, queries) * HD ** (-0.5)
    d_values = nn(probs.astype(bf16).T, cot)

    @pl.when(own == 0)
    def _():
        dk_ref[...] = d_keys
        dv_ref[...] = d_values

    @pl.when(own != 0)
    def _():
        rows = 2 * half
        for block, ref in enumerate(out):
            part = slice(block * rows, (block + 1) * rows)
            for first, total, last in ((0, dk_ref, d_keys), (KVH * HD, dv_ref, d_values)):
                columns = pl.ds(pl.multiple_of(first + group * HD, HD), HD)
                ref[:, columns] = (total[part, :] + last[part]).astype(bf16)


def attend_back_call(ids, queries, key_value, cot):
    rows, seq_len = (queries.shape[0], key_value.shape[0])
    by_head, keys, values = attend_specs(rows, seq_len)
    blocks = seq_len // rows
    wide = 2 * KVH * HD
    result = pl.pallas_call(
        attend_back_kernel,
        grid_spec=pltpu.PrefetchScalarGridSpec(
            num_scalar_prefetch=1,
            grid=(KVH, 2),
            in_specs=[by_head, keys, values, by_head],
            out_specs=[by_head] + [pl.BlockSpec((rows, wide), lambda g, h, ids: (0, 0))] * blocks,
            scratch_shapes=[pltpu.VMEM((seq_len, HD), f32)] * 2,
        ),
        out_shape=[jax.ShapeDtypeStruct((rows, QH * HD), bf16)]
        + [jax.ShapeDtypeStruct((rows, wide), bf16)] * blocks,
        compiler_params=kernel_params(),
        cost_estimate=cost(1),
        name="attend_back",
    )(ids, queries, key_value, key_value, cot)
    return (result[0], result[1:])


def gelu_parts(gate):
    root = 0.7978845608028654
    inner = root * (gate + 0.044715 * gate * gate * gate)
    bent = jnp.tanh(inner)
    value = 0.5 * gate * (1.0 + bent)
    slope = root * (1.0 + 3.0 * 0.044715 * gate * gate)
    return value, 0.5 * (1.0 + bent) + 0.5 * gate * (1.0 - bent * bent) * slope


def give_back(pick_ref, total_ref, share_ref, before, out):
    blocks, capacity, _ = pick_ref.shape
    for d in range(blocks):
        part = total_ref[d * capacity : (d + 1) * capacity, :]
        if share_ref is not None:
            part = part * share_ref[d]
        back = nn(pick_ref[d].T, part.astype(bf16))
        if before:
            back = back + before[d][...]
        out[d][...] = back.astype(out[d].dtype)


def flat(ref):
    value = ref[...]
    return value.reshape(-1, value.shape[-1])


def add_up(total_ref, part, step):
    @pl.when(step == 0)
    def _():
        total_ref[...] = part

    @pl.when(step != 0)
    def _():
        total_ref[...] += part


def expert_kernel(blocks, adds, pick_ref, share_ref, gate_ref, up_ref, down_ref, *refs):
    rows, refs = (refs[:blocks], refs[blocks:])
    before, refs = (refs[: blocks * adds], refs[blocks * adds :])
    out, (picked_ref, gate_pre_ref, up_pre_ref, total_ref) = (refs[:blocks], refs[blocks:])
    step = pl.program_id(0)
    capacity = pick_ref.shape[1]

    @pl.when(step == 0)
    def _():
        for d in range(blocks):
            block = nn(pick_ref[d], rows[d][...]).astype(bf16)
            picked_ref[d * capacity : (d + 1) * capacity, :] = block

    gate_pre = nn(picked_ref[...], flat(gate_ref))
    up_pre = nn(picked_ref[...], flat(up_ref))
    gate_pre_ref[...] = gate_pre
    up_pre_ref[...] = up_pre
    active = (gelu_parts(gate_pre)[0] * up_pre).astype(bf16)
    add_up(total_ref, nn(active, flat(down_ref)), step)

    @pl.when(step == pl.num_programs(0) - 1)
    def _():
        give_back(pick_ref, total_ref, share_ref, before, out)


def whole_spec(shape):
    return pl.BlockSpec(
        shape, lambda step: (0,) * len(shape), pipeline_mode=pl.Buffered(buffer_count=1)
    )


def weight_operands(weights, deep, cut):
    if len(weights) == 1:
        unit = weights[0]
        shards, tall, width = unit.shape
        specs = [
            pl.BlockSpec((shards, deep, cut), lambda step: (0, 0, 2 * step)),
            pl.BlockSpec((shards, deep, cut), lambda step: (0, 0, 2 * step + 1)),
            pl.BlockSpec(
                (shards // 2, tall - deep, width), lambda step: (step, deep // (tall - deep), 0)
            ),
        ]
        return specs, [unit, unit, unit]
    pair, down = weights
    specs = [
        pl.BlockSpec((pair.shape[0], cut), lambda step: (0, 2 * step)),
        pl.BlockSpec((pair.shape[0], cut), lambda step: (0, 2 * step + 1)),
        pl.BlockSpec((cut, down.shape[1]), lambda step: (step, 0)),
    ]
    return specs, [pair, pair, down]


def expert_call(picks, shares, rows, weights, deep, hidden, before, micros):
    blocks, capacity, _ = picks.shape
    width, cut, tall = (rows[0].shape[1], hidden // 2, blocks * capacity)
    columns = pl.BlockSpec((tall, cut), lambda step: (0, step))
    row_specs = [whole_spec(block.shape) for block in rows]
    specs, operands = weight_operands(weights, deep, cut)
    result = pl.pallas_call(
        functools.partial(expert_kernel, blocks, 1 if before else 0),
        grid=(2,),
        in_specs=[whole_spec(picks.shape), whole_spec(shares.shape)]
        + specs
        + row_specs * (2 if before else 1),
        out_specs=row_specs + [whole_spec((tall, width)), columns, columns],
        out_shape=[jax.ShapeDtypeStruct(block.shape, bf16) for block in rows]
        + [
            jax.ShapeDtypeStruct((tall, width), bf16),
            jax.ShapeDtypeStruct((tall, hidden), f32),
            jax.ShapeDtypeStruct((tall, hidden), f32),
        ],
        scratch_shapes=[pltpu.VMEM((tall, width), f32)],
        compiler_params=kernel_params(),
        cost_estimate=cost(micros),
        name="expert",
    )(picks, shares, *operands, *rows, *before)
    return (list(result[:blocks]), list(result[blocks:]))


def expert_back_kernel(
    blocks, adds, pick_ref, share_ref, gate_pre_ref, up_pre_ref, gate_ref, up_ref, down_ref, *refs
):
    rows, refs = (refs[:blocks], refs[blocks:])
    before, refs = (refs[: blocks * adds], refs[blocks * adds :])
    out, refs = (refs[:blocks], refs[blocks:])
    slots_ref, d_gate_ref, d_up_ref, active_ref, total_ref = refs
    step = pl.program_id(0)
    capacity = pick_ref.shape[1]

    @pl.when(step == 0)
    def _():
        for d in range(blocks):
            block = nn(pick_ref[d], rows[d][...]) * share_ref[d]
            slots_ref[d * capacity : (d + 1) * capacity, :] = block.astype(bf16)

    d_active = nt(slots_ref[...], flat(down_ref))
    value, slope = gelu_parts(gate_pre_ref[...])
    up_pre = up_pre_ref[...]
    d_gate = (d_active * up_pre * slope).astype(bf16)
    d_up = (d_active * value).astype(bf16)
    active_ref[...] = (value * up_pre).astype(bf16)
    d_gate_ref[...] = d_gate
    d_up_ref[...] = d_up
    add_up(total_ref, nt(d_gate, flat(gate_ref)) + nt(d_up, flat(up_ref)), step)

    @pl.when(step == pl.num_programs(0) - 1)
    def _():
        give_back(pick_ref, total_ref, None, before, out)


def expert_back_call(picks, shares, rows, kept, weights, deep, before, micros):
    _, gate_pre, up_pre = kept
    blocks, capacity, _ = picks.shape
    width, (tall, hidden) = (rows[0].shape[1], gate_pre.shape)
    cut = hidden // 2
    columns = pl.BlockSpec((tall, cut), lambda step: (0, step))
    row_specs = [whole_spec(block.shape) for block in rows]
    specs, operands = weight_operands(weights, deep, cut)
    result = pl.pallas_call(
        functools.partial(expert_back_kernel, blocks, 1 if before else 0),
        grid=(2,),
        in_specs=[whole_spec(picks.shape), whole_spec(shares.shape), columns, columns]
        + specs
        + row_specs * (2 if before else 1),
        out_specs=row_specs + [whole_spec((tall, width)), columns, columns, columns],
        out_shape=[jax.ShapeDtypeStruct(block.shape, bf16) for block in rows]
        + [jax.ShapeDtypeStruct((tall, width), bf16)]
        + [jax.ShapeDtypeStruct((tall, hidden), bf16)] * 3,
        scratch_shapes=[pltpu.VMEM((tall, width), f32)],
        compiler_params=kernel_params(),
        cost_estimate=cost(micros),
        name="expert_back",
    )(picks, shares, gate_pre, up_pre, *operands, *rows, *before)
    return (list(result[:blocks]), list(result[blocks:]))


def expert_grads_kernel(parts, deep, *refs):
    picked, slots, d_gate, d_up, active = (refs[i * parts : (i + 1) * parts] for i in range(5))
    grad_refs, turned_ref = (refs[5 * parts : -1], refs[-1])
    step = pl.program_id(0)

    def below(some):
        return jnp.concatenate([ref[...] for ref in some], axis=0)

    @pl.when(step == 0)
    def _():
        turned_ref[...] = below(picked).T

    grad_gate = nn(turned_ref[...], below(d_gate)).astype(bf16)
    grad_up = nn(turned_ref[...], below(d_up)).astype(bf16)
    grad_down = nn(below(active).T, below(slots)).astype(bf16)
    cut = grad_gate.shape[1]
    if len(grad_refs) == 1:
        unit_ref = grad_refs[0]
        shards, tall, width = unit_ref.shape
        for side in range(2):

            @pl.when(step == side)
            def _():
                left, some = (2 * side * cut, shards // 2)
                unit_ref[:, :deep, left : left + cut] = grad_gate.reshape(shards, deep, cut)
                left = left + cut
                unit_ref[:, :deep, left : left + cut] = grad_up.reshape(shards, deep, cut)
                rest = grad_down.reshape(some, tall - deep, width)
                unit_ref[side * some : (side + 1) * some, deep:, :] = rest
    else:
        grad_refs[0][:, :cut] = grad_gate
        grad_refs[0][:, cut:] = grad_up
        grad_refs[1][...] = grad_down


def expert_grads_call(picked, saved, weights, deep):
    slots, d_gate, d_up, active = zip(*saved)
    width, hidden = (picked[0].shape[1], d_gate[0].shape[1])
    cut = hidden // 2
    columns = [pl.BlockSpec((part.shape[0], cut), lambda step: (0, step)) for part in picked]
    if len(weights) == 1:
        grad_specs = [whole_spec(weights[0].shape)]
    else:
        grad_specs = [
            pl.BlockSpec((width, 2 * cut), lambda step: (0, step)),
            pl.BlockSpec((cut, width), lambda step: (step, 0)),
        ]
    return list(
        pl.pallas_call(
            functools.partial(expert_grads_kernel, len(picked), deep),
            grid=(2,),
            in_specs=[whole_spec(part.shape) for part in picked] * 2 + columns * 3,
            out_specs=grad_specs,
            out_shape=[jax.ShapeDtypeStruct(part.shape, bf16) for part in weights],
            scratch_shapes=[pltpu.VMEM((width, sum(part.shape[0] for part in picked)), bf16)],
            compiler_params=kernel_params(),
            cost_estimate=cost(1),
            name="expert_grads",
        )(*picked, *slots, *d_gate, *d_up, *active)
    )


def norm_parts(value):
    scale = lax.rsqrt(jnp.mean(value * value, axis=1, keepdims=True) + epsilon)
    return scale, value * scale


def norm_back(grad, gain, value):
    scale, scaled = norm_parts(value)
    grown = grad * gain
    back = scale * (grown - scaled * jnp.mean(scaled * grown, axis=1, keepdims=True))
    return back, (grad * scaled).astype(bf16)


def add_all(refs):
    total = refs[0][...].astype(f32)
    for ref in refs[1:]:
        total = total + ref[...].astype(f32)
    return total


def side_offsets(core_ref, steps, cut):
    step, core = (pl.program_id(0), core_ref[0])
    own = pl.multiple_of((core * steps + step) * cut, cut)
    other = pl.multiple_of(((1 - core) * steps + step) * cut, cut)
    return own, other


def dense_call(kernel, core, steps, whole, halves, out, scratch, name, micros):
    cut = halves[0].shape[1] // steps

    def keep(shape):
        return pl.BlockSpec(
            shape, lambda step, core: (0,) * len(shape), pipeline_mode=pl.Buffered(buffer_count=1)
        )

    def tile(tall):
        return pl.BlockSpec((tall, cut), lambda step, core: (0, step))

    return pl.pallas_call(
        kernel,
        grid_spec=pltpu.PrefetchScalarGridSpec(
            num_scalar_prefetch=1,
            grid=(steps,),
            in_specs=[keep(part.shape) for part in whole] + [tile(halves[0].shape[0])] * 2,
            out_specs=[
                tile(part.shape[0]) if tiled else keep(part.shape) for part, tiled in out
            ],
            scratch_shapes=scratch,
        ),
        out_shape=[part for part, _ in out],
        compiler_params=kernel_params(),
        cost_estimate=cost(micros),
        name=name,
    )(core.astype(jnp.int32).reshape(1), *whole, *halves)


def shape_of(kind, *shape):
    return jax.ShapeDtypeStruct(shape, kind)


def enter_kernel(steps, terms, core_ref, gain_ref, *refs):
    parts, (own_ref, other_ref, sent_ref, normed_ref, out_ref) = (refs[:terms], refs[terms:])
    own, other = side_offsets(core_ref, steps, own_ref.shape[1])

    @pl.when(pl.program_id(0) == 0)
    def _():
        sent = add_all(parts).astype(bf16)
        sent_ref[...] = sent
        normed_ref[...] = (norm_parts(sent.astype(f32))[1] * gain_ref[...]).astype(bf16)

    cut = own_ref.shape[1]
    out_ref[:, pl.ds(own, cut)] = nn(normed_ref[...], own_ref[...]).astype(bf16)
    out_ref[:, pl.ds(other, cut)] = nn(normed_ref[...], other_ref[...]).astype(bf16)


def enter_call(core, parts, gain, halves):
    rows, width = parts[0].shape
    return dense_call(
        functools.partial(enter_kernel, 3, len(parts)),
        core,
        3,
        [gain] + parts,
        halves,
        [
            (shape_of(bf16, rows, width), False),
            (shape_of(bf16, rows, width), False),
            (shape_of(bf16, rows, 2 * halves[0].shape[1]), False),
        ],
        [],
        "enter",
        6,
    )


def leave_kernel(steps, core_ref, gain_ref, rows_ref, attended_ref, own_ref, other_ref,
                 mid_ref, normed_ref):
    cut = own_ref.shape[1]
    for start, ref in zip(side_offsets(core_ref, steps, cut), (own_ref, other_ref)):
        part = pl.ds(start, cut)
        mid_ref[:, part] = rows_ref[:, part].astype(f32) + nn(attended_ref[...], ref[...])

    @pl.when(pl.program_id(0) == steps - 1)
    def _():
        normed_ref[...] = (norm_parts(mid_ref[...])[1] * gain_ref[...]).astype(bf16)


def leave_call(core, rows_in, attended, gain, halves):
    rows, width = rows_in.shape
    return dense_call(
        functools.partial(leave_kernel, 2),
        core,
        2,
        [gain, rows_in, attended],
        halves,
        [(shape_of(f32, rows, width), False), (shape_of(bf16, rows, width), False)],
        [],
        "leave",
        5,
    )


def leave_back_kernel(steps, terms, core_ref, gain_ref, mid_ref, cot_ref, attended_ref, *refs):
    parts, refs = (refs[:terms], refs[terms:])
    own_ref, other_ref, after_ref, term_ref, d_attended_ref, *refs = refs
    own_grad_ref, other_grad_ref, branch_ref, turned_ref, total_ref = refs
    step, cut = (pl.program_id(0), own_ref.shape[1])

    @pl.when(step == 0)
    def _():
        back, term_ref[...] = norm_back(add_all(parts), gain_ref[...], mid_ref[...])
        back = back + cot_ref[...].astype(f32)
        after_ref[...] = back
        branch_ref[...] = back.astype(bf16)
        turned_ref[...] = attended_ref[...].T

    own, other = side_offsets(core_ref, steps, cut)
    d_own, d_other = (branch_ref[:, pl.ds(own, cut)], branch_ref[:, pl.ds(other, cut)])
    own_grad_ref[...] = nn(turned_ref[...], d_own).astype(bf16)
    other_grad_ref[...] = nn(turned_ref[...], d_other).astype(bf16)
    add_up(total_ref, nt(d_own, own_ref[...]) + nt(d_other, other_ref[...]), step)

    @pl.when(step == steps - 1)
    def _():
        d_attended_ref[...] = total_ref[...].astype(bf16)


def leave_back_call(core, parts, gain, mid, cotangent, attended, halves):
    rows, width = mid.shape
    half = (halves[0].shape[0], halves[0].shape[1])
    return dense_call(
        functools.partial(leave_back_kernel, 2, len(parts)),
        core,
        2,
        [gain, mid, cotangent, attended] + parts,
        halves,
        [
            (shape_of(f32, rows, width), False),
            (shape_of(bf16, rows, width), False),
            (shape_of(bf16, rows, width), False),
            (shape_of(bf16, *half), True),
            (shape_of(bf16, *half), True),
        ],
        [
            pltpu.VMEM((rows, width), bf16),
            pltpu.VMEM((width, rows), bf16),
            pltpu.VMEM((rows, width), f32),
        ],
        "leave_back",
        8,
    )


def enter_back_kernel(steps, terms, core_ref, gain_ref, rows_ref, normed_ref, after_ref, term_ref,
                      dq_ref, *refs):
    parts, refs = (refs[:terms], refs[terms:])
    own_ref, other_ref, entry_ref, sent_ref, own_grad_ref, other_grad_ref, *refs = refs
    entered_ref, turned_ref, total_ref = refs
    step, cut = (pl.program_id(0), own_ref.shape[1])
    rows, qw = dq_ref.shape

    @pl.when(step == 0)
    def _():
        entered_ref[:, :qw] = dq_ref[...]
        wide = parts[0].shape[1]
        entered_ref[:, qw : qw + wide] = add_all(parts).astype(bf16)
        entered_ref[:, qw + wide :] = jnp.zeros((rows, gap), bf16)
        turned_ref[...] = normed_ref[...].T

    own, other = side_offsets(core_ref, steps, cut)
    d_own, d_other = (entered_ref[:, pl.ds(own, cut)], entered_ref[:, pl.ds(other, cut)])
    own_grad_ref[...] = nn(turned_ref[...], d_own).astype(bf16)
    other_grad_ref[...] = nn(turned_ref[...], d_other).astype(bf16)
    add_up(total_ref, nt(d_own, own_ref[...]) + nt(d_other, other_ref[...]), step)

    @pl.when(step == steps - 1)
    def _():
        back, attn_term = norm_back(total_ref[...], gain_ref[...], rows_ref[...].astype(f32))
        back = back + after_ref[...]
        entry_ref[...] = back
        sent_ref[...] = back.astype(bf16)
        lane = lax.broadcasted_iota(jnp.int32, (rows, 128), 1)
        sums = nn(attn_term.T, (lane == 0).astype(bf16))
        sums = (sums + nn(term_ref[...].T, (lane == 1).astype(bf16))).astype(bf16)
        left = cut - gap

        @pl.when(core_ref[0] == 0)
        def _():
            other_grad_ref[:, left : left + 128] = sums

        @pl.when(core_ref[0] != 0)
        def _():
            own_grad_ref[:, left : left + 128] = sums


def enter_back_call(core, dq, parts, gain, rows_in, normed, after, term, halves):
    rows, width = rows_in.shape
    return dense_call(
        functools.partial(enter_back_kernel, 3, len(parts)),
        core,
        3,
        [gain, rows_in, normed, after, term, dq] + parts,
        halves,
        [
            (shape_of(f32, rows, width), False),
            (shape_of(bf16, rows, width), False),
            (shape_of(bf16, *halves[0].shape), True),
            (shape_of(bf16, *halves[0].shape), True),
        ],
        [
            pltpu.VMEM((rows, 2 * halves[0].shape[1]), bf16),
            pltpu.VMEM((width, rows), bf16),
            pltpu.VMEM((rows, width), f32),
        ],
        "enter_back",
        13,
    )


def place_kernel(count, joined, index_ref, *refs):
    step = pl.program_id(0)
    for bit in range(count):

        @pl.when(step == bit)
        def _():
            if joined:
                refs[count][...] = refs[bit][...]
            else:
                refs[count][0] = refs[bit][...]


def place_call(blocks, index):
    count = len(blocks)
    shape = blocks[0].shape
    zeros = (0,) * len(shape)
    joined = len(shape) == 2 and shape[0] % 16 == 0
    if joined:
        out_spec = pl.BlockSpec(shape, lambda step, at: (at[0] ^ step, 0))
        out_shape = (count * shape[0], shape[1])
    else:
        out_spec = pl.BlockSpec((1,) + shape, lambda step, at: (at[0] ^ step,) + zeros)
        out_shape = (count,) + shape
    return pl.pallas_call(
        functools.partial(place_kernel, count, joined),
        grid_spec=pltpu.PrefetchScalarGridSpec(
            num_scalar_prefetch=1,
            grid=(count,),
            in_specs=[pl.BlockSpec(shape, lambda step, at: zeros)] * count,
            out_specs=out_spec,
        ),
        out_shape=jax.ShapeDtypeStruct(out_shape, blocks[0].dtype),
        compiler_params=kernel_params(),
        cost_estimate=cost(2),
        name="place",
    )(index.astype(jnp.int32).reshape(1), *blocks)


def deal_kernel(count, index_ref, *refs):
    step = pl.program_id(0)
    for bit in range(count):

        @pl.when(step == bit)
        def _():
            for layer, ref in enumerate(refs[count:]):
                ref[0] = refs[bit][layer]


def deal_call(blocks, index):
    count = len(blocks)
    layers, *shape = blocks[0].shape
    shape = tuple(shape)
    zeros = (0,) * len(shape)
    return pl.pallas_call(
        functools.partial(deal_kernel, count),
        grid_spec=pltpu.PrefetchScalarGridSpec(
            num_scalar_prefetch=1,
            grid=(count,),
            in_specs=[pl.BlockSpec((layers,) + shape, lambda step, at: (0,) + zeros)] * count,
            out_specs=[pl.BlockSpec((1,) + shape, lambda step, at: (at[0] ^ step,) + zeros)]
            * layers,
        ),
        out_shape=[jax.ShapeDtypeStruct((count,) + shape, blocks[0].dtype)] * layers,
        compiler_params=kernel_params(),
        cost_estimate=cost(2),
        name="deal",
    )(index.astype(jnp.int32).reshape(1), *blocks)


def order_kernel(count, order_ref, *refs):
    step = pl.program_id(0)
    for i in range(count):

        @pl.when(step == i)
        def _():
            refs[count][:, 0] = refs[i][:, 0]


def order_call(blocks, order, unit):
    count = len(blocks)
    n_ctx, _, tall, wide = blocks[0].shape
    shape = (n_ctx, 1, tall, wide)
    source = pl.BlockSpec(
        shape, lambda step, at: (0, unit, 0, 0), pipeline_mode=pl.Buffered(buffer_count=1)
    )
    result = pl.pallas_call(
        functools.partial(order_kernel, count),
        grid_spec=pltpu.PrefetchScalarGridSpec(
            num_scalar_prefetch=1,
            grid=(count,),
            in_specs=[source] * count,
            out_specs=pl.BlockSpec(shape, lambda step, at: (0, at[step], 0, 0)),
        ),
        out_shape=jax.ShapeDtypeStruct((n_ctx, count, tall, wide), bf16),
        compiler_params=kernel_params(),
        cost_estimate=cost(4),
        name="order",
    )(order.astype(jnp.int32), *blocks)
    return result.reshape(n_ctx * count, tall, wide)


def finish_kernel(deep, index_ref, own_ref, other_ref, gate_ref, up_ref, down_ref):
    side = pl.program_id(1)
    wide = gate_ref.shape[2] // 2

    def write(source):
        for half in range(2):
            left, target = (2 * half * wide, slice(half * wide, (half + 1) * wide))
            gate_ref[:, :, target] = source[0, :, :deep, left : left + wide].astype(f32)
            left = left + wide
            up_ref[:, :, target] = source[0, :, :deep, left : left + wide].astype(f32)
        down_ref[...] = source[0, :, deep:, :].astype(f32)

    @pl.when(side == index_ref[1])
    def _():
        write(own_ref)

    @pl.when(side != index_ref[1])
    def _():
        write(other_ref)


def finish_call(own, other, deep, hidden, place, core):
    n_ctx, units, tall, width = own.shape
    experts = 2 * n_ctx * units
    source = pl.BlockSpec((1, units, tall, width), lambda bit, side, at: (bit, 0, 0, 0))
    target = lambda bit, side, at: (2 * (at[0] ^ bit) + side, 0, 0)
    return pl.pallas_call(
        functools.partial(finish_kernel, deep),
        grid_spec=pltpu.PrefetchScalarGridSpec(
            num_scalar_prefetch=1,
            grid=(n_ctx, 2),
            in_specs=[source, source],
            out_specs=[
                pl.BlockSpec((units, deep, hidden), target),
                pl.BlockSpec((units, deep, hidden), target),
                pl.BlockSpec((units, tall - deep, width), target),
            ],
        ),
        out_shape=[
            jax.ShapeDtypeStruct((experts, deep, hidden), f32),
            jax.ShapeDtypeStruct((experts, deep, hidden), f32),
            jax.ShapeDtypeStruct((experts, tall - deep, width), f32),
        ],
        compiler_params=kernel_params(),
        cost_estimate=cost(8),
        name="finish",
    )(jnp.stack([place, core]).astype(jnp.int32), own, other)


def body(
    tokens,
    block_of,
    routes,
    combine,
    attn_norm,
    w_query,
    w_key,
    w_value,
    w_out,
    ffn_norm,
    w_gate,
    w_up,
    w_down,
    out_grad,
):
    rows = tokens.shape[2]
    width = tokens.shape[3]
    half = rows // 2
    n_ctx = lax.axis_size("ctx")
    n_fsdp = lax.axis_size("fsdp")
    core, place, depth = (
        lax.axis_index(axis).astype(jnp.uint32) for axis in ("section", "ctx", "fsdp")
    )
    seq_len = rows * n_ctx
    capacity = rows * TOP * 5 // (4 * EXPERTS)
    score_scale = HD ** (-0.5)
    own_experts = EXPERTS // n_ctx
    hidden = w_gate.shape[3]
    shard_rows = w_query.shape[1]
    down_rows = w_down.shape[2]
    qw = w_query.shape[2]
    kw = w_key.shape[2]
    pieces = max(1, 2 * n_ctx // EXPERTS)
    per_core = max(1, EXPERTS // (2 * n_ctx))
    unit_rows = shard_rows + down_rows
    aligned = shard_rows % 16 == 0 and down_rows % 16 == 0

    def on_core(former, latter):
        return jnp.where(core == 0, former, latter)

    def own_other(low, high):
        return (on_core(low, high), on_core(high, low))

    early, late = (range(1, n_ctx // 2 + 1), range(n_ctx // 2 + 1, n_ctx))

    def send(value, bits):
        return [swap(value, "ctx", bit) for bit in bits]

    def spread(value):
        return [value] + send(value, early) + send(value, late)

    def spread_rows(value):
        near_blocks = send(value, early)
        value, near_blocks = tie(value, near_blocks)
        return [value] + near_blocks + send(value, late)

    def gather_back(blocks):
        return [blocks[0]] + [swap(blocks[bit], "ctx", bit) for bit in range(1, n_ctx)]

    info = jnp.concatenate([routes.astype(f32), combine], axis=-1)[0, :, 0].transpose(0, 2, 1)
    info_own, info_other = (at(info, core), swap(at(info, 1 - core), "section", 1))
    info = jnp.stack(own_other(info_own, info_other))
    info = jnp.stack([info] + [swap(info, "ctx", bit) for bit in range(1, n_ctx)], axis=1)

    gain_columns = jnp.stack([attn_norm[0], ffn_norm[0]], axis=1)
    gain_columns = jnp.pad(gain_columns, ((0, 0), (0, gap - 2)))
    enter_shard = jnp.concatenate([w_query[0], w_key[0], w_value[0], gain_columns], axis=1)
    enter_cut = enter_shard.shape[1] // 2
    leave_cut = w_out.shape[2] // 2
    low_shard = jnp.concatenate([enter_shard[:, :enter_cut], w_out[0, :, :leave_cut]], axis=1)
    high_shard = jnp.concatenate([enter_shard[:, enter_cut:], w_out[0, :, leave_cut:]], axis=1)
    lent = swap(on_core(high_shard, low_shard), "section", 1)
    dense_shards = (on_core(low_shard, lent), on_core(lent, high_shard))

    def gather_deep(shard):
        blocks = [shard] + [swap(shard, "fsdp", bit) for bit in range(1, n_fsdp)]
        return place_call(blocks, depth).reshape(-1, shard.shape[1])

    def join_square(blocks):
        return place_call(blocks, place).reshape(-1, blocks[0].shape[1])

    def gather_square(deep):
        return join_square(spread(deep))

    cut = hidden // 2
    unit_stack = jnp.concatenate(
        [
            jnp.concatenate(
                [w_gate[0, ..., :cut], w_up[0, ..., :cut], w_gate[0, ..., cut:], w_up[0, ..., cut:]],
                axis=2,
            ),
            w_down[0],
        ],
        axis=1,
    )
    if pieces == 2:
        unit_stack = jnp.stack(jnp.split(unit_stack, 2, axis=2), axis=1)
    unit_stack = unit_stack.reshape(n_ctx, 2, per_core, unit_rows, width // pieces)
    units_lent = swap(at(unit_stack, 1 - core, 1), "section", 1)
    unit_stacks = jnp.stack(own_other(at(unit_stack, core, 1), units_lent), axis=1)

    def deal_units(stack):
        blocks = [at(stack, place)]
        blocks += [swap(at(stack, place ^ bit), "ctx", bit) for bit in range(1, n_ctx)]
        return deal_call(blocks, place)

    ring = list(range(0, n_fsdp, 2)) + list(range(1, n_fsdp, 2))[::-1]
    ring_steps = [(ring[i], ring[(i + 1) % n_fsdp]) for i in range(n_fsdp)]
    ring_table = [[ring[ring.index(z) - i] for i in range(n_fsdp)] for z in range(n_fsdp)]
    behind_here = at(jnp.array(ring_table, jnp.uint32), depth)

    def ring_send(moved):
        return [blocks + [lax.ppermute(blocks[-1], "fsdp", ring_steps)] for blocks in moved]

    def own_units(blocks):
        return [order_call(blocks, behind_here, unit) for unit in range(per_core)]

    def pair_units(mine):
        other = [swap(part, "section", 1) for part in mine]
        units = list(mine) + other
        if pieces == 2:
            units = [jnp.concatenate(own_other(mine[0], other[0]), axis=2)]
        if aligned:
            return [[unit] for unit in units]
        return [
            [unit[:, :shard_rows].reshape(-1, width), unit[:, shard_rows:].reshape(-1, width)]
            for unit in units
        ]

    def cut_units(grads):
        if aligned:
            units = [unit for (unit,) in grads]
        else:
            units = [
                jnp.concatenate(
                    [part.reshape(n_ctx * n_fsdp, -1, width) for part in parts], axis=1
                )
                for parts in grads
            ]
        if pieces == 1:
            return (units[:per_core], units[per_core:])
        own, other = own_other(*jnp.split(units[0], 2, axis=2))
        return ([own], [other])

    def ring_part(terms, behind):
        spot = behind_here[behind % n_fsdp]
        return sum(at(term, spot, 1).astype(f32) for term in terms)

    def ring_start(own, received):
        terms = [part.reshape((n_ctx, n_fsdp) + part.shape[1:]) for part in (own, received)]
        return (terms, ring_part(terms, 1).astype(bf16))

    def ring_move(state):
        return [(terms, lax.ppermute(moving, "fsdp", ring_steps)) for terms, moving in state]

    def ring_add(state, step):
        return [
            (terms, (moved.astype(f32) + ring_part(terms, step + 1)).astype(bf16))
            for terms, moved in state
        ]

    def ring_step(state, step):
        return ring_add(ring_move(state), step)

    def ring_last(state):
        state = ring_add(state, 2)
        for step in range(3, n_fsdp - 1):
            state = ring_step(state, step)
        return ring_move(state)

    def ring_rest(state, first):
        for step in range(first, n_fsdp):
            state = ring_step(state, step)
        return [moving for _, moving in state]

    def scatter_units(moved):
        whole = jnp.stack(moved, axis=1)
        blocks = [at(whole, place)]
        blocks += [swap(at(whole, place ^ bit), "ctx", bit) for bit in range(1, n_ctx)]
        return jnp.stack(blocks)

    def trade_square(own, received, bits):
        own, received = (part.reshape(n_ctx, -1, part.shape[1]) for part in (own, received))

        def part(bit):
            return at(own, place ^ bit).astype(f32) + at(received, place ^ bit).astype(f32)

        return [part(bit) if bit == 0 else swap(part(bit).astype(bf16), "ctx", bit) for bit in bits]

    def sum_square(parts):
        return sum(part.astype(f32) for part in parts).astype(bf16)

    def reduce_deep(mine):
        mine = mine.reshape(n_fsdp, shard_rows, -1)
        total = at(mine, depth).astype(f32)
        for bit in range(1, n_fsdp):
            total = total + swap(at(mine, depth ^ bit), "fsdp", bit).astype(f32)
        return total

    if pieces == 1:
        units_here = jnp.arange(per_core, dtype=jnp.uint32)
        units_here = jnp.concatenate(
            [core * per_core + units_here, (1 - core) * per_core + units_here]
        )
    else:
        units_here = jnp.zeros((1,), jnp.uint32)
    named = (place * own_experts + units_here).astype(f32)
    matches = info[:, None, :, :TOP] == named[None, :, None, None, None]
    hits = jnp.any(matches, axis=3)
    shares = jnp.sum(jnp.where(matches, info[:, None, :, TOP:], 0.0), axis=3)
    earlier = jnp.arange(rows)[:, None] < jnp.arange(rows)[None, :]
    rank = dot("ledr,rq->ledq", hits.astype(bf16), earlier.astype(bf16))
    slots = jnp.arange(capacity, dtype=f32)
    picks = hits[:, :, :, None, :] & (rank[:, :, :, None, :] == slots[:, None])
    slot_shares = jnp.sum(jnp.where(picks, shares[:, :, :, None, :], 0.0), axis=-1, keepdims=True)
    picks = picks.astype(bf16)

    order = place.astype(jnp.int32) ^ jnp.arange(n_ctx, dtype=jnp.int32)
    block_ids = jnp.take(block_of.reshape(n_ctx, 2), order, axis=0)
    block_ids = block_ids.reshape(-1)

    def gains_of(halves):
        pair = on_core(halves[1][:, -gap : 2 - gap], halves[0][:, -gap : 2 - gap])
        pair = pair.astype(f32).T
        return (pair[:1], pair[1:])

    near = 1 + len(early)
    parts = (slice(0, near), slice(near, n_ctx))

    def experts(layer, blocks, weights, answer, beside=lambda: []):
        kept, arrived = ({}, [])
        back = {}
        for index, part in enumerate(parts):
            rows_here = blocks[part]
            if index:
                back[0], rows_here = tie(back[0], rows_here)
                arrived = [swap(block, "ctx", bit) for bit, block in zip(early, back[0][1:])]
            back[index] = []
            for j in range(own_experts):
                back[index], kept[index, j] = expert_call(
                    picks[layer, j, part],
                    slot_shares[layer, j, part],
                    rows_here,
                    weights[j],
                    shard_rows,
                    hidden,
                    back[index],
                    3 if index == 0 else 1,
                )
        if not answer:
            return (back[0] + back[1], kept)
        back[1], arrived, found = tie(back[1], arrived, beside())
        arrived += [swap(block, "ctx", bit) for bit, block in zip(late, back[1])]
        return (back[0][:1] + arrived, kept, found)

    def experts_back(layer, blocks, weights, kept, delay, beside_near, beside_far, beside_end):
        back, saved = ({}, {})
        for index, part in enumerate(parts):
            rows_here = blocks[part]
            if index:
                back[0], rows_here, found_near = tie(back[0], rows_here, beside_near())
                arrived = [swap(block, "ctx", bit) for bit, block in zip(early, back[0][1:])]
            back[index] = []
            for j in range(own_experts):
                back[index], saved[index, j] = expert_back_call(
                    picks[layer, j, part],
                    slot_shares[layer, j, part],
                    rows_here,
                    kept[index, j],
                    weights[j],
                    shard_rows,
                    back[index],
                    4 if index == 0 else 1,
                )
        back[1], arrived, saved, found_far = tie(back[1], arrived, saved, beside_far(found_near))
        arrived += [swap(block, "ctx", bit) for bit, block in zip(late, back[1])]

        def grads_of(j, saved):
            picked = [kept[index, j][0] for index in range(2)]
            both = [saved[index, j] for index in range(2)]
            return expert_grads_call(picked, both, weights[j], shard_rows)

        now = [j for j in reversed(range(own_experts)) if not delay or j >= per_core]
        grads = {j: grads_of(j, saved) for j in now}
        arrived, grads, found_end = tie(arrived, grads, beside_end(found_far))
        returned = back[0][:1] + arrived
        if len(now) == own_experts:
            own, other = cut_units([grads[j] for j in range(own_experts)])
            received = [swap(part, "section", 1) for part in other]
            return (returned, lambda earlier: (own, received), found_end)
        received = [swap(grads[j][0], "section", 1) for j in reversed(now)]

        def finish(earlier):
            ready = after(saved, earlier)
            return ([grads_of(j, ready)[0] for j in range(per_core)], received)

        return (returned, finish, found_end)

    def keep_own(first, second):
        other = swap(on_core(second, first), "section", 1)
        return own_other(on_core(first, second), other)

    dense_first, dense_second = dense_shards
    deep = gather_deep(jnp.concatenate([dense_first, dense_second[:, :enter_cut]], axis=1))
    dealt_first, dealt_second = deal_units(unit_stacks)
    deep, dealt_first, dealt_second, picks, dense_second = tie(
        deep, dealt_first, dealt_second, picks, dense_second
    )
    dense_blocks, moved, leave_shard, enter_shard = tie(
        spread(deep[:, :enter_cut]),
        ring_send([[dealt_first]]),
        deep[:, enter_cut : enter_cut + leave_cut],
        deep[:, enter_cut + leave_cut :],
    )
    leave_blocks = [leave_shard] + send(leave_shard, early)
    enter_own = join_square(dense_blocks)
    enter_first = (enter_own, swap(enter_own, "section", 1))

    first_gains = gains_of(enter_first)
    first_in = after(at(tokens, core)[0], slot_shares)
    _, first_normed, first_entered = enter_call(core, [first_in], first_gains[0], enter_first)
    first_entered, leave_blocks = tie(first_entered, leave_blocks)
    key_value = first_entered[:, qw : qw + 2 * kw]
    first_kv, leave_shard = tie(jnp.concatenate(spread(key_value)), leave_shard)
    first_attended = attend_call(block_ids, first_entered, first_kv)
    moved = ring_send(moved)
    first_attended, leave_blocks, dealt_second, moved, enter_shard, dense_second = tie(
        first_attended,
        leave_blocks + send(leave_shard, late),
        dealt_second,
        moved,
        enter_shard,
        dense_second,
    )
    enter_blocks = [enter_shard] + send(enter_shard, early)
    for _ in range(2, n_fsdp - 1):
        moved = ring_send(moved)
    leave_own = join_square(leave_blocks)
    leave_first = (leave_own, swap(leave_own, "section", 1))
    first_mid, ffn_normed = leave_call(core, first_in, first_attended, first_gains[1], leave_first)
    ffn_normed, enter_blocks = tie(ffn_normed, enter_blocks)
    blocks = spread_rows(ffn_normed)
    blocks[:near], moved, dealt_second, enter_shard, leave_shard = tie(
        blocks[:near], moved, dealt_second, enter_shard, dense_second[:, enter_cut:]
    )
    first_weights = pair_units(own_units(moved[0]))
    returned, first_kept, (moved, leave_shard, enter_blocks) = experts(
        0,
        blocks,
        first_weights,
        True,
        lambda: (
            ring_send([[dealt_second]]),
            leave_shard,
            enter_blocks + send(enter_shard, late),
        ),
    )
    moved = ring_send(moved)
    enter_own = join_square(enter_blocks)
    enter_second = (enter_own, swap(enter_own, "section", 1))
    returned, moved, leave_shard = tie(returned, moved, gather_deep(leave_shard))
    moved = ring_send(moved)
    leave_blocks = [leave_shard] + send(leave_shard, early)

    second_gains = gains_of(enter_second)
    second_in, second_normed, second_entered = enter_call(
        core, [first_mid] + returned, second_gains[0], enter_second
    )
    second_entered, leave_blocks = tie(second_entered, leave_blocks)
    key_value = second_entered[:, qw : qw + 2 * kw]
    for _ in range(4, n_fsdp):
        moved = ring_send(moved)
    second_kv, leave_shard = tie(jnp.concatenate(spread(key_value)), leave_shard)
    second_attended = attend_call(block_ids, second_entered, second_kv)
    second_attended, leave_blocks, moved = tie(
        second_attended, leave_blocks + send(leave_shard, late), moved
    )
    leave_own = join_square(leave_blocks)
    leave_second = (leave_own, swap(leave_own, "section", 1))
    second_mid, ffn_normed = leave_call(
        core, second_in, second_attended, second_gains[1], leave_second
    )
    second_weights = pair_units(own_units(after(moved, ffn_normed)[0]))
    blocks = spread_rows(ffn_normed)
    second_returned, second_kept = experts(1, blocks, second_weights, False)
    cotangent = after(at(out_grad, core)[0], second_returned[:near])
    cot_blocks = spread_rows(cotangent)
    cot_blocks[:near], second_returned[near:] = tie(cot_blocks[:near], second_returned[near:])

    returned, finish, (second_returned, near_parts) = experts_back(
        1,
        cot_blocks,
        second_weights,
        second_kept,
        False,
        lambda: second_returned,
        lambda found: found,
        lambda found: (found, [swap(found[bit], "ctx", bit) for bit in early]),
    )
    far_parts = [swap(second_returned[bit], "ctx", bit) for bit in late]
    units_moving = [ring_start(*pair) for pair in zip(*finish(()))]
    after_rows, term, d_attended, *grads = leave_back_call(
        core,
        returned,
        second_gains[1],
        second_mid,
        cotangent,
        second_attended,
        leave_second,
    )
    leave_grads = (grads[0], swap(grads[1], "section", 1))
    d_queries, d_key_value = attend_back_call(block_ids, second_entered, second_kv, d_attended)
    d_queries, d_key_value, leave_grads, far_parts = tie(
        d_queries, d_key_value, leave_grads, far_parts
    )
    second_parts = second_returned[:1] + near_parts + far_parts
    second_out = second_mid + sum(part.astype(f32) for part in second_parts)
    d_key_value, units_moving = tie(gather_back(d_key_value), ring_move(units_moving))
    units_moving = ring_move(ring_add(units_moving, 1))
    leave_parts = trade_square(*leave_grads, range(n_ctx))
    second_entry, cotangent, *grads = enter_back_call(
        core,
        d_queries,
        d_key_value,
        second_gains[0],
        second_in,
        second_normed,
        after_rows,
        term,
        enter_second,
    )
    cotangent, grads, leave_parts, layer_rows = tie(
        cotangent, grads, leave_parts, (second_in, second_out.astype(bf16))
    )
    enter_grads = (grads[0], swap(grads[1], "section", 1))

    blocks = spread_rows(cotangent)
    blocks[:near], enter_grads, layer_rows = tie(blocks[:near], enter_grads, layer_rows)

    def dense_sums(parts):
        moving = [sum_square(some) for some in (parts, leave_parts)]
        return reduce_deep(jnp.concatenate(moving, axis=1))

    returned, finish, (units_moving, layer_outs, second_dense) = experts_back(
        0,
        blocks,
        first_weights,
        first_kept,
        False,
        lambda: (units_moving, trade_square(*enter_grads, [0, *early]), enter_grads),
        lambda found: (
            found[0],
            keep_own(*layer_rows),
            found[1] + trade_square(*found[2], late),
        ),
        lambda found: (ring_last(found[0]), found[1], dense_sums(found[2])),
    )
    second_moved = [moving for _, moving in ring_add(units_moving, n_fsdp - 1)]
    own, received = finish(())
    after_rows, term, d_attended, *grads = leave_back_call(
        core,
        returned,
        first_gains[1],
        first_mid,
        cotangent,
        first_attended,
        leave_first,
    )
    units_moving = [ring_start(*pair) for pair in zip(own, received)]
    leave_grads = (grads[0], swap(grads[1], "section", 1))
    d_queries, d_key_value = attend_back_call(block_ids, first_entered, first_kv, d_attended)
    d_queries, d_key_value, leave_grads = tie(d_queries, d_key_value, leave_grads)
    d_key_value, units_moving, leave_grads = tie(
        gather_back(d_key_value), ring_move(units_moving), leave_grads
    )
    leave_parts = trade_square(*leave_grads, [0, *early])
    units_moving = ring_move(ring_add(units_moving, 1))
    first_entry, _, *grads = enter_back_call(
        core,
        d_queries,
        d_key_value,
        first_gains[0],
        first_in,
        first_normed,
        after_rows,
        term,
        enter_first,
    )
    grads, leave_parts, leave_grads = tie(grads, leave_parts, leave_grads)
    enter_grads = (grads[0], swap(grads[1], "section", 1))
    enter_parts, leave_parts, first_entry = tie(
        trade_square(*enter_grads, range(n_ctx)),
        leave_parts + trade_square(*leave_grads, late),
        first_entry,
    )
    first_moving = [sum_square(parts) for parts in (enter_parts, leave_parts)]
    first_dense = reduce_deep(jnp.concatenate(first_moving, axis=1))
    scattered = scatter_units(ring_rest(ring_add(units_moving, 2), 3) + second_moved)
    first_scattered, second_scattered = (scattered[:, :per_core], scattered[:, per_core:])

    layer_out = jnp.stack(layer_outs)
    input_grads = jnp.stack(keep_own(first_entry, second_entry))
    low_dense, high_dense = keep_own(first_dense, second_dense)
    enter_grad = jnp.concatenate([low_dense[:, :enter_cut], high_dense[:, :enter_cut]], axis=1)
    grad_out = jnp.concatenate([low_dense[:, enter_cut:], high_dense[:, enter_cut:]], axis=1)
    grad_gains = enter_grad[:, qw + 2 * kw :]
    mine = on_core(first_scattered, second_scattered)
    other = swap(on_core(second_scattered, first_scattered), "section", 1)
    if aligned and pieces == 1:
        grad_gate, grad_up, grad_down = finish_call(mine, other, shard_rows, hidden, place, core)
    else:
        sides = [jnp.take(part, order, axis=0) for part in own_other(mine, other)]
        if pieces == 1:
            whole = jnp.stack(sides, axis=1).reshape(EXPERTS, unit_rows, width)
        else:
            whole = jnp.concatenate([side[:, 0] for side in sides], axis=2)
        pairs = whole[:, :shard_rows].astype(f32).reshape(EXPERTS, shard_rows, 2, 2, cut)
        grad_gate = pairs[:, :, :, 0].reshape(EXPERTS, shard_rows, hidden)
        grad_up = pairs[:, :, :, 1].reshape(EXPERTS, shard_rows, hidden)
        grad_down = whole[:, shard_rows:].astype(f32)
    return (
        layer_out[None, :, None],
        input_grads[None, :, None],
        grad_gains[:, 0][None],
        enter_grad[:, :qw][None],
        enter_grad[:, qw : qw + kw][None],
        enter_grad[:, qw + kw : qw + 2 * kw][None],
        grad_out[None],
        grad_gains[:, 1][None],
        grad_gate[None],
        grad_up[None],
        grad_down[None],
    )


def solution(mesh):
    rows_placed = P(None, "fsdp", "ctx", None)
    kept_placed = P("section", None, "fsdp", "ctx", None)
    gain_placed = P("section", ("ctx", "fsdp"))
    dense_placed = P("section", ("ctx", "fsdp"), None)
    expert_placed = P("section", None, ("ctx", "fsdp"), None)
    dense_all = (dense_placed,) * 4
    expert_all = (expert_placed,) * 3
    layer_placed = (gain_placed,) + dense_all + (gain_placed,) + expert_all
    return jax.shard_map(
        body,
        mesh=mesh,
        in_specs=(rows_placed, P(), kept_placed, kept_placed) + layer_placed + (rows_placed,),
        out_specs=(kept_placed, kept_placed) + layer_placed,
        check_vma=False,
    )
```

```python
import functools

import jax
import jax.numpy as jnp
from jax import lax
from jax.experimental import pallas as pl
from jax.experimental.pallas import tpu as pltpu
from jax.sharding import PartitionSpec as P

QH = 12
KVH = 2
HD = 128
GROUP = QH // KVH
TOP = 4
EXPERTS = 8
bf16 = jnp.bfloat16
f32 = jnp.float32


epsilon = 1e-06
masked_out = -1e30
gap = 256


def swap(value, axis, bit):
    count = lax.axis_size(axis)
    return lax.ppermute(value, axis, [(source, source ^ bit) for source in range(count)])


def tie(*values):
    return lax.optimization_barrier(values)


def after(value, earlier):
    return tie(value, earlier)[0]


def at(value, index, axis=0):
    return lax.dynamic_index_in_dim(value, index, axis, keepdims=False)


def dot(spec, left, right, kind=f32):
    return jnp.einsum(spec, left, right, preferred_element_type=kind)


def cost(micros):
    return pl.CostEstimate(
        flops=int(micros * 1e9), bytes_accessed=int(micros * 3e6), transcendentals=0
    )


def kernel_params():
    return pltpu.CompilerParams(vmem_limit_bytes=56 * 1024 * 1024)


def nt(left, right):
    return lax.dot_general(left, right, (((1,), (1,)), ((), ())), preferred_element_type=f32)


def nn(left, right):
    return jnp.dot(left, right, preferred_element_type=f32)


def head_rows(ref):
    return jnp.concatenate([ref[:, i * HD : (i + 1) * HD] for i in range(GROUP)], axis=0)


def softmax_rows(ids_ref, queries, keys, half, own):
    scores = nt(queries, keys) * HD ** (-0.5)
    tall, wide = scores.shape
    row = lax.broadcasted_iota(jnp.int32, (half, 1), 0)
    row = jnp.concatenate([row] * (tall // half), axis=0) + ids_ref[own] * half
    lane = lax.broadcasted_iota(jnp.int32, (1, half), 1)
    column = [lane + ids_ref[block] * half for block in range(wide // half)]
    column = jnp.concatenate(column, axis=1)
    scores = jnp.where(row >= column, scores, masked_out)
    shifted = jnp.exp(scores - jnp.max(scores, axis=1, keepdims=True))
    return shifted / jnp.sum(shifted, axis=1, keepdims=True)


def attend_kernel(ids_ref, query_ref, key_ref, value_ref, out_ref):
    half = query_ref.shape[0]
    probs = softmax_rows(ids_ref, head_rows(query_ref), key_ref[...], half, pl.program_id(1))
    out = nn(probs.astype(bf16), value_ref[...]).astype(bf16)
    for i in range(GROUP):
        out_ref[:, i * HD : (i + 1) * HD] = out[i * half : (i + 1) * half]


def attend_specs(rows, seq_len):
    half = rows // 2
    by_head = pl.BlockSpec((half, GROUP * HD), lambda g, h, ids: (h, g))
    keys = pl.BlockSpec((seq_len, HD), lambda g, h, ids: (0, g))
    values = pl.BlockSpec((seq_len, HD), lambda g, h, ids: (0, KVH + g))
    return by_head, keys, values


def attend_call(ids, queries, key_value):
    rows, seq_len = (queries.shape[0], key_value.shape[0])
    by_head, keys, values = attend_specs(rows, seq_len)
    return pl.pallas_call(
        attend_kernel,
        grid_spec=pltpu.PrefetchScalarGridSpec(
            num_scalar_prefetch=1,
            grid=(KVH, 2),
            in_specs=[by_head, keys, values],
            out_specs=by_head,
        ),
        out_shape=jax.ShapeDtypeStruct((rows, QH * HD), bf16),
        compiler_params=kernel_params(),
        cost_estimate=cost(1),
        name="attend",
    )(ids, queries, key_value, key_value)


def attend_back_kernel(ids_ref, query_ref, key_ref, value_ref, cot_ref, dq_ref, *refs):
    out, (dk_ref, dv_ref) = (refs[:-2], refs[-2:])
    half = query_ref.shape[0]
    group, own = (pl.program_id(0), pl.program_id(1))
    queries, cot = (head_rows(query_ref), head_rows(cot_ref))
    probs = softmax_rows(ids_ref, queries, key_ref[...], half, own)
    d_probs = nt(cot, value_ref[...])
    inner = jnp.sum(probs * d_probs, axis=1, keepdims=True)
    d_scores = (probs * (d_probs - inner)).astype(bf16)
    d_queries = (nn(d_scores, key_ref[...]) * HD ** (-0.5)).astype(bf16)
    for i in range(GROUP):
        dq_ref[:, i * HD : (i + 1) * HD] = d_queries[i * half : (i + 1) * half]
    d_keys = nn(d_scores.T, queries) * HD ** (-0.5)
    d_values = nn(probs.astype(bf16).T, cot)

    @pl.when(own == 0)
    def _():
        dk_ref[...] = d_keys
        dv_ref[...] = d_values

    @pl.when(own != 0)
    def _():
        rows = 2 * half
        for block, ref in enumerate(out):
            part = slice(block * rows, (block + 1) * rows)
            for first, total, last in ((0, dk_ref, d_keys), (KVH * HD, dv_ref, d_values)):
                columns = pl.ds(pl.multiple_of(first + group * HD, HD), HD)
                ref[:, columns] = (total[part, :] + last[part]).astype(bf16)


def attend_back_call(ids, queries, key_value, cot):
    rows, seq_len = (queries.shape[0], key_value.shape[0])
    by_head, keys, values = attend_specs(rows, seq_len)
    blocks = seq_len // rows
    wide = 2 * KVH * HD
    result = pl.pallas_call(
        attend_back_kernel,
        grid_spec=pltpu.PrefetchScalarGridSpec(
            num_scalar_prefetch=1,
            grid=(KVH, 2),
            in_specs=[by_head, keys, values, by_head],
            out_specs=[by_head] + [pl.BlockSpec((rows, wide), lambda g, h, ids: (0, 0))] * blocks,
            scratch_shapes=[pltpu.VMEM((seq_len, HD), f32)] * 2,
        ),
        out_shape=[jax.ShapeDtypeStruct((rows, QH * HD), bf16)]
        + [jax.ShapeDtypeStruct((rows, wide), bf16)] * blocks,
        compiler_params=kernel_params(),
        cost_estimate=cost(1),
        name="attend_back",
    )(ids, queries, key_value, key_value, cot)
    return (result[0], result[1:])


def gelu_parts(gate):
    root = 0.7978845608028654
    inner = root * (gate + 0.044715 * gate * gate * gate)
    bent = jnp.tanh(inner)
    value = 0.5 * gate * (1.0 + bent)
    slope = root * (1.0 + 3.0 * 0.044715 * gate * gate)
    return value, 0.5 * (1.0 + bent) + 0.5 * gate * (1.0 - bent * bent) * slope


def give_back(pick_ref, total_ref, share_ref, before, out):
    blocks, capacity, _ = pick_ref.shape
    for d in range(blocks):
        part = total_ref[d * capacity : (d + 1) * capacity, :]
        if share_ref is not None:
            part = part * share_ref[d]
        back = nn(pick_ref[d].T, part.astype(bf16))
        if before:
            back = back + before[d][...]
        out[d][...] = back.astype(out[d].dtype)


def flat(ref):
    value = ref[...]
    return value.reshape(-1, value.shape[-1])


def add_up(total_ref, part, step):
    @pl.when(step == 0)
    def _():
        total_ref[...] = part

    @pl.when(step != 0)
    def _():
        total_ref[...] += part


def expert_kernel(blocks, adds, pick_ref, share_ref, gate_ref, up_ref, down_ref, *refs):
    rows, refs = (refs[:blocks], refs[blocks:])
    before, refs = (refs[: blocks * adds], refs[blocks * adds :])
    out, (picked_ref, gate_pre_ref, up_pre_ref, total_ref) = (refs[:blocks], refs[blocks:])
    step = pl.program_id(0)
    capacity = pick_ref.shape[1]

    @pl.when(step == 0)
    def _():
        for d in range(blocks):
            block = nn(pick_ref[d], rows[d][...]).astype(bf16)
            picked_ref[d * capacity : (d + 1) * capacity, :] = block

    gate_pre = nn(picked_ref[...], flat(gate_ref))
    up_pre = nn(picked_ref[...], flat(up_ref))
    gate_pre_ref[...] = gate_pre
    up_pre_ref[...] = up_pre
    active = (gelu_parts(gate_pre)[0] * up_pre).astype(bf16)
    add_up(total_ref, nn(active, flat(down_ref)), step)

    @pl.when(step == pl.num_programs(0) - 1)
    def _():
        give_back(pick_ref, total_ref, share_ref, before, out)


def whole_spec(shape):
    return pl.BlockSpec(
        shape, lambda step: (0,) * len(shape), pipeline_mode=pl.Buffered(buffer_count=1)
    )


def weight_operands(weights, deep, cut):
    if len(weights) == 1:
        unit = weights[0]
        shards, tall, width = unit.shape
        specs = [
            pl.BlockSpec((shards, deep, cut), lambda step: (0, 0, 2 * step)),
            pl.BlockSpec((shards, deep, cut), lambda step: (0, 0, 2 * step + 1)),
            pl.BlockSpec(
                (shards // 2, tall - deep, width), lambda step: (step, deep // (tall - deep), 0)
            ),
        ]
        return specs, [unit, unit, unit]
    pair, down = weights
    specs = [
        pl.BlockSpec((pair.shape[0], cut), lambda step: (0, 2 * step)),
        pl.BlockSpec((pair.shape[0], cut), lambda step: (0, 2 * step + 1)),
        pl.BlockSpec((cut, down.shape[1]), lambda step: (step, 0)),
    ]
    return specs, [pair, pair, down]


def expert_call(picks, shares, rows, weights, deep, hidden, before, micros):
    blocks, capacity, _ = picks.shape
    width, cut, tall = (rows[0].shape[1], hidden // 2, blocks * capacity)
    columns = pl.BlockSpec((tall, cut), lambda step: (0, step))
    row_specs = [whole_spec(block.shape) for block in rows]
    specs, operands = weight_operands(weights, deep, cut)
    result = pl.pallas_call(
        functools.partial(expert_kernel, blocks, 1 if before else 0),
        grid=(2,),
        in_specs=[whole_spec(picks.shape), whole_spec(shares.shape)]
        + specs
        + row_specs * (2 if before else 1),
        out_specs=row_specs + [whole_spec((tall, width)), columns, columns],
        out_shape=[jax.ShapeDtypeStruct(block.shape, bf16) for block in rows]
        + [
            jax.ShapeDtypeStruct((tall, width), bf16),
            jax.ShapeDtypeStruct((tall, hidden), f32),
            jax.ShapeDtypeStruct((tall, hidden), f32),
        ],
        scratch_shapes=[pltpu.VMEM((tall, width), f32)],
        compiler_params=kernel_params(),
        cost_estimate=cost(micros),
        name="expert",
    )(picks, shares, *operands, *rows, *before)
    return (list(result[:blocks]), list(result[blocks:]))


def expert_back_kernel(
    blocks, adds, pick_ref, share_ref, gate_pre_ref, up_pre_ref, gate_ref, up_ref, down_ref, *refs
):
    rows, refs = (refs[:blocks], refs[blocks:])
    before, refs = (refs[: blocks * adds], refs[blocks * adds :])
    out, refs = (refs[:blocks], refs[blocks:])
    slots_ref, d_gate_ref, d_up_ref, active_ref, total_ref = refs
    step = pl.program_id(0)
    capacity = pick_ref.shape[1]

    @pl.when(step == 0)
    def _():
        for d in range(blocks):
            block = nn(pick_ref[d], rows[d][...]) * share_ref[d]
            slots_ref[d * capacity : (d + 1) * capacity, :] = block.astype(bf16)

    d_active = nt(slots_ref[...], flat(down_ref))
    value, slope = gelu_parts(gate_pre_ref[...])
    up_pre = up_pre_ref[...]
    d_gate = (d_active * up_pre * slope).astype(bf16)
    d_up = (d_active * value).astype(bf16)
    active_ref[...] = (value * up_pre).astype(bf16)
    d_gate_ref[...] = d_gate
    d_up_ref[...] = d_up
    add_up(total_ref, nt(d_gate, flat(gate_ref)) + nt(d_up, flat(up_ref)), step)

    @pl.when(step == pl.num_programs(0) - 1)
    def _():
        give_back(pick_ref, total_ref, None, before, out)


def expert_back_call(picks, shares, rows, kept, weights, deep, before, micros):
    _, gate_pre, up_pre = kept
    blocks, capacity, _ = picks.shape
    width, (tall, hidden) = (rows[0].shape[1], gate_pre.shape)
    cut = hidden // 2
    columns = pl.BlockSpec((tall, cut), lambda step: (0, step))
    row_specs = [whole_spec(block.shape) for block in rows]
    specs, operands = weight_operands(weights, deep, cut)
    result = pl.pallas_call(
        functools.partial(expert_back_kernel, blocks, 1 if before else 0),
        grid=(2,),
        in_specs=[whole_spec(picks.shape), whole_spec(shares.shape), columns, columns]
        + specs
        + row_specs * (2 if before else 1),
        out_specs=row_specs + [whole_spec((tall, width)), columns, columns, columns],
        out_shape=[jax.ShapeDtypeStruct(block.shape, bf16) for block in rows]
        + [jax.ShapeDtypeStruct((tall, width), bf16)]
        + [jax.ShapeDtypeStruct((tall, hidden), bf16)] * 3,
        scratch_shapes=[pltpu.VMEM((tall, width), f32)],
        compiler_params=kernel_params(),
        cost_estimate=cost(micros),
        name="expert_back",
    )(picks, shares, gate_pre, up_pre, *operands, *rows, *before)
    return (list(result[:blocks]), list(result[blocks:]))


def expert_grads_kernel(parts, deep, *refs):
    picked, slots, d_gate, d_up, active = (refs[i * parts : (i + 1) * parts] for i in range(5))
    grad_refs, turned_ref = (refs[5 * parts : -1], refs[-1])
    step = pl.program_id(0)

    def below(some):
        return jnp.concatenate([ref[...] for ref in some], axis=0)

    @pl.when(step == 0)
    def _():
        turned_ref[...] = below(picked).T

    grad_gate = nn(turned_ref[...], below(d_gate)).astype(bf16)
    grad_up = nn(turned_ref[...], below(d_up)).astype(bf16)
    grad_down = nn(below(active).T, below(slots)).astype(bf16)
    cut = grad_gate.shape[1]
    if len(grad_refs) == 1:
        unit_ref = grad_refs[0]
        shards, tall, width = unit_ref.shape
        for side in range(2):

            @pl.when(step == side)
            def _():
                left, some = (2 * side * cut, shards // 2)
                unit_ref[:, :deep, left : left + cut] = grad_gate.reshape(shards, deep, cut)
                left = left + cut
                unit_ref[:, :deep, left : left + cut] = grad_up.reshape(shards, deep, cut)
                rest = grad_down.reshape(some, tall - deep, width)
                unit_ref[side * some : (side + 1) * some, deep:, :] = rest
    else:
        grad_refs[0][:, :cut] = grad_gate
        grad_refs[0][:, cut:] = grad_up
        grad_refs[1][...] = grad_down


def expert_grads_call(picked, saved, weights, deep):
    slots, d_gate, d_up, active = zip(*saved)
    width, hidden = (picked[0].shape[1], d_gate[0].shape[1])
    cut = hidden // 2
    columns = [pl.BlockSpec((part.shape[0], cut), lambda step: (0, step)) for part in picked]
    if len(weights) == 1:
        grad_specs = [whole_spec(weights[0].shape)]
    else:
        grad_specs = [
            pl.BlockSpec((width, 2 * cut), lambda step: (0, step)),
            pl.BlockSpec((cut, width), lambda step: (step, 0)),
        ]
    return list(
        pl.pallas_call(
            functools.partial(expert_grads_kernel, len(picked), deep),
            grid=(2,),
            in_specs=[whole_spec(part.shape) for part in picked] * 2 + columns * 3,
            out_specs=grad_specs,
            out_shape=[jax.ShapeDtypeStruct(part.shape, bf16) for part in weights],
            scratch_shapes=[pltpu.VMEM((width, sum(part.shape[0] for part in picked)), bf16)],
            compiler_params=kernel_params(),
            cost_estimate=cost(1),
            name="expert_grads",
        )(*picked, *slots, *d_gate, *d_up, *active)
    )


def norm_parts(value):
    scale = lax.rsqrt(jnp.mean(value * value, axis=1, keepdims=True) + epsilon)
    return scale, value * scale


def norm_back(grad, gain, value):
    scale, scaled = norm_parts(value)
    grown = grad * gain
    back = scale * (grown - scaled * jnp.mean(scaled * grown, axis=1, keepdims=True))
    return back, (grad * scaled).astype(bf16)


def add_all(refs):
    total = refs[0][...].astype(f32)
    for ref in refs[1:]:
        total = total + ref[...].astype(f32)
    return total


def side_offsets(core_ref, steps, cut):
    step, core = (pl.program_id(0), core_ref[0])
    own = pl.multiple_of((core * steps + step) * cut, cut)
    other = pl.multiple_of(((1 - core) * steps + step) * cut, cut)
    return own, other


def dense_call(kernel, core, steps, whole, halves, out, scratch, name, micros):
    cut = halves[0].shape[1] // steps

    def keep(shape):
        return pl.BlockSpec(
            shape, lambda step, core: (0,) * len(shape), pipeline_mode=pl.Buffered(buffer_count=1)
        )

    def tile(tall):
        return pl.BlockSpec((tall, cut), lambda step, core: (0, step))

    return pl.pallas_call(
        kernel,
        grid_spec=pltpu.PrefetchScalarGridSpec(
            num_scalar_prefetch=1,
            grid=(steps,),
            in_specs=[keep(part.shape) for part in whole] + [tile(halves[0].shape[0])] * 2,
            out_specs=[
                tile(part.shape[0]) if tiled else keep(part.shape) for part, tiled in out
            ],
            scratch_shapes=scratch,
        ),
        out_shape=[part for part, _ in out],
        compiler_params=kernel_params(),
        cost_estimate=cost(micros),
        name=name,
    )(core.astype(jnp.int32).reshape(1), *whole, *halves)


def shape_of(kind, *shape):
    return jax.ShapeDtypeStruct(shape, kind)


def enter_kernel(steps, terms, core_ref, gain_ref, *refs):
    parts, (own_ref, other_ref, sent_ref, normed_ref, out_ref) = (refs[:terms], refs[terms:])
    own, other = side_offsets(core_ref, steps, own_ref.shape[1])

    @pl.when(pl.program_id(0) == 0)
    def _():
        sent = add_all(parts).astype(bf16)
        sent_ref[...] = sent
        normed_ref[...] = (norm_parts(sent.astype(f32))[1] * gain_ref[...]).astype(bf16)

    cut = own_ref.shape[1]
    out_ref[:, pl.ds(own, cut)] = nn(normed_ref[...], own_ref[...]).astype(bf16)
    out_ref[:, pl.ds(other, cut)] = nn(normed_ref[...], other_ref[...]).astype(bf16)


def enter_call(core, parts, gain, halves):
    rows, width = parts[0].shape
    return dense_call(
        functools.partial(enter_kernel, 3, len(parts)),
        core,
        3,
        [gain] + parts,
        halves,
        [
            (shape_of(bf16, rows, width), False),
            (shape_of(bf16, rows, width), False),
            (shape_of(bf16, rows, 2 * halves[0].shape[1]), False),
        ],
        [],
        "enter",
        6,
    )


def leave_kernel(steps, core_ref, gain_ref, rows_ref, attended_ref, own_ref, other_ref,
                 mid_ref, normed_ref):
    cut = own_ref.shape[1]
    for start, ref in zip(side_offsets(core_ref, steps, cut), (own_ref, other_ref)):
        part = pl.ds(start, cut)
        mid_ref[:, part] = rows_ref[:, part].astype(f32) + nn(attended_ref[...], ref[...])

    @pl.when(pl.program_id(0) == steps - 1)
    def _():
        normed_ref[...] = (norm_parts(mid_ref[...])[1] * gain_ref[...]).astype(bf16)


def leave_call(core, rows_in, attended, gain, halves):
    rows, width = rows_in.shape
    return dense_call(
        functools.partial(leave_kernel, 2),
        core,
        2,
        [gain, rows_in, attended],
        halves,
        [(shape_of(f32, rows, width), False), (shape_of(bf16, rows, width), False)],
        [],
        "leave",
        5,
    )


def leave_back_kernel(steps, terms, core_ref, gain_ref, mid_ref, cot_ref, attended_ref, *refs):
    parts, refs = (refs[:terms], refs[terms:])
    own_ref, other_ref, after_ref, term_ref, d_attended_ref, *refs = refs
    own_grad_ref, other_grad_ref, branch_ref, turned_ref, total_ref = refs
    step, cut = (pl.program_id(0), own_ref.shape[1])

    @pl.when(step == 0)
    def _():
        back, term_ref[...] = norm_back(add_all(parts), gain_ref[...], mid_ref[...])
        back = back + cot_ref[...].astype(f32)
        after_ref[...] = back
        branch_ref[...] = back.astype(bf16)
        turned_ref[...] = attended_ref[...].T

    own, other = side_offsets(core_ref, steps, cut)
    d_own, d_other = (branch_ref[:, pl.ds(own, cut)], branch_ref[:, pl.ds(other, cut)])
    own_grad_ref[...] = nn(turned_ref[...], d_own).astype(bf16)
    other_grad_ref[...] = nn(turned_ref[...], d_other).astype(bf16)
    add_up(total_ref, nt(d_own, own_ref[...]) + nt(d_other, other_ref[...]), step)

    @pl.when(step == steps - 1)
    def _():
        d_attended_ref[...] = total_ref[...].astype(bf16)


def leave_back_call(core, parts, gain, mid, cotangent, attended, halves):
    rows, width = mid.shape
    half = (halves[0].shape[0], halves[0].shape[1])
    return dense_call(
        functools.partial(leave_back_kernel, 2, len(parts)),
        core,
        2,
        [gain, mid, cotangent, attended] + parts,
        halves,
        [
            (shape_of(f32, rows, width), False),
            (shape_of(bf16, rows, width), False),
            (shape_of(bf16, rows, width), False),
            (shape_of(bf16, *half), True),
            (shape_of(bf16, *half), True),
        ],
        [
            pltpu.VMEM((rows, width), bf16),
            pltpu.VMEM((width, rows), bf16),
            pltpu.VMEM((rows, width), f32),
        ],
        "leave_back",
        8,
    )


def enter_back_kernel(steps, terms, core_ref, gain_ref, rows_ref, normed_ref, after_ref, term_ref,
                      dq_ref, *refs):
    parts, refs = (refs[:terms], refs[terms:])
    own_ref, other_ref, entry_ref, sent_ref, own_grad_ref, other_grad_ref, *refs = refs
    entered_ref, turned_ref, total_ref = refs
    step, cut = (pl.program_id(0), own_ref.shape[1])
    rows, qw = dq_ref.shape

    @pl.when(step == 0)
    def _():
        entered_ref[:, :qw] = dq_ref[...]
        wide = parts[0].shape[1]
        entered_ref[:, qw : qw + wide] = add_all(parts).astype(bf16)
        entered_ref[:, qw + wide :] = jnp.zeros((rows, gap), bf16)
        turned_ref[...] = normed_ref[...].T

    own, other = side_offsets(core_ref, steps, cut)
    d_own, d_other = (entered_ref[:, pl.ds(own, cut)], entered_ref[:, pl.ds(other, cut)])
    own_grad_ref[...] = nn(turned_ref[...], d_own).astype(bf16)
    other_grad_ref[...] = nn(turned_ref[...], d_other).astype(bf16)
    add_up(total_ref, nt(d_own, own_ref[...]) + nt(d_other, other_ref[...]), step)

    @pl.when(step == steps - 1)
    def _():
        back, attn_term = norm_back(total_ref[...], gain_ref[...], rows_ref[...].astype(f32))
        back = back + after_ref[...]
        entry_ref[...] = back
        sent_ref[...] = back.astype(bf16)
        lane = lax.broadcasted_iota(jnp.int32, (rows, 128), 1)
        sums = nn(attn_term.T, (lane == 0).astype(bf16))
        sums = (sums + nn(term_ref[...].T, (lane == 1).astype(bf16))).astype(bf16)
        left = cut - gap

        @pl.when(core_ref[0] == 0)
        def _():
            other_grad_ref[:, left : left + 128] = sums

        @pl.when(core_ref[0] != 0)
        def _():
            own_grad_ref[:, left : left + 128] = sums


def enter_back_call(core, dq, parts, gain, rows_in, normed, after, term, halves):
    rows, width = rows_in.shape
    return dense_call(
        functools.partial(enter_back_kernel, 3, len(parts)),
        core,
        3,
        [gain, rows_in, normed, after, term, dq] + parts,
        halves,
        [
            (shape_of(f32, rows, width), False),
            (shape_of(bf16, rows, width), False),
            (shape_of(bf16, *halves[0].shape), True),
            (shape_of(bf16, *halves[0].shape), True),
        ],
        [
            pltpu.VMEM((rows, 2 * halves[0].shape[1]), bf16),
            pltpu.VMEM((width, rows), bf16),
            pltpu.VMEM((rows, width), f32),
        ],
        "enter_back",
        13,
    )


def place_kernel(count, joined, index_ref, *refs):
    step = pl.program_id(0)
    for bit in range(count):

        @pl.when(step == bit)
        def _():
            if joined:
                refs[count][...] = refs[bit][...]
            else:
                refs[count][0] = refs[bit][...]


def place_call(blocks, index):
    count = len(blocks)
    shape = blocks[0].shape
    zeros = (0,) * len(shape)
    joined = len(shape) == 2 and shape[0] % 16 == 0
    if joined:
        out_spec = pl.BlockSpec(shape, lambda step, at: (at[0] ^ step, 0))
        out_shape = (count * shape[0], shape[1])
    else:
        out_spec = pl.BlockSpec((1,) + shape, lambda step, at: (at[0] ^ step,) + zeros)
        out_shape = (count,) + shape
    return pl.pallas_call(
        functools.partial(place_kernel, count, joined),
        grid_spec=pltpu.PrefetchScalarGridSpec(
            num_scalar_prefetch=1,
            grid=(count,),
            in_specs=[pl.BlockSpec(shape, lambda step, at: zeros)] * count,
            out_specs=out_spec,
        ),
        out_shape=jax.ShapeDtypeStruct(out_shape, blocks[0].dtype),
        compiler_params=kernel_params(),
        cost_estimate=cost(2),
        name="place",
    )(index.astype(jnp.int32).reshape(1), *blocks)


def deal_kernel(count, index_ref, *refs):
    step = pl.program_id(0)
    for bit in range(count):

        @pl.when(step == bit)
        def _():
            for layer, ref in enumerate(refs[count:]):
                ref[0] = refs[bit][layer]


def deal_call(blocks, index):
    count = len(blocks)
    layers, *shape = blocks[0].shape
    shape = tuple(shape)
    zeros = (0,) * len(shape)
    return pl.pallas_call(
        functools.partial(deal_kernel, count),
        grid_spec=pltpu.PrefetchScalarGridSpec(
            num_scalar_prefetch=1,
            grid=(count,),
            in_specs=[pl.BlockSpec((layers,) + shape, lambda step, at: (0,) + zeros)] * count,
            out_specs=[pl.BlockSpec((1,) + shape, lambda step, at: (at[0] ^ step,) + zeros)]
            * layers,
        ),
        out_shape=[jax.ShapeDtypeStruct((count,) + shape, blocks[0].dtype)] * layers,
        compiler_params=kernel_params(),
        cost_estimate=cost(2),
        name="deal",
    )(index.astype(jnp.int32).reshape(1), *blocks)


def order_kernel(count, order_ref, *refs):
    step = pl.program_id(0)
    for i in range(count):

        @pl.when(step == i)
        def _():
            refs[count][:, 0] = refs[i][:, 0]


def order_call(blocks, order, unit):
    count = len(blocks)
    n_ctx, _, tall, wide = blocks[0].shape
    shape = (n_ctx, 1, tall, wide)
    source = pl.BlockSpec(
        shape, lambda step, at: (0, unit, 0, 0), pipeline_mode=pl.Buffered(buffer_count=1)
    )
    result = pl.pallas_call(
        functools.partial(order_kernel, count),
        grid_spec=pltpu.PrefetchScalarGridSpec(
            num_scalar_prefetch=1,
            grid=(count,),
            in_specs=[source] * count,
            out_specs=pl.BlockSpec(shape, lambda step, at: (0, at[step], 0, 0)),
        ),
        out_shape=jax.ShapeDtypeStruct((n_ctx, count, tall, wide), bf16),
        compiler_params=kernel_params(),
        cost_estimate=cost(4),
        name="order",
    )(order.astype(jnp.int32), *blocks)
    return result.reshape(n_ctx * count, tall, wide)


def finish_kernel(deep, index_ref, own_ref, other_ref, gate_ref, up_ref, down_ref):
    side = pl.program_id(1)
    wide = gate_ref.shape[2] // 2

    def write(source):
        for half in range(2):
            left, target = (2 * half * wide, slice(half * wide, (half + 1) * wide))
            gate_ref[:, :, target] = source[0, :, :deep, left : left + wide].astype(f32)
            left = left + wide
            up_ref[:, :, target] = source[0, :, :deep, left : left + wide].astype(f32)
        down_ref[...] = source[0, :, deep:, :].astype(f32)

    @pl.when(side == index_ref[1])
    def _():
        write(own_ref)

    @pl.when(side != index_ref[1])
    def _():
        write(other_ref)


def finish_call(own, other, deep, hidden, place, core):
    n_ctx, units, tall, width = own.shape
    experts = 2 * n_ctx * units
    source = pl.BlockSpec((1, units, tall, width), lambda bit, side, at: (bit, 0, 0, 0))
    target = lambda bit, side, at: (2 * (at[0] ^ bit) + side, 0, 0)
    return pl.pallas_call(
        functools.partial(finish_kernel, deep),
        grid_spec=pltpu.PrefetchScalarGridSpec(
            num_scalar_prefetch=1,
            grid=(n_ctx, 2),
            in_specs=[source, source],
            out_specs=[
                pl.BlockSpec((units, deep, hidden), target),
                pl.BlockSpec((units, deep, hidden), target),
                pl.BlockSpec((units, tall - deep, width), target),
            ],
        ),
        out_shape=[
            jax.ShapeDtypeStruct((experts, deep, hidden), f32),
            jax.ShapeDtypeStruct((experts, deep, hidden), f32),
            jax.ShapeDtypeStruct((experts, tall - deep, width), f32),
        ],
        compiler_params=kernel_params(),
        cost_estimate=cost(8),
        name="finish",
    )(jnp.stack([place, core]).astype(jnp.int32), own, other)


def body(
    tokens,
    block_of,
    routes,
    combine,
    attn_norm,
    w_query,
    w_key,
    w_value,
    w_out,
    ffn_norm,
    w_gate,
    w_up,
    w_down,
    out_grad,
):
    rows = tokens.shape[2]
    width = tokens.shape[3]
    half = rows // 2
    n_ctx = lax.axis_size("ctx")
    n_fsdp = lax.axis_size("fsdp")
    core, place, depth = (
        lax.axis_index(axis).astype(jnp.uint32) for axis in ("section", "ctx", "fsdp")
    )
    seq_len = rows * n_ctx
    capacity = rows * TOP * 5 // (4 * EXPERTS)
    score_scale = HD ** (-0.5)
    own_experts = EXPERTS // n_ctx
    hidden = w_gate.shape[3]
    shard_rows = w_query.shape[1]
    down_rows = w_down.shape[2]
    qw = w_query.shape[2]
    kw = w_key.shape[2]
    pieces = max(1, 2 * n_ctx // EXPERTS)
    per_core = max(1, EXPERTS // (2 * n_ctx))
    unit_rows = shard_rows + down_rows
    aligned = shard_rows % 16 == 0 and down_rows % 16 == 0

    def on_core(former, latter):
        return jnp.where(core == 0, former, latter)

    def own_other(low, high):
        return (on_core(low, high), on_core(high, low))

    early, late = (range(1, n_ctx // 2 + 1), range(n_ctx // 2 + 1, n_ctx))

    def send(value, bits):
        return [swap(value, "ctx", bit) for bit in bits]

    def spread(value):
        return [value] + send(value, early) + send(value, late)

    def spread_rows(value):
        near_blocks = send(value, early)
        value, near_blocks = tie(value, near_blocks)
        return [value] + near_blocks + send(value, late)

    def gather_back(blocks):
        return [blocks[0]] + [swap(blocks[bit], "ctx", bit) for bit in range(1, n_ctx)]

    info = jnp.concatenate([routes.astype(f32), combine], axis=-1)[0, :, 0].transpose(0, 2, 1)
    info_own, info_other = (at(info, core), swap(at(info, 1 - core), "section", 1))
    info = jnp.stack(own_other(info_own, info_other))
    info = jnp.stack([info] + [swap(info, "ctx", bit) for bit in range(1, n_ctx)], axis=1)

    gain_columns = jnp.stack([attn_norm[0], ffn_norm[0]], axis=1)
    gain_columns = jnp.pad(gain_columns, ((0, 0), (0, gap - 2)))
    enter_shard = jnp.concatenate([w_query[0], w_key[0], w_value[0], gain_columns], axis=1)
    enter_cut = enter_shard.shape[1] // 2
    leave_cut = w_out.shape[2] // 2
    low_shard = jnp.concatenate([enter_shard[:, :enter_cut], w_out[0, :, :leave_cut]], axis=1)
    high_shard = jnp.concatenate([enter_shard[:, enter_cut:], w_out[0, :, leave_cut:]], axis=1)
    lent = swap(on_core(high_shard, low_shard), "section", 1)
    dense_shards = (on_core(low_shard, lent), on_core(lent, high_shard))

    def gather_deep(shard):
        blocks = [shard] + [swap(shard, "fsdp", bit) for bit in range(1, n_fsdp)]
        return place_call(blocks, depth).reshape(-1, shard.shape[1])

    def join_square(blocks):
        return place_call(blocks, place).reshape(-1, blocks[0].shape[1])

    def gather_square(deep):
        return join_square(spread(deep))

    cut = hidden // 2
    unit_stack = jnp.concatenate(
        [
            jnp.concatenate(
                [w_gate[0, ..., :cut], w_up[0, ..., :cut], w_gate[0, ..., cut:], w_up[0, ..., cut:]],
                axis=2,
            ),
            w_down[0],
        ],
        axis=1,
    )
    if pieces == 2:
        unit_stack = jnp.stack(jnp.split(unit_stack, 2, axis=2), axis=1)
    unit_stack = unit_stack.reshape(n_ctx, 2, per_core, unit_rows, width // pieces)
    units_lent = swap(at(unit_stack, 1 - core, 1), "section", 1)
    unit_stacks = jnp.stack(own_other(at(unit_stack, core, 1), units_lent), axis=1)

    def deal_units(stack):
        blocks = [at(stack, place)]
        blocks += [swap(at(stack, place ^ bit), "ctx", bit) for bit in range(1, n_ctx)]
        return deal_call(blocks, place)

    ring = list(range(0, n_fsdp, 2)) + list(range(1, n_fsdp, 2))[::-1]
    ring_steps = [(ring[i], ring[(i + 1) % n_fsdp]) for i in range(n_fsdp)]
    ring_table = [[ring[ring.index(z) - i] for i in range(n_fsdp)] for z in range(n_fsdp)]
    behind_here = at(jnp.array(ring_table, jnp.uint32), depth)

    def ring_send(moved):
        return [blocks + [lax.ppermute(blocks[-1], "fsdp", ring_steps)] for blocks in moved]

    def own_units(blocks):
        return [order_call(blocks, behind_here, unit) for unit in range(per_core)]

    def pair_units(mine):
        other = [swap(part, "section", 1) for part in mine]
        units = list(mine) + other
        if pieces == 2:
            units = [jnp.concatenate(own_other(mine[0], other[0]), axis=2)]
        if aligned:
            return [[unit] for unit in units]
        return [
            [unit[:, :shard_rows].reshape(-1, width), unit[:, shard_rows:].reshape(-1, width)]
            for unit in units
        ]

    def cut_units(grads):
        if aligned:
            units = [unit for (unit,) in grads]
        else:
            units = [
                jnp.concatenate(
                    [part.reshape(n_ctx * n_fsdp, -1, width) for part in parts], axis=1
                )
                for parts in grads
            ]
        if pieces == 1:
            return (units[:per_core], units[per_core:])
        own, other = own_other(*jnp.split(units[0], 2, axis=2))
        return ([own], [other])

    def ring_part(terms, behind):
        spot = behind_here[behind % n_fsdp]
        return sum(at(term, spot, 1).astype(f32) for term in terms)

    def ring_start(own, received):
        terms = [part.reshape((n_ctx, n_fsdp) + part.shape[1:]) for part in (own, received)]
        return (terms, ring_part(terms, 1).astype(bf16))

    def ring_move(state):
        return [(terms, lax.ppermute(moving, "fsdp", ring_steps)) for terms, moving in state]

    def ring_add(state, step):
        return [
            (terms, (moved.astype(f32) + ring_part(terms, step + 1)).astype(bf16))
            for terms, moved in state
        ]

    def ring_step(state, step):
        return ring_add(ring_move(state), step)

    def ring_last(state):
        state = ring_add(state, 2)
        for step in range(3, n_fsdp - 1):
            state = ring_step(state, step)
        return ring_move(state)

    def ring_rest(state, first):
        for step in range(first, n_fsdp):
            state = ring_step(state, step)
        return [moving for _, moving in state]

    def scatter_units(moved):
        whole = jnp.stack(moved, axis=1)
        blocks = [at(whole, place)]
        blocks += [swap(at(whole, place ^ bit), "ctx", bit) for bit in range(1, n_ctx)]
        return jnp.stack(blocks)

    def trade_square(own, received, bits):
        own, received = (part.reshape(n_ctx, -1, part.shape[1]) for part in (own, received))

        def part(bit):
            return at(own, place ^ bit).astype(f32) + at(received, place ^ bit).astype(f32)

        return [part(bit) if bit == 0 else swap(part(bit).astype(bf16), "ctx", bit) for bit in bits]

    def sum_square(parts):
        return sum(part.astype(f32) for part in parts).astype(bf16)

    def reduce_deep(mine):
        mine = mine.reshape(n_fsdp, shard_rows, -1)
        total = at(mine, depth).astype(f32)
        for bit in range(1, n_fsdp):
            total = total + swap(at(mine, depth ^ bit), "fsdp", bit).astype(f32)
        return total

    if pieces == 1:
        units_here = jnp.arange(per_core, dtype=jnp.uint32)
        units_here = jnp.concatenate(
            [core * per_core + units_here, (1 - core) * per_core + units_here]
        )
    else:
        units_here = jnp.zeros((1,), jnp.uint32)
    named = (place * own_experts + units_here).astype(f32)
    matches = info[:, None, :, :TOP] == named[None, :, None, None, None]
    hits = jnp.any(matches, axis=3)
    shares = jnp.sum(jnp.where(matches, info[:, None, :, TOP:], 0.0), axis=3)
    earlier = jnp.arange(rows)[:, None] < jnp.arange(rows)[None, :]
    rank = dot("ledr,rq->ledq", hits.astype(bf16), earlier.astype(bf16))
    slots = jnp.arange(capacity, dtype=f32)
    picks = hits[:, :, :, None, :] & (rank[:, :, :, None, :] == slots[:, None])
    slot_shares = jnp.sum(jnp.where(picks, shares[:, :, :, None, :], 0.0), axis=-1, keepdims=True)
    picks = picks.astype(bf16)

    order = place.astype(jnp.int32) ^ jnp.arange(n_ctx, dtype=jnp.int32)
    block_ids = jnp.take(block_of.reshape(n_ctx, 2), order, axis=0)
    block_ids = block_ids.reshape(-1)

    def gains_of(halves):
        pair = on_core(halves[1][:, -gap : 2 - gap], halves[0][:, -gap : 2 - gap])
        pair = pair.astype(f32).T
        return (pair[:1], pair[1:])

    near = 1 + len(early)
    parts = (slice(0, near), slice(near, n_ctx))

    def experts(layer, blocks, weights, answer, beside_near=tuple, beside_far=lambda found: ()):
        kept, arrived = ({}, [])
        back = {}
        for index, part in enumerate(parts):
            rows_here = blocks[part]
            if index:
                back[0], rows_here, found = tie(back[0], rows_here, beside_near())
                if answer:
                    arrived = [swap(block, "ctx", bit) for bit, block in zip(early, back[0][1:])]
            back[index] = []
            for j in range(own_experts):
                back[index], kept[index, j] = expert_call(
                    picks[layer, j, part],
                    slot_shares[layer, j, part],
                    rows_here,
                    weights[j],
                    shard_rows,
                    hidden,
                    back[index],
                    3 if index == 0 else 1,
                )
        if not answer:
            return (back[0] + back[1], kept)
        back[1], arrived, found = tie(back[1], arrived, beside_far(found))
        arrived += [swap(block, "ctx", bit) for bit, block in zip(late, back[1])]
        return (back[0][:1] + arrived, kept, found)

    def experts_back(layer, blocks, weights, kept, delay, beside_near, beside_far, beside_end):
        back, saved = ({}, {})
        for index, part in enumerate(parts):
            rows_here = blocks[part]
            if index:
                back[0], rows_here, found_near = tie(back[0], rows_here, beside_near())
                arrived = [swap(block, "ctx", bit) for bit, block in zip(early, back[0][1:])]
            back[index] = []
            for j in range(own_experts):
                back[index], saved[index, j] = expert_back_call(
                    picks[layer, j, part],
                    slot_shares[layer, j, part],
                    rows_here,
                    kept[index, j],
                    weights[j],
                    shard_rows,
                    back[index],
                    4 if index == 0 else 1,
                )
        back[1], arrived, saved, found_far = tie(back[1], arrived, saved, beside_far(found_near))
        arrived += [swap(block, "ctx", bit) for bit, block in zip(late, back[1])]

        def grads_of(j, saved):
            picked = [kept[index, j][0] for index in range(2)]
            both = [saved[index, j] for index in range(2)]
            return expert_grads_call(picked, both, weights[j], shard_rows)

        now = [j for j in reversed(range(own_experts)) if not delay or j >= per_core]
        grads = {j: grads_of(j, saved) for j in now}
        arrived, grads, found_end = tie(arrived, grads, beside_end(found_far))
        returned = back[0][:1] + arrived
        if len(now) == own_experts:
            own, other = cut_units([grads[j] for j in range(own_experts)])
            received = [swap(part, "section", 1) for part in other]
            return (returned, lambda earlier: (own, received), found_end)
        received = [swap(grads[j][0], "section", 1) for j in reversed(now)]

        def finish(earlier):
            ready = after(saved, earlier)
            return ([grads_of(j, ready)[0] for j in range(per_core)], received)

        return (returned, finish, found_end)

    def keep_own(first, second):
        other = swap(on_core(second, first), "section", 1)
        return own_other(on_core(first, second), other)

    dense_first, dense_second = dense_shards
    deep = gather_deep(jnp.concatenate([dense_first, dense_second[:, :enter_cut]], axis=1))
    dealt_first, dealt_second = deal_units(unit_stacks)
    deep, dealt_first, dealt_second, picks, dense_second = tie(
        deep, dealt_first, dealt_second, picks, dense_second
    )
    dense_blocks, moved, leave_shard, enter_shard = tie(
        spread(deep[:, :enter_cut]),
        ring_send([[dealt_first]]),
        deep[:, enter_cut : enter_cut + leave_cut],
        deep[:, enter_cut + leave_cut :],
    )
    leave_blocks = [leave_shard] + send(leave_shard, early)
    enter_own = join_square(dense_blocks)
    enter_first = (enter_own, swap(enter_own, "section", 1))

    first_gains = gains_of(enter_first)
    first_in = after(at(tokens, core)[0], slot_shares)
    _, first_normed, first_entered = enter_call(core, [first_in], first_gains[0], enter_first)
    first_entered, leave_blocks = tie(first_entered, leave_blocks)
    key_value = first_entered[:, qw : qw + 2 * kw]
    first_kv, leave_shard = tie(jnp.concatenate(spread(key_value)), leave_shard)
    first_attended = attend_call(block_ids, first_entered, first_kv)
    moved = ring_send(moved)
    first_attended, leave_blocks, dealt_second, moved, enter_shard, dense_second = tie(
        first_attended,
        leave_blocks + send(leave_shard, late),
        dealt_second,
        moved,
        enter_shard,
        dense_second,
    )
    enter_blocks = [enter_shard] + send(enter_shard, early)
    for _ in range(2, n_fsdp - 1):
        moved = ring_send(moved)
    leave_own = join_square(leave_blocks)
    leave_first = (leave_own, swap(leave_own, "section", 1))
    first_mid, ffn_normed = leave_call(core, first_in, first_attended, first_gains[1], leave_first)
    ffn_normed, enter_blocks = tie(ffn_normed, enter_blocks)
    blocks = spread_rows(ffn_normed)
    blocks[:near], moved, dealt_second, enter_shard, leave_shard = tie(
        blocks[:near], moved, dealt_second, enter_shard, dense_second[:, enter_cut:]
    )
    first_weights = pair_units(own_units(moved[0]))
    returned, first_kept, (moved, leave_shard, enter_blocks) = experts(
        0,
        blocks,
        first_weights,
        True,
        lambda: gather_deep(leave_shard),
        lambda found: (dealt_second, found, enter_blocks + send(enter_shard, late)),
    )
    moved = ring_send([[moved]])
    enter_own = join_square(enter_blocks)
    enter_second = (enter_own, swap(enter_own, "section", 1))
    returned, leave_shard = tie(returned, leave_shard)
    leave_blocks = [leave_shard] + send(leave_shard, early)

    second_gains = gains_of(enter_second)
    second_in, second_normed, second_entered = enter_call(
        core, [first_mid] + returned, second_gains[0], enter_second
    )
    second_entered, leave_blocks, moved = tie(second_entered, leave_blocks, moved)
    moved = ring_send(moved)
    key_value = second_entered[:, qw : qw + 2 * kw]
    for _ in range(4, n_fsdp):
        moved = ring_send(moved)
    second_kv, leave_shard = tie(jnp.concatenate(spread(key_value)), leave_shard)
    second_attended = attend_call(block_ids, second_entered, second_kv)
    second_attended, leave_blocks, moved = tie(
        second_attended, leave_blocks + send(leave_shard, late), moved
    )
    moved = ring_send(moved)
    leave_own = join_square(leave_blocks)
    leave_second = (leave_own, swap(leave_own, "section", 1))
    second_mid, ffn_normed = leave_call(
        core, second_in, second_attended, second_gains[1], leave_second
    )
    blocks = spread_rows(ffn_normed)
    blocks[:near], moved = tie(blocks[:near], moved)
    second_weights = pair_units(own_units(moved[0]))
    second_returned, second_kept = experts(1, blocks, second_weights, False)
    cotangent = after(at(out_grad, core)[0], second_returned[:near])
    cot_blocks = spread_rows(cotangent)
    cot_blocks[:near], second_returned[near:] = tie(cot_blocks[:near], second_returned[near:])

    returned, finish, (second_returned, near_parts) = experts_back(
        1,
        cot_blocks,
        second_weights,
        second_kept,
        False,
        lambda: second_returned,
        lambda found: found,
        lambda found: (found, [swap(found[bit], "ctx", bit) for bit in early]),
    )
    far_parts = [swap(second_returned[bit], "ctx", bit) for bit in late]
    units_moving = [ring_start(*pair) for pair in zip(*finish(()))]
    after_rows, term, d_attended, *grads = leave_back_call(
        core,
        returned,
        second_gains[1],
        second_mid,
        cotangent,
        second_attended,
        leave_second,
    )
    leave_grads = (grads[0], swap(grads[1], "section", 1))
    d_queries, d_key_value = attend_back_call(block_ids, second_entered, second_kv, d_attended)
    d_queries, d_key_value, leave_grads, far_parts = tie(
        d_queries, d_key_value, leave_grads, far_parts
    )
    second_parts = second_returned[:1] + near_parts + far_parts
    second_out = second_mid + sum(part.astype(f32) for part in second_parts)
    d_key_value, units_moving = tie(gather_back(d_key_value), ring_move(units_moving))
    units_moving = ring_move(ring_add(units_moving, 1))
    leave_parts = trade_square(*leave_grads, range(n_ctx))
    second_entry, cotangent, *grads = enter_back_call(
        core,
        d_queries,
        d_key_value,
        second_gains[0],
        second_in,
        second_normed,
        after_rows,
        term,
        enter_second,
    )
    cotangent, grads, leave_parts, layer_rows = tie(
        cotangent, grads, leave_parts, (second_in, second_out.astype(bf16))
    )
    enter_grads = (grads[0], swap(grads[1], "section", 1))

    blocks = spread_rows(cotangent)
    blocks[:near], enter_grads, layer_rows = tie(blocks[:near], enter_grads, layer_rows)

    def dense_sums(parts):
        moving = [sum_square(some) for some in (parts, leave_parts)]
        return reduce_deep(jnp.concatenate(moving, axis=1))

    returned, finish, (units_moving, layer_outs, second_dense) = experts_back(
        0,
        blocks,
        first_weights,
        first_kept,
        False,
        lambda: (units_moving, trade_square(*enter_grads, [0, *early]), enter_grads),
        lambda found: (
            ring_last(found[0]),
            keep_own(*layer_rows),
            found[1] + trade_square(*found[2], late),
        ),
        lambda found: (found[0], found[1], dense_sums(found[2])),
    )
    second_moved = [moving for _, moving in ring_add(units_moving, n_fsdp - 1)]
    own, received = finish(())
    after_rows, term, d_attended, *grads = leave_back_call(
        core,
        returned,
        first_gains[1],
        first_mid,
        cotangent,
        first_attended,
        leave_first,
    )
    units_moving = [ring_start(*pair) for pair in zip(own, received)]
    leave_grads = (grads[0], swap(grads[1], "section", 1))
    d_queries, d_key_value = attend_back_call(block_ids, first_entered, first_kv, d_attended)
    d_queries, d_key_value, leave_grads = tie(d_queries, d_key_value, leave_grads)
    d_key_value, units_moving, leave_grads = tie(
        gather_back(d_key_value), ring_move(units_moving), leave_grads
    )
    leave_parts = trade_square(*leave_grads, [0, *early])
    units_moving = ring_move(ring_add(units_moving, 1))
    first_entry, _, *grads = enter_back_call(
        core,
        d_queries,
        d_key_value,
        first_gains[0],
        first_in,
        first_normed,
        after_rows,
        term,
        enter_first,
    )
    grads, leave_parts, leave_grads = tie(grads, leave_parts, leave_grads)
    enter_grads = (grads[0], swap(grads[1], "section", 1))
    enter_parts, leave_parts, first_entry = tie(
        trade_square(*enter_grads, range(n_ctx)),
        leave_parts + trade_square(*leave_grads, late),
        first_entry,
    )
    first_moving = [sum_square(parts) for parts in (enter_parts, leave_parts)]
    first_dense = reduce_deep(jnp.concatenate(first_moving, axis=1))
    scattered = scatter_units(ring_rest(ring_add(units_moving, 2), 3) + second_moved)
    first_scattered, second_scattered = (scattered[:, :per_core], scattered[:, per_core:])

    layer_out = jnp.stack(layer_outs)
    input_grads = jnp.stack(keep_own(first_entry, second_entry))
    low_dense, high_dense = keep_own(first_dense, second_dense)
    enter_grad = jnp.concatenate([low_dense[:, :enter_cut], high_dense[:, :enter_cut]], axis=1)
    grad_out = jnp.concatenate([low_dense[:, enter_cut:], high_dense[:, enter_cut:]], axis=1)
    grad_gains = enter_grad[:, qw + 2 * kw :]
    mine = on_core(first_scattered, second_scattered)
    other = swap(on_core(second_scattered, first_scattered), "section", 1)
    if aligned and pieces == 1:
        grad_gate, grad_up, grad_down = finish_call(mine, other, shard_rows, hidden, place, core)
    else:
        sides = [jnp.take(part, order, axis=0) for part in own_other(mine, other)]
        if pieces == 1:
            whole = jnp.stack(sides, axis=1).reshape(EXPERTS, unit_rows, width)
        else:
            whole = jnp.concatenate([side[:, 0] for side in sides], axis=2)
        pairs = whole[:, :shard_rows].astype(f32).reshape(EXPERTS, shard_rows, 2, 2, cut)
        grad_gate = pairs[:, :, :, 0].reshape(EXPERTS, shard_rows, hidden)
        grad_up = pairs[:, :, :, 1].reshape(EXPERTS, shard_rows, hidden)
        grad_down = whole[:, shard_rows:].astype(f32)
    return (
        layer_out[None, :, None],
        input_grads[None, :, None],
        grad_gains[:, 0][None],
        enter_grad[:, :qw][None],
        enter_grad[:, qw : qw + kw][None],
        enter_grad[:, qw + kw : qw + 2 * kw][None],
        grad_out[None],
        grad_gains[:, 1][None],
        grad_gate[None],
        grad_up[None],
        grad_down[None],
    )


def solution(mesh):
    rows_placed = P(None, "fsdp", "ctx", None)
    kept_placed = P("section", None, "fsdp", "ctx", None)
    gain_placed = P("section", ("ctx", "fsdp"))
    dense_placed = P("section", ("ctx", "fsdp"), None)
    expert_placed = P("section", None, ("ctx", "fsdp"), None)
    dense_all = (dense_placed,) * 4
    expert_all = (expert_placed,) * 3
    layer_placed = (gain_placed,) + dense_all + (gain_placed,) + expert_all
    return jax.shard_map(
        body,
        mesh=mesh,
        in_specs=(rows_placed, P(), kept_placed, kept_placed) + layer_placed + (rows_placed,),
        out_specs=(kept_placed, kept_placed) + layer_placed,
        check_vma=False,
    )
```

```python
import functools

import jax
import jax.numpy as jnp
from jax import lax
from jax.experimental import pallas as pl
from jax.experimental.pallas import tpu as pltpu
from jax.sharding import PartitionSpec as P

QH = 12
KVH = 2
HD = 128
GROUP = QH // KVH
TOP = 4
EXPERTS = 8
bf16 = jnp.bfloat16
f32 = jnp.float32


epsilon = 1e-06
masked_out = -1e30
gap = 256


def swap(value, axis, bit):
    count = lax.axis_size(axis)
    return lax.ppermute(value, axis, [(source, source ^ bit) for source in range(count)])


def tie(*values):
    return lax.optimization_barrier(values)


def after(value, earlier):
    return tie(value, earlier)[0]


def at(value, index, axis=0):
    return lax.dynamic_index_in_dim(value, index, axis, keepdims=False)


def dot(spec, left, right, kind=f32):
    return jnp.einsum(spec, left, right, preferred_element_type=kind)


def cost(micros):
    return pl.CostEstimate(
        flops=int(micros * 1e9), bytes_accessed=int(micros * 3e6), transcendentals=0
    )


def kernel_params():
    return pltpu.CompilerParams(vmem_limit_bytes=56 * 1024 * 1024)


def nt(left, right):
    return lax.dot_general(left, right, (((1,), (1,)), ((), ())), preferred_element_type=f32)


def nn(left, right):
    return jnp.dot(left, right, preferred_element_type=f32)


def head_rows(ref):
    return jnp.concatenate([ref[:, i * HD : (i + 1) * HD] for i in range(GROUP)], axis=0)


def softmax_rows(ids_ref, queries, keys, half, own):
    scores = nt(queries, keys) * HD ** (-0.5)
    tall, wide = scores.shape
    row = lax.broadcasted_iota(jnp.int32, (half, 1), 0)
    row = jnp.concatenate([row] * (tall // half), axis=0) + ids_ref[own] * half
    lane = lax.broadcasted_iota(jnp.int32, (1, half), 1)
    column = [lane + ids_ref[block] * half for block in range(wide // half)]
    column = jnp.concatenate(column, axis=1)
    scores = jnp.where(row >= column, scores, masked_out)
    shifted = jnp.exp(scores - jnp.max(scores, axis=1, keepdims=True))
    return shifted / jnp.sum(shifted, axis=1, keepdims=True)


def attend_kernel(ids_ref, query_ref, key_ref, value_ref, out_ref):
    half = query_ref.shape[0]
    probs = softmax_rows(ids_ref, head_rows(query_ref), key_ref[...], half, pl.program_id(1))
    out = nn(probs.astype(bf16), value_ref[...]).astype(bf16)
    for i in range(GROUP):
        out_ref[:, i * HD : (i + 1) * HD] = out[i * half : (i + 1) * half]


def attend_specs(rows, seq_len):
    half = rows // 2
    by_head = pl.BlockSpec((half, GROUP * HD), lambda g, h, ids: (h, g))
    keys = pl.BlockSpec((seq_len, HD), lambda g, h, ids: (0, g))
    values = pl.BlockSpec((seq_len, HD), lambda g, h, ids: (0, KVH + g))
    return by_head, keys, values


def attend_call(ids, queries, key_value):
    rows, seq_len = (queries.shape[0], key_value.shape[0])
    by_head, keys, values = attend_specs(rows, seq_len)
    return pl.pallas_call(
        attend_kernel,
        grid_spec=pltpu.PrefetchScalarGridSpec(
            num_scalar_prefetch=1,
            grid=(KVH, 2),
            in_specs=[by_head, keys, values],
            out_specs=by_head,
        ),
        out_shape=jax.ShapeDtypeStruct((rows, QH * HD), bf16),
        compiler_params=kernel_params(),
        cost_estimate=cost(1),
        name="attend",
    )(ids, queries, key_value, key_value)


def attend_back_kernel(ids_ref, query_ref, key_ref, value_ref, cot_ref, dq_ref, *refs):
    out, (dk_ref, dv_ref) = (refs[:-2], refs[-2:])
    half = query_ref.shape[0]
    group, own = (pl.program_id(0), pl.program_id(1))
    queries, cot = (head_rows(query_ref), head_rows(cot_ref))
    probs = softmax_rows(ids_ref, queries, key_ref[...], half, own)
    d_probs = nt(cot, value_ref[...])
    inner = jnp.sum(probs * d_probs, axis=1, keepdims=True)
    d_scores = (probs * (d_probs - inner)).astype(bf16)
    d_queries = (nn(d_scores, key_ref[...]) * HD ** (-0.5)).astype(bf16)
    for i in range(GROUP):
        dq_ref[:, i * HD : (i + 1) * HD] = d_queries[i * half : (i + 1) * half]
    d_keys = nn(d_scores.T, queries) * HD ** (-0.5)
    d_values = nn(probs.astype(bf16).T, cot)

    @pl.when(own == 0)
    def _():
        dk_ref[...] = d_keys
        dv_ref[...] = d_values

    @pl.when(own != 0)
    def _():
        rows = 2 * half
        for block, ref in enumerate(out):
            part = slice(block * rows, (block + 1) * rows)
            for first, total, last in ((0, dk_ref, d_keys), (KVH * HD, dv_ref, d_values)):
                columns = pl.ds(pl.multiple_of(first + group * HD, HD), HD)
                ref[:, columns] = (total[part, :] + last[part]).astype(bf16)


def attend_back_call(ids, queries, key_value, cot):
    rows, seq_len = (queries.shape[0], key_value.shape[0])
    by_head, keys, values = attend_specs(rows, seq_len)
    blocks = seq_len // rows
    wide = 2 * KVH * HD
    result = pl.pallas_call(
        attend_back_kernel,
        grid_spec=pltpu.PrefetchScalarGridSpec(
            num_scalar_prefetch=1,
            grid=(KVH, 2),
            in_specs=[by_head, keys, values, by_head],
            out_specs=[by_head] + [pl.BlockSpec((rows, wide), lambda g, h, ids: (0, 0))] * blocks,
            scratch_shapes=[pltpu.VMEM((seq_len, HD), f32)] * 2,
        ),
        out_shape=[jax.ShapeDtypeStruct((rows, QH * HD), bf16)]
        + [jax.ShapeDtypeStruct((rows, wide), bf16)] * blocks,
        compiler_params=kernel_params(),
        cost_estimate=cost(1),
        name="attend_back",
    )(ids, queries, key_value, key_value, cot)
    return (result[0], result[1:])


def gelu_parts(gate):
    root = 0.7978845608028654
    inner = root * (gate + 0.044715 * gate * gate * gate)
    bent = jnp.tanh(inner)
    value = 0.5 * gate * (1.0 + bent)
    slope = root * (1.0 + 3.0 * 0.044715 * gate * gate)
    return value, 0.5 * (1.0 + bent) + 0.5 * gate * (1.0 - bent * bent) * slope


def give_back(pick_ref, total_ref, share_ref, before, out):
    blocks, capacity, _ = pick_ref.shape
    for d in range(blocks):
        part = total_ref[d * capacity : (d + 1) * capacity, :]
        if share_ref is not None:
            part = part * share_ref[d]
        back = nn(pick_ref[d].T, part.astype(bf16))
        if before:
            back = back + before[d][...]
        out[d][...] = back.astype(out[d].dtype)


def flat(ref):
    value = ref[...]
    return value.reshape(-1, value.shape[-1])


def add_up(total_ref, part, step):
    @pl.when(step == 0)
    def _():
        total_ref[...] = part

    @pl.when(step != 0)
    def _():
        total_ref[...] += part


def expert_kernel(blocks, adds, pick_ref, share_ref, gate_ref, up_ref, down_ref, *refs):
    rows, refs = (refs[:blocks], refs[blocks:])
    before, refs = (refs[: blocks * adds], refs[blocks * adds :])
    out, (picked_ref, gate_pre_ref, up_pre_ref, total_ref) = (refs[:blocks], refs[blocks:])
    step = pl.program_id(0)
    capacity = pick_ref.shape[1]

    @pl.when(step == 0)
    def _():
        for d in range(blocks):
            block = nn(pick_ref[d], rows[d][...]).astype(bf16)
            picked_ref[d * capacity : (d + 1) * capacity, :] = block

    gate_pre = nn(picked_ref[...], flat(gate_ref))
    up_pre = nn(picked_ref[...], flat(up_ref))
    gate_pre_ref[...] = gate_pre
    up_pre_ref[...] = up_pre
    active = (gelu_parts(gate_pre)[0] * up_pre).astype(bf16)
    add_up(total_ref, nn(active, flat(down_ref)), step)

    @pl.when(step == pl.num_programs(0) - 1)
    def _():
        give_back(pick_ref, total_ref, share_ref, before, out)


def whole_spec(shape):
    return pl.BlockSpec(
        shape, lambda step: (0,) * len(shape), pipeline_mode=pl.Buffered(buffer_count=1)
    )


def weight_operands(weights, deep, cut):
    if len(weights) == 1:
        unit = weights[0]
        shards, tall, width = unit.shape
        specs = [
            pl.BlockSpec((shards, deep, cut), lambda step: (0, 0, 2 * step)),
            pl.BlockSpec((shards, deep, cut), lambda step: (0, 0, 2 * step + 1)),
            pl.BlockSpec(
                (shards // 2, tall - deep, width), lambda step: (step, deep // (tall - deep), 0)
            ),
        ]
        return specs, [unit, unit, unit]
    pair, down = weights
    specs = [
        pl.BlockSpec((pair.shape[0], cut), lambda step: (0, 2 * step)),
        pl.BlockSpec((pair.shape[0], cut), lambda step: (0, 2 * step + 1)),
        pl.BlockSpec((cut, down.shape[1]), lambda step: (step, 0)),
    ]
    return specs, [pair, pair, down]


def expert_call(picks, shares, rows, weights, deep, hidden, before, micros):
    blocks, capacity, _ = picks.shape
    width, cut, tall = (rows[0].shape[1], hidden // 2, blocks * capacity)
    columns = pl.BlockSpec((tall, cut), lambda step: (0, step))
    row_specs = [whole_spec(block.shape) for block in rows]
    specs, operands = weight_operands(weights, deep, cut)
    result = pl.pallas_call(
        functools.partial(expert_kernel, blocks, 1 if before else 0),
        grid=(2,),
        in_specs=[whole_spec(picks.shape), whole_spec(shares.shape)]
        + specs
        + row_specs * (2 if before else 1),
        out_specs=row_specs + [whole_spec((tall, width)), columns, columns],
        out_shape=[jax.ShapeDtypeStruct(block.shape, bf16) for block in rows]
        + [
            jax.ShapeDtypeStruct((tall, width), bf16),
            jax.ShapeDtypeStruct((tall, hidden), f32),
            jax.ShapeDtypeStruct((tall, hidden), f32),
        ],
        scratch_shapes=[pltpu.VMEM((tall, width), f32)],
        compiler_params=kernel_params(),
        cost_estimate=cost(micros),
        name="expert",
    )(picks, shares, *operands, *rows, *before)
    return (list(result[:blocks]), list(result[blocks:]))


def expert_back_kernel(
    blocks, adds, pick_ref, share_ref, gate_pre_ref, up_pre_ref, gate_ref, up_ref, down_ref, *refs
):
    rows, refs = (refs[:blocks], refs[blocks:])
    before, refs = (refs[: blocks * adds], refs[blocks * adds :])
    out, refs = (refs[:blocks], refs[blocks:])
    slots_ref, d_gate_ref, d_up_ref, active_ref, total_ref = refs
    step = pl.program_id(0)
    capacity = pick_ref.shape[1]

    @pl.when(step == 0)
    def _():
        for d in range(blocks):
            block = nn(pick_ref[d], rows[d][...]) * share_ref[d]
            slots_ref[d * capacity : (d + 1) * capacity, :] = block.astype(bf16)

    d_active = nt(slots_ref[...], flat(down_ref))
    value, slope = gelu_parts(gate_pre_ref[...])
    up_pre = up_pre_ref[...]
    d_gate = (d_active * up_pre * slope).astype(bf16)
    d_up = (d_active * value).astype(bf16)
    active_ref[...] = (value * up_pre).astype(bf16)
    d_gate_ref[...] = d_gate
    d_up_ref[...] = d_up
    add_up(total_ref, nt(d_gate, flat(gate_ref)) + nt(d_up, flat(up_ref)), step)

    @pl.when(step == pl.num_programs(0) - 1)
    def _():
        give_back(pick_ref, total_ref, None, before, out)


def expert_back_call(picks, shares, rows, kept, weights, deep, before, micros):
    _, gate_pre, up_pre = kept
    blocks, capacity, _ = picks.shape
    width, (tall, hidden) = (rows[0].shape[1], gate_pre.shape)
    cut = hidden // 2
    columns = pl.BlockSpec((tall, cut), lambda step: (0, step))
    row_specs = [whole_spec(block.shape) for block in rows]
    specs, operands = weight_operands(weights, deep, cut)
    result = pl.pallas_call(
        functools.partial(expert_back_kernel, blocks, 1 if before else 0),
        grid=(2,),
        in_specs=[whole_spec(picks.shape), whole_spec(shares.shape), columns, columns]
        + specs
        + row_specs * (2 if before else 1),
        out_specs=row_specs + [whole_spec((tall, width)), columns, columns, columns],
        out_shape=[jax.ShapeDtypeStruct(block.shape, bf16) for block in rows]
        + [jax.ShapeDtypeStruct((tall, width), bf16)]
        + [jax.ShapeDtypeStruct((tall, hidden), bf16)] * 3,
        scratch_shapes=[pltpu.VMEM((tall, width), f32)],
        compiler_params=kernel_params(),
        cost_estimate=cost(micros),
        name="expert_back",
    )(picks, shares, gate_pre, up_pre, *operands, *rows, *before)
    return (list(result[:blocks]), list(result[blocks:]))


def expert_grads_kernel(parts, deep, *refs):
    picked, slots, d_gate, d_up, active = (refs[i * parts : (i + 1) * parts] for i in range(5))
    grad_refs, turned_ref = (refs[5 * parts : -1], refs[-1])
    step = pl.program_id(0)

    def below(some):
        return jnp.concatenate([ref[...] for ref in some], axis=0)

    @pl.when(step == 0)
    def _():
        turned_ref[...] = below(picked).T

    grad_gate = nn(turned_ref[...], below(d_gate)).astype(bf16)
    grad_up = nn(turned_ref[...], below(d_up)).astype(bf16)
    grad_down = nn(below(active).T, below(slots)).astype(bf16)
    cut = grad_gate.shape[1]
    if len(grad_refs) == 1:
        unit_ref = grad_refs[0]
        shards, tall, width = unit_ref.shape
        for side in range(2):

            @pl.when(step == side)
            def _():
                left, some = (2 * side * cut, shards // 2)
                unit_ref[:, :deep, left : left + cut] = grad_gate.reshape(shards, deep, cut)
                left = left + cut
                unit_ref[:, :deep, left : left + cut] = grad_up.reshape(shards, deep, cut)
                rest = grad_down.reshape(some, tall - deep, width)
                unit_ref[side * some : (side + 1) * some, deep:, :] = rest
    else:
        grad_refs[0][:, :cut] = grad_gate
        grad_refs[0][:, cut:] = grad_up
        grad_refs[1][...] = grad_down


def expert_grads_call(picked, saved, weights, deep):
    slots, d_gate, d_up, active = zip(*saved)
    width, hidden = (picked[0].shape[1], d_gate[0].shape[1])
    cut = hidden // 2
    columns = [pl.BlockSpec((part.shape[0], cut), lambda step: (0, step)) for part in picked]
    if len(weights) == 1:
        grad_specs = [whole_spec(weights[0].shape)]
    else:
        grad_specs = [
            pl.BlockSpec((width, 2 * cut), lambda step: (0, step)),
            pl.BlockSpec((cut, width), lambda step: (step, 0)),
        ]
    return list(
        pl.pallas_call(
            functools.partial(expert_grads_kernel, len(picked), deep),
            grid=(2,),
            in_specs=[whole_spec(part.shape) for part in picked] * 2 + columns * 3,
            out_specs=grad_specs,
            out_shape=[jax.ShapeDtypeStruct(part.shape, bf16) for part in weights],
            scratch_shapes=[pltpu.VMEM((width, sum(part.shape[0] for part in picked)), bf16)],
            compiler_params=kernel_params(),
            cost_estimate=cost(1),
            name="expert_grads",
        )(*picked, *slots, *d_gate, *d_up, *active)
    )


def norm_parts(value):
    scale = lax.rsqrt(jnp.mean(value * value, axis=1, keepdims=True) + epsilon)
    return scale, value * scale


def norm_back(grad, gain, value):
    scale, scaled = norm_parts(value)
    grown = grad * gain
    back = scale * (grown - scaled * jnp.mean(scaled * grown, axis=1, keepdims=True))
    return back, (grad * scaled).astype(bf16)


def add_all(refs):
    total = refs[0][...].astype(f32)
    for ref in refs[1:]:
        total = total + ref[...].astype(f32)
    return total


def side_offsets(core_ref, steps, cut):
    step, core = (pl.program_id(0), core_ref[0])
    own = pl.multiple_of((core * steps + step) * cut, cut)
    other = pl.multiple_of(((1 - core) * steps + step) * cut, cut)
    return own, other


def dense_call(kernel, core, steps, whole, halves, out, scratch, name, micros):
    cut = halves[0].shape[1] // steps

    def keep(shape):
        return pl.BlockSpec(
            shape, lambda step, core: (0,) * len(shape), pipeline_mode=pl.Buffered(buffer_count=1)
        )

    def tile(tall):
        return pl.BlockSpec((tall, cut), lambda step, core: (0, step))

    return pl.pallas_call(
        kernel,
        grid_spec=pltpu.PrefetchScalarGridSpec(
            num_scalar_prefetch=1,
            grid=(steps,),
            in_specs=[keep(part.shape) for part in whole] + [tile(halves[0].shape[0])] * 2,
            out_specs=[
                tile(part.shape[0]) if tiled else keep(part.shape) for part, tiled in out
            ],
            scratch_shapes=scratch,
        ),
        out_shape=[part for part, _ in out],
        compiler_params=kernel_params(),
        cost_estimate=cost(micros),
        name=name,
    )(core.astype(jnp.int32).reshape(1), *whole, *halves)


def shape_of(kind, *shape):
    return jax.ShapeDtypeStruct(shape, kind)


def enter_kernel(steps, terms, core_ref, gain_ref, *refs):
    parts, (own_ref, other_ref, sent_ref, normed_ref, out_ref) = (refs[:terms], refs[terms:])
    own, other = side_offsets(core_ref, steps, own_ref.shape[1])

    @pl.when(pl.program_id(0) == 0)
    def _():
        sent = add_all(parts).astype(bf16)
        sent_ref[...] = sent
        normed_ref[...] = (norm_parts(sent.astype(f32))[1] * gain_ref[...]).astype(bf16)

    cut = own_ref.shape[1]
    out_ref[:, pl.ds(own, cut)] = nn(normed_ref[...], own_ref[...]).astype(bf16)
    out_ref[:, pl.ds(other, cut)] = nn(normed_ref[...], other_ref[...]).astype(bf16)


def enter_call(core, parts, gain, halves):
    rows, width = parts[0].shape
    return dense_call(
        functools.partial(enter_kernel, 3, len(parts)),
        core,
        3,
        [gain] + parts,
        halves,
        [
            (shape_of(bf16, rows, width), False),
            (shape_of(bf16, rows, width), False),
            (shape_of(bf16, rows, 2 * halves[0].shape[1]), False),
        ],
        [],
        "enter",
        6,
    )


def leave_kernel(steps, core_ref, gain_ref, rows_ref, attended_ref, own_ref, other_ref,
                 mid_ref, normed_ref):
    cut = own_ref.shape[1]
    for start, ref in zip(side_offsets(core_ref, steps, cut), (own_ref, other_ref)):
        part = pl.ds(start, cut)
        mid_ref[:, part] = rows_ref[:, part].astype(f32) + nn(attended_ref[...], ref[...])

    @pl.when(pl.program_id(0) == steps - 1)
    def _():
        normed_ref[...] = (norm_parts(mid_ref[...])[1] * gain_ref[...]).astype(bf16)


def leave_call(core, rows_in, attended, gain, halves):
    rows, width = rows_in.shape
    return dense_call(
        functools.partial(leave_kernel, 2),
        core,
        2,
        [gain, rows_in, attended],
        halves,
        [(shape_of(f32, rows, width), False), (shape_of(bf16, rows, width), False)],
        [],
        "leave",
        5,
    )


def leave_back_kernel(steps, terms, core_ref, gain_ref, mid_ref, cot_ref, attended_ref, *refs):
    parts, refs = (refs[:terms], refs[terms:])
    own_ref, other_ref, after_ref, term_ref, d_attended_ref, *refs = refs
    own_grad_ref, other_grad_ref, branch_ref, turned_ref, total_ref = refs
    step, cut = (pl.program_id(0), own_ref.shape[1])

    @pl.when(step == 0)
    def _():
        back, term_ref[...] = norm_back(add_all(parts), gain_ref[...], mid_ref[...])
        back = back + cot_ref[...].astype(f32)
        after_ref[...] = back
        branch_ref[...] = back.astype(bf16)
        turned_ref[...] = attended_ref[...].T

    own, other = side_offsets(core_ref, steps, cut)
    d_own, d_other = (branch_ref[:, pl.ds(own, cut)], branch_ref[:, pl.ds(other, cut)])
    own_grad_ref[...] = nn(turned_ref[...], d_own).astype(bf16)
    other_grad_ref[...] = nn(turned_ref[...], d_other).astype(bf16)
    add_up(total_ref, nt(d_own, own_ref[...]) + nt(d_other, other_ref[...]), step)

    @pl.when(step == steps - 1)
    def _():
        d_attended_ref[...] = total_ref[...].astype(bf16)


def leave_back_call(core, parts, gain, mid, cotangent, attended, halves):
    rows, width = mid.shape
    half = (halves[0].shape[0], halves[0].shape[1])
    return dense_call(
        functools.partial(leave_back_kernel, 2, len(parts)),
        core,
        2,
        [gain, mid, cotangent, attended] + parts,
        halves,
        [
            (shape_of(f32, rows, width), False),
            (shape_of(bf16, rows, width), False),
            (shape_of(bf16, rows, width), False),
            (shape_of(bf16, *half), True),
            (shape_of(bf16, *half), True),
        ],
        [
            pltpu.VMEM((rows, width), bf16),
            pltpu.VMEM((width, rows), bf16),
            pltpu.VMEM((rows, width), f32),
        ],
        "leave_back",
        8,
    )


def enter_back_kernel(steps, terms, core_ref, gain_ref, rows_ref, normed_ref, after_ref, term_ref,
                      dq_ref, *refs):
    parts, refs = (refs[:terms], refs[terms:])
    own_ref, other_ref, entry_ref, sent_ref, own_grad_ref, other_grad_ref, *refs = refs
    entered_ref, turned_ref, total_ref = refs
    step, cut = (pl.program_id(0), own_ref.shape[1])
    rows, qw = dq_ref.shape

    @pl.when(step == 0)
    def _():
        entered_ref[:, :qw] = dq_ref[...]
        wide = parts[0].shape[1]
        entered_ref[:, qw : qw + wide] = add_all(parts).astype(bf16)
        entered_ref[:, qw + wide :] = jnp.zeros((rows, gap), bf16)
        turned_ref[...] = normed_ref[...].T

    own, other = side_offsets(core_ref, steps, cut)
    d_own, d_other = (entered_ref[:, pl.ds(own, cut)], entered_ref[:, pl.ds(other, cut)])
    own_grad_ref[...] = nn(turned_ref[...], d_own).astype(bf16)
    other_grad_ref[...] = nn(turned_ref[...], d_other).astype(bf16)
    add_up(total_ref, nt(d_own, own_ref[...]) + nt(d_other, other_ref[...]), step)

    @pl.when(step == steps - 1)
    def _():
        back, attn_term = norm_back(total_ref[...], gain_ref[...], rows_ref[...].astype(f32))
        back = back + after_ref[...]
        entry_ref[...] = back
        sent_ref[...] = back.astype(bf16)
        lane = lax.broadcasted_iota(jnp.int32, (rows, 128), 1)
        sums = nn(attn_term.T, (lane == 0).astype(bf16))
        sums = (sums + nn(term_ref[...].T, (lane == 1).astype(bf16))).astype(bf16)
        left = cut - gap

        @pl.when(core_ref[0] == 0)
        def _():
            other_grad_ref[:, left : left + 128] = sums

        @pl.when(core_ref[0] != 0)
        def _():
            own_grad_ref[:, left : left + 128] = sums


def enter_back_call(core, dq, parts, gain, rows_in, normed, after, term, halves):
    rows, width = rows_in.shape
    return dense_call(
        functools.partial(enter_back_kernel, 3, len(parts)),
        core,
        3,
        [gain, rows_in, normed, after, term, dq] + parts,
        halves,
        [
            (shape_of(f32, rows, width), False),
            (shape_of(bf16, rows, width), False),
            (shape_of(bf16, *halves[0].shape), True),
            (shape_of(bf16, *halves[0].shape), True),
        ],
        [
            pltpu.VMEM((rows, 2 * halves[0].shape[1]), bf16),
            pltpu.VMEM((width, rows), bf16),
            pltpu.VMEM((rows, width), f32),
        ],
        "enter_back",
        13,
    )


def place_kernel(count, joined, index_ref, *refs):
    step = pl.program_id(0)
    for bit in range(count):

        @pl.when(step == bit)
        def _():
            if joined:
                refs[count][...] = refs[bit][...]
            else:
                refs[count][0] = refs[bit][...]


def place_call(blocks, index):
    count = len(blocks)
    shape = blocks[0].shape
    zeros = (0,) * len(shape)
    joined = len(shape) == 2 and shape[0] % 16 == 0
    if joined:
        out_spec = pl.BlockSpec(shape, lambda step, at: (at[0] ^ step, 0))
        out_shape = (count * shape[0], shape[1])
    else:
        out_spec = pl.BlockSpec((1,) + shape, lambda step, at: (at[0] ^ step,) + zeros)
        out_shape = (count,) + shape
    return pl.pallas_call(
        functools.partial(place_kernel, count, joined),
        grid_spec=pltpu.PrefetchScalarGridSpec(
            num_scalar_prefetch=1,
            grid=(count,),
            in_specs=[pl.BlockSpec(shape, lambda step, at: zeros)] * count,
            out_specs=out_spec,
        ),
        out_shape=jax.ShapeDtypeStruct(out_shape, blocks[0].dtype),
        compiler_params=kernel_params(),
        cost_estimate=cost(2),
        name="place",
    )(index.astype(jnp.int32).reshape(1), *blocks)


def deal_kernel(count, index_ref, *refs):
    step = pl.program_id(0)
    for bit in range(count):

        @pl.when(step == bit)
        def _():
            for layer, ref in enumerate(refs[count:]):
                ref[0] = refs[bit][layer]


def deal_call(blocks, index):
    count = len(blocks)
    layers, *shape = blocks[0].shape
    shape = tuple(shape)
    zeros = (0,) * len(shape)
    return pl.pallas_call(
        functools.partial(deal_kernel, count),
        grid_spec=pltpu.PrefetchScalarGridSpec(
            num_scalar_prefetch=1,
            grid=(count,),
            in_specs=[pl.BlockSpec((layers,) + shape, lambda step, at: (0,) + zeros)] * count,
            out_specs=[pl.BlockSpec((1,) + shape, lambda step, at: (at[0] ^ step,) + zeros)]
            * layers,
        ),
        out_shape=[jax.ShapeDtypeStruct((count,) + shape, blocks[0].dtype)] * layers,
        compiler_params=kernel_params(),
        cost_estimate=cost(2),
        name="deal",
    )(index.astype(jnp.int32).reshape(1), *blocks)


def order_kernel(count, order_ref, *refs):
    step = pl.program_id(0)
    for i in range(count):

        @pl.when(step == i)
        def _():
            refs[count][:, 0] = refs[i][:, 0]


def order_call(blocks, order, unit):
    count = len(blocks)
    n_ctx, _, tall, wide = blocks[0].shape
    shape = (n_ctx, 1, tall, wide)
    source = pl.BlockSpec(
        shape, lambda step, at: (0, unit, 0, 0), pipeline_mode=pl.Buffered(buffer_count=1)
    )
    result = pl.pallas_call(
        functools.partial(order_kernel, count),
        grid_spec=pltpu.PrefetchScalarGridSpec(
            num_scalar_prefetch=1,
            grid=(count,),
            in_specs=[source] * count,
            out_specs=pl.BlockSpec(shape, lambda step, at: (0, at[step], 0, 0)),
        ),
        out_shape=jax.ShapeDtypeStruct((n_ctx, count, tall, wide), bf16),
        compiler_params=kernel_params(),
        cost_estimate=cost(4),
        name="order",
    )(order.astype(jnp.int32), *blocks)
    return result.reshape(n_ctx * count, tall, wide)


def finish_kernel(deep, index_ref, own_ref, other_ref, gate_ref, up_ref, down_ref):
    side = pl.program_id(1)
    wide = gate_ref.shape[2] // 2

    def write(source):
        for half in range(2):
            left, target = (2 * half * wide, slice(half * wide, (half + 1) * wide))
            gate_ref[:, :, target] = source[0, :, :deep, left : left + wide].astype(f32)
            left = left + wide
            up_ref[:, :, target] = source[0, :, :deep, left : left + wide].astype(f32)
        down_ref[...] = source[0, :, deep:, :].astype(f32)

    @pl.when(side == index_ref[1])
    def _():
        write(own_ref)

    @pl.when(side != index_ref[1])
    def _():
        write(other_ref)


def finish_call(own, other, deep, hidden, place, core):
    n_ctx, units, tall, width = own.shape
    experts = 2 * n_ctx * units
    source = pl.BlockSpec((1, units, tall, width), lambda bit, side, at: (bit, 0, 0, 0))
    target = lambda bit, side, at: (2 * (at[0] ^ bit) + side, 0, 0)
    return pl.pallas_call(
        functools.partial(finish_kernel, deep),
        grid_spec=pltpu.PrefetchScalarGridSpec(
            num_scalar_prefetch=1,
            grid=(n_ctx, 2),
            in_specs=[source, source],
            out_specs=[
                pl.BlockSpec((units, deep, hidden), target),
                pl.BlockSpec((units, deep, hidden), target),
                pl.BlockSpec((units, tall - deep, width), target),
            ],
        ),
        out_shape=[
            jax.ShapeDtypeStruct((experts, deep, hidden), f32),
            jax.ShapeDtypeStruct((experts, deep, hidden), f32),
            jax.ShapeDtypeStruct((experts, tall - deep, width), f32),
        ],
        compiler_params=kernel_params(),
        cost_estimate=cost(8),
        name="finish",
    )(jnp.stack([place, core]).astype(jnp.int32), own, other)


def body(
    tokens,
    block_of,
    routes,
    combine,
    attn_norm,
    w_query,
    w_key,
    w_value,
    w_out,
    ffn_norm,
    w_gate,
    w_up,
    w_down,
    out_grad,
):
    rows = tokens.shape[2]
    width = tokens.shape[3]
    half = rows // 2
    n_ctx = lax.axis_size("ctx")
    n_fsdp = lax.axis_size("fsdp")
    core, place, depth = (
        lax.axis_index(axis).astype(jnp.uint32) for axis in ("section", "ctx", "fsdp")
    )
    seq_len = rows * n_ctx
    capacity = rows * TOP * 5 // (4 * EXPERTS)
    score_scale = HD ** (-0.5)
    own_experts = EXPERTS // n_ctx
    hidden = w_gate.shape[3]
    shard_rows = w_query.shape[1]
    down_rows = w_down.shape[2]
    qw = w_query.shape[2]
    kw = w_key.shape[2]
    pieces = max(1, 2 * n_ctx // EXPERTS)
    per_core = max(1, EXPERTS // (2 * n_ctx))
    unit_rows = shard_rows + down_rows
    aligned = shard_rows % 16 == 0 and down_rows % 16 == 0

    def on_core(former, latter):
        return jnp.where(core == 0, former, latter)

    def own_other(low, high):
        return (on_core(low, high), on_core(high, low))

    early, late = (range(1, n_ctx // 2 + 1), range(n_ctx // 2 + 1, n_ctx))

    def send(value, bits):
        return [swap(value, "ctx", bit) for bit in bits]

    def spread(value):
        return [value] + send(value, early) + send(value, late)

    def spread_rows(value):
        near_blocks = send(value, early)
        value, near_blocks = tie(value, near_blocks)
        return [value] + near_blocks + send(value, late)

    def gather_back(blocks):
        return [blocks[0]] + [swap(blocks[bit], "ctx", bit) for bit in range(1, n_ctx)]

    info = jnp.concatenate([routes.astype(f32), combine], axis=-1)[0, :, 0].transpose(0, 2, 1)
    info_own, info_other = (at(info, core), swap(at(info, 1 - core), "section", 1))
    info = jnp.stack(own_other(info_own, info_other))
    info = jnp.stack([info] + [swap(info, "ctx", bit) for bit in range(1, n_ctx)], axis=1)

    gain_columns = jnp.stack([attn_norm[0], ffn_norm[0]], axis=1)
    gain_columns = jnp.pad(gain_columns, ((0, 0), (0, gap - 2)))
    enter_shard = jnp.concatenate([w_query[0], w_key[0], w_value[0], gain_columns], axis=1)
    enter_cut = enter_shard.shape[1] // 2
    leave_cut = w_out.shape[2] // 2
    low_shard = jnp.concatenate([enter_shard[:, :enter_cut], w_out[0, :, :leave_cut]], axis=1)
    high_shard = jnp.concatenate([enter_shard[:, enter_cut:], w_out[0, :, leave_cut:]], axis=1)
    lent = swap(on_core(high_shard, low_shard), "section", 1)
    dense_shards = (on_core(low_shard, lent), on_core(lent, high_shard))

    def gather_deep(shard):
        blocks = [shard] + [swap(shard, "fsdp", bit) for bit in range(1, n_fsdp)]
        return place_call(blocks, depth).reshape(-1, shard.shape[1])

    def join_square(blocks):
        return place_call(blocks, place).reshape(-1, blocks[0].shape[1])

    def gather_square(deep):
        return join_square(spread(deep))

    cut = hidden // 2
    unit_stack = jnp.concatenate(
        [
            jnp.concatenate(
                [w_gate[0, ..., :cut], w_up[0, ..., :cut], w_gate[0, ..., cut:], w_up[0, ..., cut:]],
                axis=2,
            ),
            w_down[0],
        ],
        axis=1,
    )
    if pieces == 2:
        unit_stack = jnp.stack(jnp.split(unit_stack, 2, axis=2), axis=1)
    unit_stack = unit_stack.reshape(n_ctx, 2, per_core, unit_rows, width // pieces)
    units_lent = swap(at(unit_stack, 1 - core, 1), "section", 1)
    unit_stacks = jnp.stack(own_other(at(unit_stack, core, 1), units_lent), axis=1)

    def deal_units(stack):
        blocks = [at(stack, place)]
        blocks += [swap(at(stack, place ^ bit), "ctx", bit) for bit in range(1, n_ctx)]
        return deal_call(blocks, place)

    ring = list(range(0, n_fsdp, 2)) + list(range(1, n_fsdp, 2))[::-1]
    ring_steps = [(ring[i], ring[(i + 1) % n_fsdp]) for i in range(n_fsdp)]
    ring_table = [[ring[ring.index(z) - i] for i in range(n_fsdp)] for z in range(n_fsdp)]
    behind_here = at(jnp.array(ring_table, jnp.uint32), depth)

    def ring_send(moved):
        return [blocks + [lax.ppermute(blocks[-1], "fsdp", ring_steps)] for blocks in moved]

    def own_units(blocks):
        return [order_call(blocks, behind_here, unit) for unit in range(per_core)]

    def pair_units(mine):
        other = [swap(part, "section", 1) for part in mine]
        units = list(mine) + other
        if pieces == 2:
            units = [jnp.concatenate(own_other(mine[0], other[0]), axis=2)]
        if aligned:
            return [[unit] for unit in units]
        return [
            [unit[:, :shard_rows].reshape(-1, width), unit[:, shard_rows:].reshape(-1, width)]
            for unit in units
        ]

    def cut_units(grads):
        if aligned:
            units = [unit for (unit,) in grads]
        else:
            units = [
                jnp.concatenate(
                    [part.reshape(n_ctx * n_fsdp, -1, width) for part in parts], axis=1
                )
                for parts in grads
            ]
        if pieces == 1:
            return (units[:per_core], units[per_core:])
        own, other = own_other(*jnp.split(units[0], 2, axis=2))
        return ([own], [other])

    def ring_part(terms, behind):
        spot = behind_here[behind % n_fsdp]
        return sum(at(term, spot, 1).astype(f32) for term in terms)

    def ring_start(own, received):
        terms = [part.reshape((n_ctx, n_fsdp) + part.shape[1:]) for part in (own, received)]
        return (terms, ring_part(terms, 1).astype(bf16))

    def ring_move(state):
        return [(terms, lax.ppermute(moving, "fsdp", ring_steps)) for terms, moving in state]

    def ring_add(state, step):
        return [
            (terms, (moved.astype(f32) + ring_part(terms, step + 1)).astype(bf16))
            for terms, moved in state
        ]

    def ring_step(state, step):
        return ring_add(ring_move(state), step)

    def ring_last(state):
        state = ring_add(state, 2)
        for step in range(3, n_fsdp - 1):
            state = ring_step(state, step)
        return ring_move(state)

    def ring_rest(state, first):
        for step in range(first, n_fsdp):
            state = ring_step(state, step)
        return [moving for _, moving in state]

    def scatter_units(moved):
        whole = jnp.stack(moved, axis=1)
        blocks = [at(whole, place)]
        blocks += [swap(at(whole, place ^ bit), "ctx", bit) for bit in range(1, n_ctx)]
        return jnp.stack(blocks)

    def trade_square(own, received, bits):
        own, received = (part.reshape(n_ctx, -1, part.shape[1]) for part in (own, received))

        def part(bit):
            return at(own, place ^ bit).astype(f32) + at(received, place ^ bit).astype(f32)

        return [part(bit) if bit == 0 else swap(part(bit).astype(bf16), "ctx", bit) for bit in bits]

    def sum_square(parts):
        return sum(part.astype(f32) for part in parts).astype(bf16)

    def reduce_deep(mine):
        mine = mine.reshape(n_fsdp, shard_rows, -1)
        total = at(mine, depth).astype(f32)
        for bit in range(1, n_fsdp):
            total = total + swap(at(mine, depth ^ bit), "fsdp", bit).astype(f32)
        return total

    if pieces == 1:
        units_here = jnp.arange(per_core, dtype=jnp.uint32)
        units_here = jnp.concatenate(
            [core * per_core + units_here, (1 - core) * per_core + units_here]
        )
    else:
        units_here = jnp.zeros((1,), jnp.uint32)
    named = (place * own_experts + units_here).astype(f32)
    matches = info[:, None, :, :TOP] == named[None, :, None, None, None]
    hits = jnp.any(matches, axis=3)
    shares = jnp.sum(jnp.where(matches, info[:, None, :, TOP:], 0.0), axis=3)
    earlier = jnp.arange(rows)[:, None] < jnp.arange(rows)[None, :]
    rank = dot("ledr,rq->ledq", hits.astype(bf16), earlier.astype(bf16))
    slots = jnp.arange(capacity, dtype=f32)
    picks = hits[:, :, :, None, :] & (rank[:, :, :, None, :] == slots[:, None])
    slot_shares = jnp.sum(jnp.where(picks, shares[:, :, :, None, :], 0.0), axis=-1, keepdims=True)
    picks = picks.astype(bf16)

    order = place.astype(jnp.int32) ^ jnp.arange(n_ctx, dtype=jnp.int32)
    block_ids = jnp.take(block_of.reshape(n_ctx, 2), order, axis=0)
    block_ids = block_ids.reshape(-1)

    def gains_of(halves):
        pair = on_core(halves[1][:, -gap : 2 - gap], halves[0][:, -gap : 2 - gap])
        pair = pair.astype(f32).T
        return (pair[:1], pair[1:])

    near = 1 + len(early)
    parts = (slice(0, near), slice(near, n_ctx))

    def experts(layer, blocks, weights, answer, beside_near=tuple, beside_far=None):
        kept, arrived = ({}, [])
        back = {}
        for index, part in enumerate(parts):
            rows_here = blocks[part]
            if index:
                back[0], rows_here, found = tie(back[0], rows_here, beside_near())
                if answer:
                    arrived = [swap(block, "ctx", bit) for bit, block in zip(early, back[0][1:])]
            back[index] = []
            for j in range(own_experts):
                back[index], kept[index, j] = expert_call(
                    picks[layer, j, part],
                    slot_shares[layer, j, part],
                    rows_here,
                    weights[j],
                    shard_rows,
                    hidden,
                    back[index],
                    3 if index == 0 else 1,
                )
        if not answer:
            return (back[0] + back[1], kept)
        back[1], arrived, far = tie(back[1], arrived, beside_far(found))
        arrived += [swap(block, "ctx", bit) for bit, block in zip(late, back[1])]
        return (back[0][:1] + arrived, kept, found, far)

    def experts_back(layer, blocks, weights, kept, delay, beside_near, beside_far, beside_end):
        back, saved = ({}, {})
        for index, part in enumerate(parts):
            rows_here = blocks[part]
            if index:
                back[0], rows_here, found_near = tie(back[0], rows_here, beside_near())
                arrived = [swap(block, "ctx", bit) for bit, block in zip(early, back[0][1:])]
            back[index] = []
            for j in range(own_experts):
                back[index], saved[index, j] = expert_back_call(
                    picks[layer, j, part],
                    slot_shares[layer, j, part],
                    rows_here,
                    kept[index, j],
                    weights[j],
                    shard_rows,
                    back[index],
                    4 if index == 0 else 1,
                )
        back[1], arrived, saved, found_far = tie(back[1], arrived, saved, beside_far(found_near))
        arrived += [swap(block, "ctx", bit) for bit, block in zip(late, back[1])]

        def grads_of(j, saved):
            picked = [kept[index, j][0] for index in range(2)]
            both = [saved[index, j] for index in range(2)]
            return expert_grads_call(picked, both, weights[j], shard_rows)

        now = [j for j in reversed(range(own_experts)) if not delay or j >= per_core]
        grads = {j: grads_of(j, saved) for j in now}
        arrived, grads, found_end = tie(arrived, grads, beside_end(found_far))
        returned = back[0][:1] + arrived
        if len(now) == own_experts:
            own, other = cut_units([grads[j] for j in range(own_experts)])
            received = [swap(part, "section", 1) for part in other]
            return (returned, lambda earlier: (own, received), found_end)
        received = [swap(grads[j][0], "section", 1) for j in reversed(now)]

        def finish(earlier):
            ready = after(saved, earlier)
            return ([grads_of(j, ready)[0] for j in range(per_core)], received)

        return (returned, finish, found_end)

    def keep_own(first, second):
        other = swap(on_core(second, first), "section", 1)
        return own_other(on_core(first, second), other)

    dense_first, dense_second = dense_shards
    deep = gather_deep(jnp.concatenate([dense_first, dense_second[:, :enter_cut]], axis=1))
    dealt_first, dealt_second = deal_units(unit_stacks)
    deep, dealt_first, dealt_second, picks, dense_second = tie(
        deep, dealt_first, dealt_second, picks, dense_second
    )
    dense_blocks, moved, leave_shard, enter_shard = tie(
        spread(deep[:, :enter_cut]),
        ring_send([[dealt_first]]),
        deep[:, enter_cut : enter_cut + leave_cut],
        deep[:, enter_cut + leave_cut :],
    )
    leave_blocks = [leave_shard] + send(leave_shard, early)
    enter_own = join_square(dense_blocks)
    enter_first = (enter_own, swap(enter_own, "section", 1))

    first_gains = gains_of(enter_first)
    first_in = after(at(tokens, core)[0], slot_shares)
    _, first_normed, first_entered = enter_call(core, [first_in], first_gains[0], enter_first)
    first_entered, leave_blocks = tie(first_entered, leave_blocks)
    key_value = first_entered[:, qw : qw + 2 * kw]
    first_kv, leave_shard = tie(jnp.concatenate(spread(key_value)), leave_shard)
    first_attended = attend_call(block_ids, first_entered, first_kv)
    moved = ring_send(moved)
    first_attended, leave_blocks, dealt_second, moved, enter_shard, dense_second = tie(
        first_attended,
        leave_blocks + send(leave_shard, late),
        dealt_second,
        moved,
        enter_shard,
        dense_second,
    )
    enter_blocks = [enter_shard] + send(enter_shard, early)
    for _ in range(2, n_fsdp - 1):
        moved = ring_send(moved)
    leave_own = join_square(leave_blocks)
    leave_first = (leave_own, swap(leave_own, "section", 1))
    first_mid, ffn_normed = leave_call(core, first_in, first_attended, first_gains[1], leave_first)
    blocks = spread_rows(ffn_normed)
    blocks[:near], moved, dealt_second, enter_shard, leave_shard, enter_blocks = tie(
        blocks[:near], moved, dealt_second, enter_shard, dense_second[:, enter_cut:], enter_blocks
    )
    first_weights = pair_units(own_units(moved[0]))
    returned, first_kept, leave_shard, (enter_blocks, dealt_second) = experts(
        0,
        blocks,
        first_weights,
        True,
        lambda: gather_deep(leave_shard),
        lambda found: (enter_blocks + send(enter_shard, late), dealt_second),
    )
    moved = ring_send([[dealt_second]])
    returned, leave_shard = tie(returned, leave_shard)
    enter_own = join_square(enter_blocks)
    enter_second = (enter_own, swap(enter_own, "section", 1))
    leave_blocks = [leave_shard] + send(leave_shard, early)

    second_gains = gains_of(enter_second)
    second_in, second_normed, second_entered = enter_call(
        core, [first_mid] + returned, second_gains[0], enter_second
    )
    second_entered, leave_blocks, moved = tie(second_entered, leave_blocks, moved)
    moved = ring_send(moved)
    key_value = second_entered[:, qw : qw + 2 * kw]
    for _ in range(4, n_fsdp):
        moved = ring_send(moved)
    second_kv, leave_shard = tie(jnp.concatenate(spread(key_value)), leave_shard)
    second_attended = attend_call(block_ids, second_entered, second_kv)
    second_attended, leave_blocks, moved = tie(
        second_attended, leave_blocks + send(leave_shard, late), moved
    )
    moved = ring_send(moved)
    leave_own = join_square(leave_blocks)
    leave_second = (leave_own, swap(leave_own, "section", 1))
    second_mid, ffn_normed = leave_call(
        core, second_in, second_attended, second_gains[1], leave_second
    )
    blocks = spread_rows(ffn_normed)
    blocks[:near], moved = tie(blocks[:near], moved)
    second_weights = pair_units(own_units(moved[0]))
    second_returned, second_kept = experts(1, blocks, second_weights, False)
    cotangent = after(at(out_grad, core)[0], second_returned[:near])
    cot_blocks = spread_rows(cotangent)
    cot_blocks[:near], second_returned[near:] = tie(cot_blocks[:near], second_returned[near:])

    returned, finish, (second_returned, near_parts) = experts_back(
        1,
        cot_blocks,
        second_weights,
        second_kept,
        False,
        lambda: second_returned,
        lambda found: found,
        lambda found: (found, [swap(found[bit], "ctx", bit) for bit in early]),
    )
    far_parts = [swap(second_returned[bit], "ctx", bit) for bit in late]
    units_moving = [ring_start(*pair) for pair in zip(*finish(()))]
    after_rows, term, d_attended, *grads = leave_back_call(
        core,
        returned,
        second_gains[1],
        second_mid,
        cotangent,
        second_attended,
        leave_second,
    )
    leave_grads = (grads[0], swap(grads[1], "section", 1))
    d_queries, d_key_value = attend_back_call(block_ids, second_entered, second_kv, d_attended)
    d_queries, d_key_value, leave_grads, far_parts = tie(
        d_queries, d_key_value, leave_grads, far_parts
    )
    second_parts = second_returned[:1] + near_parts + far_parts
    second_out = second_mid + sum(part.astype(f32) for part in second_parts)
    d_key_value, units_moving = tie(gather_back(d_key_value), ring_move(units_moving))
    units_moving = ring_move(ring_add(units_moving, 1))
    leave_parts = trade_square(*leave_grads, range(n_ctx))
    second_entry, cotangent, *grads = enter_back_call(
        core,
        d_queries,
        d_key_value,
        second_gains[0],
        second_in,
        second_normed,
        after_rows,
        term,
        enter_second,
    )
    cotangent, grads, leave_parts, layer_rows = tie(
        cotangent, grads, leave_parts, (second_in, second_out.astype(bf16))
    )
    enter_grads = (grads[0], swap(grads[1], "section", 1))

    blocks = spread_rows(cotangent)
    blocks[:near], enter_grads, layer_rows = tie(blocks[:near], enter_grads, layer_rows)

    def dense_sums(parts):
        moving = [sum_square(some) for some in (parts, leave_parts)]
        return reduce_deep(jnp.concatenate(moving, axis=1))

    returned, finish, (units_moving, layer_outs, second_dense) = experts_back(
        0,
        blocks,
        first_weights,
        first_kept,
        False,
        lambda: (units_moving, trade_square(*enter_grads, [0, *early]), enter_grads),
        lambda found: (
            ring_last(found[0]),
            keep_own(*layer_rows),
            found[1] + trade_square(*found[2], late),
        ),
        lambda found: (found[0], found[1], dense_sums(found[2])),
    )
    second_moved = [moving for _, moving in ring_add(units_moving, n_fsdp - 1)]
    own, received = finish(())
    after_rows, term, d_attended, *grads = leave_back_call(
        core,
        returned,
        first_gains[1],
        first_mid,
        cotangent,
        first_attended,
        leave_first,
    )
    units_moving = [ring_start(*pair) for pair in zip(own, received)]
    leave_grads = (grads[0], swap(grads[1], "section", 1))
    d_queries, d_key_value = attend_back_call(block_ids, first_entered, first_kv, d_attended)
    d_queries, d_key_value, leave_grads = tie(d_queries, d_key_value, leave_grads)
    d_key_value, leave_grads = tie(gather_back(d_key_value), leave_grads)
    leave_parts = trade_square(*leave_grads, [0, *early])
    first_entry, _, *grads = enter_back_call(
        core,
        d_queries,
        d_key_value,
        first_gains[0],
        first_in,
        first_normed,
        after_rows,
        term,
        enter_first,
    )
    grads, leave_parts, leave_grads, units_moving = tie(
        grads, leave_parts, leave_grads, ring_move(units_moving)
    )
    enter_grads = (grads[0], swap(grads[1], "section", 1))
    units_moving = after(ring_move(ring_add(units_moving, 1)), enter_grads)
    enter_parts, leave_parts, first_entry = tie(
        trade_square(*enter_grads, range(n_ctx)),
        leave_parts + trade_square(*leave_grads, late),
        first_entry,
    )
    first_moving = [sum_square(parts) for parts in (enter_parts, leave_parts)]
    first_dense = reduce_deep(jnp.concatenate(first_moving, axis=1))
    scattered = scatter_units(ring_rest(ring_add(units_moving, 2), 3) + second_moved)
    first_scattered, second_scattered = (scattered[:, :per_core], scattered[:, per_core:])

    layer_out = jnp.stack(layer_outs)
    input_grads = jnp.stack(keep_own(first_entry, second_entry))
    low_dense, high_dense = keep_own(first_dense, second_dense)
    enter_grad = jnp.concatenate([low_dense[:, :enter_cut], high_dense[:, :enter_cut]], axis=1)
    grad_out = jnp.concatenate([low_dense[:, enter_cut:], high_dense[:, enter_cut:]], axis=1)
    grad_gains = enter_grad[:, qw + 2 * kw :]
    mine = on_core(first_scattered, second_scattered)
    other = swap(on_core(second_scattered, first_scattered), "section", 1)
    if aligned and pieces == 1:
        grad_gate, grad_up, grad_down = finish_call(mine, other, shard_rows, hidden, place, core)
    else:
        sides = [jnp.take(part, order, axis=0) for part in own_other(mine, other)]
        if pieces == 1:
            whole = jnp.stack(sides, axis=1).reshape(EXPERTS, unit_rows, width)
        else:
            whole = jnp.concatenate([side[:, 0] for side in sides], axis=2)
        pairs = whole[:, :shard_rows].astype(f32).reshape(EXPERTS, shard_rows, 2, 2, cut)
        grad_gate = pairs[:, :, :, 0].reshape(EXPERTS, shard_rows, hidden)
        grad_up = pairs[:, :, :, 1].reshape(EXPERTS, shard_rows, hidden)
        grad_down = whole[:, shard_rows:].astype(f32)
    return (
        layer_out[None, :, None],
        input_grads[None, :, None],
        grad_gains[:, 0][None],
        enter_grad[:, :qw][None],
        enter_grad[:, qw : qw + kw][None],
        enter_grad[:, qw + kw : qw + 2 * kw][None],
        grad_out[None],
        grad_gains[:, 1][None],
        grad_gate[None],
        grad_up[None],
        grad_down[None],
    )


def solution(mesh):
    rows_placed = P(None, "fsdp", "ctx", None)
    kept_placed = P("section", None, "fsdp", "ctx", None)
    gain_placed = P("section", ("ctx", "fsdp"))
    dense_placed = P("section", ("ctx", "fsdp"), None)
    expert_placed = P("section", None, ("ctx", "fsdp"), None)
    dense_all = (dense_placed,) * 4
    expert_all = (expert_placed,) * 3
    layer_placed = (gain_placed,) + dense_all + (gain_placed,) + expert_all
    return jax.shard_map(
        body,
        mesh=mesh,
        in_specs=(rows_placed, P(), kept_placed, kept_placed) + layer_placed + (rows_placed,),
        out_specs=(kept_placed, kept_placed) + layer_placed,
        check_vma=False,
    )
```

```python
import functools

import jax
import jax.numpy as jnp
from jax import lax
from jax.experimental import pallas as pl
from jax.experimental.pallas import tpu as pltpu
from jax.sharding import PartitionSpec as P

QH = 12
KVH = 2
HD = 128
GROUP = QH // KVH
TOP = 4
EXPERTS = 8
bf16 = jnp.bfloat16
f32 = jnp.float32


epsilon = 1e-06
masked_out = -1e30
gap = 256


def swap(value, axis, bit):
    count = lax.axis_size(axis)
    return lax.ppermute(value, axis, [(source, source ^ bit) for source in range(count)])


def tie(*values):
    return lax.optimization_barrier(values)


def after(value, earlier):
    return tie(value, earlier)[0]


def at(value, index, axis=0):
    return lax.dynamic_index_in_dim(value, index, axis, keepdims=False)


def dot(spec, left, right, kind=f32):
    return jnp.einsum(spec, left, right, preferred_element_type=kind)


def cost(micros):
    return pl.CostEstimate(
        flops=int(micros * 1e9), bytes_accessed=int(micros * 3e6), transcendentals=0
    )


def kernel_params():
    return pltpu.CompilerParams(vmem_limit_bytes=56 * 1024 * 1024)


def nt(left, right):
    return lax.dot_general(left, right, (((1,), (1,)), ((), ())), preferred_element_type=f32)


def nn(left, right):
    return jnp.dot(left, right, preferred_element_type=f32)


def head_rows(ref):
    return jnp.concatenate([ref[:, i * HD : (i + 1) * HD] for i in range(GROUP)], axis=0)


def softmax_rows(ids_ref, queries, keys, half, own):
    scores = nt(queries, keys) * HD ** (-0.5)
    tall, wide = scores.shape
    row = lax.broadcasted_iota(jnp.int32, (half, 1), 0)
    row = jnp.concatenate([row] * (tall // half), axis=0) + ids_ref[own] * half
    lane = lax.broadcasted_iota(jnp.int32, (1, half), 1)
    column = [lane + ids_ref[block] * half for block in range(wide // half)]
    column = jnp.concatenate(column, axis=1)
    scores = jnp.where(row >= column, scores, masked_out)
    shifted = jnp.exp(scores - jnp.max(scores, axis=1, keepdims=True))
    return shifted / jnp.sum(shifted, axis=1, keepdims=True)


def attend_kernel(ids_ref, query_ref, key_ref, value_ref, out_ref):
    half = query_ref.shape[0]
    probs = softmax_rows(ids_ref, head_rows(query_ref), key_ref[...], half, pl.program_id(1))
    out = nn(probs.astype(bf16), value_ref[...]).astype(bf16)
    for i in range(GROUP):
        out_ref[:, i * HD : (i + 1) * HD] = out[i * half : (i + 1) * half]


def attend_specs(rows, seq_len):
    half = rows // 2
    by_head = pl.BlockSpec((half, GROUP * HD), lambda g, h, ids: (h, g))
    keys = pl.BlockSpec((seq_len, HD), lambda g, h, ids: (0, g))
    values = pl.BlockSpec((seq_len, HD), lambda g, h, ids: (0, KVH + g))
    return by_head, keys, values


def attend_call(ids, queries, key_value):
    rows, seq_len = (queries.shape[0], key_value.shape[0])
    by_head, keys, values = attend_specs(rows, seq_len)
    return pl.pallas_call(
        attend_kernel,
        grid_spec=pltpu.PrefetchScalarGridSpec(
            num_scalar_prefetch=1,
            grid=(KVH, 2),
            in_specs=[by_head, keys, values],
            out_specs=by_head,
        ),
        out_shape=jax.ShapeDtypeStruct((rows, QH * HD), bf16),
        compiler_params=kernel_params(),
        cost_estimate=cost(1),
        name="attend",
    )(ids, queries, key_value, key_value)


def attend_back_kernel(ids_ref, query_ref, key_ref, value_ref, cot_ref, dq_ref, *refs):
    out, (dk_ref, dv_ref) = (refs[:-2], refs[-2:])
    half = query_ref.shape[0]
    group, own = (pl.program_id(0), pl.program_id(1))
    queries, cot = (head_rows(query_ref), head_rows(cot_ref))
    probs = softmax_rows(ids_ref, queries, key_ref[...], half, own)
    d_probs = nt(cot, value_ref[...])
    inner = jnp.sum(probs * d_probs, axis=1, keepdims=True)
    d_scores = (probs * (d_probs - inner)).astype(bf16)
    d_queries = (nn(d_scores, key_ref[...]) * HD ** (-0.5)).astype(bf16)
    for i in range(GROUP):
        dq_ref[:, i * HD : (i + 1) * HD] = d_queries[i * half : (i + 1) * half]
    d_keys = nn(d_scores.T, queries) * HD ** (-0.5)
    d_values = nn(probs.astype(bf16).T, cot)

    @pl.when(own == 0)
    def _():
        dk_ref[...] = d_keys
        dv_ref[...] = d_values

    @pl.when(own != 0)
    def _():
        rows = 2 * half
        for block, ref in enumerate(out):
            part = slice(block * rows, (block + 1) * rows)
            for first, total, last in ((0, dk_ref, d_keys), (KVH * HD, dv_ref, d_values)):
                columns = pl.ds(pl.multiple_of(first + group * HD, HD), HD)
                ref[:, columns] = (total[part, :] + last[part]).astype(bf16)


def attend_back_call(ids, queries, key_value, cot):
    rows, seq_len = (queries.shape[0], key_value.shape[0])
    by_head, keys, values = attend_specs(rows, seq_len)
    blocks = seq_len // rows
    wide = 2 * KVH * HD
    result = pl.pallas_call(
        attend_back_kernel,
        grid_spec=pltpu.PrefetchScalarGridSpec(
            num_scalar_prefetch=1,
            grid=(KVH, 2),
            in_specs=[by_head, keys, values, by_head],
            out_specs=[by_head] + [pl.BlockSpec((rows, wide), lambda g, h, ids: (0, 0))] * blocks,
            scratch_shapes=[pltpu.VMEM((seq_len, HD), f32)] * 2,
        ),
        out_shape=[jax.ShapeDtypeStruct((rows, QH * HD), bf16)]
        + [jax.ShapeDtypeStruct((rows, wide), bf16)] * blocks,
        compiler_params=kernel_params(),
        cost_estimate=cost(1),
        name="attend_back",
    )(ids, queries, key_value, key_value, cot)
    return (result[0], result[1:])


def gelu_parts(gate):
    root = 0.7978845608028654
    inner = root * (gate + 0.044715 * gate * gate * gate)
    bent = jnp.tanh(inner)
    value = 0.5 * gate * (1.0 + bent)
    slope = root * (1.0 + 3.0 * 0.044715 * gate * gate)
    return value, 0.5 * (1.0 + bent) + 0.5 * gate * (1.0 - bent * bent) * slope


def give_back(pick_ref, total_ref, share_ref, before, out):
    blocks, capacity, _ = pick_ref.shape
    for d in range(blocks):
        part = total_ref[d * capacity : (d + 1) * capacity, :]
        if share_ref is not None:
            part = part * share_ref[d]
        back = nn(pick_ref[d].T, part.astype(bf16))
        if before:
            back = back + before[d][...]
        out[d][...] = back.astype(out[d].dtype)


def flat(ref):
    value = ref[...]
    return value.reshape(-1, value.shape[-1])


def add_up(total_ref, part, step):
    @pl.when(step == 0)
    def _():
        total_ref[...] = part

    @pl.when(step != 0)
    def _():
        total_ref[...] += part


def expert_kernel(blocks, adds, pick_ref, share_ref, gate_ref, up_ref, down_ref, *refs):
    rows, refs = (refs[:blocks], refs[blocks:])
    before, refs = (refs[: blocks * adds], refs[blocks * adds :])
    out, (picked_ref, gate_pre_ref, up_pre_ref, total_ref) = (refs[:blocks], refs[blocks:])
    step = pl.program_id(0)
    capacity = pick_ref.shape[1]

    @pl.when(step == 0)
    def _():
        for d in range(blocks):
            block = nn(pick_ref[d], rows[d][...]).astype(bf16)
            picked_ref[d * capacity : (d + 1) * capacity, :] = block

    gate_pre = nn(picked_ref[...], flat(gate_ref))
    up_pre = nn(picked_ref[...], flat(up_ref))
    gate_pre_ref[...] = gate_pre
    up_pre_ref[...] = up_pre
    active = (gelu_parts(gate_pre)[0] * up_pre).astype(bf16)
    add_up(total_ref, nn(active, flat(down_ref)), step)

    @pl.when(step == pl.num_programs(0) - 1)
    def _():
        give_back(pick_ref, total_ref, share_ref, before, out)


def whole_spec(shape):
    return pl.BlockSpec(
        shape, lambda step: (0,) * len(shape), pipeline_mode=pl.Buffered(buffer_count=1)
    )


def weight_operands(weights, deep, cut):
    if len(weights) == 1:
        unit = weights[0]
        shards, tall, width = unit.shape
        specs = [
            pl.BlockSpec((shards, deep, cut), lambda step: (0, 0, 2 * step)),
            pl.BlockSpec((shards, deep, cut), lambda step: (0, 0, 2 * step + 1)),
            pl.BlockSpec(
                (shards // 2, tall - deep, width), lambda step: (step, deep // (tall - deep), 0)
            ),
        ]
        return specs, [unit, unit, unit]
    pair, down = weights
    specs = [
        pl.BlockSpec((pair.shape[0], cut), lambda step: (0, 2 * step)),
        pl.BlockSpec((pair.shape[0], cut), lambda step: (0, 2 * step + 1)),
        pl.BlockSpec((cut, down.shape[1]), lambda step: (step, 0)),
    ]
    return specs, [pair, pair, down]


def expert_call(picks, shares, rows, weights, deep, hidden, before, micros):
    blocks, capacity, _ = picks.shape
    width, cut, tall = (rows[0].shape[1], hidden // 2, blocks * capacity)
    columns = pl.BlockSpec((tall, cut), lambda step: (0, step))
    row_specs = [whole_spec(block.shape) for block in rows]
    specs, operands = weight_operands(weights, deep, cut)
    result = pl.pallas_call(
        functools.partial(expert_kernel, blocks, 1 if before else 0),
        grid=(2,),
        in_specs=[whole_spec(picks.shape), whole_spec(shares.shape)]
        + specs
        + row_specs * (2 if before else 1),
        out_specs=row_specs + [whole_spec((tall, width)), columns, columns],
        out_shape=[jax.ShapeDtypeStruct(block.shape, bf16) for block in rows]
        + [
            jax.ShapeDtypeStruct((tall, width), bf16),
            jax.ShapeDtypeStruct((tall, hidden), f32),
            jax.ShapeDtypeStruct((tall, hidden), f32),
        ],
        scratch_shapes=[pltpu.VMEM((tall, width), f32)],
        compiler_params=kernel_params(),
        cost_estimate=cost(micros),
        name="expert",
    )(picks, shares, *operands, *rows, *before)
    return (list(result[:blocks]), list(result[blocks:]))


def expert_back_kernel(
    blocks, adds, pick_ref, share_ref, gate_pre_ref, up_pre_ref, gate_ref, up_ref, down_ref, *refs
):
    rows, refs = (refs[:blocks], refs[blocks:])
    before, refs = (refs[: blocks * adds], refs[blocks * adds :])
    out, refs = (refs[:blocks], refs[blocks:])
    slots_ref, d_gate_ref, d_up_ref, active_ref, total_ref = refs
    step = pl.program_id(0)
    capacity = pick_ref.shape[1]

    @pl.when(step == 0)
    def _():
        for d in range(blocks):
            block = nn(pick_ref[d], rows[d][...]) * share_ref[d]
            slots_ref[d * capacity : (d + 1) * capacity, :] = block.astype(bf16)

    d_active = nt(slots_ref[...], flat(down_ref))
    value, slope = gelu_parts(gate_pre_ref[...])
    up_pre = up_pre_ref[...]
    d_gate = (d_active * up_pre * slope).astype(bf16)
    d_up = (d_active * value).astype(bf16)
    active_ref[...] = (value * up_pre).astype(bf16)
    d_gate_ref[...] = d_gate
    d_up_ref[...] = d_up
    add_up(total_ref, nt(d_gate, flat(gate_ref)) + nt(d_up, flat(up_ref)), step)

    @pl.when(step == pl.num_programs(0) - 1)
    def _():
        give_back(pick_ref, total_ref, None, before, out)


def expert_back_call(picks, shares, rows, kept, weights, deep, before, micros):
    _, gate_pre, up_pre = kept
    blocks, capacity, _ = picks.shape
    width, (tall, hidden) = (rows[0].shape[1], gate_pre.shape)
    cut = hidden // 2
    columns = pl.BlockSpec((tall, cut), lambda step: (0, step))
    row_specs = [whole_spec(block.shape) for block in rows]
    specs, operands = weight_operands(weights, deep, cut)
    result = pl.pallas_call(
        functools.partial(expert_back_kernel, blocks, 1 if before else 0),
        grid=(2,),
        in_specs=[whole_spec(picks.shape), whole_spec(shares.shape), columns, columns]
        + specs
        + row_specs * (2 if before else 1),
        out_specs=row_specs + [whole_spec((tall, width)), columns, columns, columns],
        out_shape=[jax.ShapeDtypeStruct(block.shape, bf16) for block in rows]
        + [jax.ShapeDtypeStruct((tall, width), bf16)]
        + [jax.ShapeDtypeStruct((tall, hidden), bf16)] * 3,
        scratch_shapes=[pltpu.VMEM((tall, width), f32)],
        compiler_params=kernel_params(),
        cost_estimate=cost(micros),
        name="expert_back",
    )(picks, shares, gate_pre, up_pre, *operands, *rows, *before)
    return (list(result[:blocks]), list(result[blocks:]))


def expert_grads_kernel(parts, deep, *refs):
    picked, slots, d_gate, d_up, active = (refs[i * parts : (i + 1) * parts] for i in range(5))
    grad_refs, turned_ref = (refs[5 * parts : -1], refs[-1])
    step = pl.program_id(0)

    def below(some):
        return jnp.concatenate([ref[...] for ref in some], axis=0)

    @pl.when(step == 0)
    def _():
        turned_ref[...] = below(picked).T

    grad_gate = nn(turned_ref[...], below(d_gate)).astype(bf16)
    grad_up = nn(turned_ref[...], below(d_up)).astype(bf16)
    grad_down = nn(below(active).T, below(slots)).astype(bf16)
    cut = grad_gate.shape[1]
    if len(grad_refs) == 1:
        unit_ref = grad_refs[0]
        shards, tall, width = unit_ref.shape
        for side in range(2):

            @pl.when(step == side)
            def _():
                left, some = (2 * side * cut, shards // 2)
                unit_ref[:, :deep, left : left + cut] = grad_gate.reshape(shards, deep, cut)
                left = left + cut
                unit_ref[:, :deep, left : left + cut] = grad_up.reshape(shards, deep, cut)
                rest = grad_down.reshape(some, tall - deep, width)
                unit_ref[side * some : (side + 1) * some, deep:, :] = rest
    else:
        grad_refs[0][:, :cut] = grad_gate
        grad_refs[0][:, cut:] = grad_up
        grad_refs[1][...] = grad_down


def expert_grads_call(picked, saved, weights, deep):
    slots, d_gate, d_up, active = zip(*saved)
    width, hidden = (picked[0].shape[1], d_gate[0].shape[1])
    cut = hidden // 2
    columns = [pl.BlockSpec((part.shape[0], cut), lambda step: (0, step)) for part in picked]
    if len(weights) == 1:
        grad_specs = [whole_spec(weights[0].shape)]
    else:
        grad_specs = [
            pl.BlockSpec((width, 2 * cut), lambda step: (0, step)),
            pl.BlockSpec((cut, width), lambda step: (step, 0)),
        ]
    return list(
        pl.pallas_call(
            functools.partial(expert_grads_kernel, len(picked), deep),
            grid=(2,),
            in_specs=[whole_spec(part.shape) for part in picked] * 2 + columns * 3,
            out_specs=grad_specs,
            out_shape=[jax.ShapeDtypeStruct(part.shape, bf16) for part in weights],
            scratch_shapes=[pltpu.VMEM((width, sum(part.shape[0] for part in picked)), bf16)],
            compiler_params=kernel_params(),
            cost_estimate=cost(1),
            name="expert_grads",
        )(*picked, *slots, *d_gate, *d_up, *active)
    )


def norm_parts(value):
    scale = lax.rsqrt(jnp.mean(value * value, axis=1, keepdims=True) + epsilon)
    return scale, value * scale


def norm_back(grad, gain, value):
    scale, scaled = norm_parts(value)
    grown = grad * gain
    back = scale * (grown - scaled * jnp.mean(scaled * grown, axis=1, keepdims=True))
    return back, (grad * scaled).astype(bf16)


def add_all(refs):
    total = refs[0][...].astype(f32)
    for ref in refs[1:]:
        total = total + ref[...].astype(f32)
    return total


def side_offsets(core_ref, steps, cut):
    step, core = (pl.program_id(0), core_ref[0])
    own = pl.multiple_of((core * steps + step) * cut, cut)
    other = pl.multiple_of(((1 - core) * steps + step) * cut, cut)
    return own, other


def dense_call(kernel, core, steps, whole, halves, out, scratch, name, micros):
    cut = halves[0].shape[1] // steps

    def keep(shape):
        return pl.BlockSpec(
            shape, lambda step, core: (0,) * len(shape), pipeline_mode=pl.Buffered(buffer_count=1)
        )

    def tile(tall):
        return pl.BlockSpec((tall, cut), lambda step, core: (0, step))

    return pl.pallas_call(
        kernel,
        grid_spec=pltpu.PrefetchScalarGridSpec(
            num_scalar_prefetch=1,
            grid=(steps,),
            in_specs=[keep(part.shape) for part in whole] + [tile(halves[0].shape[0])] * 2,
            out_specs=[
                tile(part.shape[0]) if tiled else keep(part.shape) for part, tiled in out
            ],
            scratch_shapes=scratch,
        ),
        out_shape=[part for part, _ in out],
        compiler_params=kernel_params(),
        cost_estimate=cost(micros),
        name=name,
    )(core.astype(jnp.int32).reshape(1), *whole, *halves)


def shape_of(kind, *shape):
    return jax.ShapeDtypeStruct(shape, kind)


def enter_kernel(steps, terms, core_ref, gain_ref, *refs):
    parts, (own_ref, other_ref, sent_ref, normed_ref, out_ref) = (refs[:terms], refs[terms:])
    own, other = side_offsets(core_ref, steps, own_ref.shape[1])

    @pl.when(pl.program_id(0) == 0)
    def _():
        sent = add_all(parts).astype(bf16)
        sent_ref[...] = sent
        normed_ref[...] = (norm_parts(sent.astype(f32))[1] * gain_ref[...]).astype(bf16)

    cut = own_ref.shape[1]
    out_ref[:, pl.ds(own, cut)] = nn(normed_ref[...], own_ref[...]).astype(bf16)
    out_ref[:, pl.ds(other, cut)] = nn(normed_ref[...], other_ref[...]).astype(bf16)


def enter_call(core, parts, gain, halves):
    rows, width = parts[0].shape
    return dense_call(
        functools.partial(enter_kernel, 3, len(parts)),
        core,
        3,
        [gain] + parts,
        halves,
        [
            (shape_of(bf16, rows, width), False),
            (shape_of(bf16, rows, width), False),
            (shape_of(bf16, rows, 2 * halves[0].shape[1]), False),
        ],
        [],
        "enter",
        6,
    )


def leave_kernel(steps, core_ref, gain_ref, rows_ref, attended_ref, own_ref, other_ref,
                 mid_ref, normed_ref):
    cut = own_ref.shape[1]
    for start, ref in zip(side_offsets(core_ref, steps, cut), (own_ref, other_ref)):
        part = pl.ds(start, cut)
        mid_ref[:, part] = rows_ref[:, part].astype(f32) + nn(attended_ref[...], ref[...])

    @pl.when(pl.program_id(0) == steps - 1)
    def _():
        normed_ref[...] = (norm_parts(mid_ref[...])[1] * gain_ref[...]).astype(bf16)


def leave_call(core, rows_in, attended, gain, halves):
    rows, width = rows_in.shape
    return dense_call(
        functools.partial(leave_kernel, 2),
        core,
        2,
        [gain, rows_in, attended],
        halves,
        [(shape_of(f32, rows, width), False), (shape_of(bf16, rows, width), False)],
        [],
        "leave",
        5,
    )


def leave_back_kernel(steps, terms, core_ref, gain_ref, mid_ref, cot_ref, attended_ref, *refs):
    parts, refs = (refs[:terms], refs[terms:])
    own_ref, other_ref, after_ref, term_ref, d_attended_ref, *refs = refs
    own_grad_ref, other_grad_ref, branch_ref, turned_ref, total_ref = refs
    step, cut = (pl.program_id(0), own_ref.shape[1])

    @pl.when(step == 0)
    def _():
        back, term_ref[...] = norm_back(add_all(parts), gain_ref[...], mid_ref[...])
        back = back + cot_ref[...].astype(f32)
        after_ref[...] = back
        branch_ref[...] = back.astype(bf16)
        turned_ref[...] = attended_ref[...].T

    own, other = side_offsets(core_ref, steps, cut)
    d_own, d_other = (branch_ref[:, pl.ds(own, cut)], branch_ref[:, pl.ds(other, cut)])
    own_grad_ref[...] = nn(turned_ref[...], d_own).astype(bf16)
    other_grad_ref[...] = nn(turned_ref[...], d_other).astype(bf16)
    add_up(total_ref, nt(d_own, own_ref[...]) + nt(d_other, other_ref[...]), step)

    @pl.when(step == steps - 1)
    def _():
        d_attended_ref[...] = total_ref[...].astype(bf16)


def leave_back_call(core, parts, gain, mid, cotangent, attended, halves):
    rows, width = mid.shape
    half = (halves[0].shape[0], halves[0].shape[1])
    return dense_call(
        functools.partial(leave_back_kernel, 2, len(parts)),
        core,
        2,
        [gain, mid, cotangent, attended] + parts,
        halves,
        [
            (shape_of(f32, rows, width), False),
            (shape_of(bf16, rows, width), False),
            (shape_of(bf16, rows, width), False),
            (shape_of(bf16, *half), True),
            (shape_of(bf16, *half), True),
        ],
        [
            pltpu.VMEM((rows, width), bf16),
            pltpu.VMEM((width, rows), bf16),
            pltpu.VMEM((rows, width), f32),
        ],
        "leave_back",
        8,
    )


def enter_back_kernel(steps, terms, core_ref, gain_ref, rows_ref, normed_ref, after_ref, term_ref,
                      dq_ref, *refs):
    parts, refs = (refs[:terms], refs[terms:])
    own_ref, other_ref, entry_ref, sent_ref, own_grad_ref, other_grad_ref, *refs = refs
    entered_ref, turned_ref, total_ref = refs
    step, cut = (pl.program_id(0), own_ref.shape[1])
    rows, qw = dq_ref.shape

    @pl.when(step == 0)
    def _():
        entered_ref[:, :qw] = dq_ref[...]
        wide = parts[0].shape[1]
        entered_ref[:, qw : qw + wide] = add_all(parts).astype(bf16)
        entered_ref[:, qw + wide :] = jnp.zeros((rows, gap), bf16)
        turned_ref[...] = normed_ref[...].T

    own, other = side_offsets(core_ref, steps, cut)
    d_own, d_other = (entered_ref[:, pl.ds(own, cut)], entered_ref[:, pl.ds(other, cut)])
    own_grad_ref[...] = nn(turned_ref[...], d_own).astype(bf16)
    other_grad_ref[...] = nn(turned_ref[...], d_other).astype(bf16)
    add_up(total_ref, nt(d_own, own_ref[...]) + nt(d_other, other_ref[...]), step)

    @pl.when(step == steps - 1)
    def _():
        back, attn_term = norm_back(total_ref[...], gain_ref[...], rows_ref[...].astype(f32))
        back = back + after_ref[...]
        entry_ref[...] = back
        sent_ref[...] = back.astype(bf16)
        lane = lax.broadcasted_iota(jnp.int32, (rows, 128), 1)
        sums = nn(attn_term.T, (lane == 0).astype(bf16))
        sums = (sums + nn(term_ref[...].T, (lane == 1).astype(bf16))).astype(bf16)
        left = cut - gap

        @pl.when(core_ref[0] == 0)
        def _():
            other_grad_ref[:, left : left + 128] = sums

        @pl.when(core_ref[0] != 0)
        def _():
            own_grad_ref[:, left : left + 128] = sums


def enter_back_call(core, dq, parts, gain, rows_in, normed, after, term, halves):
    rows, width = rows_in.shape
    return dense_call(
        functools.partial(enter_back_kernel, 3, len(parts)),
        core,
        3,
        [gain, rows_in, normed, after, term, dq] + parts,
        halves,
        [
            (shape_of(f32, rows, width), False),
            (shape_of(bf16, rows, width), False),
            (shape_of(bf16, *halves[0].shape), True),
            (shape_of(bf16, *halves[0].shape), True),
        ],
        [
            pltpu.VMEM((rows, 2 * halves[0].shape[1]), bf16),
            pltpu.VMEM((width, rows), bf16),
            pltpu.VMEM((rows, width), f32),
        ],
        "enter_back",
        1,
    )


def place_kernel(count, joined, index_ref, *refs):
    step = pl.program_id(0)
    for bit in range(count):

        @pl.when(step == bit)
        def _():
            if joined:
                refs[count][...] = refs[bit][...]
            else:
                refs[count][0] = refs[bit][...]


def place_call(blocks, index):
    count = len(blocks)
    shape = blocks[0].shape
    zeros = (0,) * len(shape)
    joined = len(shape) == 2 and shape[0] % 16 == 0
    if joined:
        out_spec = pl.BlockSpec(shape, lambda step, at: (at[0] ^ step, 0))
        out_shape = (count * shape[0], shape[1])
    else:
        out_spec = pl.BlockSpec((1,) + shape, lambda step, at: (at[0] ^ step,) + zeros)
        out_shape = (count,) + shape
    return pl.pallas_call(
        functools.partial(place_kernel, count, joined),
        grid_spec=pltpu.PrefetchScalarGridSpec(
            num_scalar_prefetch=1,
            grid=(count,),
            in_specs=[pl.BlockSpec(shape, lambda step, at: zeros)] * count,
            out_specs=out_spec,
        ),
        out_shape=jax.ShapeDtypeStruct(out_shape, blocks[0].dtype),
        compiler_params=kernel_params(),
        cost_estimate=cost(2),
        name="place",
    )(index.astype(jnp.int32).reshape(1), *blocks)


def deal_kernel(count, index_ref, *refs):
    step = pl.program_id(0)
    for bit in range(count):

        @pl.when(step == bit)
        def _():
            for layer, ref in enumerate(refs[count:]):
                ref[0] = refs[bit][layer]


def deal_call(blocks, index):
    count = len(blocks)
    layers, *shape = blocks[0].shape
    shape = tuple(shape)
    zeros = (0,) * len(shape)
    return pl.pallas_call(
        functools.partial(deal_kernel, count),
        grid_spec=pltpu.PrefetchScalarGridSpec(
            num_scalar_prefetch=1,
            grid=(count,),
            in_specs=[pl.BlockSpec((layers,) + shape, lambda step, at: (0,) + zeros)] * count,
            out_specs=[pl.BlockSpec((1,) + shape, lambda step, at: (at[0] ^ step,) + zeros)]
            * layers,
        ),
        out_shape=[jax.ShapeDtypeStruct((count,) + shape, blocks[0].dtype)] * layers,
        compiler_params=kernel_params(),
        cost_estimate=cost(2),
        name="deal",
    )(index.astype(jnp.int32).reshape(1), *blocks)


def order_kernel(count, order_ref, *refs):
    step = pl.program_id(0)
    for i in range(count):

        @pl.when(step == i)
        def _():
            refs[count][:, 0] = refs[i][:, 0]


def order_call(blocks, order, unit):
    count = len(blocks)
    n_ctx, _, tall, wide = blocks[0].shape
    shape = (n_ctx, 1, tall, wide)
    source = pl.BlockSpec(
        shape, lambda step, at: (0, unit, 0, 0), pipeline_mode=pl.Buffered(buffer_count=1)
    )
    result = pl.pallas_call(
        functools.partial(order_kernel, count),
        grid_spec=pltpu.PrefetchScalarGridSpec(
            num_scalar_prefetch=1,
            grid=(count,),
            in_specs=[source] * count,
            out_specs=pl.BlockSpec(shape, lambda step, at: (0, at[step], 0, 0)),
        ),
        out_shape=jax.ShapeDtypeStruct((n_ctx, count, tall, wide), bf16),
        compiler_params=kernel_params(),
        cost_estimate=cost(4),
        name="order",
    )(order.astype(jnp.int32), *blocks)
    return result.reshape(n_ctx * count, tall, wide)


def finish_kernel(deep, index_ref, own_ref, other_ref, gate_ref, up_ref, down_ref):
    side = pl.program_id(1)
    wide = gate_ref.shape[2] // 2

    def write(source):
        for half in range(2):
            left, target = (2 * half * wide, slice(half * wide, (half + 1) * wide))
            gate_ref[:, :, target] = source[0, :, :deep, left : left + wide].astype(f32)
            left = left + wide
            up_ref[:, :, target] = source[0, :, :deep, left : left + wide].astype(f32)
        down_ref[...] = source[0, :, deep:, :].astype(f32)

    @pl.when(side == index_ref[1])
    def _():
        write(own_ref)

    @pl.when(side != index_ref[1])
    def _():
        write(other_ref)


def finish_call(own, other, deep, hidden, place, core):
    n_ctx, units, tall, width = own.shape
    experts = 2 * n_ctx * units
    source = pl.BlockSpec((1, units, tall, width), lambda bit, side, at: (bit, 0, 0, 0))
    target = lambda bit, side, at: (2 * (at[0] ^ bit) + side, 0, 0)
    return pl.pallas_call(
        functools.partial(finish_kernel, deep),
        grid_spec=pltpu.PrefetchScalarGridSpec(
            num_scalar_prefetch=1,
            grid=(n_ctx, 2),
            in_specs=[source, source],
            out_specs=[
                pl.BlockSpec((units, deep, hidden), target),
                pl.BlockSpec((units, deep, hidden), target),
                pl.BlockSpec((units, tall - deep, width), target),
            ],
        ),
        out_shape=[
            jax.ShapeDtypeStruct((experts, deep, hidden), f32),
            jax.ShapeDtypeStruct((experts, deep, hidden), f32),
            jax.ShapeDtypeStruct((experts, tall - deep, width), f32),
        ],
        compiler_params=kernel_params(),
        cost_estimate=cost(8),
        name="finish",
    )(jnp.stack([place, core]).astype(jnp.int32), own, other)


def body(
    tokens,
    block_of,
    routes,
    combine,
    attn_norm,
    w_query,
    w_key,
    w_value,
    w_out,
    ffn_norm,
    w_gate,
    w_up,
    w_down,
    out_grad,
):
    rows = tokens.shape[2]
    width = tokens.shape[3]
    half = rows // 2
    n_ctx = lax.axis_size("ctx")
    n_fsdp = lax.axis_size("fsdp")
    core, place, depth = (
        lax.axis_index(axis).astype(jnp.uint32) for axis in ("section", "ctx", "fsdp")
    )
    seq_len = rows * n_ctx
    capacity = rows * TOP * 5 // (4 * EXPERTS)
    score_scale = HD ** (-0.5)
    own_experts = EXPERTS // n_ctx
    hidden = w_gate.shape[3]
    shard_rows = w_query.shape[1]
    down_rows = w_down.shape[2]
    qw = w_query.shape[2]
    kw = w_key.shape[2]
    pieces = max(1, 2 * n_ctx // EXPERTS)
    per_core = max(1, EXPERTS // (2 * n_ctx))
    unit_rows = shard_rows + down_rows
    aligned = shard_rows % 16 == 0 and down_rows % 16 == 0

    def on_core(former, latter):
        return jnp.where(core == 0, former, latter)

    def own_other(low, high):
        return (on_core(low, high), on_core(high, low))

    early, late = (range(1, n_ctx // 2 + 1), range(n_ctx // 2 + 1, n_ctx))

    def send(value, bits):
        return [swap(value, "ctx", bit) for bit in bits]

    def spread(value):
        return [value] + send(value, early) + send(value, late)

    def spread_rows(value):
        near_blocks = send(value, early)
        value, near_blocks = tie(value, near_blocks)
        return [value] + near_blocks + send(value, late)

    def gather_back(blocks):
        return [blocks[0]] + [swap(blocks[bit], "ctx", bit) for bit in range(1, n_ctx)]

    info = jnp.concatenate([routes.astype(f32), combine], axis=-1)[0, :, 0].transpose(0, 2, 1)
    info_own, info_other = (at(info, core), swap(at(info, 1 - core), "section", 1))
    info = jnp.stack(own_other(info_own, info_other))
    info = jnp.stack([info] + [swap(info, "ctx", bit) for bit in range(1, n_ctx)], axis=1)

    gain_columns = jnp.stack([attn_norm[0], ffn_norm[0]], axis=1)
    gain_columns = jnp.pad(gain_columns, ((0, 0), (0, gap - 2)))
    enter_shard = jnp.concatenate([w_query[0], w_key[0], w_value[0], gain_columns], axis=1)
    enter_cut = enter_shard.shape[1] // 2
    leave_cut = w_out.shape[2] // 2
    low_shard = jnp.concatenate([enter_shard[:, :enter_cut], w_out[0, :, :leave_cut]], axis=1)
    high_shard = jnp.concatenate([enter_shard[:, enter_cut:], w_out[0, :, leave_cut:]], axis=1)
    lent = swap(on_core(high_shard, low_shard), "section", 1)
    dense_shards = (on_core(low_shard, lent), on_core(lent, high_shard))

    def gather_deep(shard):
        blocks = [shard] + [swap(shard, "fsdp", bit) for bit in range(1, n_fsdp)]
        return place_call(blocks, depth).reshape(-1, shard.shape[1])

    def join_square(blocks):
        return place_call(blocks, place).reshape(-1, blocks[0].shape[1])

    def gather_square(deep):
        return join_square(spread(deep))

    cut = hidden // 2
    unit_stack = jnp.concatenate(
        [
            jnp.concatenate(
                [w_gate[0, ..., :cut], w_up[0, ..., :cut], w_gate[0, ..., cut:], w_up[0, ..., cut:]],
                axis=2,
            ),
            w_down[0],
        ],
        axis=1,
    )
    if pieces == 2:
        unit_stack = jnp.stack(jnp.split(unit_stack, 2, axis=2), axis=1)
    unit_stack = unit_stack.reshape(n_ctx, 2, per_core, unit_rows, width // pieces)
    units_lent = swap(at(unit_stack, 1 - core, 1), "section", 1)
    unit_stacks = jnp.stack(own_other(at(unit_stack, core, 1), units_lent), axis=1)

    def deal_units(stack):
        blocks = [at(stack, place)]
        blocks += [swap(at(stack, place ^ bit), "ctx", bit) for bit in range(1, n_ctx)]
        return deal_call(blocks, place)

    ring = list(range(0, n_fsdp, 2)) + list(range(1, n_fsdp, 2))[::-1]
    ring_steps = [(ring[i], ring[(i + 1) % n_fsdp]) for i in range(n_fsdp)]
    ring_table = [[ring[ring.index(z) - i] for i in range(n_fsdp)] for z in range(n_fsdp)]
    behind_here = at(jnp.array(ring_table, jnp.uint32), depth)

    def ring_send(moved):
        return [blocks + [lax.ppermute(blocks[-1], "fsdp", ring_steps)] for blocks in moved]

    def own_units(blocks):
        return [order_call(blocks, behind_here, unit) for unit in range(per_core)]

    def pair_units(mine):
        other = [swap(part, "section", 1) for part in mine]
        units = list(mine) + other
        if pieces == 2:
            units = [jnp.concatenate(own_other(mine[0], other[0]), axis=2)]
        if aligned:
            return [[unit] for unit in units]
        return [
            [unit[:, :shard_rows].reshape(-1, width), unit[:, shard_rows:].reshape(-1, width)]
            for unit in units
        ]

    def cut_units(grads):
        if aligned:
            units = [unit for (unit,) in grads]
        else:
            units = [
                jnp.concatenate(
                    [part.reshape(n_ctx * n_fsdp, -1, width) for part in parts], axis=1
                )
                for parts in grads
            ]
        if pieces == 1:
            return (units[:per_core], units[per_core:])
        own, other = own_other(*jnp.split(units[0], 2, axis=2))
        return ([own], [other])

    def ring_part(terms, behind):
        spot = behind_here[behind % n_fsdp]
        return sum(at(term, spot, 1).astype(f32) for term in terms)

    def ring_start(own, received):
        terms = [part.reshape((n_ctx, n_fsdp) + part.shape[1:]) for part in (own, received)]
        return (terms, ring_part(terms, 1).astype(bf16))

    def ring_move(state):
        return [(terms, lax.ppermute(moving, "fsdp", ring_steps)) for terms, moving in state]

    def ring_add(state, step):
        return [
            (terms, (moved.astype(f32) + ring_part(terms, step + 1)).astype(bf16))
            for terms, moved in state
        ]

    def ring_step(state, step):
        return ring_add(ring_move(state), step)

    def ring_last(state):
        state = ring_add(state, 2)
        for step in range(3, n_fsdp - 1):
            state = ring_step(state, step)
        return ring_move(state)

    def ring_rest(state, first):
        for step in range(first, n_fsdp):
            state = ring_step(state, step)
        return [moving for _, moving in state]

    def scatter_units(moved):
        whole = jnp.stack(moved, axis=1)
        blocks = [at(whole, place)]
        blocks += [swap(at(whole, place ^ bit), "ctx", bit) for bit in range(1, n_ctx)]
        return jnp.stack(blocks)

    def trade_square(own, received, bits):
        own, received = (part.reshape(n_ctx, -1, part.shape[1]) for part in (own, received))

        def part(bit):
            return at(own, place ^ bit).astype(f32) + at(received, place ^ bit).astype(f32)

        return [part(bit) if bit == 0 else swap(part(bit).astype(bf16), "ctx", bit) for bit in bits]

    def sum_square(parts):
        return sum(part.astype(f32) for part in parts).astype(bf16)

    def send_deep(mine):
        mine = mine.reshape(n_fsdp, shard_rows, -1)
        parts = [swap(at(mine, depth ^ bit), "fsdp", bit) for bit in range(1, n_fsdp)]
        return [at(mine, depth)] + parts

    def reduce_deep(mine):
        return sum(part.astype(f32) for part in send_deep(mine))

    if pieces == 1:
        units_here = jnp.arange(per_core, dtype=jnp.uint32)
        units_here = jnp.concatenate(
            [core * per_core + units_here, (1 - core) * per_core + units_here]
        )
    else:
        units_here = jnp.zeros((1,), jnp.uint32)
    named = (place * own_experts + units_here).astype(f32)
    matches = info[:, None, :, :TOP] == named[None, :, None, None, None]
    hits = jnp.any(matches, axis=3)
    shares = jnp.sum(jnp.where(matches, info[:, None, :, TOP:], 0.0), axis=3)
    earlier = jnp.arange(rows)[:, None] < jnp.arange(rows)[None, :]
    rank = dot("ledr,rq->ledq", hits.astype(bf16), earlier.astype(bf16))
    slots = jnp.arange(capacity, dtype=f32)
    picks = hits[:, :, :, None, :] & (rank[:, :, :, None, :] == slots[:, None])
    slot_shares = jnp.sum(jnp.where(picks, shares[:, :, :, None, :], 0.0), axis=-1, keepdims=True)
    picks = picks.astype(bf16)

    order = place.astype(jnp.int32) ^ jnp.arange(n_ctx, dtype=jnp.int32)
    block_ids = jnp.take(block_of.reshape(n_ctx, 2), order, axis=0)
    block_ids = block_ids.reshape(-1)

    def gains_of(halves):
        pair = on_core(halves[1][:, -gap : 2 - gap], halves[0][:, -gap : 2 - gap])
        pair = pair.astype(f32).T
        return (pair[:1], pair[1:])

    near = 1 + len(early)
    parts = (slice(0, near), slice(near, n_ctx))

    def experts(layer, blocks, weights, answer, beside_near=tuple, beside_far=None):
        kept, arrived = ({}, [])
        back = {}
        for index, part in enumerate(parts):
            rows_here = blocks[part]
            if index:
                back[0], rows_here, found = tie(back[0], rows_here, beside_near())
                if answer:
                    arrived = [swap(block, "ctx", bit) for bit, block in zip(early, back[0][1:])]
            back[index] = []
            for j in range(own_experts):
                back[index], kept[index, j] = expert_call(
                    picks[layer, j, part],
                    slot_shares[layer, j, part],
                    rows_here,
                    weights[j],
                    shard_rows,
                    hidden,
                    back[index],
                    3 if index == 0 else 1,
                )
        if not answer:
            return (back[0] + back[1], kept)
        back[1], arrived, far = tie(back[1], arrived, beside_far(found))
        arrived += [swap(block, "ctx", bit) for bit, block in zip(late, back[1])]
        return (back[0][:1] + arrived, kept, found, far)

    def experts_back(layer, blocks, weights, kept, delay, beside_near, beside_far, beside_end):
        back, saved = ({}, {})
        for index, part in enumerate(parts):
            rows_here = blocks[part]
            if index:
                back[0], rows_here, found_near = tie(back[0], rows_here, beside_near())
                arrived = [swap(block, "ctx", bit) for bit, block in zip(early, back[0][1:])]
            back[index] = []
            for j in range(own_experts):
                back[index], saved[index, j] = expert_back_call(
                    picks[layer, j, part],
                    slot_shares[layer, j, part],
                    rows_here,
                    kept[index, j],
                    weights[j],
                    shard_rows,
                    back[index],
                    4 if index == 0 else 1,
                )
        back[1], arrived, saved, found_far = tie(back[1], arrived, saved, beside_far(found_near))
        arrived += [swap(block, "ctx", bit) for bit, block in zip(late, back[1])]

        def grads_of(j, saved):
            picked = [kept[index, j][0] for index in range(2)]
            both = [saved[index, j] for index in range(2)]
            return expert_grads_call(picked, both, weights[j], shard_rows)

        now = [j for j in reversed(range(own_experts)) if not delay or j >= per_core]
        grads = {j: grads_of(j, saved) for j in now}
        arrived, grads, found_end = tie(arrived, grads, beside_end(found_far))
        returned = back[0][:1] + arrived
        if len(now) == own_experts:
            own, other = cut_units([grads[j] for j in range(own_experts)])
            received = [swap(part, "section", 1) for part in other]
            return (returned, lambda earlier: (own, received), found_end)
        received = [swap(grads[j][0], "section", 1) for j in reversed(now)]

        def finish(earlier):
            ready = after(saved, earlier)
            return ([grads_of(j, ready)[0] for j in range(per_core)], received)

        return (returned, finish, found_end)

    def keep_own(first, second):
        other = swap(on_core(second, first), "section", 1)
        return own_other(on_core(first, second), other)

    dense_first, dense_second = dense_shards
    deep = gather_deep(jnp.concatenate([dense_first, dense_second[:, :enter_cut]], axis=1))
    dealt_first, dealt_second = deal_units(unit_stacks)
    deep, dealt_first, dealt_second, picks, dense_second = tie(
        deep, dealt_first, dealt_second, picks, dense_second
    )
    dense_blocks, moved, leave_shard, enter_shard = tie(
        spread(deep[:, :enter_cut]),
        ring_send([[dealt_first]]),
        deep[:, enter_cut : enter_cut + leave_cut],
        deep[:, enter_cut + leave_cut :],
    )
    leave_blocks = [leave_shard] + send(leave_shard, early)
    enter_own = join_square(dense_blocks)
    enter_first = (enter_own, swap(enter_own, "section", 1))

    first_gains = gains_of(enter_first)
    first_in = after(at(tokens, core)[0], slot_shares)
    _, first_normed, first_entered = enter_call(core, [first_in], first_gains[0], enter_first)
    first_entered, leave_blocks = tie(first_entered, leave_blocks)
    key_value = first_entered[:, qw : qw + 2 * kw]
    first_kv, leave_shard = tie(jnp.concatenate(spread(key_value)), leave_shard)
    first_attended = attend_call(block_ids, first_entered, first_kv)
    moved = ring_send(moved)
    first_attended, leave_blocks, dealt_second, moved, enter_shard, dense_second = tie(
        first_attended,
        leave_blocks + send(leave_shard, late),
        dealt_second,
        moved,
        enter_shard,
        dense_second,
    )
    enter_blocks = [enter_shard] + send(enter_shard, early)
    for _ in range(2, n_fsdp - 1):
        moved = ring_send(moved)
    leave_own = join_square(leave_blocks)
    leave_first = (leave_own, swap(leave_own, "section", 1))
    first_mid, ffn_normed = leave_call(core, first_in, first_attended, first_gains[1], leave_first)
    blocks = spread_rows(ffn_normed)
    blocks[:near], moved, dealt_second, enter_shard, leave_shard, enter_blocks = tie(
        blocks[:near], moved, dealt_second, enter_shard, dense_second[:, enter_cut:], enter_blocks
    )
    first_weights = pair_units(own_units(moved[0]))
    returned, first_kept, leave_shard, (enter_blocks, dealt_second) = experts(
        0,
        blocks,
        first_weights,
        True,
        lambda: gather_deep(leave_shard),
        lambda found: (enter_blocks + send(enter_shard, late), dealt_second),
    )
    moved = ring_send([[dealt_second]])
    returned, leave_shard = tie(returned, leave_shard)
    enter_own = join_square(enter_blocks)
    enter_second = (enter_own, swap(enter_own, "section", 1))
    leave_blocks = [leave_shard] + send(leave_shard, early)

    second_gains = gains_of(enter_second)
    second_in, second_normed, second_entered = enter_call(
        core, [first_mid] + returned, second_gains[0], enter_second
    )
    second_entered, leave_blocks, moved = tie(second_entered, leave_blocks, moved)
    moved = ring_send(moved)
    key_value = second_entered[:, qw : qw + 2 * kw]
    for _ in range(4, n_fsdp):
        moved = ring_send(moved)
    second_kv, leave_shard = tie(jnp.concatenate(spread(key_value)), leave_shard)
    second_attended = attend_call(block_ids, second_entered, second_kv)
    second_attended, leave_blocks, moved = tie(
        second_attended, leave_blocks + send(leave_shard, late), moved
    )
    moved = ring_send(moved)
    leave_own = join_square(leave_blocks)
    leave_second = (leave_own, swap(leave_own, "section", 1))
    second_mid, ffn_normed = leave_call(
        core, second_in, second_attended, second_gains[1], leave_second
    )
    blocks = spread_rows(ffn_normed)
    blocks[:near], moved = tie(blocks[:near], moved)
    second_weights = pair_units(own_units(moved[0]))
    second_returned, second_kept = experts(1, blocks, second_weights, False)
    cotangent = after(at(out_grad, core)[0], second_returned[:near])
    cot_blocks = spread_rows(cotangent)
    cot_blocks[:near], second_returned[near:] = tie(cot_blocks[:near], second_returned[near:])

    returned, finish, (second_returned, near_parts) = experts_back(
        1,
        cot_blocks,
        second_weights,
        second_kept,
        False,
        lambda: second_returned,
        lambda found: found,
        lambda found: (found, [swap(found[bit], "ctx", bit) for bit in early]),
    )
    far_parts = [swap(second_returned[bit], "ctx", bit) for bit in late]
    units_moving = [ring_start(*pair) for pair in zip(*finish(()))]
    after_rows, term, d_attended, *grads = leave_back_call(
        core,
        returned,
        second_gains[1],
        second_mid,
        cotangent,
        second_attended,
        leave_second,
    )
    leave_grads = (grads[0], swap(grads[1], "section", 1))
    d_queries, d_key_value = attend_back_call(block_ids, second_entered, second_kv, d_attended)
    d_queries, d_key_value, leave_grads, far_parts = tie(
        d_queries, d_key_value, leave_grads, far_parts
    )
    second_parts = second_returned[:1] + near_parts + far_parts
    second_out = second_mid + sum(part.astype(f32) for part in second_parts)
    d_key_value, units_moving = tie(gather_back(d_key_value), ring_move(units_moving))
    units_moving = ring_move(ring_add(units_moving, 1))
    leave_parts = trade_square(*leave_grads, range(n_ctx))
    second_entry, cotangent, *grads = enter_back_call(
        core,
        d_queries,
        d_key_value,
        second_gains[0],
        second_in,
        second_normed,
        after_rows,
        term,
        enter_second,
    )
    cotangent, grads, leave_parts, layer_rows = tie(
        cotangent, grads, leave_parts, (second_in, second_out.astype(bf16))
    )
    enter_grads = (grads[0], swap(grads[1], "section", 1))

    blocks = spread_rows(cotangent)
    blocks[:near], enter_grads, layer_rows = tie(blocks[:near], enter_grads, layer_rows)

    def dense_sums(parts):
        moving = [sum_square(some) for some in (parts, leave_parts)]
        return reduce_deep(jnp.concatenate(moving, axis=1))

    returned, finish, (units_moving, layer_outs, second_dense) = experts_back(
        0,
        blocks,
        first_weights,
        first_kept,
        False,
        lambda: (units_moving, trade_square(*enter_grads, [0, *early]), enter_grads),
        lambda found: (
            ring_last(found[0]),
            keep_own(*layer_rows),
            found[1] + trade_square(*found[2], late),
        ),
        lambda found: (found[0], found[1], dense_sums(found[2])),
    )
    second_moved = [moving for _, moving in ring_add(units_moving, n_fsdp - 1)]
    own, received = finish(())
    after_rows, term, d_attended, *grads = leave_back_call(
        core,
        returned,
        first_gains[1],
        first_mid,
        cotangent,
        first_attended,
        leave_first,
    )
    units_moving = [ring_start(*pair) for pair in zip(own, received)]
    leave_grads = (grads[0], swap(grads[1], "section", 1))
    d_queries, d_key_value = attend_back_call(block_ids, first_entered, first_kv, d_attended)
    d_queries, d_key_value, leave_grads = tie(d_queries, d_key_value, leave_grads)
    d_key_value, leave_grads = tie(gather_back(d_key_value), leave_grads)
    leave_parts = trade_square(*leave_grads, [0, *early])
    first_entry, _, *grads = enter_back_call(
        core,
        d_queries,
        d_key_value,
        first_gains[0],
        first_in,
        first_normed,
        after_rows,
        term,
        enter_first,
    )
    grads, leave_parts, leave_grads, units_moving, second_moved = tie(
        grads, leave_parts, leave_grads, ring_move(units_moving), second_moved
    )
    enter_grads, second_scattered = tie(
        (grads[0], swap(grads[1], "section", 1)), scatter_units(second_moved)
    )
    units_moving = after(ring_move(ring_add(units_moving, 1)), enter_grads)
    enter_parts, leave_parts, first_entry = tie(
        trade_square(*enter_grads, range(n_ctx)),
        leave_parts + trade_square(*leave_grads, late),
        first_entry,
    )
    first_moving = [sum_square(parts) for parts in (enter_parts, leave_parts)]
    first_dense, first_scattered = tie(
        send_deep(jnp.concatenate(first_moving, axis=1)),
        scatter_units(ring_rest(ring_add(units_moving, 2), 3)),
    )
    first_dense = sum(part.astype(f32) for part in first_dense)

    layer_out = jnp.stack(layer_outs)
    input_grads = jnp.stack(keep_own(first_entry, second_entry))
    low_dense, high_dense = keep_own(first_dense, second_dense)
    enter_grad = jnp.concatenate([low_dense[:, :enter_cut], high_dense[:, :enter_cut]], axis=1)
    grad_out = jnp.concatenate([low_dense[:, enter_cut:], high_dense[:, enter_cut:]], axis=1)
    grad_gains = enter_grad[:, qw + 2 * kw :]
    mine = on_core(first_scattered, second_scattered)
    other = swap(on_core(second_scattered, first_scattered), "section", 1)
    if aligned and pieces == 1:
        grad_gate, grad_up, grad_down = finish_call(mine, other, shard_rows, hidden, place, core)
    else:
        sides = [jnp.take(part, order, axis=0) for part in own_other(mine, other)]
        if pieces == 1:
            whole = jnp.stack(sides, axis=1).reshape(EXPERTS, unit_rows, width)
        else:
            whole = jnp.concatenate([side[:, 0] for side in sides], axis=2)
        pairs = whole[:, :shard_rows].astype(f32).reshape(EXPERTS, shard_rows, 2, 2, cut)
        grad_gate = pairs[:, :, :, 0].reshape(EXPERTS, shard_rows, hidden)
        grad_up = pairs[:, :, :, 1].reshape(EXPERTS, shard_rows, hidden)
        grad_down = whole[:, shard_rows:].astype(f32)
    return (
        layer_out[None, :, None],
        input_grads[None, :, None],
        grad_gains[:, 0][None],
        enter_grad[:, :qw][None],
        enter_grad[:, qw : qw + kw][None],
        enter_grad[:, qw + kw : qw + 2 * kw][None],
        grad_out[None],
        grad_gains[:, 1][None],
        grad_gate[None],
        grad_up[None],
        grad_down[None],
    )


def solution(mesh):
    rows_placed = P(None, "fsdp", "ctx", None)
    kept_placed = P("section", None, "fsdp", "ctx", None)
    gain_placed = P("section", ("ctx", "fsdp"))
    dense_placed = P("section", ("ctx", "fsdp"), None)
    expert_placed = P("section", None, ("ctx", "fsdp"), None)
    dense_all = (dense_placed,) * 4
    expert_all = (expert_placed,) * 3
    layer_placed = (gain_placed,) + dense_all + (gain_placed,) + expert_all
    return jax.shard_map(
        body,
        mesh=mesh,
        in_specs=(rows_placed, P(), kept_placed, kept_placed) + layer_placed + (rows_placed,),
        out_specs=(kept_placed, kept_placed) + layer_placed,
        check_vma=False,
    )
```

```python
import functools

import jax
import jax.numpy as jnp
from jax import lax
from jax.experimental import pallas as pl
from jax.experimental.pallas import tpu as pltpu
from jax.sharding import PartitionSpec as P

QH = 12
KVH = 2
HD = 128
GROUP = QH // KVH
TOP = 4
EXPERTS = 8
bf16 = jnp.bfloat16
f32 = jnp.float32


epsilon = 1e-06
masked_out = -1e30
gap = 256


def swap(value, axis, bit):
    count = lax.axis_size(axis)
    return lax.ppermute(value, axis, [(source, source ^ bit) for source in range(count)])


def tie(*values):
    return lax.optimization_barrier(values)


def after(value, earlier):
    return tie(value, earlier)[0]


def at(value, index, axis=0):
    return lax.dynamic_index_in_dim(value, index, axis, keepdims=False)


def dot(spec, left, right, kind=f32):
    return jnp.einsum(spec, left, right, preferred_element_type=kind)


def cost(micros):
    return pl.CostEstimate(
        flops=int(micros * 1e9), bytes_accessed=int(micros * 3e6), transcendentals=0
    )


def kernel_params():
    return pltpu.CompilerParams(vmem_limit_bytes=56 * 1024 * 1024)


def nt(left, right):
    return lax.dot_general(left, right, (((1,), (1,)), ((), ())), preferred_element_type=f32)


def nn(left, right):
    return jnp.dot(left, right, preferred_element_type=f32)


def head_rows(ref):
    return jnp.concatenate([ref[:, i * HD : (i + 1) * HD] for i in range(GROUP)], axis=0)


def softmax_rows(ids_ref, queries, keys, half, own):
    scores = nt(queries, keys) * HD ** (-0.5)
    tall, wide = scores.shape
    row = lax.broadcasted_iota(jnp.int32, (half, 1), 0)
    row = jnp.concatenate([row] * (tall // half), axis=0) + ids_ref[own] * half
    lane = lax.broadcasted_iota(jnp.int32, (1, half), 1)
    column = [lane + ids_ref[block] * half for block in range(wide // half)]
    column = jnp.concatenate(column, axis=1)
    scores = jnp.where(row >= column, scores, masked_out)
    shifted = jnp.exp(scores - jnp.max(scores, axis=1, keepdims=True))
    return shifted / jnp.sum(shifted, axis=1, keepdims=True)


def attend_kernel(ids_ref, query_ref, key_ref, value_ref, out_ref):
    half = query_ref.shape[0]
    probs = softmax_rows(ids_ref, head_rows(query_ref), key_ref[...], half, pl.program_id(1))
    out = nn(probs.astype(bf16), value_ref[...]).astype(bf16)
    for i in range(GROUP):
        out_ref[:, i * HD : (i + 1) * HD] = out[i * half : (i + 1) * half]


def attend_specs(rows, seq_len):
    half = rows // 2
    by_head = pl.BlockSpec((half, GROUP * HD), lambda g, h, ids: (h, g))
    keys = pl.BlockSpec((seq_len, HD), lambda g, h, ids: (0, g))
    values = pl.BlockSpec((seq_len, HD), lambda g, h, ids: (0, KVH + g))
    return by_head, keys, values


def attend_call(ids, queries, key_value):
    rows, seq_len = (queries.shape[0], key_value.shape[0])
    by_head, keys, values = attend_specs(rows, seq_len)
    return pl.pallas_call(
        attend_kernel,
        grid_spec=pltpu.PrefetchScalarGridSpec(
            num_scalar_prefetch=1,
            grid=(KVH, 2),
            in_specs=[by_head, keys, values],
            out_specs=by_head,
        ),
        out_shape=jax.ShapeDtypeStruct((rows, QH * HD), bf16),
        compiler_params=kernel_params(),
        cost_estimate=cost(1),
        name="attend",
    )(ids, queries, key_value, key_value)


def attend_back_kernel(ids_ref, query_ref, key_ref, value_ref, cot_ref, dq_ref, *refs):
    out, (dk_ref, dv_ref) = (refs[:-2], refs[-2:])
    half = query_ref.shape[0]
    group, own = (pl.program_id(0), pl.program_id(1))
    queries, cot = (head_rows(query_ref), head_rows(cot_ref))
    probs = softmax_rows(ids_ref, queries, key_ref[...], half, own)
    d_probs = nt(cot, value_ref[...])
    inner = jnp.sum(probs * d_probs, axis=1, keepdims=True)
    d_scores = (probs * (d_probs - inner)).astype(bf16)
    d_queries = (nn(d_scores, key_ref[...]) * HD ** (-0.5)).astype(bf16)
    for i in range(GROUP):
        dq_ref[:, i * HD : (i + 1) * HD] = d_queries[i * half : (i + 1) * half]
    d_keys = nn(d_scores.T, queries) * HD ** (-0.5)
    d_values = nn(probs.astype(bf16).T, cot)

    @pl.when(own == 0)
    def _():
        dk_ref[...] = d_keys
        dv_ref[...] = d_values

    @pl.when(own != 0)
    def _():
        rows = 2 * half
        for block, ref in enumerate(out):
            part = slice(block * rows, (block + 1) * rows)
            for first, total, last in ((0, dk_ref, d_keys), (KVH * HD, dv_ref, d_values)):
                columns = pl.ds(pl.multiple_of(first + group * HD, HD), HD)
                ref[:, columns] = (total[part, :] + last[part]).astype(bf16)


def attend_back_call(ids, queries, key_value, cot):
    rows, seq_len = (queries.shape[0], key_value.shape[0])
    by_head, keys, values = attend_specs(rows, seq_len)
    blocks = seq_len // rows
    wide = 2 * KVH * HD
    result = pl.pallas_call(
        attend_back_kernel,
        grid_spec=pltpu.PrefetchScalarGridSpec(
            num_scalar_prefetch=1,
            grid=(KVH, 2),
            in_specs=[by_head, keys, values, by_head],
            out_specs=[by_head] + [pl.BlockSpec((rows, wide), lambda g, h, ids: (0, 0))] * blocks,
            scratch_shapes=[pltpu.VMEM((seq_len, HD), f32)] * 2,
        ),
        out_shape=[jax.ShapeDtypeStruct((rows, QH * HD), bf16)]
        + [jax.ShapeDtypeStruct((rows, wide), bf16)] * blocks,
        compiler_params=kernel_params(),
        cost_estimate=cost(1),
        name="attend_back",
    )(ids, queries, key_value, key_value, cot)
    return (result[0], result[1:])


def gelu_parts(gate):
    root = 0.7978845608028654
    inner = root * (gate + 0.044715 * gate * gate * gate)
    bent = jnp.tanh(inner)
    value = 0.5 * gate * (1.0 + bent)
    slope = root * (1.0 + 3.0 * 0.044715 * gate * gate)
    return value, 0.5 * (1.0 + bent) + 0.5 * gate * (1.0 - bent * bent) * slope


def give_back(pick_ref, total_ref, share_ref, before, out):
    blocks, capacity, _ = pick_ref.shape
    for d in range(blocks):
        part = total_ref[d * capacity : (d + 1) * capacity, :]
        if share_ref is not None:
            part = part * share_ref[d]
        back = nn(pick_ref[d].T, part.astype(bf16))
        if before:
            back = back + before[d][...]
        out[d][...] = back.astype(out[d].dtype)


def flat(ref):
    value = ref[...]
    return value.reshape(-1, value.shape[-1])


def add_up(total_ref, part, step):
    @pl.when(step == 0)
    def _():
        total_ref[...] = part

    @pl.when(step != 0)
    def _():
        total_ref[...] += part


def expert_kernel(blocks, adds, pick_ref, share_ref, gate_ref, up_ref, down_ref, *refs):
    rows, refs = (refs[:blocks], refs[blocks:])
    before, refs = (refs[: blocks * adds], refs[blocks * adds :])
    out, (picked_ref, gate_pre_ref, up_pre_ref, total_ref) = (refs[:blocks], refs[blocks:])
    step = pl.program_id(0)
    capacity = pick_ref.shape[1]

    @pl.when(step == 0)
    def _():
        for d in range(blocks):
            block = nn(pick_ref[d], rows[d][...]).astype(bf16)
            picked_ref[d * capacity : (d + 1) * capacity, :] = block

    gate_pre = nn(picked_ref[...], flat(gate_ref))
    up_pre = nn(picked_ref[...], flat(up_ref))
    gate_pre_ref[...] = gate_pre
    up_pre_ref[...] = up_pre
    active = (gelu_parts(gate_pre)[0] * up_pre).astype(bf16)
    add_up(total_ref, nn(active, flat(down_ref)), step)

    @pl.when(step == pl.num_programs(0) - 1)
    def _():
        give_back(pick_ref, total_ref, share_ref, before, out)


def whole_spec(shape):
    return pl.BlockSpec(
        shape, lambda step: (0,) * len(shape), pipeline_mode=pl.Buffered(buffer_count=1)
    )


def weight_operands(weights, deep, cut):
    if len(weights) == 1:
        unit = weights[0]
        shards, tall, width = unit.shape
        specs = [
            pl.BlockSpec((shards, deep, cut), lambda step: (0, 0, 2 * step)),
            pl.BlockSpec((shards, deep, cut), lambda step: (0, 0, 2 * step + 1)),
            pl.BlockSpec(
                (shards // 2, tall - deep, width), lambda step: (step, deep // (tall - deep), 0)
            ),
        ]
        return specs, [unit, unit, unit]
    pair, down = weights
    specs = [
        pl.BlockSpec((pair.shape[0], cut), lambda step: (0, 2 * step)),
        pl.BlockSpec((pair.shape[0], cut), lambda step: (0, 2 * step + 1)),
        pl.BlockSpec((cut, down.shape[1]), lambda step: (step, 0)),
    ]
    return specs, [pair, pair, down]


def expert_call(picks, shares, rows, weights, deep, hidden, before, micros):
    blocks, capacity, _ = picks.shape
    width, cut, tall = (rows[0].shape[1], hidden // 2, blocks * capacity)
    columns = pl.BlockSpec((tall, cut), lambda step: (0, step))
    row_specs = [whole_spec(block.shape) for block in rows]
    specs, operands = weight_operands(weights, deep, cut)
    result = pl.pallas_call(
        functools.partial(expert_kernel, blocks, 1 if before else 0),
        grid=(2,),
        in_specs=[whole_spec(picks.shape), whole_spec(shares.shape)]
        + specs
        + row_specs * (2 if before else 1),
        out_specs=row_specs + [whole_spec((tall, width)), columns, columns],
        out_shape=[jax.ShapeDtypeStruct(block.shape, bf16) for block in rows]
        + [
            jax.ShapeDtypeStruct((tall, width), bf16),
            jax.ShapeDtypeStruct((tall, hidden), f32),
            jax.ShapeDtypeStruct((tall, hidden), f32),
        ],
        scratch_shapes=[pltpu.VMEM((tall, width), f32)],
        compiler_params=kernel_params(),
        cost_estimate=cost(micros),
        name="expert",
    )(picks, shares, *operands, *rows, *before)
    return (list(result[:blocks]), list(result[blocks:]))


def expert_back_kernel(
    blocks, adds, pick_ref, share_ref, gate_pre_ref, up_pre_ref, gate_ref, up_ref, down_ref, *refs
):
    rows, refs = (refs[:blocks], refs[blocks:])
    before, refs = (refs[: blocks * adds], refs[blocks * adds :])
    out, refs = (refs[:blocks], refs[blocks:])
    slots_ref, d_gate_ref, d_up_ref, active_ref, total_ref = refs
    step = pl.program_id(0)
    capacity = pick_ref.shape[1]

    @pl.when(step == 0)
    def _():
        for d in range(blocks):
            block = nn(pick_ref[d], rows[d][...]) * share_ref[d]
            slots_ref[d * capacity : (d + 1) * capacity, :] = block.astype(bf16)

    d_active = nt(slots_ref[...], flat(down_ref))
    value, slope = gelu_parts(gate_pre_ref[...])
    up_pre = up_pre_ref[...]
    d_gate = (d_active * up_pre * slope).astype(bf16)
    d_up = (d_active * value).astype(bf16)
    active_ref[...] = (value * up_pre).astype(bf16)
    d_gate_ref[...] = d_gate
    d_up_ref[...] = d_up
    add_up(total_ref, nt(d_gate, flat(gate_ref)) + nt(d_up, flat(up_ref)), step)

    @pl.when(step == pl.num_programs(0) - 1)
    def _():
        give_back(pick_ref, total_ref, None, before, out)


def expert_back_call(picks, shares, rows, kept, weights, deep, before, micros):
    _, gate_pre, up_pre = kept
    blocks, capacity, _ = picks.shape
    width, (tall, hidden) = (rows[0].shape[1], gate_pre.shape)
    cut = hidden // 2
    columns = pl.BlockSpec((tall, cut), lambda step: (0, step))
    row_specs = [whole_spec(block.shape) for block in rows]
    specs, operands = weight_operands(weights, deep, cut)
    result = pl.pallas_call(
        functools.partial(expert_back_kernel, blocks, 1 if before else 0),
        grid=(2,),
        in_specs=[whole_spec(picks.shape), whole_spec(shares.shape), columns, columns]
        + specs
        + row_specs * (2 if before else 1),
        out_specs=row_specs + [whole_spec((tall, width)), columns, columns, columns],
        out_shape=[jax.ShapeDtypeStruct(block.shape, bf16) for block in rows]
        + [jax.ShapeDtypeStruct((tall, width), bf16)]
        + [jax.ShapeDtypeStruct((tall, hidden), bf16)] * 3,
        scratch_shapes=[pltpu.VMEM((tall, width), f32)],
        compiler_params=kernel_params(),
        cost_estimate=cost(micros),
        name="expert_back",
    )(picks, shares, gate_pre, up_pre, *operands, *rows, *before)
    return (list(result[:blocks]), list(result[blocks:]))


def expert_grads_kernel(parts, deep, *refs):
    picked, slots, d_gate, d_up, active = (refs[i * parts : (i + 1) * parts] for i in range(5))
    grad_refs, turned_ref = (refs[5 * parts : -1], refs[-1])
    step = pl.program_id(0)

    def below(some):
        return jnp.concatenate([ref[...] for ref in some], axis=0)

    @pl.when(step == 0)
    def _():
        turned_ref[...] = below(picked).T

    grad_gate = nn(turned_ref[...], below(d_gate)).astype(bf16)
    grad_up = nn(turned_ref[...], below(d_up)).astype(bf16)
    grad_down = nn(below(active).T, below(slots)).astype(bf16)
    cut = grad_gate.shape[1]
    if len(grad_refs) == 1:
        unit_ref = grad_refs[0]
        shards, tall, width = unit_ref.shape
        for side in range(2):

            @pl.when(step == side)
            def _():
                left, some = (2 * side * cut, shards // 2)
                unit_ref[:, :deep, left : left + cut] = grad_gate.reshape(shards, deep, cut)
                left = left + cut
                unit_ref[:, :deep, left : left + cut] = grad_up.reshape(shards, deep, cut)
                rest = grad_down.reshape(some, tall - deep, width)
                unit_ref[side * some : (side + 1) * some, deep:, :] = rest
    else:
        grad_refs[0][:, :cut] = grad_gate
        grad_refs[0][:, cut:] = grad_up
        grad_refs[1][...] = grad_down


def expert_grads_call(picked, saved, weights, deep):
    slots, d_gate, d_up, active = zip(*saved)
    width, hidden = (picked[0].shape[1], d_gate[0].shape[1])
    cut = hidden // 2
    columns = [pl.BlockSpec((part.shape[0], cut), lambda step: (0, step)) for part in picked]
    if len(weights) == 1:
        grad_specs = [whole_spec(weights[0].shape)]
    else:
        grad_specs = [
            pl.BlockSpec((width, 2 * cut), lambda step: (0, step)),
            pl.BlockSpec((cut, width), lambda step: (step, 0)),
        ]
    return list(
        pl.pallas_call(
            functools.partial(expert_grads_kernel, len(picked), deep),
            grid=(2,),
            in_specs=[whole_spec(part.shape) for part in picked] * 2 + columns * 3,
            out_specs=grad_specs,
            out_shape=[jax.ShapeDtypeStruct(part.shape, bf16) for part in weights],
            scratch_shapes=[pltpu.VMEM((width, sum(part.shape[0] for part in picked)), bf16)],
            compiler_params=kernel_params(),
            cost_estimate=cost(1),
            name="expert_grads",
        )(*picked, *slots, *d_gate, *d_up, *active)
    )


def norm_parts(value):
    scale = lax.rsqrt(jnp.mean(value * value, axis=1, keepdims=True) + epsilon)
    return scale, value * scale


def norm_back(grad, gain, value):
    scale, scaled = norm_parts(value)
    grown = grad * gain
    back = scale * (grown - scaled * jnp.mean(scaled * grown, axis=1, keepdims=True))
    return back, (grad * scaled).astype(bf16)


def add_all(refs):
    total = refs[0][...].astype(f32)
    for ref in refs[1:]:
        total = total + ref[...].astype(f32)
    return total


def side_offsets(core_ref, steps, cut):
    step, core = (pl.program_id(0), core_ref[0])
    own = pl.multiple_of((core * steps + step) * cut, cut)
    other = pl.multiple_of(((1 - core) * steps + step) * cut, cut)
    return own, other


def dense_call(kernel, core, steps, whole, halves, out, scratch, name, micros):
    cut = halves[0].shape[1] // steps

    def keep(shape):
        return pl.BlockSpec(
            shape, lambda step, core: (0,) * len(shape), pipeline_mode=pl.Buffered(buffer_count=1)
        )

    def tile(tall):
        return pl.BlockSpec((tall, cut), lambda step, core: (0, step))

    return pl.pallas_call(
        kernel,
        grid_spec=pltpu.PrefetchScalarGridSpec(
            num_scalar_prefetch=1,
            grid=(steps,),
            in_specs=[keep(part.shape) for part in whole] + [tile(halves[0].shape[0])] * 2,
            out_specs=[
                tile(part.shape[0]) if tiled else keep(part.shape) for part, tiled in out
            ],
            scratch_shapes=scratch,
        ),
        out_shape=[part for part, _ in out],
        compiler_params=kernel_params(),
        cost_estimate=cost(micros),
        name=name,
    )(core.astype(jnp.int32).reshape(1), *whole, *halves)


def shape_of(kind, *shape):
    return jax.ShapeDtypeStruct(shape, kind)


def enter_kernel(steps, terms, core_ref, gain_ref, *refs):
    parts, (own_ref, other_ref, sent_ref, normed_ref, out_ref) = (refs[:terms], refs[terms:])
    own, other = side_offsets(core_ref, steps, own_ref.shape[1])

    @pl.when(pl.program_id(0) == 0)
    def _():
        sent = add_all(parts).astype(bf16)
        sent_ref[...] = sent
        normed_ref[...] = (norm_parts(sent.astype(f32))[1] * gain_ref[...]).astype(bf16)

    cut = own_ref.shape[1]
    out_ref[:, pl.ds(own, cut)] = nn(normed_ref[...], own_ref[...]).astype(bf16)
    out_ref[:, pl.ds(other, cut)] = nn(normed_ref[...], other_ref[...]).astype(bf16)


def enter_call(core, parts, gain, halves):
    rows, width = parts[0].shape
    return dense_call(
        functools.partial(enter_kernel, 3, len(parts)),
        core,
        3,
        [gain] + parts,
        halves,
        [
            (shape_of(bf16, rows, width), False),
            (shape_of(bf16, rows, width), False),
            (shape_of(bf16, rows, 2 * halves[0].shape[1]), False),
        ],
        [],
        "enter",
        6,
    )


def leave_kernel(steps, core_ref, gain_ref, rows_ref, attended_ref, own_ref, other_ref,
                 mid_ref, normed_ref):
    cut = own_ref.shape[1]
    for start, ref in zip(side_offsets(core_ref, steps, cut), (own_ref, other_ref)):
        part = pl.ds(start, cut)
        mid_ref[:, part] = rows_ref[:, part].astype(f32) + nn(attended_ref[...], ref[...])

    @pl.when(pl.program_id(0) == steps - 1)
    def _():
        normed_ref[...] = (norm_parts(mid_ref[...])[1] * gain_ref[...]).astype(bf16)


def leave_call(core, rows_in, attended, gain, halves):
    rows, width = rows_in.shape
    return dense_call(
        functools.partial(leave_kernel, 2),
        core,
        2,
        [gain, rows_in, attended],
        halves,
        [(shape_of(f32, rows, width), False), (shape_of(bf16, rows, width), False)],
        [],
        "leave",
        5,
    )


def leave_back_kernel(steps, terms, core_ref, gain_ref, mid_ref, cot_ref, attended_ref, *refs):
    parts, refs = (refs[:terms], refs[terms:])
    own_ref, other_ref, after_ref, term_ref, d_attended_ref, *refs = refs
    own_grad_ref, other_grad_ref, branch_ref, turned_ref, total_ref = refs
    step, cut = (pl.program_id(0), own_ref.shape[1])

    @pl.when(step == 0)
    def _():
        back, term_ref[...] = norm_back(add_all(parts), gain_ref[...], mid_ref[...])
        back = back + cot_ref[...].astype(f32)
        after_ref[...] = back
        branch_ref[...] = back.astype(bf16)
        turned_ref[...] = attended_ref[...].T

    own, other = side_offsets(core_ref, steps, cut)
    d_own, d_other = (branch_ref[:, pl.ds(own, cut)], branch_ref[:, pl.ds(other, cut)])
    own_grad_ref[...] = nn(turned_ref[...], d_own).astype(bf16)
    other_grad_ref[...] = nn(turned_ref[...], d_other).astype(bf16)
    add_up(total_ref, nt(d_own, own_ref[...]) + nt(d_other, other_ref[...]), step)

    @pl.when(step == steps - 1)
    def _():
        d_attended_ref[...] = total_ref[...].astype(bf16)


def leave_back_call(core, parts, gain, mid, cotangent, attended, halves):
    rows, width = mid.shape
    half = (halves[0].shape[0], halves[0].shape[1])
    return dense_call(
        functools.partial(leave_back_kernel, 2, len(parts)),
        core,
        2,
        [gain, mid, cotangent, attended] + parts,
        halves,
        [
            (shape_of(f32, rows, width), False),
            (shape_of(bf16, rows, width), False),
            (shape_of(bf16, rows, width), False),
            (shape_of(bf16, *half), True),
            (shape_of(bf16, *half), True),
        ],
        [
            pltpu.VMEM((rows, width), bf16),
            pltpu.VMEM((width, rows), bf16),
            pltpu.VMEM((rows, width), f32),
        ],
        "leave_back",
        8,
    )


def enter_back_kernel(steps, terms, core_ref, gain_ref, rows_ref, normed_ref, after_ref, term_ref,
                      dq_ref, *refs):
    parts, refs = (refs[:terms], refs[terms:])
    own_ref, other_ref, entry_ref, sent_ref, own_grad_ref, other_grad_ref, *refs = refs
    entered_ref, turned_ref, total_ref = refs
    step, cut = (pl.program_id(0), own_ref.shape[1])
    rows, qw = dq_ref.shape

    @pl.when(step == 0)
    def _():
        entered_ref[:, :qw] = dq_ref[...]
        wide = parts[0].shape[1]
        entered_ref[:, qw : qw + wide] = add_all(parts).astype(bf16)
        entered_ref[:, qw + wide :] = jnp.zeros((rows, gap), bf16)
        turned_ref[...] = normed_ref[...].T

    own, other = side_offsets(core_ref, steps, cut)
    d_own, d_other = (entered_ref[:, pl.ds(own, cut)], entered_ref[:, pl.ds(other, cut)])
    own_grad_ref[...] = nn(turned_ref[...], d_own).astype(bf16)
    other_grad_ref[...] = nn(turned_ref[...], d_other).astype(bf16)
    add_up(total_ref, nt(d_own, own_ref[...]) + nt(d_other, other_ref[...]), step)

    @pl.when(step == steps - 1)
    def _():
        back, attn_term = norm_back(total_ref[...], gain_ref[...], rows_ref[...].astype(f32))
        back = back + after_ref[...]
        entry_ref[...] = back
        sent_ref[...] = back.astype(bf16)
        lane = lax.broadcasted_iota(jnp.int32, (rows, 128), 1)
        sums = nn(attn_term.T, (lane == 0).astype(bf16))
        sums = (sums + nn(term_ref[...].T, (lane == 1).astype(bf16))).astype(bf16)
        left = cut - gap

        @pl.when(core_ref[0] == 0)
        def _():
            other_grad_ref[:, left : left + 128] = sums

        @pl.when(core_ref[0] != 0)
        def _():
            own_grad_ref[:, left : left + 128] = sums


def enter_back_call(core, dq, parts, gain, rows_in, normed, after, term, halves):
    rows, width = rows_in.shape
    return dense_call(
        functools.partial(enter_back_kernel, 3, len(parts)),
        core,
        3,
        [gain, rows_in, normed, after, term, dq] + parts,
        halves,
        [
            (shape_of(f32, rows, width), False),
            (shape_of(bf16, rows, width), False),
            (shape_of(bf16, *halves[0].shape), True),
            (shape_of(bf16, *halves[0].shape), True),
        ],
        [
            pltpu.VMEM((rows, 2 * halves[0].shape[1]), bf16),
            pltpu.VMEM((width, rows), bf16),
            pltpu.VMEM((rows, width), f32),
        ],
        "enter_back",
        1,
    )


def place_kernel(count, joined, index_ref, *refs):
    step = pl.program_id(0)
    for bit in range(count):

        @pl.when(step == bit)
        def _():
            if joined:
                refs[count][...] = refs[bit][...]
            else:
                refs[count][0] = refs[bit][...]


def place_call(blocks, index):
    count = len(blocks)
    shape = blocks[0].shape
    zeros = (0,) * len(shape)
    joined = len(shape) == 2 and shape[0] % 16 == 0
    if joined:
        out_spec = pl.BlockSpec(shape, lambda step, at: (at[0] ^ step, 0))
        out_shape = (count * shape[0], shape[1])
    else:
        out_spec = pl.BlockSpec((1,) + shape, lambda step, at: (at[0] ^ step,) + zeros)
        out_shape = (count,) + shape
    return pl.pallas_call(
        functools.partial(place_kernel, count, joined),
        grid_spec=pltpu.PrefetchScalarGridSpec(
            num_scalar_prefetch=1,
            grid=(count,),
            in_specs=[pl.BlockSpec(shape, lambda step, at: zeros)] * count,
            out_specs=out_spec,
        ),
        out_shape=jax.ShapeDtypeStruct(out_shape, blocks[0].dtype),
        compiler_params=kernel_params(),
        cost_estimate=cost(2),
        name="place",
    )(index.astype(jnp.int32).reshape(1), *blocks)


def deal_kernel(count, index_ref, *refs):
    step = pl.program_id(0)
    for bit in range(count):

        @pl.when(step == bit)
        def _():
            for layer, ref in enumerate(refs[count:]):
                ref[0] = refs[bit][layer]


def deal_call(blocks, index):
    count = len(blocks)
    layers, *shape = blocks[0].shape
    shape = tuple(shape)
    zeros = (0,) * len(shape)
    return pl.pallas_call(
        functools.partial(deal_kernel, count),
        grid_spec=pltpu.PrefetchScalarGridSpec(
            num_scalar_prefetch=1,
            grid=(count,),
            in_specs=[pl.BlockSpec((layers,) + shape, lambda step, at: (0,) + zeros)] * count,
            out_specs=[pl.BlockSpec((1,) + shape, lambda step, at: (at[0] ^ step,) + zeros)]
            * layers,
        ),
        out_shape=[jax.ShapeDtypeStruct((count,) + shape, blocks[0].dtype)] * layers,
        compiler_params=kernel_params(),
        cost_estimate=cost(2),
        name="deal",
    )(index.astype(jnp.int32).reshape(1), *blocks)


def order_kernel(count, order_ref, *refs):
    step = pl.program_id(0)
    for i in range(count):

        @pl.when(step == i)
        def _():
            refs[count][:, 0] = refs[i][:, 0]


def order_call(blocks, order, unit):
    count = len(blocks)
    n_ctx, _, tall, wide = blocks[0].shape
    shape = (n_ctx, 1, tall, wide)
    source = pl.BlockSpec(
        shape, lambda step, at: (0, unit, 0, 0), pipeline_mode=pl.Buffered(buffer_count=1)
    )
    result = pl.pallas_call(
        functools.partial(order_kernel, count),
        grid_spec=pltpu.PrefetchScalarGridSpec(
            num_scalar_prefetch=1,
            grid=(count,),
            in_specs=[source] * count,
            out_specs=pl.BlockSpec(shape, lambda step, at: (0, at[step], 0, 0)),
        ),
        out_shape=jax.ShapeDtypeStruct((n_ctx, count, tall, wide), bf16),
        compiler_params=kernel_params(),
        cost_estimate=cost(4),
        name="order",
    )(order.astype(jnp.int32), *blocks)
    return result.reshape(n_ctx * count, tall, wide)


def finish_kernel(deep, index_ref, own_ref, other_ref, gate_ref, up_ref, down_ref):
    side = pl.program_id(1)
    wide = gate_ref.shape[2] // 2

    def write(source):
        for half in range(2):
            left, target = (2 * half * wide, slice(half * wide, (half + 1) * wide))
            gate_ref[:, :, target] = source[0, :, :deep, left : left + wide].astype(f32)
            left = left + wide
            up_ref[:, :, target] = source[0, :, :deep, left : left + wide].astype(f32)
        down_ref[...] = source[0, :, deep:, :].astype(f32)

    @pl.when(side == index_ref[1])
    def _():
        write(own_ref)

    @pl.when(side != index_ref[1])
    def _():
        write(other_ref)


def finish_call(own, other, deep, hidden, place, core):
    n_ctx, units, tall, width = own.shape
    experts = 2 * n_ctx * units
    source = pl.BlockSpec((1, units, tall, width), lambda bit, side, at: (bit, 0, 0, 0))
    target = lambda bit, side, at: (2 * (at[0] ^ bit) + side, 0, 0)
    return pl.pallas_call(
        functools.partial(finish_kernel, deep),
        grid_spec=pltpu.PrefetchScalarGridSpec(
            num_scalar_prefetch=1,
            grid=(n_ctx, 2),
            in_specs=[source, source],
            out_specs=[
                pl.BlockSpec((units, deep, hidden), target),
                pl.BlockSpec((units, deep, hidden), target),
                pl.BlockSpec((units, tall - deep, width), target),
            ],
        ),
        out_shape=[
            jax.ShapeDtypeStruct((experts, deep, hidden), f32),
            jax.ShapeDtypeStruct((experts, deep, hidden), f32),
            jax.ShapeDtypeStruct((experts, tall - deep, width), f32),
        ],
        compiler_params=kernel_params(),
        cost_estimate=cost(8),
        name="finish",
    )(jnp.stack([place, core]).astype(jnp.int32), own, other)


def body(
    tokens,
    block_of,
    routes,
    combine,
    attn_norm,
    w_query,
    w_key,
    w_value,
    w_out,
    ffn_norm,
    w_gate,
    w_up,
    w_down,
    out_grad,
):
    rows = tokens.shape[2]
    width = tokens.shape[3]
    half = rows // 2
    n_ctx = lax.axis_size("ctx")
    n_fsdp = lax.axis_size("fsdp")
    core, place, depth = (
        lax.axis_index(axis).astype(jnp.uint32) for axis in ("section", "ctx", "fsdp")
    )
    seq_len = rows * n_ctx
    capacity = rows * TOP * 5 // (4 * EXPERTS)
    score_scale = HD ** (-0.5)
    own_experts = EXPERTS // n_ctx
    hidden = w_gate.shape[3]
    shard_rows = w_query.shape[1]
    down_rows = w_down.shape[2]
    qw = w_query.shape[2]
    kw = w_key.shape[2]
    pieces = max(1, 2 * n_ctx // EXPERTS)
    per_core = max(1, EXPERTS // (2 * n_ctx))
    unit_rows = shard_rows + down_rows
    aligned = shard_rows % 16 == 0 and down_rows % 16 == 0

    def on_core(former, latter):
        return jnp.where(core == 0, former, latter)

    def own_other(low, high):
        return (on_core(low, high), on_core(high, low))

    early, late = (range(1, n_ctx // 2 + 1), range(n_ctx // 2 + 1, n_ctx))

    def send(value, bits):
        return [swap(value, "ctx", bit) for bit in bits]

    def spread(value):
        return [value] + send(value, early) + send(value, late)

    def spread_rows(value):
        near_blocks = send(value, early)
        value, near_blocks = tie(value, near_blocks)
        return [value] + near_blocks + send(value, late)

    def gather_back(blocks):
        return [blocks[0]] + [swap(blocks[bit], "ctx", bit) for bit in range(1, n_ctx)]

    info = jnp.concatenate([routes.astype(f32), combine], axis=-1)[0, :, 0].transpose(0, 2, 1)
    info_own, info_other = (at(info, core), swap(at(info, 1 - core), "section", 1))
    info = jnp.stack(own_other(info_own, info_other))
    info = jnp.stack([info] + [swap(info, "ctx", bit) for bit in range(1, n_ctx)], axis=1)

    gain_columns = jnp.stack([attn_norm[0], ffn_norm[0]], axis=1)
    gain_columns = jnp.pad(gain_columns, ((0, 0), (0, gap - 2)))
    enter_shard = jnp.concatenate([w_query[0], w_key[0], w_value[0], gain_columns], axis=1)
    enter_cut = enter_shard.shape[1] // 2
    leave_cut = w_out.shape[2] // 2
    low_shard = jnp.concatenate([enter_shard[:, :enter_cut], w_out[0, :, :leave_cut]], axis=1)
    high_shard = jnp.concatenate([enter_shard[:, enter_cut:], w_out[0, :, leave_cut:]], axis=1)
    lent = swap(on_core(high_shard, low_shard), "section", 1)
    dense_shards = (on_core(low_shard, lent), on_core(lent, high_shard))

    def gather_deep(shard):
        blocks = [shard] + [swap(shard, "fsdp", bit) for bit in range(1, n_fsdp)]
        return place_call(blocks, depth).reshape(-1, shard.shape[1])

    def join_square(blocks):
        return place_call(blocks, place).reshape(-1, blocks[0].shape[1])

    def gather_square(deep):
        return join_square(spread(deep))

    cut = hidden // 2
    unit_stack = jnp.concatenate(
        [
            jnp.concatenate(
                [w_gate[0, ..., :cut], w_up[0, ..., :cut], w_gate[0, ..., cut:], w_up[0, ..., cut:]],
                axis=2,
            ),
            w_down[0],
        ],
        axis=1,
    )
    if pieces == 2:
        unit_stack = jnp.stack(jnp.split(unit_stack, 2, axis=2), axis=1)
    unit_stack = unit_stack.reshape(n_ctx, 2, per_core, unit_rows, width // pieces)
    units_lent = swap(at(unit_stack, 1 - core, 1), "section", 1)
    unit_stacks = jnp.stack(own_other(at(unit_stack, core, 1), units_lent), axis=1)

    def deal_units(stack):
        blocks = [at(stack, place)]
        blocks += [swap(at(stack, place ^ bit), "ctx", bit) for bit in range(1, n_ctx)]
        return deal_call(blocks, place)

    ring = list(range(0, n_fsdp, 2)) + list(range(1, n_fsdp, 2))[::-1]
    ring_steps = [(ring[i], ring[(i + 1) % n_fsdp]) for i in range(n_fsdp)]
    ring_table = [[ring[ring.index(z) - i] for i in range(n_fsdp)] for z in range(n_fsdp)]
    behind_here = at(jnp.array(ring_table, jnp.uint32), depth)

    def ring_send(moved):
        return [blocks + [lax.ppermute(blocks[-1], "fsdp", ring_steps)] for blocks in moved]

    def own_units(blocks):
        return [order_call(blocks, behind_here, unit) for unit in range(per_core)]

    def pair_units(mine):
        other = [swap(part, "section", 1) for part in mine]
        units = list(mine) + other
        if pieces == 2:
            units = [jnp.concatenate(own_other(mine[0], other[0]), axis=2)]
        if aligned:
            return [[unit] for unit in units]
        return [
            [unit[:, :shard_rows].reshape(-1, width), unit[:, shard_rows:].reshape(-1, width)]
            for unit in units
        ]

    def cut_units(grads):
        if aligned:
            units = [unit for (unit,) in grads]
        else:
            units = [
                jnp.concatenate(
                    [part.reshape(n_ctx * n_fsdp, -1, width) for part in parts], axis=1
                )
                for parts in grads
            ]
        if pieces == 1:
            return (units[:per_core], units[per_core:])
        own, other = own_other(*jnp.split(units[0], 2, axis=2))
        return ([own], [other])

    def ring_part(terms, behind):
        spot = behind_here[behind % n_fsdp]
        return sum(at(term, spot, 1).astype(f32) for term in terms)

    def ring_start(own, received):
        terms = [part.reshape((n_ctx, n_fsdp) + part.shape[1:]) for part in (own, received)]
        return (terms, ring_part(terms, 1).astype(bf16))

    def ring_move(state):
        return [(terms, lax.ppermute(moving, "fsdp", ring_steps)) for terms, moving in state]

    def ring_add(state, step):
        return [
            (terms, (moved.astype(f32) + ring_part(terms, step + 1)).astype(bf16))
            for terms, moved in state
        ]

    def ring_step(state, step):
        return ring_add(ring_move(state), step)

    def ring_last(state):
        state = ring_add(state, 2)
        for step in range(3, n_fsdp - 1):
            state = ring_step(state, step)
        return ring_move(state)

    def ring_rest(state, first):
        for step in range(first, n_fsdp):
            state = ring_step(state, step)
        return [moving for _, moving in state]

    def scatter_units(moved):
        whole = jnp.stack(moved, axis=1)
        blocks = [at(whole, place)]
        blocks += [swap(at(whole, place ^ bit), "ctx", bit) for bit in range(1, n_ctx)]
        return jnp.stack(blocks)

    def trade_square(own, received, bits):
        own, received = (part.reshape(n_ctx, -1, part.shape[1]) for part in (own, received))

        def part(bit):
            return at(own, place ^ bit).astype(f32) + at(received, place ^ bit).astype(f32)

        return [part(bit) if bit == 0 else swap(part(bit).astype(bf16), "ctx", bit) for bit in bits]

    def sum_square(parts):
        return sum(part.astype(f32) for part in parts).astype(bf16)

    def send_deep(mine):
        mine = mine.reshape(n_fsdp, shard_rows, -1)
        parts = [swap(at(mine, depth ^ bit), "fsdp", bit) for bit in range(1, n_fsdp)]
        return [at(mine, depth)] + parts

    def reduce_deep(mine):
        return sum(part.astype(f32) for part in send_deep(mine))

    if pieces == 1:
        units_here = jnp.arange(per_core, dtype=jnp.uint32)
        units_here = jnp.concatenate(
            [core * per_core + units_here, (1 - core) * per_core + units_here]
        )
    else:
        units_here = jnp.zeros((1,), jnp.uint32)
    named = (place * own_experts + units_here).astype(f32)
    matches = info[:, None, :, :TOP] == named[None, :, None, None, None]
    hits = jnp.any(matches, axis=3)
    shares = jnp.sum(jnp.where(matches, info[:, None, :, TOP:], 0.0), axis=3)
    earlier = jnp.arange(rows)[:, None] < jnp.arange(rows)[None, :]
    rank = dot("ledr,rq->ledq", hits.astype(bf16), earlier.astype(bf16))
    slots = jnp.arange(capacity, dtype=f32)
    picks = hits[:, :, :, None, :] & (rank[:, :, :, None, :] == slots[:, None])
    slot_shares = jnp.sum(jnp.where(picks, shares[:, :, :, None, :], 0.0), axis=-1, keepdims=True)
    picks = picks.astype(bf16)

    order = place.astype(jnp.int32) ^ jnp.arange(n_ctx, dtype=jnp.int32)
    block_ids = jnp.take(block_of.reshape(n_ctx, 2), order, axis=0)
    block_ids = block_ids.reshape(-1)

    def gains_of(halves):
        pair = on_core(halves[1][:, -gap : 2 - gap], halves[0][:, -gap : 2 - gap])
        pair = pair.astype(f32).T
        return (pair[:1], pair[1:])

    near = 1 + len(early)
    parts = (slice(0, near), slice(near, n_ctx))

    def experts(layer, blocks, weights, answer, beside_near=tuple, beside_far=None):
        kept, arrived = ({}, [])
        back = {}
        for index, part in enumerate(parts):
            rows_here = blocks[part]
            if index:
                back[0], rows_here, found = tie(back[0], rows_here, beside_near())
                if answer:
                    arrived = [swap(block, "ctx", bit) for bit, block in zip(early, back[0][1:])]
            back[index] = []
            for j in range(own_experts):
                back[index], kept[index, j] = expert_call(
                    picks[layer, j, part],
                    slot_shares[layer, j, part],
                    rows_here,
                    weights[j],
                    shard_rows,
                    hidden,
                    back[index],
                    3 if index == 0 else 1,
                )
        if not answer:
            return (back[0] + back[1], kept)
        back[1], arrived, far = tie(back[1], arrived, beside_far(found))
        arrived += [swap(block, "ctx", bit) for bit, block in zip(late, back[1])]
        return (back[0][:1] + arrived, kept, found, far)

    def experts_back(layer, blocks, weights, kept, delay, beside_near, beside_far, beside_end):
        back, saved = ({}, {})
        for index, part in enumerate(parts):
            rows_here = blocks[part]
            if index:
                back[0], rows_here, found_near = tie(back[0], rows_here, beside_near())
                arrived = [swap(block, "ctx", bit) for bit, block in zip(early, back[0][1:])]
            back[index] = []
            for j in range(own_experts):
                back[index], saved[index, j] = expert_back_call(
                    picks[layer, j, part],
                    slot_shares[layer, j, part],
                    rows_here,
                    kept[index, j],
                    weights[j],
                    shard_rows,
                    back[index],
                    4 if index == 0 else 1,
                )
        back[1], arrived, saved, found_far = tie(back[1], arrived, saved, beside_far(found_near))
        arrived += [swap(block, "ctx", bit) for bit, block in zip(late, back[1])]

        def grads_of(j, saved):
            picked = [kept[index, j][0] for index in range(2)]
            both = [saved[index, j] for index in range(2)]
            return expert_grads_call(picked, both, weights[j], shard_rows)

        now = [j for j in reversed(range(own_experts)) if not delay or j >= per_core]
        grads = {j: grads_of(j, saved) for j in now}
        arrived, grads, found_end = tie(arrived, grads, beside_end(found_far))
        returned = back[0][:1] + arrived
        if len(now) == own_experts:
            own, other = cut_units([grads[j] for j in range(own_experts)])
            received = [swap(part, "section", 1) for part in other]
            return (returned, lambda earlier: (own, received), found_end)
        received = [swap(grads[j][0], "section", 1) for j in reversed(now)]

        def finish(earlier):
            ready = after(saved, earlier)
            return ([grads_of(j, ready)[0] for j in range(per_core)], received)

        return (returned, finish, found_end)

    def keep_own(first, second):
        other = swap(on_core(second, first), "section", 1)
        return own_other(on_core(first, second), other)

    dense_first, dense_second = dense_shards
    deep = gather_deep(jnp.concatenate([dense_first, dense_second[:, :enter_cut]], axis=1))
    dealt_first, dealt_second = deal_units(unit_stacks)
    deep, dealt_first, dealt_second, picks, dense_second = tie(
        deep, dealt_first, dealt_second, picks, dense_second
    )
    dense_blocks, moved, leave_shard, enter_shard = tie(
        spread(deep[:, :enter_cut]),
        ring_send([[dealt_first]]),
        deep[:, enter_cut : enter_cut + leave_cut],
        deep[:, enter_cut + leave_cut :],
    )
    leave_blocks = [leave_shard] + send(leave_shard, early)
    enter_own = join_square(dense_blocks)
    enter_first = (enter_own, swap(enter_own, "section", 1))

    first_gains = gains_of(enter_first)
    first_in = after(at(tokens, core)[0], slot_shares)
    _, first_normed, first_entered = enter_call(core, [first_in], first_gains[0], enter_first)
    first_entered, leave_blocks = tie(first_entered, leave_blocks)
    key_value = first_entered[:, qw : qw + 2 * kw]
    first_kv, leave_shard = tie(jnp.concatenate(spread(key_value)), leave_shard)
    first_attended = attend_call(block_ids, first_entered, first_kv)
    moved = ring_send(moved)
    first_attended, leave_blocks, dealt_second, moved, enter_shard, dense_second = tie(
        first_attended,
        leave_blocks + send(leave_shard, late),
        dealt_second,
        moved,
        enter_shard,
        dense_second,
    )
    enter_blocks = [enter_shard] + send(enter_shard, early)
    for _ in range(2, n_fsdp - 1):
        moved = ring_send(moved)
    leave_own = join_square(leave_blocks)
    leave_first = (leave_own, swap(leave_own, "section", 1))
    first_mid, ffn_normed = leave_call(core, first_in, first_attended, first_gains[1], leave_first)
    blocks = spread_rows(ffn_normed)
    blocks[:near], moved, dealt_second, enter_shard, leave_shard, enter_blocks = tie(
        blocks[:near], moved, dealt_second, enter_shard, dense_second[:, enter_cut:], enter_blocks
    )
    first_weights = pair_units(own_units(moved[0]))
    returned, first_kept, leave_shard, (enter_blocks, dealt_second) = experts(
        0,
        blocks,
        first_weights,
        True,
        lambda: gather_deep(leave_shard),
        lambda found: (enter_blocks + send(enter_shard, late), dealt_second),
    )
    moved = ring_send([[dealt_second]])
    returned, leave_shard = tie(returned, leave_shard)
    enter_own = join_square(enter_blocks)
    enter_second = (enter_own, swap(enter_own, "section", 1))
    leave_blocks = [leave_shard] + send(leave_shard, early)

    second_gains = gains_of(enter_second)
    second_in, second_normed, second_entered = enter_call(
        core, [first_mid] + returned, second_gains[0], enter_second
    )
    second_entered, leave_blocks, moved = tie(second_entered, leave_blocks, moved)
    moved = ring_send(moved)
    key_value = second_entered[:, qw : qw + 2 * kw]
    for _ in range(4, n_fsdp):
        moved = ring_send(moved)
    second_kv, leave_shard = tie(jnp.concatenate(spread(key_value)), leave_shard)
    second_attended = attend_call(block_ids, second_entered, second_kv)
    second_attended, leave_blocks, moved = tie(
        second_attended, leave_blocks + send(leave_shard, late), moved
    )
    moved = ring_send(moved)
    leave_own = join_square(leave_blocks)
    leave_second = (leave_own, swap(leave_own, "section", 1))
    second_mid, ffn_normed = leave_call(
        core, second_in, second_attended, second_gains[1], leave_second
    )
    blocks = spread_rows(ffn_normed)
    blocks[:near], moved = tie(blocks[:near], moved)
    second_weights = pair_units(own_units(moved[0]))
    second_returned, second_kept = experts(1, blocks, second_weights, False)
    cotangent = after(at(out_grad, core)[0], second_returned[:near])
    cot_blocks = spread_rows(cotangent)
    cot_blocks[:near], second_returned[near:] = tie(cot_blocks[:near], second_returned[near:])

    returned, finish, (second_returned, near_parts) = experts_back(
        1,
        cot_blocks,
        second_weights,
        second_kept,
        False,
        lambda: second_returned,
        lambda found: found,
        lambda found: (found, [swap(found[bit], "ctx", bit) for bit in early]),
    )
    far_parts = [swap(second_returned[bit], "ctx", bit) for bit in late]
    units_moving = [ring_start(*pair) for pair in zip(*finish(()))]
    after_rows, term, d_attended, *grads = leave_back_call(
        core,
        returned,
        second_gains[1],
        second_mid,
        cotangent,
        second_attended,
        leave_second,
    )
    leave_grads = (grads[0], swap(grads[1], "section", 1))
    d_queries, d_key_value = attend_back_call(block_ids, second_entered, second_kv, d_attended)
    d_queries, d_key_value, leave_grads, far_parts = tie(
        d_queries, d_key_value, leave_grads, far_parts
    )
    second_parts = second_returned[:1] + near_parts + far_parts
    second_out = second_mid + sum(part.astype(f32) for part in second_parts)
    d_key_value, units_moving = tie(gather_back(d_key_value), ring_move(units_moving))
    units_moving = ring_move(ring_add(units_moving, 1))
    leave_parts = trade_square(*leave_grads, range(n_ctx))
    second_entry, cotangent, *grads = enter_back_call(
        core,
        d_queries,
        d_key_value,
        second_gains[0],
        second_in,
        second_normed,
        after_rows,
        term,
        enter_second,
    )
    cotangent, grads, leave_parts, layer_rows = tie(
        cotangent, grads, leave_parts, (second_in, second_out.astype(bf16))
    )
    enter_grads = (grads[0], swap(grads[1], "section", 1))

    blocks = spread_rows(cotangent)
    blocks[:near], enter_grads, layer_rows = tie(blocks[:near], enter_grads, layer_rows)

    def dense_sums(parts):
        moving = [sum_square(some) for some in (parts, leave_parts)]
        return reduce_deep(jnp.concatenate(moving, axis=1))

    returned, finish, (units_moving, layer_outs, second_dense) = experts_back(
        0,
        blocks,
        first_weights,
        first_kept,
        False,
        lambda: (units_moving, trade_square(*enter_grads, [0, *early]), enter_grads),
        lambda found: (
            ring_last(found[0]),
            keep_own(*layer_rows),
            found[1] + trade_square(*found[2], late),
        ),
        lambda found: (found[0], found[1], dense_sums(found[2])),
    )
    second_moved = [moving for _, moving in ring_add(units_moving, n_fsdp - 1)]
    own, received = finish(())
    after_rows, term, d_attended, *grads = leave_back_call(
        core,
        returned,
        first_gains[1],
        first_mid,
        cotangent,
        first_attended,
        leave_first,
    )
    units_moving = [ring_start(*pair) for pair in zip(own, received)]
    leave_grads = (grads[0], swap(grads[1], "section", 1))
    d_queries, d_key_value = attend_back_call(block_ids, first_entered, first_kv, d_attended)
    d_queries, d_key_value, leave_grads = tie(d_queries, d_key_value, leave_grads)
    d_key_value, leave_grads = tie(gather_back(d_key_value), leave_grads)
    leave_parts = trade_square(*leave_grads, [0, *early])
    first_entry, _, *grads = enter_back_call(
        core,
        d_queries,
        d_key_value,
        first_gains[0],
        first_in,
        first_normed,
        after_rows,
        term,
        enter_first,
    )
    grads, leave_parts, leave_grads, units_moving, second_moved = tie(
        grads, leave_parts, leave_grads, ring_move(units_moving), second_moved
    )
    enter_grads = (grads[0], swap(grads[1], "section", 1))
    enter_parts, units_moving = tie(
        trade_square(*enter_grads, [0, *early]), ring_move(ring_add(units_moving, 1))
    )
    enter_parts, leave_parts, first_entry = tie(
        enter_parts + trade_square(*enter_grads, late),
        leave_parts + trade_square(*leave_grads, late),
        first_entry,
    )
    first_moving = [sum_square(parts) for parts in (enter_parts, leave_parts)]
    first_dense, scattered = tie(
        send_deep(jnp.concatenate(first_moving, axis=1)),
        scatter_units(ring_rest(ring_add(units_moving, 2), 3) + second_moved),
    )
    first_scattered, second_scattered = (scattered[:, :per_core], scattered[:, per_core:])
    first_dense = sum(part.astype(f32) for part in first_dense)

    layer_out = jnp.stack(layer_outs)
    input_grads = jnp.stack(keep_own(first_entry, second_entry))
    low_dense, high_dense = keep_own(first_dense, second_dense)
    enter_grad = jnp.concatenate([low_dense[:, :enter_cut], high_dense[:, :enter_cut]], axis=1)
    grad_out = jnp.concatenate([low_dense[:, enter_cut:], high_dense[:, enter_cut:]], axis=1)
    grad_gains = enter_grad[:, qw + 2 * kw :]
    mine = on_core(first_scattered, second_scattered)
    other = swap(on_core(second_scattered, first_scattered), "section", 1)
    if aligned and pieces == 1:
        grad_gate, grad_up, grad_down = finish_call(mine, other, shard_rows, hidden, place, core)
    else:
        sides = [jnp.take(part, order, axis=0) for part in own_other(mine, other)]
        if pieces == 1:
            whole = jnp.stack(sides, axis=1).reshape(EXPERTS, unit_rows, width)
        else:
            whole = jnp.concatenate([side[:, 0] for side in sides], axis=2)
        pairs = whole[:, :shard_rows].astype(f32).reshape(EXPERTS, shard_rows, 2, 2, cut)
        grad_gate = pairs[:, :, :, 0].reshape(EXPERTS, shard_rows, hidden)
        grad_up = pairs[:, :, :, 1].reshape(EXPERTS, shard_rows, hidden)
        grad_down = whole[:, shard_rows:].astype(f32)
    return (
        layer_out[None, :, None],
        input_grads[None, :, None],
        grad_gains[:, 0][None],
        enter_grad[:, :qw][None],
        enter_grad[:, qw : qw + kw][None],
        enter_grad[:, qw + kw : qw + 2 * kw][None],
        grad_out[None],
        grad_gains[:, 1][None],
        grad_gate[None],
        grad_up[None],
        grad_down[None],
    )


def solution(mesh):
    rows_placed = P(None, "fsdp", "ctx", None)
    kept_placed = P("section", None, "fsdp", "ctx", None)
    gain_placed = P("section", ("ctx", "fsdp"))
    dense_placed = P("section", ("ctx", "fsdp"), None)
    expert_placed = P("section", None, ("ctx", "fsdp"), None)
    dense_all = (dense_placed,) * 4
    expert_all = (expert_placed,) * 3
    layer_placed = (gain_placed,) + dense_all + (gain_placed,) + expert_all
    return jax.shard_map(
        body,
        mesh=mesh,
        in_specs=(rows_placed, P(), kept_placed, kept_placed) + layer_placed + (rows_placed,),
        out_specs=(kept_placed, kept_placed) + layer_placed,
        check_vma=False,
    )
```
